32 devices in a mesh: seq: 16 (over z, y, x), exp: 2 (over core).
Axes of the slice: x: 2, y: 2, z: 4, core: 2. Of those that a mesh axis runs over, the one named last changes fastest.
Arguments:
- x_in: bfloat16 [1024, 8192], P('seq', 'exp'), may hold values from -6 to 6
- z_gate: bfloat16 [1024, 8192], P('seq', 'exp'), may hold values from -6 to 6
- dt_low: bfloat16 [1024, 256], P('seq'), may hold values from -6 to 6
- dt_weight: bfloat16 [256, 8192], P(None, 'exp'), may hold values from -0.375 to 0.375
- dt_bias: float32 [8192], P('exp'), may hold values from -9 to -1
- a_log: float32 [16, 8192], P(None, 'exp'), may hold values from -4 to 0
- conv_weight: float32 [4, 8192], P(None, 'exp'), may hold values from -3 to 3
- conv_bias: float32 [8192], P('exp'), may hold values from -0.5 to 0.5
- d_skip: float32 [8192], P('exp'), may hold values from 0.5 to 1.5
- b_and_c: float32 [2, 16, 1024], P(None, None, 'seq'), may hold values from -6 to 6
- hidden: bfloat16 [1024, 4096], P('seq', 'exp'), may hold values from -6 to 6
- router: bfloat16 [4096, 8], P('exp'), may hold values from -0.09375 to 0.09375
- expert_ids: int32 [1024, 2], P('seq'), may hold values from 0 to 7, all different within a row; in each aligned block of 64 rows (0 to 63, 64 to 127, ...) at most 18 rows name the same one
- w_gate: bfloat16 [4096, 98304], P('exp', 'seq'), may hold values from -0.09375 to 0.09375
- w_down: bfloat16 [98304, 4096], P('seq', 'exp'), may hold values from -0.0546875 to 0.0546875
Outputs:
- mamba_out: bfloat16 [1024, 8192], P('seq', 'exp')
- moe_out: bfloat16 [1024, 4096], P('seq', 'exp')
The draws below stay inside these ranges and needn't reach their ends.
Inputs may be any that keep to these rules, and one draw needn't show every extreme that they name: `expert_ids`: each token names 2 different experts; among the 64 tokens of one block no expert is named more than 18 times, a bound that some expert reaches in every block.
All inputs are finite; a program needn't handle non-finite values.
Results may differ from the reference program's by a relative error of at most 0.018.
Values may be sent and summed in bfloat16 or wider, within the bound.
No kernel may reach another device: no remote copies, remote signals or barrier semaphores. Data moves between devices by JAX's collectives and lax.ppermute only.
A program may use at most 128 MiB of HBM per device.

```python
import math
import jax
import jax.numpy as jnp
import numpy as np
from jax import lax

D = 4096
INNER = 8192
STATE = 16
CONV = 4
RANK = 256
EXPERTS = 8
TOPK = 2
FF = 12288
TOK_DEV = 64
CAP = 18
TOKENS = 1024
N_SEQ = 16
N_EXP = 2


def levels(own_key, dims, pieces, low, high):
    gain = 1.0
    for axis_at, blocks in pieces:
        draws = jax.random.uniform(jax.random.fold_in(jax.random.fold_in(own_key, 6), axis_at), (blocks,), jnp.float32, low / len(pieces), high / len(pieces))
        gain = gain * jnp.repeat(jnp.exp(draws), dims[axis_at] // blocks).reshape((-1,) + (1,) * (len(dims) - 1 - axis_at))
    return gain


def shared_out(stream_key, own, number, rows, amount, top, reach, skew):
    ranking = jax.random.permutation(stream_key, amount)
    crowded, common = portions_of(amount, rows * top, reach, skew, True), portions_of(amount, rows * top, reach, skew, False)
    places = jnp.arange(amount)

    def named(sizes, offset_by):
        used = int((sizes > 0).sum())
        fixed = max(1, used // 4)
        moved = fixed + (places - fixed + offset_by * (used - fixed)) % max(1, amount - fixed)
        return jnp.zeros((amount,), jnp.int32).at[ranking[jnp.where(places < fixed, places, moved)]].set(jnp.asarray(sizes, jnp.int32))

    sizes = jnp.where(number % 4 == 0, named(crowded, number // 4), named(common, number - number // 4 - 1))
    mixed = jax.random.permutation(jax.random.fold_in(own, 3), amount)
    donor, sink = mixed[0:amount // 2 * 2:2], mixed[1:amount // 2 * 2:2]
    room = jnp.minimum(sizes[donor] - 1, reach - sizes[sink]) // 2
    room = jnp.where((donor == ranking[0]) | (sink == ranking[0]) | (sizes[sink] == 0), 0, jnp.maximum(room, 0))
    moved = jax.random.randint(jax.random.fold_in(own, 4), (amount // 2,), 0, 1 << 20) % (room + 1)
    sizes = sizes.at[donor].add(-moved).at[sink].add(moved)
    labels = jnp.searchsorted(jnp.cumsum(sizes), jnp.arange(rows * top), side="right").astype(jnp.int32)
    table = labels.reshape(top, rows).T
    table = table[jax.random.permutation(jax.random.fold_in(own, 1), rows)]
    offset_by = jax.random.randint(jax.random.fold_in(own, 2), (rows, 1), 0, top)
    return jnp.take_along_axis(table, (jnp.arange(top)[None, :] + offset_by) % top, axis=1)


def portions_of(number_of, total, reach, slope, full):
    loads = [(1 << 20) // math.isqrt(grade ** slope) + 1 for grade in range(1, number_of + 1)]
    largest = reach if full else min(reach, max(-(-total // number_of), total * loads[0] // sum(loads)))
    least = 1 if total - largest >= number_of - 1 else 0
    holding, spare = [largest] + [least] * (number_of - 1), total - largest - least * (number_of - 1)
    while spare > 0:
        movable = [i for i in range(1, number_of) if holding[i] < largest] or [i for i in range(1, number_of) if holding[i] < reach]
        mass, budget = sum([loads[i] for i in movable]), spare
        for i in movable:
            extra = min(reach - holding[i], max(1, budget * loads[i] // mass), spare)
            holding[i] = holding[i] + extra
            spare = spare - extra
    return np.array(holding)


def gaussian(rng, shape, deviation, reach, shards=(), kind=jnp.bfloat16):
    result = deviation * jax.random.normal(rng, shape, jnp.float32)
    if shards:
        result = result * levels(rng, shape, shards, -0.22, 0.18)
    return jnp.clip(result, -reach, reach).astype(kind)


def setup_inputs(seed: int = 0) -> dict:
    key_of = jax.random.split(jax.random.key(seed), 16)
    x_in = gaussian(key_of[0], (TOKENS, INNER), 1.0, 6.0, ((0, 16), (1, 2)))
    z_gate = gaussian(key_of[1], (TOKENS, INNER), 1.0, 6.0, ((0, 16), (1, 2)))
    dt_low = gaussian(key_of[2], (TOKENS, RANK), 1.0, 6.0, ((0, 16),))
    dt_weight = gaussian(key_of[3], (RANK, INNER), RANK ** -0.5, 0.375, ((1, 2),))
    dt_bias = jnp.clip(-9.0 + 8.0 * jax.random.uniform(key_of[4], (INNER,), jnp.float32) ** levels(key_of[4], (INNER,), ((0, 2),), -0.2, 0.2), -9.0, -1.0)
    a_log = jnp.clip(-4.0 + 4.0 * jax.random.uniform(key_of[5], (STATE, INNER), jnp.float32) ** levels(key_of[5], (STATE, INNER), ((1, 2),), -0.2, 0.2), -4.0, 0.0)
    conv_weight = gaussian(key_of[6], (CONV, INNER), CONV ** -0.5, 3.0, ((1, 2),), jnp.float32)
    conv_bias = jnp.clip(jax.random.uniform(key_of[7], (INNER,), jnp.float32, -0.5, 0.5) * levels(key_of[7], (INNER,), ((0, 2),), -0.4, 0.0), -0.5, 0.5)
    d_skip = jnp.clip(0.5 + 1.0 * jax.random.uniform(key_of[8], (INNER,), jnp.float32) ** levels(key_of[8], (INNER,), ((0, 2),), -0.2, 0.2), 0.5, 1.5)
    b_and_c = gaussian(key_of[9], (2, STATE, TOKENS), 1.0, 6.0, ((2, 16),), jnp.float32)
    hidden = gaussian(key_of[10], (TOKENS, D), 1.0, 6.0, ((0, 16), (1, 2)))
    router = gaussian(key_of[11], (D, EXPERTS), D ** -0.5, 0.09375, ((0, 2),))
    expert_ids_keys = jax.random.split(jax.random.fold_in(key_of[12], 1), TOKENS // TOK_DEV)
    expert_ids_turns = jax.random.permutation(jax.random.fold_in(key_of[12], 3), TOKENS // TOK_DEV)
    expert_ids = jax.vmap(lambda own, number: shared_out(jax.random.fold_in(key_of[12], 2), own, number, TOK_DEV, EXPERTS, TOPK, CAP, 2))(expert_ids_keys, expert_ids_turns).reshape((TOKENS, TOPK))
    w_gate = gaussian(key_of[13], (D, EXPERTS * FF), D ** -0.5, 0.09375, ((0, 2), (1, 16)))
    w_down = gaussian(key_of[14], (EXPERTS * FF, D), FF ** -0.5, 0.0546875, ((0, 16), (1, 2)))
    return dict(x_in=x_in, z_gate=z_gate, dt_low=dt_low, dt_weight=dt_weight, dt_bias=dt_bias, a_log=a_log, conv_weight=conv_weight, conv_bias=conv_bias, d_skip=d_skip, b_and_c=b_and_c, hidden=hidden, router=router, expert_ids=expert_ids, w_gate=w_gate, w_down=w_down)


def reference(x_in, z_gate, dt_low, dt_weight, dt_bias, a_log, conv_weight, conv_bias, d_skip, b_and_c, hidden, router, expert_ids, w_gate, w_down):
    padded = jnp.concatenate([jnp.zeros((CONV - 1, INNER), jnp.float32), x_in.astype(jnp.float32)], axis=0)
    convolved = jnp.zeros((TOKENS, INNER), jnp.float32) + conv_bias[None, :]
    for offset in range(CONV):
        convolved = convolved + conv_weight[offset][None, :] * padded[offset:offset + TOKENS]
    activated = jax.nn.silu(convolved)
    delta = jax.nn.softplus(jnp.dot(dt_low, dt_weight, preferred_element_type=jnp.float32) + dt_bias[None, :])
    rates = -jnp.exp(a_log)

    def advance(state, inputs):
        step_delta, step_x, step_b, step_c = inputs
        state = jnp.exp(step_delta[None, :] * rates) * state + step_b[:, None] * (step_delta * step_x)[None, :]
        return state, jnp.sum(step_c[:, None] * state, axis=0)

    start_state = jnp.zeros((STATE, INNER), jnp.float32)
    final_state, readout = lax.scan(advance, start_state, (delta, activated, b_and_c[0].T, b_and_c[1].T))
    mamba_out = ((readout + d_skip[None, :] * activated) * jax.nn.silu(z_gate.astype(jnp.float32))).astype(jnp.bfloat16)

    logits = jnp.dot(hidden, router, preferred_element_type=jnp.float32)
    picked = jnp.take_along_axis(logits, expert_ids, axis=1)
    gates = jax.nn.sigmoid(picked - picked[:, ::-1])
    blocks = expert_ids.reshape(N_SEQ, TOK_DEV * TOPK)
    onehot = (blocks[:, :, None] == jnp.arange(EXPERTS, dtype=jnp.int32)[None, None, :]).astype(jnp.int32)
    before = (jnp.cumsum(onehot, axis=1) - onehot).astype(jnp.int32)
    slots = jnp.sum(before * onehot, axis=2).astype(jnp.int32).reshape(TOKENS, TOPK)
    block_of = (jnp.arange(TOKENS, dtype=jnp.int32) // TOK_DEV)[:, None]
    rows_at = (block_of * CAP + slots).astype(jnp.int32)
    token_index = jnp.broadcast_to(jnp.arange(TOKENS, dtype=jnp.int32)[:, None], (TOKENS, TOPK))
    table = jnp.zeros((EXPERTS, N_SEQ * CAP), jnp.int32).at[expert_ids.reshape(-1), rows_at.reshape(-1)].set(token_index.reshape(-1))
    filled = jnp.zeros((EXPERTS, N_SEQ * CAP), jnp.bool_).at[expert_ids.reshape(-1), rows_at.reshape(-1)].set(True)
    slice_width = D // N_EXP

    def one_expert(index):
        routed = jnp.where(filled[index][:, None], hidden[table[index]], jnp.zeros((), jnp.bfloat16))
        gate_cols = lax.dynamic_slice_in_dim(w_gate, index * FF, FF, 1)
        split_in = routed.astype(jnp.float32).reshape(N_SEQ * CAP, N_EXP, slice_width)
        split_w = gate_cols.astype(jnp.float32).reshape(N_EXP, slice_width, FF)
        parts = jnp.einsum("rqd,qdf->rqf", split_in, split_w).astype(jnp.bfloat16)
        parts = lax.optimization_barrier(parts).astype(jnp.float32)
        acted = jax.nn.silu(jnp.sum(parts, axis=1)).astype(jnp.bfloat16)
        down_rows = lax.dynamic_slice_in_dim(w_down, index * FF, FF, 0)
        return jnp.dot(acted.astype(jnp.float32), down_rows.astype(jnp.float32), preferred_element_type=jnp.float32)

    expert_out = lax.map(one_expert, jnp.arange(EXPERTS, dtype=jnp.int32))
    chosen = expert_out[expert_ids, rows_at]
    moe_out = jnp.sum(gates[:, :, None] * chosen, axis=1).astype(jnp.bfloat16)
    return mamba_out, moe_out
```

```python
import functools
import math

import jax
import jax.numpy as jnp
from jax import lax
from jax.experimental import pallas as pl
from jax.experimental.pallas import tpu as pltpu
from jax.sharding import PartitionSpec as P

CAP = 18
MIB = 1 << 20
LOG2E = math.log2(math.e)
F32 = jnp.float32
BF16 = jnp.bfloat16
GATE_PARTS = 2


def params(limit):
    return pltpu.CompilerParams(vmem_limit_bytes=limit * MIB)


def cost(flops, moved, transcendentals=0):
    return pl.CostEstimate(
        flops=int(flops), bytes_accessed=int(moved), transcendentals=int(transcendentals)
    )


def iota(shape, dim):
    return lax.broadcasted_iota(jnp.int32, shape, dim)


def dot(a, b):
    return jnp.dot(a, b, preferred_element_type=F32)


def dot_nt(a, b):
    return lax.dot_general(a, b, (((1,), (1,)), ((), ())), preferred_element_type=F32)


def packing(features):
    main = CAP // 16 * 16
    extra = CAP - main
    cuts = main // extra if extra and main % extra == 0 else 0
    if cuts and features % (cuts * 128) == 0:
        return main, extra, cuts, features // cuts
    return -(-CAP // 16) * 16, 0, 0, 0


def hits_and_slots(ids, experts):
    tokens = ids.shape[1]
    of = iota((experts, tokens), 0)
    hits = [(of == ids[k : k + 1]).astype(F32) for k in range(2)]
    before = (iota((tokens, tokens), 0) < iota((tokens, tokens), 1)).astype(BF16)
    earlier = dot((hits[0] + hits[1]).astype(BF16), before)
    slots = [jnp.sum(h * earlier, axis=0, keepdims=True).astype(jnp.int32) for h in hits]
    return hits, slots


def route_kernel(pack, ids_ref, hidden_ref, router_ref, out_ref, logits_ref):
    main, extra, cuts, width = pack
    experts, copies = out_ref.shape[:2]
    tokens, features = hidden_ref.shape
    ids = ids_ref[...]
    _, slots = hits_and_slots(ids, experts)
    hidden = hidden_ref[...]
    row = iota((experts * main, tokens), 0)
    picked = None
    for k in range(2):
        key = jnp.where(slots[k] < main, ids[k : k + 1] * main + slots[k], -1)
        hit = row == key
        picked = hit if picked is None else picked | hit
    packed = dot(picked.astype(BF16), hidden).astype(BF16)
    for e in range(experts):
        for m in range(copies):
            out_ref[e, m, :, :features] = packed[e * main : (e + 1) * main]
    if extra:
        picked = None
        for k in range(2):
            key = jnp.where(slots[k] >= main, ids[k : k + 1] * extra + slots[k] - main, -1)
            hit = row // cuts == key
            picked = hit if picked is None else picked | hit
        total = None
        for c in range(cuts):
            chosen = (picked & (row % cuts == c)).astype(BF16)
            part = dot(chosen, hidden[:, c * width : (c + 1) * width])
            total = part if total is None else total + part
        total = total.astype(BF16)
        for e in range(experts):
            for m in range(copies):
                out_ref[e, m, :, features:] = total[e * main : (e + 1) * main]
    logits_ref[...] = dot_nt(hidden, router_ref[...])


def route(ids, hidden, router, copies, pack):
    main, _, _, width = pack
    tokens, features = hidden.shape
    experts = router.shape[0]
    return pl.pallas_call(
        functools.partial(route_kernel, pack),
        out_shape=(
            jax.ShapeDtypeStruct((experts, copies, main, features + width), BF16),
            jax.ShapeDtypeStruct((tokens, experts), F32),
        ),
        compiler_params=params(40),
        cost_estimate=cost(2 * tokens * experts * main * features * 2, hidden.size * 8),
        name="route",
    )(ids, hidden, router)


def weights_kernel(pack, copies, ids_ref, logits_ref, main_ref, extra_ref, gates_ref):
    main, extra, cuts, _ = pack
    tokens, experts = logits_ref.shape
    ids = ids_ref[...]
    hits, slots = hits_and_slots(ids, experts)
    eye = (iota((tokens, tokens), 0) == iota((tokens, tokens), 1)).astype(BF16)
    logits = logits_ref[...]
    columns = [dot_nt(eye, h.astype(BF16)) for h in hits]
    picked = [jnp.sum(c * logits, axis=1, keepdims=True) for c in columns]
    expert = iota((tokens, experts), 1).astype(F32)
    total = experts * copies * main
    col = iota((tokens, total), 1)
    for k in range(2):
        gate = jax.nn.sigmoid(picked[k] - picked[1 - k])
        gates_ref[k] = jnp.broadcast_to(gate, gates_ref.shape[1:])
        named = jnp.sum(columns[k] * expert, axis=1, keepdims=True).astype(jnp.int32)
        wide = jnp.broadcast_to(slots[k].astype(F32), (8, tokens)).astype(BF16)
        slot = dot_nt(eye, wide)[:, :1].astype(jnp.int32)
        mine = col // (copies * main) == named
        main_ref[k] = (mine & (col % main == slot)).astype(BF16)
        if extra:
            place = (col % main) // cuts + main
            extra_ref[k] = (mine & (place == slot)).astype(BF16)
        else:
            extra_ref[k] = jnp.zeros(extra_ref.shape[1:], BF16)


def blend_weights(ids, logits, copies, pack):
    tokens, experts = logits.shape
    total = experts * copies * pack[0]
    return pl.pallas_call(
        functools.partial(weights_kernel, pack, copies),
        out_shape=(
            jax.ShapeDtypeStruct((2, tokens, total), BF16),
            jax.ShapeDtypeStruct((2, tokens, total), BF16),
            jax.ShapeDtypeStruct((2, tokens, 128), F32),
        ),
        compiler_params=params(40),
        cost_estimate=cost(2 * tokens * total * 16, tokens * total * 8),
        name="blend_weights",
    )(ids, logits)


def gate_kernel(pack, arrived_ref, w_ref, out_ref, x_ref):
    main, extra, cuts, width = pack
    sources = arrived_ref.shape[0]
    features = x_ref.shape[1]

    @pl.when(pl.program_id(0) == 0)
    def _():
        x_ref[: sources * main] = arrived_ref[:, :, :features].reshape(sources * main, features)
        if extra:
            folded = arrived_ref[:, :, features:].reshape(sources * main, width)
            shape = (sources * extra, sources * main)
            for c in range(cuts):
                pick = (iota(shape, 1) == iota(shape, 0) * cuts + c).astype(BF16)
                x_ref[sources * main :, c * width : (c + 1) * width] = dot(pick, folded).astype(BF16)

    out_ref[...] = dot(x_ref[...], w_ref[...]).astype(BF16)


def gate_part(arrived, w_gate, first, amount, pack):
    main, extra, _, _ = pack
    sources = arrived.shape[0]
    rows = sources * (main + extra)
    features = w_gate.shape[0]
    block = math.gcd(512, amount)
    start = first // block
    return pl.pallas_call(
        functools.partial(gate_kernel, pack),
        grid=(amount // block,),
        in_specs=[
            pl.BlockSpec(arrived.shape, lambda i: (0, 0, 0)),
            pl.BlockSpec((features, block), lambda i: (0, i + start)),
        ],
        out_specs=pl.BlockSpec((rows, block), lambda i: (0, i)),
        out_shape=jax.ShapeDtypeStruct((rows, amount), BF16),
        scratch_shapes=[pltpu.VMEM((rows, features), BF16)],
        compiler_params=params(40),
        cost_estimate=cost(2 * rows * features * amount, features * amount * 2),
        name="gate",
    )(arrived, w_gate)


def down_kernel(pack, sums, last, *refs):
    main, extra, cuts, width = pack
    part_refs, w_ref = refs[:sums], refs[sums]
    out_ref, acc_ref = refs[-2], refs[-1]
    before_ref = refs[sums + 1] if len(refs) == sums + 4 else None
    step = pl.program_id(0)
    total = part_refs[0][...].astype(F32)
    for ref in part_refs[1:]:
        total = total + ref[...].astype(F32)
    acted = (total * jax.nn.sigmoid(total)).astype(BF16)
    product = dot(acted, w_ref[...])

    @pl.when(step == 0)
    def _():
        acc_ref[...] = product if before_ref is None else product + before_ref[...]

    @pl.when(step > 0)
    def _():
        acc_ref[...] += product

    @pl.when(step == pl.num_programs(0) - 1)
    def _():
        if not last:
            out_ref[...] = acc_ref[...]
            return
        sources = out_ref.shape[0]
        features = acc_ref.shape[1]
        made = acc_ref[: sources * main].astype(BF16)
        out_ref[:, :, :features] = made.reshape(sources, main, features)
        if extra:
            shape = (sources * main, sources * extra)
            folded = None
            for c in range(cuts):
                piece = acc_ref[sources * main :, c * width : (c + 1) * width].astype(BF16)
                pick = (iota(shape, 0) == iota(shape, 1) * cuts + c).astype(BF16)
                part = dot(pick, piece)
                folded = part if folded is None else folded + part
            out_ref[:, :, features:] = folded.astype(BF16).reshape(sources, main, width)


def down_part(parts, w_down, first, before, last, sources, pack):
    main, extra, _, width = pack
    rows, amount = parts[0].shape
    features = w_down.shape[1]
    block = math.gcd(512, amount)
    start = first // block
    in_specs = [pl.BlockSpec((rows, block), lambda i: (0, i)) for _ in parts]
    in_specs.append(pl.BlockSpec((block, features), lambda i: (i + start, 0)))
    args = [*parts, w_down]
    if before is not None:
        in_specs.append(pl.BlockSpec((rows, features), lambda i: (0, 0)))
        args.append(before)
    if last:
        shape = jax.ShapeDtypeStruct((sources, main, features + width), BF16)
    else:
        shape = jax.ShapeDtypeStruct((rows, features), F32)
    zeros = (0,) * len(shape.shape)
    return pl.pallas_call(
        functools.partial(down_kernel, pack, len(parts), last),
        grid=(amount // block,),
        in_specs=in_specs,
        out_specs=pl.BlockSpec(shape.shape, lambda i: zeros),
        out_shape=shape,
        scratch_shapes=[pltpu.VMEM((rows, features), F32)],
        compiler_params=params(48),
        cost_estimate=cost(2 * rows * features * amount, features * amount * 2),
        name="down",
    )(*args)


def combine_kernel(pack, back_ref, main_ref, extra_ref, gates_ref, out_ref):
    main, extra, cuts, width = pack
    sources = back_ref.shape[0]
    tokens, features = out_ref.shape
    piece = width if extra else features
    back = back_ref[:, :, :features].reshape(sources * main, features)
    folded = back_ref[:, :, features:].reshape(sources * main, width) if extra else None
    total = None
    for k in range(2):
        rows = dot(main_ref[k], back)
        if extra:
            chosen = extra_ref[k]
            at = iota(chosen.shape, 1) % cuts
            pieces = [
                dot(jnp.where(at == c, chosen, jnp.zeros_like(chosen)), folded) for c in range(cuts)
            ]
            rows = rows + jnp.concatenate(pieces, axis=1)
        weighed = rows * gates_ref[k][:, :1]
        total = weighed if total is None else total + weighed
    out_ref[...] = total.astype(BF16)


def combine(back, weights, tokens, features, pack):
    return pl.pallas_call(
        functools.partial(combine_kernel, pack),
        out_shape=jax.ShapeDtypeStruct((tokens, features), BF16),
        compiler_params=params(40),
        cost_estimate=cost(4 * tokens * back.size, back.size * 2),
        name="combine",
    )(back, *weights)


def spread_states(bc, place, spread_ref):
    for t in range(spread_ref.shape[0]):
        spread_ref[t] = jnp.broadcast_to(bc[place][:, t : t + 1], spread_ref.shape[1:])


def tiled_lanes(value, lanes):
    return jnp.concatenate([value] * (lanes // value.shape[1]), axis=1)


def scan_kernel(
    x_ref, edge_ref, low_ref, dtw_ref, dtb_ref, alog_ref, cw_ref, cb_ref, skip_ref, bc_ref,
    read_ref, cum_ref, ends_ref, padded, delta_ref, fed_ref, b_ref, c_ref,
):
    tokens, lanes = x_ref.shape
    taps = cw_ref.shape[0]
    states = alog_ref.shape[0]

    @pl.when(pl.program_id(0) == 0)
    def _():
        spread_states(bc_ref, 0, b_ref)
        spread_states(bc_ref, 1, c_ref)

    padded[8:] = x_ref[...].astype(F32)
    padded[8 - (taps - 1) : 8] = edge_ref[...].astype(F32)
    conv = jnp.broadcast_to(cb_ref[...], (tokens, lanes))
    for k in range(taps):
        at = 8 - (taps - 1) + k
        conv = conv + cw_ref[k : k + 1] * padded[at : at + tokens]
    act = conv * jax.nn.sigmoid(conv)
    raw = dot(low_ref[...], dtw_ref[...]) + dtb_ref[...]
    delta = jnp.maximum(raw, 0.0) + jnp.log1p(jnp.exp(-jnp.abs(raw)))
    delta_ref[...] = delta
    fed_ref[...] = delta * act
    read_ref[...] = skip_ref[...] * act
    rates = -jnp.exp(alog_ref[...]) * LOG2E

    def eight(g, carry):
        state, running = carry
        at = pl.multiple_of(g * 8, 8)
        delta8 = delta_ref[pl.ds(at, 8)]
        fed8 = fed_ref[pl.ds(at, 8)]
        reads, sums = [], []
        for i in range(8):
            step = delta8[i : i + 1]
            running = running + step
            factor = jnp.exp2(rates * step)
            state = factor * state + tiled_lanes(b_ref[at + i], lanes) * fed8[i : i + 1]
            reads.append(jnp.sum(tiled_lanes(c_ref[at + i], lanes) * state, axis=0, keepdims=True))
            sums.append(running)
        read_ref[pl.ds(at, 8)] += jnp.concatenate(reads, axis=0)
        cum_ref[pl.ds(at, 8)] = jnp.concatenate(sums, axis=0)
        return state, running

    state, running = lax.fori_loop(
        0, tokens // 8, eight, (jnp.zeros((states, lanes), F32), jnp.zeros((1, lanes), F32))
    )
    ends_ref[:states] = state.astype(BF16)
    ends_ref[states:] = jnp.exp2(rates * running).astype(BF16)


def scan(x_in, edge, dt_low, dt_weight, dt_bias, a_log, conv_weight, conv_bias, d_skip, b_and_c):
    tokens, channels = x_in.shape
    states = a_log.shape[0]
    lanes = math.gcd(512, channels)

    def cut(rows):
        return pl.BlockSpec((rows, lanes), lambda i: (0, i))

    def whole(a):
        zeros = (0,) * a.ndim
        return pl.BlockSpec(a.shape, lambda i: zeros)

    return pl.pallas_call(
        scan_kernel,
        grid=(channels // lanes,),
        in_specs=[
            cut(tokens), cut(edge.shape[0]), whole(dt_low), cut(dt_weight.shape[0]), cut(1),
            cut(states), cut(conv_weight.shape[0]), cut(1), cut(1), whole(b_and_c),
        ],
        out_specs=(cut(tokens), cut(tokens), cut(2 * states)),
        out_shape=(
            jax.ShapeDtypeStruct((tokens, channels), F32),
            jax.ShapeDtypeStruct((tokens, channels), F32),
            jax.ShapeDtypeStruct((2 * states, channels), BF16),
        ),
        scratch_shapes=[
            pltpu.VMEM((tokens + 8, lanes), F32),
            pltpu.VMEM((tokens, lanes), F32),
            pltpu.VMEM((tokens, lanes), F32),
            pltpu.VMEM((tokens, states, 128), F32),
            pltpu.VMEM((tokens, states, 128), F32),
        ],
        compiler_params=params(40),
        cost_estimate=cost(
            tokens * channels * states * 8, tokens * channels * 12, tokens * channels * states
        ),
        name="scan",
    )(
        x_in, edge, dt_low, dt_weight, dt_bias[None], a_log, conv_weight, conv_bias[None],
        d_skip[None], b_and_c,
    )


def prefix_kernel(ends_ref, out_ref):
    blocks, states, lanes = out_ref.shape
    entering = jnp.zeros((states, lanes), F32)
    for i in range(blocks):
        out_ref[i] = entering.astype(BF16)
        entering = (
            ends_ref[i, states:].astype(F32) * entering + ends_ref[i, :states].astype(F32)
        )


def prefix(ends):
    blocks, both, lanes = ends.shape
    return pl.pallas_call(
        prefix_kernel,
        out_shape=jax.ShapeDtypeStruct((blocks, both // 2, lanes), BF16),
        compiler_params=params(16),
        cost_estimate=cost(ends.size, ends.size * 3),
        name="prefix",
    )(ends)


def finish_kernel(read_ref, cum_ref, z_ref, enter_ref, alog_ref, bc_ref, out_ref, sum_ref, c_ref):
    tokens, lanes = z_ref.shape

    @pl.when(pl.program_id(0) == 0)
    def _():
        spread_states(bc_ref, 1, c_ref)

    rates = -jnp.exp(alog_ref[...]) * LOG2E
    entering = enter_ref[...].astype(F32)

    def eight(g, carry):
        at = pl.multiple_of(g * 8, 8)
        cum8 = cum_ref[pl.ds(at, 8)]
        reads = []
        for i in range(8):
            kept = jnp.exp2(rates * cum8[i : i + 1]) * entering
            reads.append(jnp.sum(tiled_lanes(c_ref[at + i], lanes) * kept, axis=0, keepdims=True))
        sum_ref[pl.ds(at, 8)] = jnp.concatenate(reads, axis=0)
        return carry

    lax.fori_loop(0, tokens // 8, eight, 0)
    z = z_ref[...].astype(F32)
    out_ref[...] = ((read_ref[...] + sum_ref[...]) * (z * jax.nn.sigmoid(z))).astype(BF16)


def finish(read, cum, z_gate, entering, a_log, b_and_c):
    tokens, channels = z_gate.shape
    states = a_log.shape[0]
    lanes = math.gcd(512, channels)

    def cut(rows):
        return pl.BlockSpec((rows, lanes), lambda i: (0, i))

    return pl.pallas_call(
        finish_kernel,
        grid=(channels // lanes,),
        in_specs=[
            cut(tokens), cut(tokens), cut(tokens), cut(states), cut(states),
            pl.BlockSpec(b_and_c.shape, lambda i: (0, 0, 0)),
        ],
        out_specs=cut(tokens),
        out_shape=jax.ShapeDtypeStruct((tokens, channels), BF16),
        scratch_shapes=[
            pltpu.VMEM((tokens, lanes), F32),
            pltpu.VMEM((tokens, states, 128), F32),
        ],
        compiler_params=params(40),
        cost_estimate=cost(
            tokens * channels * states * 5, tokens * channels * 12, tokens * channels * states
        ),
        name="finish",
    )(read, cum, z_gate, entering, a_log, b_and_c)


def turned(value, axis, by):
    count = lax.axis_size(axis)
    return lax.ppermute(value, axis, [(i, (i + by) % count) for i in range(count)])


def local(
    x_in,
    z_gate,
    dt_low,
    dt_weight,
    dt_bias,
    a_log,
    conv_weight,
    conv_bias,
    d_skip,
    b_and_c,
    hidden,
    router,
    expert_ids,
    w_gate,
    w_down,
):
    blocks = lax.axis_size("seq")
    feature_parts = lax.axis_size("exp")
    tokens, features = hidden.shape
    experts = router.shape[1]
    copies = blocks // experts
    pack = packing(features)
    ids = expert_ids.T

    outgoing, logits = route(ids, hidden, router.T, copies, pack)
    outgoing = outgoing.reshape((blocks,) + outgoing.shape[2:])
    arrived = lax.all_to_all(outgoing, "seq", split_axis=0, concat_axis=0, tiled=True)

    edge, _ = lax.optimization_barrier((x_in[tokens - (conv_weight.shape[0] - 1) :], logits))
    edge = lax.ppermute(edge, "seq", [(i, i + 1) for i in range(blocks - 1)])
    logits = lax.psum(logits, "exp")
    weights = blend_weights(ids, logits, copies, pack)

    read, cum, ends = scan(
        x_in, edge, dt_low, dt_weight, dt_bias, a_log, conv_weight, conv_bias, d_skip, b_and_c
    )
    both, channels = ends.shape
    ends = lax.all_to_all(
        ends.reshape(both, blocks, channels // blocks).transpose(1, 0, 2),
        "seq", split_axis=0, concat_axis=0, tiled=True,
    )
    entering = lax.all_to_all(prefix(ends), "seq", split_axis=0, concat_axis=0, tiled=True)
    entering = entering.transpose(1, 0, 2).reshape(both // 2, channels)
    mamba_out = finish(read, cum, z_gate, entering, a_log, b_and_c)

    amount = w_gate.shape[1] // GATE_PARTS
    halves = []
    for q in range(GATE_PARTS):
        own = gate_part(arrived, w_gate, q * amount, amount, pack)
        halves.append([own] + [turned(own, "exp", d) for d in range(1, feature_parts)])
    produced = None
    for q in range(GATE_PARTS):
        produced = down_part(
            halves[q], w_down, q * amount, produced, q == GATE_PARTS - 1, blocks, pack
        )
    back = lax.all_to_all(produced, "seq", split_axis=0, concat_axis=0, tiled=True)
    moe_out = combine(back, weights, tokens, features, pack)
    return mamba_out, moe_out


def solution(mesh):
    return jax.shard_map(
        local,
        mesh=mesh,
        in_specs=(
            P("seq", "exp"),
            P("seq", "exp"),
            P("seq", None),
            P(None, "exp"),
            P("exp"),
            P(None, "exp"),
            P(None, "exp"),
            P("exp"),
            P("exp"),
            P(None, None, "seq"),
            P("seq", "exp"),
            P("exp", None),
            P("seq", None),
            P("exp", "seq"),
            P("seq", "exp"),
        ),
        out_specs=(P("seq", "exp"), P("seq", "exp")),
        check_vma=False,
    )
```

```python
import functools
import math

import jax
import jax.numpy as jnp
from jax import lax
from jax.experimental import pallas as pl
from jax.experimental.pallas import tpu as pltpu
from jax.sharding import PartitionSpec as P

CAP = 18
MIB = 1 << 20
LOG2E = math.log2(math.e)
F32 = jnp.float32
BF16 = jnp.bfloat16


def params(limit):
    return pltpu.CompilerParams(vmem_limit_bytes=limit * MIB)


def cost(flops, moved, transcendentals=0):
    return pl.CostEstimate(
        flops=int(flops), bytes_accessed=int(moved), transcendentals=int(transcendentals)
    )


def iota(shape, dim):
    return lax.broadcasted_iota(jnp.int32, shape, dim)


def dot(a, b):
    return jnp.dot(a, b, preferred_element_type=F32)


def dot_nt(a, b):
    return lax.dot_general(a, b, (((1,), (1,)), ((), ())), preferred_element_type=F32)


def packing(features):
    main = CAP // 16 * 16
    extra = CAP - main
    cuts = main // extra if extra and main % extra == 0 else 0
    if cuts and features % (cuts * 128) == 0:
        return main, extra, cuts, features // cuts
    return -(-CAP // 16) * 16, 0, 0, 0


def hits_and_slots(ids, experts):
    tokens = ids.shape[1]
    of = iota((experts, tokens), 0)
    hits = [(of == ids[k : k + 1]).astype(F32) for k in range(2)]
    before = (iota((tokens, tokens), 0) < iota((tokens, tokens), 1)).astype(BF16)
    earlier = dot((hits[0] + hits[1]).astype(BF16), before)
    slots = [jnp.sum(h * earlier, axis=0, keepdims=True).astype(jnp.int32) for h in hits]
    return hits, slots


def route_kernel(pack, ids_ref, hidden_ref, router_ref, out_ref, logits_ref):
    main, extra, cuts, width = pack
    experts, copies = out_ref.shape[:2]
    tokens, features = hidden_ref.shape
    ids = ids_ref[...]
    _, slots = hits_and_slots(ids, experts)
    hidden = hidden_ref[...]
    row = iota((experts * main, tokens), 0)
    picked = None
    for k in range(2):
        key = jnp.where(slots[k] < main, ids[k : k + 1] * main + slots[k], -1)
        hit = row == key
        picked = hit if picked is None else picked | hit
    packed = dot(picked.astype(BF16), hidden).astype(BF16)
    for e in range(experts):
        for m in range(copies):
            out_ref[e, m, :, :features] = packed[e * main : (e + 1) * main]
    if extra:
        picked = None
        for k in range(2):
            key = jnp.where(slots[k] >= main, ids[k : k + 1] * extra + slots[k] - main, -1)
            hit = row // cuts == key
            picked = hit if picked is None else picked | hit
        total = None
        for c in range(cuts):
            chosen = (picked & (row % cuts == c)).astype(BF16)
            part = dot(chosen, hidden[:, c * width : (c + 1) * width])
            total = part if total is None else total + part
        total = total.astype(BF16)
        for e in range(experts):
            for m in range(copies):
                out_ref[e, m, :, features:] = total[e * main : (e + 1) * main]
    logits_ref[...] = dot_nt(hidden, router_ref[...])


def route(ids, hidden, router, copies, pack):
    main, _, _, width = pack
    tokens, features = hidden.shape
    experts = router.shape[0]
    return pl.pallas_call(
        functools.partial(route_kernel, pack),
        out_shape=(
            jax.ShapeDtypeStruct((experts, copies, main, features + width), BF16),
            jax.ShapeDtypeStruct((tokens, experts), F32),
        ),
        compiler_params=params(40),
        cost_estimate=cost(2 * tokens * experts * main * features * 2, hidden.size * 8),
        name="route",
    )(ids, hidden, router)


def weights_kernel(pack, copies, ids_ref, logits_ref, main_ref, extra_ref, gates_ref):
    main, extra, cuts, _ = pack
    tokens, experts = logits_ref.shape
    ids = ids_ref[...]
    hits, slots = hits_and_slots(ids, experts)
    eye = (iota((tokens, tokens), 0) == iota((tokens, tokens), 1)).astype(BF16)
    logits = logits_ref[...]
    columns = [dot_nt(eye, h.astype(BF16)) for h in hits]
    picked = [jnp.sum(c * logits, axis=1, keepdims=True) for c in columns]
    expert = iota((tokens, experts), 1).astype(F32)
    total = experts * copies * main
    col = iota((tokens, total), 1)
    for k in range(2):
        gate = jax.nn.sigmoid(picked[k] - picked[1 - k])
        gates_ref[k] = jnp.broadcast_to(gate, gates_ref.shape[1:])
        named = jnp.sum(columns[k] * expert, axis=1, keepdims=True).astype(jnp.int32)
        wide = jnp.broadcast_to(slots[k].astype(F32), (8, tokens)).astype(BF16)
        slot = dot_nt(eye, wide)[:, :1].astype(jnp.int32)
        mine = col // (copies * main) == named
        main_ref[k] = (mine & (col % main == slot)).astype(BF16)
        if extra:
            place = (col % main) // cuts + main
            extra_ref[k] = (mine & (place == slot)).astype(BF16)
        else:
            extra_ref[k] = jnp.zeros(extra_ref.shape[1:], BF16)


def blend_weights(ids, logits, copies, pack):
    tokens, experts = logits.shape
    total = experts * copies * pack[0]
    return pl.pallas_call(
        functools.partial(weights_kernel, pack, copies),
        out_shape=(
            jax.ShapeDtypeStruct((2, tokens, total), BF16),
            jax.ShapeDtypeStruct((2, tokens, total), BF16),
            jax.ShapeDtypeStruct((2, tokens, 128), F32),
        ),
        compiler_params=params(40),
        cost_estimate=cost(2 * tokens * total * 16, tokens * total * 8),
        name="blend_weights",
    )(ids, logits)


def unpack_kernel(pack, arrived_ref, out_ref):
    main, extra, cuts, width = pack
    sources = arrived_ref.shape[0]
    features = out_ref.shape[1]
    out_ref[: sources * main] = arrived_ref[:, :, :features].reshape(sources * main, features)
    if extra:
        folded = arrived_ref[:, :, features:].reshape(sources * main, width)
        shape = (sources * extra, sources * main)
        for c in range(cuts):
            pick = (iota(shape, 1) == iota(shape, 0) * cuts + c).astype(BF16)
            out_ref[sources * main :, c * width : (c + 1) * width] = dot(pick, folded).astype(BF16)


def unpack(arrived, features, pack):
    main, extra, _, _ = pack
    rows = arrived.shape[0] * (main + extra)
    return pl.pallas_call(
        functools.partial(unpack_kernel, pack),
        out_shape=jax.ShapeDtypeStruct((rows, features), BF16),
        compiler_params=params(24),
        cost_estimate=cost(arrived.size * 16, arrived.size * 4),
        name="unpack",
    )(arrived)


def pack_kernel(pack, *refs):
    main, extra, cuts, width = pack
    part_refs, out_ref = refs[:-1], refs[-1]
    sources = out_ref.shape[0]
    features = part_refs[0].shape[1]
    first = sources * main

    def total(rows, columns):
        value = part_refs[0][rows, columns].astype(F32)
        for ref in part_refs[1:]:
            value = value + ref[rows, columns].astype(F32)
        return value.astype(BF16)

    made = total(slice(0, first), slice(0, features))
    out_ref[:, :, :features] = made.reshape(sources, main, features)
    if extra:
        shape = (sources * main, sources * extra)
        folded = None
        for c in range(cuts):
            piece = total(slice(first, None), slice(c * width, (c + 1) * width))
            pick = (iota(shape, 0) == iota(shape, 1) * cuts + c).astype(BF16)
            part = dot(pick, piece)
            folded = part if folded is None else folded + part
        out_ref[:, :, features:] = folded.astype(BF16).reshape(sources, main, width)


def pack_sum(parts, sources, pack):
    main, _, _, width = pack
    features = parts[0].shape[1]
    return pl.pallas_call(
        functools.partial(pack_kernel, pack),
        out_shape=jax.ShapeDtypeStruct((sources, main, features + width), BF16),
        compiler_params=params(24),
        cost_estimate=cost(parts[0].size * 16, parts[0].size * 8),
        name="pack_sum",
    )(*parts)


def combine_kernel(pack, back_ref, main_ref, extra_ref, gates_ref, out_ref):
    main, extra, cuts, width = pack
    sources = back_ref.shape[0]
    tokens, features = out_ref.shape
    back = back_ref[:, :, :features].reshape(sources * main, features)
    folded = back_ref[:, :, features:].reshape(sources * main, width) if extra else None
    total = None
    for k in range(2):
        rows = dot(main_ref[k], back)
        if extra:
            chosen = extra_ref[k]
            at = iota(chosen.shape, 1) % cuts
            pieces = [
                dot(jnp.where(at == c, chosen, jnp.zeros_like(chosen)), folded) for c in range(cuts)
            ]
            rows = rows + jnp.concatenate(pieces, axis=1)
        weighed = rows * gates_ref[k][:, :1]
        total = weighed if total is None else total + weighed
    out_ref[...] = total.astype(BF16)


def combine(back, weights, tokens, features, pack):
    return pl.pallas_call(
        functools.partial(combine_kernel, pack),
        out_shape=jax.ShapeDtypeStruct((tokens, features), BF16),
        compiler_params=params(40),
        cost_estimate=cost(4 * tokens * back.size, back.size * 2),
        name="combine",
    )(back, *weights)


def spread_states(bc, place, spread_ref):
    for t in range(spread_ref.shape[0]):
        spread_ref[t] = jnp.broadcast_to(bc[place][:, t : t + 1], spread_ref.shape[1:])


def tiled_lanes(value, lanes):
    return jnp.concatenate([value] * (lanes // value.shape[1]), axis=1)


def scan_kernel(
    x_ref, edge_ref, low_ref, dtw_ref, dtb_ref, alog_ref, cw_ref, cb_ref, skip_ref, bc_ref,
    read_ref, cum_ref, ends_ref, padded, delta_ref, fed_ref, b_ref, c_ref,
):
    tokens, lanes = x_ref.shape
    taps = cw_ref.shape[0]
    states = alog_ref.shape[0]

    @pl.when(pl.program_id(0) == 0)
    def _():
        spread_states(bc_ref, 0, b_ref)
        spread_states(bc_ref, 1, c_ref)

    padded[8:] = x_ref[...].astype(F32)
    padded[8 - (taps - 1) : 8] = edge_ref[...].astype(F32)
    conv = jnp.broadcast_to(cb_ref[...], (tokens, lanes))
    for k in range(taps):
        at = 8 - (taps - 1) + k
        conv = conv + cw_ref[k : k + 1] * padded[at : at + tokens]
    act = conv * jax.nn.sigmoid(conv)
    raw = dot(low_ref[...], dtw_ref[...]) + dtb_ref[...]
    delta = jnp.maximum(raw, 0.0) + jnp.log1p(jnp.exp(-jnp.abs(raw)))
    delta_ref[...] = delta
    fed_ref[...] = delta * act
    read_ref[...] = skip_ref[...] * act
    rates = -jnp.exp(alog_ref[...]) * LOG2E

    def eight(g, carry):
        state, running = carry
        at = pl.multiple_of(g * 8, 8)
        delta8 = delta_ref[pl.ds(at, 8)]
        fed8 = fed_ref[pl.ds(at, 8)]
        reads, sums = [], []
        for i in range(8):
            step = delta8[i : i + 1]
            running = running + step
            factor = jnp.exp2(rates * step)
            state = factor * state + tiled_lanes(b_ref[at + i], lanes) * fed8[i : i + 1]
            reads.append(jnp.sum(tiled_lanes(c_ref[at + i], lanes) * state, axis=0, keepdims=True))
            sums.append(running)
        read_ref[pl.ds(at, 8)] += jnp.concatenate(reads, axis=0)
        cum_ref[pl.ds(at, 8)] = jnp.concatenate(sums, axis=0)
        return state, running

    state, running = lax.fori_loop(
        0, tokens // 8, eight, (jnp.zeros((states, lanes), F32), jnp.zeros((1, lanes), F32))
    )
    ends_ref[:states] = state.astype(BF16)
    ends_ref[states:] = jnp.exp2(rates * running).astype(BF16)


def scan(x_in, edge, dt_low, dt_weight, dt_bias, a_log, conv_weight, conv_bias, d_skip, b_and_c):
    tokens, channels = x_in.shape
    states = a_log.shape[0]
    lanes = math.gcd(512, channels)

    def cut(rows):
        return pl.BlockSpec((rows, lanes), lambda i: (0, i))

    def whole(a):
        zeros = (0,) * a.ndim
        return pl.BlockSpec(a.shape, lambda i: zeros)

    return pl.pallas_call(
        scan_kernel,
        grid=(channels // lanes,),
        in_specs=[
            cut(tokens), cut(edge.shape[0]), whole(dt_low), cut(dt_weight.shape[0]), cut(1),
            cut(states), cut(conv_weight.shape[0]), cut(1), cut(1), whole(b_and_c),
        ],
        out_specs=(cut(tokens), cut(tokens), cut(2 * states)),
        out_shape=(
            jax.ShapeDtypeStruct((tokens, channels), F32),
            jax.ShapeDtypeStruct((tokens, channels), F32),
            jax.ShapeDtypeStruct((2 * states, channels), BF16),
        ),
        scratch_shapes=[
            pltpu.VMEM((tokens + 8, lanes), F32),
            pltpu.VMEM((tokens, lanes), F32),
            pltpu.VMEM((tokens, lanes), F32),
            pltpu.VMEM((tokens, states, 128), F32),
            pltpu.VMEM((tokens, states, 128), F32),
        ],
        compiler_params=params(40),
        cost_estimate=cost(
            tokens * channels * states * 8, tokens * channels * 12, tokens * channels * states
        ),
        name="scan",
    )(
        x_in, edge, dt_low, dt_weight, dt_bias[None], a_log, conv_weight, conv_bias[None],
        d_skip[None], b_and_c,
    )


def prefix_kernel(ends_ref, out_ref):
    blocks, states, lanes = out_ref.shape
    entering = jnp.zeros((states, lanes), F32)
    for i in range(blocks):
        out_ref[i] = entering.astype(BF16)
        entering = (
            ends_ref[i, states:].astype(F32) * entering + ends_ref[i, :states].astype(F32)
        )


def prefix(ends):
    blocks, both, lanes = ends.shape
    return pl.pallas_call(
        prefix_kernel,
        out_shape=jax.ShapeDtypeStruct((blocks, both // 2, lanes), BF16),
        compiler_params=params(16),
        cost_estimate=cost(ends.size, ends.size * 3),
        name="prefix",
    )(ends)


def finish_kernel(read_ref, cum_ref, z_ref, enter_ref, alog_ref, bc_ref, out_ref, sum_ref, c_ref):
    tokens, lanes = z_ref.shape

    @pl.when(pl.program_id(0) == 0)
    def _():
        spread_states(bc_ref, 1, c_ref)

    rates = -jnp.exp(alog_ref[...]) * LOG2E
    entering = enter_ref[...].astype(F32)

    def eight(g, carry):
        at = pl.multiple_of(g * 8, 8)
        cum8 = cum_ref[pl.ds(at, 8)]
        reads = []
        for i in range(8):
            kept = jnp.exp2(rates * cum8[i : i + 1]) * entering
            reads.append(jnp.sum(tiled_lanes(c_ref[at + i], lanes) * kept, axis=0, keepdims=True))
        sum_ref[pl.ds(at, 8)] = jnp.concatenate(reads, axis=0)
        return carry

    lax.fori_loop(0, tokens // 8, eight, 0)
    z = z_ref[...].astype(F32)
    out_ref[...] = ((read_ref[...] + sum_ref[...]) * (z * jax.nn.sigmoid(z))).astype(BF16)


def finish(read, cum, z_gate, entering, a_log, b_and_c):
    tokens, channels = z_gate.shape
    states = a_log.shape[0]
    lanes = math.gcd(512, channels)

    def cut(rows):
        return pl.BlockSpec((rows, lanes), lambda i: (0, i))

    return pl.pallas_call(
        finish_kernel,
        grid=(channels // lanes,),
        in_specs=[
            cut(tokens), cut(tokens), cut(tokens), cut(states), cut(states),
            pl.BlockSpec(b_and_c.shape, lambda i: (0, 0, 0)),
        ],
        out_specs=cut(tokens),
        out_shape=jax.ShapeDtypeStruct((tokens, channels), BF16),
        scratch_shapes=[
            pltpu.VMEM((tokens, lanes), F32),
            pltpu.VMEM((tokens, states, 128), F32),
        ],
        compiler_params=params(40),
        cost_estimate=cost(
            tokens * channels * states * 5, tokens * channels * 12, tokens * channels * states
        ),
        name="finish",
    )(read, cum, z_gate, entering, a_log, b_and_c)


def turned(value, axis, by):
    count = lax.axis_size(axis)
    return lax.ppermute(value, axis, [(i, (i + by) % count) for i in range(count)])


def turned_within(value, copies, by):
    count = lax.axis_size("seq")
    return lax.ppermute(
        value, "seq", [(i, i // copies * copies + (i + by) % copies) for i in range(count)]
    )


def exchanged(value, copies):
    count = lax.axis_size("seq")
    groups = [list(range(m, count, copies)) for m in range(copies)]
    return lax.all_to_all(
        value, "seq", split_axis=0, concat_axis=0, tiled=True, axis_index_groups=groups
    )


def after(value, *others):
    return lax.optimization_barrier((value, *others))[0]


def local(
    x_in,
    z_gate,
    dt_low,
    dt_weight,
    dt_bias,
    a_log,
    conv_weight,
    conv_bias,
    d_skip,
    b_and_c,
    hidden,
    router,
    expert_ids,
    w_gate,
    w_down,
):
    blocks = lax.axis_size("seq")
    feature_parts = lax.axis_size("exp")
    tokens, features = hidden.shape
    experts = router.shape[1]
    copies = blocks // experts
    pack = packing(features)
    ids = expert_ids.T

    outgoing, logits = route(ids, hidden, router.T, 1, pack)
    arrived = exchanged(outgoing.reshape((experts,) + outgoing.shape[2:]), copies)

    edge = after(x_in[tokens - (conv_weight.shape[0] - 1) :], logits)
    edge = lax.ppermute(edge, "seq", [(i, i + 1) for i in range(blocks - 1)])
    read, cum, ends = scan(
        x_in, edge, dt_low, dt_weight, dt_bias, a_log, conv_weight, conv_bias, d_skip, b_and_c
    )
    logits = lax.psum(logits, "exp")
    weights = blend_weights(ids, logits, 1, pack)

    arrived = after(arrived, ends)
    rows = [unpack(arrived, features, pack)]
    for d in range(1, copies):
        rows.append(turned_within(rows[0], copies, d))
    gated = []
    for part in rows:
        if gated:
            part = after(part, gated[-1][0])
        own = jnp.dot(part, w_gate, preferred_element_type=F32).astype(BF16)
        gated.append([own] + [turned(own, "exp", d) for d in range(1, feature_parts)])

    both, channels = ends.shape
    ends = after(ends, gated[-1][0])
    ends = lax.all_to_all(
        ends.reshape(both, blocks, channels // blocks).transpose(1, 0, 2),
        "seq", split_axis=0, concat_axis=0, tiled=True,
    )
    entering = prefix(ends)

    made = []
    for parts in gated[1:] + gated[:1]:
        total = sum(p.astype(F32) for p in parts)
        acted = (total * jax.nn.sigmoid(total)).astype(BF16)
        made.append(jnp.dot(acted, w_down, preferred_element_type=F32))
    entering = after(entering, made[0])
    sums = [made[-1]]
    for d in range(1, copies):
        sums.append(turned_within(made[d - 1].astype(BF16), copies, -d))

    entering = lax.all_to_all(entering, "seq", split_axis=0, concat_axis=0, tiled=True)
    entering = entering.transpose(1, 0, 2).reshape(both // 2, channels)
    mamba_out = finish(read, cum, z_gate, entering, a_log, b_and_c)

    back = exchanged(pack_sum(sums, experts, pack), copies)
    moe_out = combine(back, weights, tokens, features, pack)
    return mamba_out, moe_out


def solution(mesh):
    return jax.shard_map(
        local,
        mesh=mesh,
        in_specs=(
            P("seq", "exp"),
            P("seq", "exp"),
            P("seq", None),
            P(None, "exp"),
            P("exp"),
            P(None, "exp"),
            P(None, "exp"),
            P("exp"),
            P("exp"),
            P(None, None, "seq"),
            P("seq", "exp"),
            P("exp", None),
            P("seq", None),
            P("exp", "seq"),
            P("seq", "exp"),
        ),
        out_specs=(P("seq", "exp"), P("seq", "exp")),
        check_vma=False,
    )
```

```python
import functools
import math

import jax
import jax.numpy as jnp
from jax import lax
from jax.experimental import pallas as pl
from jax.experimental.pallas import tpu as pltpu
from jax.sharding import PartitionSpec as P

CAP = 18
MIB = 1 << 20
LOG2E = math.log2(math.e)
F32 = jnp.float32
BF16 = jnp.bfloat16


def params(limit):
    return pltpu.CompilerParams(vmem_limit_bytes=limit * MIB)


def cost(flops, moved, transcendentals=0):
    return pl.CostEstimate(
        flops=int(flops), bytes_accessed=int(moved), transcendentals=int(transcendentals)
    )


def in_hbm(*arrays):
    return [pltpu.with_memory_space_constraint(a, pltpu.HBM) for a in arrays]


def iota(shape, dim):
    return lax.broadcasted_iota(jnp.int32, shape, dim)


def dot(a, b):
    return jnp.dot(a, b, preferred_element_type=F32)


def dot_nt(a, b):
    return lax.dot_general(a, b, (((1,), (1,)), ((), ())), preferred_element_type=F32)


def packing(features):
    main = CAP // 16 * 16
    extra = CAP - main
    cuts = main // extra if extra and main % extra == 0 else 0
    if cuts and features % (cuts * 128) == 0:
        return main, extra, cuts, features // cuts
    return -(-CAP // 16) * 16, 0, 0, 0


def hits_and_slots(ids, experts):
    tokens = ids.shape[1]
    of = iota((experts, tokens), 0)
    hits = [(of == ids[k : k + 1]).astype(F32) for k in range(2)]
    before = (iota((tokens, tokens), 0) < iota((tokens, tokens), 1)).astype(BF16)
    earlier = dot((hits[0] + hits[1]).astype(BF16), before)
    slots = [jnp.sum(h * earlier, axis=0, keepdims=True).astype(jnp.int32) for h in hits]
    return hits, slots


def route_kernel(pack, ids_ref, hidden_ref, router_ref, out_ref, logits_ref):
    main, extra, cuts, width = pack
    experts, copies = out_ref.shape[:2]
    tokens, features = hidden_ref.shape
    ids = ids_ref[...]
    _, slots = hits_and_slots(ids, experts)
    hidden = hidden_ref[...]
    row = iota((experts * main, tokens), 0)
    picked = None
    for k in range(2):
        key = jnp.where(slots[k] < main, ids[k : k + 1] * main + slots[k], -1)
        hit = row == key
        picked = hit if picked is None else picked | hit
    packed = dot(picked.astype(BF16), hidden).astype(BF16)
    for e in range(experts):
        for m in range(copies):
            out_ref[e, m, :, :features] = packed[e * main : (e + 1) * main]
    if extra:
        picked = None
        for k in range(2):
            key = jnp.where(slots[k] >= main, ids[k : k + 1] * extra + slots[k] - main, -1)
            hit = row // cuts == key
            picked = hit if picked is None else picked | hit
        total = None
        for c in range(cuts):
            chosen = (picked & (row % cuts == c)).astype(BF16)
            part = dot(chosen, hidden[:, c * width : (c + 1) * width])
            total = part if total is None else total + part
        total = total.astype(BF16)
        for e in range(experts):
            for m in range(copies):
                out_ref[e, m, :, features:] = total[e * main : (e + 1) * main]
    logits_ref[...] = dot_nt(hidden, router_ref[...])


def route(ids, hidden, router, copies, pack):
    main, _, _, width = pack
    tokens, features = hidden.shape
    experts = router.shape[0]
    return pl.pallas_call(
        functools.partial(route_kernel, pack),
        out_shape=(
            jax.ShapeDtypeStruct((experts, copies, main, features + width), BF16),
            jax.ShapeDtypeStruct((tokens, experts), F32),
        ),
        compiler_params=params(40),
        cost_estimate=cost(2 * tokens * experts * main * features * 2, hidden.size * 8),
        name="route",
    )(ids, *in_hbm(hidden, router))


def weights_kernel(pack, copies, ids_ref, logits_ref, main_ref, extra_ref, gates_ref):
    main, extra, cuts, _ = pack
    tokens, experts = logits_ref.shape
    ids = ids_ref[...]
    hits, slots = hits_and_slots(ids, experts)
    eye = (iota((tokens, tokens), 0) == iota((tokens, tokens), 1)).astype(BF16)
    logits = logits_ref[...]
    columns = [dot_nt(eye, h.astype(BF16)) for h in hits]
    picked = [jnp.sum(c * logits, axis=1, keepdims=True) for c in columns]
    expert = iota((tokens, experts), 1).astype(F32)
    total = experts * copies * main
    col = iota((tokens, total), 1)
    for k in range(2):
        gate = jax.nn.sigmoid(picked[k] - picked[1 - k])
        gates_ref[k] = jnp.broadcast_to(gate, gates_ref.shape[1:])
        named = jnp.sum(columns[k] * expert, axis=1, keepdims=True).astype(jnp.int32)
        wide = jnp.broadcast_to(slots[k].astype(F32), (8, tokens)).astype(BF16)
        slot = dot_nt(eye, wide)[:, :1].astype(jnp.int32)
        mine = col // (copies * main) == named
        main_ref[k] = (mine & (col % main == slot)).astype(BF16)
        if extra:
            place = (col % main) // cuts + main
            extra_ref[k] = (mine & (place == slot)).astype(BF16)
        else:
            extra_ref[k] = jnp.zeros(extra_ref.shape[1:], BF16)


def blend_weights(ids, logits, copies, pack):
    tokens, experts = logits.shape
    total = experts * copies * pack[0]
    return pl.pallas_call(
        functools.partial(weights_kernel, pack, copies),
        out_shape=(
            jax.ShapeDtypeStruct((2, tokens, total), BF16),
            jax.ShapeDtypeStruct((2, tokens, total), BF16),
            jax.ShapeDtypeStruct((2, tokens, 128), F32),
        ),
        compiler_params=params(40),
        cost_estimate=cost(2 * tokens * total * 16, tokens * total * 8),
        name="blend_weights",
    )(ids, logits)


ANYWHERE = pl.BlockSpec(memory_space=pl.ANY)
INSIDE = pl.BlockSpec(memory_space=pltpu.VMEM)
AHEAD = 4


def streamed(from_ref, to_ref, sems, dim, chunk, use):
    count = from_ref.shape[dim] // chunk

    def copy(i):
        at = pl.ds(pl.multiple_of(i * chunk, chunk), chunk)
        part = (slice(None), at) if dim else (at, slice(None))
        return pltpu.make_async_copy(from_ref.at[part], to_ref.at[part], sems.at[i])

    for i in range(min(AHEAD, count)):
        copy(i).start()

    def step(i, carry):
        copy(i).wait()

        @pl.when(i + AHEAD < count)
        def _():
            copy(i + AHEAD).start()

        use(i)
        return carry

    lax.fori_loop(0, count, step, 0)


def gate_kernel(chunk, x_ref, w_ref, out_ref, held_ref, sems):
    def use(i):
        at = pl.ds(pl.multiple_of(i * chunk, chunk), chunk)
        out_ref[:, at] = dot(x_ref[...], held_ref[:, at]).astype(BF16)

    streamed(w_ref, held_ref, sems, 1, chunk, use)


def gate(x, w_gate):
    rows, features = x.shape
    amount = w_gate.shape[1]
    chunk = math.gcd(512, amount)
    return pl.pallas_call(
        functools.partial(gate_kernel, chunk),
        in_specs=[INSIDE, ANYWHERE],
        out_specs=INSIDE,
        out_shape=jax.ShapeDtypeStruct((rows, amount), BF16),
        scratch_shapes=[
            pltpu.VMEM(w_gate.shape, BF16),
            pltpu.SemaphoreType.DMA((amount // chunk,)),
        ],
        compiler_params=params(44),
        cost_estimate=cost(2 * rows * features * amount, features * amount * 2),
        name="gate",
    )(x, *in_hbm(w_gate))


def fill_acted(chunk, part_refs, acted_ref):
    def piece(i):
        at = pl.ds(pl.multiple_of(i * chunk, chunk), chunk)
        total = part_refs[0][:, at].astype(F32)
        for ref in part_refs[1:]:
            total = total + ref[:, at].astype(F32)
        acted_ref[:, at] = (total * jax.nn.sigmoid(total)).astype(BF16)

    pl.loop(0, acted_ref.shape[1] // chunk)(piece)


def down_kernel(chunk, *refs):
    part_refs, w_ref, out_ref, acted_ref, acc_ref, held_ref, sems = refs[:-6], *refs[-6:]

    def use(i):
        @pl.when(i == 0)
        def _():
            fill_acted(chunk, part_refs, acted_ref)
            acc_ref[...] = jnp.zeros_like(acc_ref)

        at = pl.ds(pl.multiple_of(i * chunk, chunk), chunk)
        acc_ref[...] += dot(acted_ref[:, at], held_ref[at])

    streamed(w_ref, held_ref, sems, 0, chunk, use)
    out_ref[...] = acc_ref[...].astype(out_ref.dtype)


def down(parts, w_down, dtype):
    rows, amount = parts[0].shape
    features = w_down.shape[1]
    chunk = math.gcd(512, amount)
    return pl.pallas_call(
        functools.partial(down_kernel, chunk),
        in_specs=[INSIDE] * len(parts) + [ANYWHERE],
        out_specs=INSIDE,
        out_shape=jax.ShapeDtypeStruct((rows, features), dtype),
        scratch_shapes=[
            pltpu.VMEM((rows, amount), BF16),
            pltpu.VMEM((rows, features), F32),
            pltpu.VMEM(w_down.shape, BF16),
            pltpu.SemaphoreType.DMA((amount // chunk,)),
        ],
        compiler_params=params(48),
        cost_estimate=cost(2 * rows * features * amount, features * amount * 2),
        name="down",
    )(*parts, *in_hbm(w_down))


def unpack_kernel(pack, arrived_ref, out_ref):
    main, extra, cuts, width = pack
    sources = arrived_ref.shape[0]
    features = out_ref.shape[1]
    out_ref[: sources * main] = arrived_ref[:, :, :features].reshape(sources * main, features)
    if extra:
        folded = arrived_ref[:, :, features:].reshape(sources * main, width)
        shape = (sources * extra, sources * main)
        for c in range(cuts):
            pick = (iota(shape, 1) == iota(shape, 0) * cuts + c).astype(BF16)
            out_ref[sources * main :, c * width : (c + 1) * width] = dot(pick, folded).astype(BF16)


def unpack(arrived, features, pack):
    main, extra, _, _ = pack
    rows = arrived.shape[0] * (main + extra)
    return pl.pallas_call(
        functools.partial(unpack_kernel, pack),
        out_shape=jax.ShapeDtypeStruct((rows, features), BF16),
        compiler_params=params(24),
        cost_estimate=cost(arrived.size * 16, arrived.size * 4),
        name="unpack",
    )(arrived)


def pack_kernel(pack, *refs):
    main, extra, cuts, width = pack
    part_refs, out_ref = refs[:-1], refs[-1]
    sources = out_ref.shape[0]
    features = part_refs[0].shape[1]
    first = sources * main

    def total(rows, columns):
        value = part_refs[0][rows, columns].astype(F32)
        for ref in part_refs[1:]:
            value = value + ref[rows, columns].astype(F32)
        return value.astype(BF16)

    made = total(slice(0, first), slice(0, features))
    out_ref[:, :, :features] = made.reshape(sources, main, features)
    if extra:
        shape = (sources * main, sources * extra)
        folded = None
        for c in range(cuts):
            piece = total(slice(first, None), slice(c * width, (c + 1) * width))
            pick = (iota(shape, 0) == iota(shape, 1) * cuts + c).astype(BF16)
            part = dot(pick, piece)
            folded = part if folded is None else folded + part
        out_ref[:, :, features:] = folded.astype(BF16).reshape(sources, main, width)


def pack_sum(parts, sources, pack):
    main, _, _, width = pack
    features = parts[0].shape[1]
    return pl.pallas_call(
        functools.partial(pack_kernel, pack),
        out_shape=jax.ShapeDtypeStruct((sources, main, features + width), BF16),
        compiler_params=params(24),
        cost_estimate=cost(parts[0].size * 16, parts[0].size * 8),
        name="pack_sum",
    )(*parts)


def combine_kernel(pack, back_ref, main_ref, extra_ref, gates_ref, out_ref):
    main, extra, cuts, width = pack
    sources = back_ref.shape[0]
    tokens, features = out_ref.shape
    back = back_ref[:, :, :features].reshape(sources * main, features)
    folded = back_ref[:, :, features:].reshape(sources * main, width) if extra else None
    total = None
    for k in range(2):
        rows = dot(main_ref[k], back)
        if extra:
            chosen = extra_ref[k]
            at = iota(chosen.shape, 1) % cuts
            pieces = [
                dot(jnp.where(at == c, chosen, jnp.zeros_like(chosen)), folded) for c in range(cuts)
            ]
            rows = rows + jnp.concatenate(pieces, axis=1)
        weighed = rows * gates_ref[k][:, :1]
        total = weighed if total is None else total + weighed
    out_ref[...] = total.astype(BF16)


def combine(back, weights, tokens, features, pack):
    return pl.pallas_call(
        functools.partial(combine_kernel, pack),
        out_shape=jax.ShapeDtypeStruct((tokens, features), BF16),
        compiler_params=params(40),
        cost_estimate=cost(4 * tokens * back.size, back.size * 2),
        name="combine",
    )(back, *weights)


def spread_states(bc, place, spread_ref):
    for t in range(spread_ref.shape[0]):
        spread_ref[t] = jnp.broadcast_to(bc[place][:, t : t + 1], spread_ref.shape[1:])


def tiled_lanes(value, lanes):
    return jnp.concatenate([value] * (lanes // value.shape[1]), axis=1)


def scan_kernel(
    x_ref, edge_ref, low_ref, dtw_ref, dtb_ref, alog_ref, cw_ref, cb_ref, skip_ref, bc_ref,
    read_ref, cum_ref, ends_ref, padded, delta_ref, fed_ref, b_ref, c_ref,
):
    tokens, lanes = x_ref.shape
    taps = cw_ref.shape[0]
    states = alog_ref.shape[0]

    @pl.when(pl.program_id(0) == 0)
    def _():
        spread_states(bc_ref, 0, b_ref)
        spread_states(bc_ref, 1, c_ref)

    padded[8:] = x_ref[...].astype(F32)
    padded[8 - (taps - 1) : 8] = edge_ref[...].astype(F32)
    conv = jnp.broadcast_to(cb_ref[...], (tokens, lanes))
    for k in range(taps):
        at = 8 - (taps - 1) + k
        conv = conv + cw_ref[k : k + 1] * padded[at : at + tokens]
    act = conv * jax.nn.sigmoid(conv)
    raw = dot(low_ref[...], dtw_ref[...]) + dtb_ref[...]
    delta = jnp.maximum(raw, 0.0) + jnp.log1p(jnp.exp(-jnp.abs(raw)))
    delta_ref[...] = delta
    fed_ref[...] = delta * act
    read_ref[...] = skip_ref[...] * act
    rates = -jnp.exp(alog_ref[...]) * LOG2E

    def eight(g, carry):
        state, running = carry
        at = pl.multiple_of(g * 8, 8)
        delta8 = delta_ref[pl.ds(at, 8)]
        fed8 = fed_ref[pl.ds(at, 8)]
        reads, sums = [], []
        for i in range(8):
            step = delta8[i : i + 1]
            running = running + step
            factor = jnp.exp2(rates * step)
            state = factor * state + tiled_lanes(b_ref[at + i], lanes) * fed8[i : i + 1]
            reads.append(jnp.sum(tiled_lanes(c_ref[at + i], lanes) * state, axis=0, keepdims=True))
            sums.append(running)
        read_ref[pl.ds(at, 8)] += jnp.concatenate(reads, axis=0)
        cum_ref[pl.ds(at, 8)] = jnp.concatenate(sums, axis=0)
        return state, running

    state, running = lax.fori_loop(
        0, tokens // 8, eight, (jnp.zeros((states, lanes), F32), jnp.zeros((1, lanes), F32))
    )
    ends_ref[:states] = state.astype(BF16)
    ends_ref[states:] = jnp.exp2(rates * running).astype(BF16)


def scan(x_in, edge, dt_low, dt_weight, dt_bias, a_log, conv_weight, conv_bias, d_skip, b_and_c):
    tokens, channels = x_in.shape
    states = a_log.shape[0]
    lanes = math.gcd(512, channels)

    def cut(rows):
        return pl.BlockSpec((rows, lanes), lambda i: (0, i))

    def whole(a):
        zeros = (0,) * a.ndim
        return pl.BlockSpec(a.shape, lambda i: zeros)

    return pl.pallas_call(
        scan_kernel,
        grid=(channels // lanes,),
        in_specs=[
            cut(tokens), cut(edge.shape[0]), whole(dt_low), cut(dt_weight.shape[0]), cut(1),
            cut(states), cut(conv_weight.shape[0]), cut(1), cut(1), whole(b_and_c),
        ],
        out_specs=(cut(tokens), cut(tokens), cut(2 * states)),
        out_shape=(
            pltpu.HBM((tokens, channels), F32),
            pltpu.HBM((tokens, channels), F32),
            jax.ShapeDtypeStruct((2 * states, channels), BF16),
        ),
        scratch_shapes=[
            pltpu.VMEM((tokens + 8, lanes), F32),
            pltpu.VMEM((tokens, lanes), F32),
            pltpu.VMEM((tokens, lanes), F32),
            pltpu.VMEM((tokens, states, 128), F32),
            pltpu.VMEM((tokens, states, 128), F32),
        ],
        compiler_params=params(40),
        cost_estimate=cost(
            tokens * channels * states * 8, tokens * channels * 12, tokens * channels * states
        ),
        name="scan",
    )(
        *in_hbm(x_in),
        edge,
        *in_hbm(
            dt_low, dt_weight, dt_bias[None], a_log, conv_weight, conv_bias[None], d_skip[None],
            b_and_c,
        ),
    )


def prefix_kernel(ends_ref, out_ref):
    blocks, states, lanes = out_ref.shape
    entering = jnp.zeros((states, lanes), F32)
    for i in range(blocks):
        out_ref[i] = entering.astype(BF16)
        entering = (
            ends_ref[i, states:].astype(F32) * entering + ends_ref[i, :states].astype(F32)
        )


def prefix(ends):
    blocks, both, lanes = ends.shape
    return pl.pallas_call(
        prefix_kernel,
        out_shape=jax.ShapeDtypeStruct((blocks, both // 2, lanes), BF16),
        compiler_params=params(16),
        cost_estimate=cost(ends.size, ends.size * 3),
        name="prefix",
    )(ends)


def finish_kernel(read_ref, cum_ref, z_ref, enter_ref, alog_ref, bc_ref, out_ref, sum_ref, c_ref):
    tokens, lanes = z_ref.shape

    @pl.when(pl.program_id(0) == 0)
    def _():
        spread_states(bc_ref, 1, c_ref)

    rates = -jnp.exp(alog_ref[...]) * LOG2E
    entering = enter_ref[...].astype(F32)

    def eight(g, carry):
        at = pl.multiple_of(g * 8, 8)
        cum8 = cum_ref[pl.ds(at, 8)]
        reads = []
        for i in range(8):
            kept = jnp.exp2(rates * cum8[i : i + 1]) * entering
            reads.append(jnp.sum(tiled_lanes(c_ref[at + i], lanes) * kept, axis=0, keepdims=True))
        sum_ref[pl.ds(at, 8)] = jnp.concatenate(reads, axis=0)
        return carry

    lax.fori_loop(0, tokens // 8, eight, 0)
    z = z_ref[...].astype(F32)
    out_ref[...] = ((read_ref[...] + sum_ref[...]) * (z * jax.nn.sigmoid(z))).astype(BF16)


def finish(read, cum, z_gate, entering, a_log, b_and_c):
    tokens, channels = z_gate.shape
    states = a_log.shape[0]
    lanes = math.gcd(512, channels)

    def cut(rows):
        return pl.BlockSpec((rows, lanes), lambda i: (0, i))

    return pl.pallas_call(
        finish_kernel,
        grid=(channels // lanes,),
        in_specs=[
            cut(tokens), cut(tokens), cut(tokens), cut(states), cut(states),
            pl.BlockSpec(b_and_c.shape, lambda i: (0, 0, 0)),
        ],
        out_specs=cut(tokens),
        out_shape=jax.ShapeDtypeStruct((tokens, channels), BF16),
        scratch_shapes=[
            pltpu.VMEM((tokens, lanes), F32),
            pltpu.VMEM((tokens, states, 128), F32),
        ],
        compiler_params=params(40),
        cost_estimate=cost(
            tokens * channels * states * 5, tokens * channels * 12, tokens * channels * states
        ),
        name="finish",
    )(*in_hbm(read, cum, z_gate), entering, *in_hbm(a_log, b_and_c))


def turned(value, axis, by):
    count = lax.axis_size(axis)
    return lax.ppermute(value, axis, [(i, (i + by) % count) for i in range(count)])


def turned_within(value, copies, by):
    count = lax.axis_size("seq")
    return lax.ppermute(
        value, "seq", [(i, i // copies * copies + (i + by) % copies) for i in range(count)]
    )


def exchanged(value, copies):
    count = lax.axis_size("seq")
    groups = [list(range(m, count, copies)) for m in range(copies)]
    return lax.all_to_all(
        value, "seq", split_axis=0, concat_axis=0, tiled=True, axis_index_groups=groups
    )


def after(value, *others):
    return lax.optimization_barrier((value, *others))[0]


def local(
    x_in,
    z_gate,
    dt_low,
    dt_weight,
    dt_bias,
    a_log,
    conv_weight,
    conv_bias,
    d_skip,
    b_and_c,
    hidden,
    router,
    expert_ids,
    w_gate,
    w_down,
):
    blocks = lax.axis_size("seq")
    feature_parts = lax.axis_size("exp")
    tokens, features = hidden.shape
    experts = router.shape[1]
    copies = blocks // experts
    pack = packing(features)
    ids = expert_ids.T

    outgoing, logits = route(ids, hidden, router.T, 1, pack)
    arrived = exchanged(outgoing.reshape((experts,) + outgoing.shape[2:]), copies)

    edge = after(x_in[tokens - (conv_weight.shape[0] - 1) :], logits)
    edge = lax.ppermute(edge, "seq", [(i, i + 1) for i in range(blocks - 1)])
    read, cum, ends = scan(
        x_in, edge, dt_low, dt_weight, dt_bias, a_log, conv_weight, conv_bias, d_skip, b_and_c
    )
    logits = lax.psum(logits, "exp")
    weights = blend_weights(ids, logits, 1, pack)

    arrived = after(arrived, ends)
    rows = [unpack(arrived, features, pack)]
    for d in range(1, copies):
        rows.append(turned_within(rows[0], copies, d))
    gated = []
    for part in rows:
        if gated:
            part = after(part, gated[-1][0])
        own = gate(part, w_gate)
        gated.append([own] + [turned(own, "exp", d) for d in range(1, feature_parts)])

    both, channels = ends.shape
    ends = after(ends, gated[-1][0])
    ends = lax.all_to_all(
        ends.reshape(both, blocks, channels // blocks).transpose(1, 0, 2),
        "seq", split_axis=0, concat_axis=0, tiled=True,
    )
    entering = prefix(ends)

    made = []
    for parts in gated[1:] + gated[:1]:
        made.append(down(parts, w_down, BF16 if len(made) < copies - 1 else F32))
    entering = after(entering, made[0])
    sums = [made[-1]]
    for d in range(1, copies):
        sums.append(turned_within(made[d - 1], copies, -d))

    entering = lax.all_to_all(entering, "seq", split_axis=0, concat_axis=0, tiled=True)
    entering = entering.transpose(1, 0, 2).reshape(both // 2, channels)
    mamba_out = finish(read, cum, z_gate, entering, a_log, b_and_c)

    back = exchanged(pack_sum(sums, experts, pack), copies)
    moe_out = combine(back, weights, tokens, features, pack)
    return mamba_out, moe_out


def solution(mesh):
    return jax.shard_map(
        local,
        mesh=mesh,
        in_specs=(
            P("seq", "exp"),
            P("seq", "exp"),
            P("seq", None),
            P(None, "exp"),
            P("exp"),
            P(None, "exp"),
            P(None, "exp"),
            P("exp"),
            P("exp"),
            P(None, None, "seq"),
            P("seq", "exp"),
            P("exp", None),
            P("seq", None),
            P("exp", "seq"),
            P("seq", "exp"),
        ),
        out_specs=(P("seq", "exp"), P("seq", "exp")),
        check_vma=False,
    )
```

```python
import functools
import math

import jax
import jax.numpy as jnp
from jax import lax
from jax.experimental import pallas as pl
from jax.experimental.pallas import tpu as pltpu
from jax.sharding import PartitionSpec as P

CAP = 18
MIB = 1 << 20
LOG2E = math.log2(math.e)
F32 = jnp.float32
BF16 = jnp.bfloat16


def params(limit):
    return pltpu.CompilerParams(vmem_limit_bytes=limit * MIB)


def cost(flops, moved, transcendentals=0):
    return pl.CostEstimate(
        flops=int(flops), bytes_accessed=int(moved), transcendentals=int(transcendentals)
    )


def in_hbm(*arrays):
    return [pltpu.with_memory_space_constraint(a, pltpu.HBM) for a in arrays]


def iota(shape, dim):
    return lax.broadcasted_iota(jnp.int32, shape, dim)


def dot(a, b):
    return jnp.dot(a, b, preferred_element_type=F32)


def dot_nt(a, b):
    return lax.dot_general(a, b, (((1,), (1,)), ((), ())), preferred_element_type=F32)


def packing(features):
    main = CAP // 16 * 16
    extra = CAP - main
    cuts = main // extra if extra and main % extra == 0 else 0
    if cuts and features % (cuts * 128) == 0:
        return main, extra, cuts, features // cuts
    return -(-CAP // 16) * 16, 0, 0, 0


def hits_and_slots(ids, experts):
    tokens = ids.shape[1]
    of = iota((experts, tokens), 0)
    hits = [(of == ids[k : k + 1]).astype(F32) for k in range(2)]
    before = (iota((tokens, tokens), 0) < iota((tokens, tokens), 1)).astype(BF16)
    earlier = dot((hits[0] + hits[1]).astype(BF16), before)
    slots = [jnp.sum(h * earlier, axis=0, keepdims=True).astype(jnp.int32) for h in hits]
    return hits, slots


def route_kernel(pack, ids_ref, hidden_ref, router_ref, out_ref, logits_ref):
    main, extra, cuts, width = pack
    experts, copies = out_ref.shape[:2]
    tokens, features = hidden_ref.shape
    ids = ids_ref[...]
    _, slots = hits_and_slots(ids, experts)
    hidden = hidden_ref[...]
    row = iota((experts * main, tokens), 0)
    picked = None
    for k in range(2):
        key = jnp.where(slots[k] < main, ids[k : k + 1] * main + slots[k], -1)
        hit = row == key
        picked = hit if picked is None else picked | hit
    packed = dot(picked.astype(BF16), hidden).astype(BF16)
    for e in range(experts):
        for m in range(copies):
            out_ref[e, m, :, :features] = packed[e * main : (e + 1) * main]
    if extra:
        picked = None
        for k in range(2):
            key = jnp.where(slots[k] >= main, ids[k : k + 1] * extra + slots[k] - main, -1)
            hit = row // cuts == key
            picked = hit if picked is None else picked | hit
        total = None
        for c in range(cuts):
            chosen = (picked & (row % cuts == c)).astype(BF16)
            part = dot(chosen, hidden[:, c * width : (c + 1) * width])
            total = part if total is None else total + part
        total = total.astype(BF16)
        for e in range(experts):
            for m in range(copies):
                out_ref[e, m, :, features:] = total[e * main : (e + 1) * main]
    logits_ref[...] = dot_nt(hidden, router_ref[...])


def route(ids, hidden, router, copies, pack):
    main, _, _, width = pack
    tokens, features = hidden.shape
    experts = router.shape[0]
    return pl.pallas_call(
        functools.partial(route_kernel, pack),
        out_shape=(
            jax.ShapeDtypeStruct((experts, copies, main, features + width), BF16),
            jax.ShapeDtypeStruct((tokens, experts), F32),
        ),
        compiler_params=params(40),
        cost_estimate=cost(2 * tokens * experts * main * features * 2, hidden.size * 8),
        name="route",
    )(ids, *in_hbm(hidden, router))


def weights_kernel(pack, copies, ids_ref, logits_ref, main_ref, extra_ref, gates_ref):
    main, extra, cuts, _ = pack
    tokens, experts = logits_ref.shape
    ids = ids_ref[...]
    hits, slots = hits_and_slots(ids, experts)
    eye = (iota((tokens, tokens), 0) == iota((tokens, tokens), 1)).astype(BF16)
    logits = logits_ref[...]
    columns = [dot_nt(eye, h.astype(BF16)) for h in hits]
    picked = [jnp.sum(c * logits, axis=1, keepdims=True) for c in columns]
    expert = iota((tokens, experts), 1).astype(F32)
    total = experts * copies * main
    col = iota((tokens, total), 1)
    for k in range(2):
        gate = jax.nn.sigmoid(picked[k] - picked[1 - k])
        gates_ref[k] = jnp.broadcast_to(gate, gates_ref.shape[1:])
        named = jnp.sum(columns[k] * expert, axis=1, keepdims=True).astype(jnp.int32)
        wide = jnp.broadcast_to(slots[k].astype(F32), (8, tokens)).astype(BF16)
        slot = dot_nt(eye, wide)[:, :1].astype(jnp.int32)
        mine = col // (copies * main) == named
        main_ref[k] = (mine & (col % main == slot)).astype(BF16)
        if extra:
            place = (col % main) // cuts + main
            extra_ref[k] = (mine & (place == slot)).astype(BF16)
        else:
            extra_ref[k] = jnp.zeros(extra_ref.shape[1:], BF16)


def blend_weights(ids, logits, copies, pack):
    tokens, experts = logits.shape
    total = experts * copies * pack[0]
    return pl.pallas_call(
        functools.partial(weights_kernel, pack, copies),
        out_shape=(
            jax.ShapeDtypeStruct((2, tokens, total), BF16),
            jax.ShapeDtypeStruct((2, tokens, total), BF16),
            jax.ShapeDtypeStruct((2, tokens, 128), F32),
        ),
        compiler_params=params(40),
        cost_estimate=cost(2 * tokens * total * 16, tokens * total * 8),
        name="blend_weights",
    )(ids, logits)


ANYWHERE = pl.BlockSpec(memory_space=pl.ANY)
INSIDE = pl.BlockSpec(memory_space=pltpu.VMEM)
AHEAD = 6


def streamed(from_ref, to_ref, sems, dim, chunk, use, begin=None):
    count = from_ref.shape[dim] // chunk

    def copy(i):
        at = pl.ds(pl.multiple_of(i * chunk, chunk), chunk)
        part = (slice(None), at) if dim else (at, slice(None))
        return pltpu.make_async_copy(from_ref.at[part], to_ref.at[part], sems.at[i])

    for i in range(min(AHEAD, count)):
        copy(i).start()
    if begin is not None:
        begin()

    def step(i, carry):
        copy(i).wait()

        @pl.when(i + AHEAD < count)
        def _():
            copy(i + AHEAD).start()

        use(i)
        return carry

    lax.fori_loop(0, count, step, 0)


def gate_kernel(chunk, x_ref, w_ref, out_ref, held_ref, sems):
    def use(i):
        at = pl.ds(pl.multiple_of(i * chunk, chunk), chunk)
        out_ref[:, at] = dot(x_ref[...], held_ref[:, at]).astype(BF16)

    streamed(w_ref, held_ref, sems, 1, chunk, use)


def gate(x, w_gate):
    rows, features = x.shape
    amount = w_gate.shape[1]
    chunk = math.gcd(256, amount)
    return pl.pallas_call(
        functools.partial(gate_kernel, chunk),
        in_specs=[INSIDE, ANYWHERE],
        out_specs=INSIDE,
        out_shape=jax.ShapeDtypeStruct((rows, amount), BF16),
        scratch_shapes=[
            pltpu.VMEM(w_gate.shape, BF16),
            pltpu.SemaphoreType.DMA((amount // chunk,)),
        ],
        compiler_params=params(44),
        cost_estimate=cost(2 * rows * features * amount, features * amount * 2),
        name="gate",
    )(x, *in_hbm(w_gate))


def fill_acted(chunk, part_refs, acted_ref):
    def piece(i):
        at = pl.ds(pl.multiple_of(i * chunk, chunk), chunk)
        total = part_refs[0][:, at].astype(F32)
        for ref in part_refs[1:]:
            total = total + ref[:, at].astype(F32)
        acted_ref[:, at] = (total * jax.nn.sigmoid(total)).astype(BF16)

    pl.loop(0, acted_ref.shape[1] // chunk)(piece)


def down_kernel(chunk, *refs):
    part_refs, w_ref, out_ref, acted_ref, held_ref, sems = refs[:-5], *refs[-5:]

    def use(i):
        at = pl.ds(pl.multiple_of(i * chunk, chunk), chunk)
        out_ref[:, at] = dot(acted_ref[...], held_ref[:, at]).astype(out_ref.dtype)

    def begin():
        fill_acted(math.gcd(512, acted_ref.shape[1]), part_refs, acted_ref)

    streamed(w_ref, held_ref, sems, 1, chunk, use, begin)


def down(parts, w_down, dtype):
    rows, amount = parts[0].shape
    features = w_down.shape[1]
    chunk = math.gcd(256, features)
    return pl.pallas_call(
        functools.partial(down_kernel, chunk),
        in_specs=[INSIDE] * len(parts) + [ANYWHERE],
        out_specs=INSIDE,
        out_shape=jax.ShapeDtypeStruct((rows, features), dtype),
        scratch_shapes=[
            pltpu.VMEM((rows, amount), BF16),
            pltpu.VMEM(w_down.shape, BF16),
            pltpu.SemaphoreType.DMA((features // chunk,)),
        ],
        compiler_params=params(48),
        cost_estimate=cost(2 * rows * features * amount, features * amount * 2),
        name="down",
    )(*parts, *in_hbm(w_down))


def unpack_kernel(pack, arrived_ref, out_ref):
    main, extra, cuts, width = pack
    sources = arrived_ref.shape[0]
    features = out_ref.shape[1]
    out_ref[: sources * main] = arrived_ref[:, :, :features].reshape(sources * main, features)
    if extra:
        folded = arrived_ref[:, :, features:].reshape(sources * main, width)
        shape = (sources * extra, sources * main)
        for c in range(cuts):
            pick = (iota(shape, 1) == iota(shape, 0) * cuts + c).astype(BF16)
            out_ref[sources * main :, c * width : (c + 1) * width] = dot(pick, folded).astype(BF16)


def unpack(arrived, features, pack):
    main, extra, _, _ = pack
    rows = arrived.shape[0] * (main + extra)
    return pl.pallas_call(
        functools.partial(unpack_kernel, pack),
        out_shape=jax.ShapeDtypeStruct((rows, features), BF16),
        compiler_params=params(24),
        cost_estimate=cost(arrived.size * 16, arrived.size * 4),
        name="unpack",
    )(arrived)


def pack_kernel(pack, *refs):
    main, extra, cuts, width = pack
    part_refs, out_ref = refs[:-1], refs[-1]
    sources = out_ref.shape[0]
    features = part_refs[0].shape[1]
    first = sources * main

    def total(rows, columns):
        value = part_refs[0][rows, columns].astype(F32)
        for ref in part_refs[1:]:
            value = value + ref[rows, columns].astype(F32)
        return value.astype(BF16)

    made = total(slice(0, first), slice(0, features))
    out_ref[:, :, :features] = made.reshape(sources, main, features)
    if extra:
        shape = (sources * main, sources * extra)
        folded = None
        for c in range(cuts):
            piece = total(slice(first, None), slice(c * width, (c + 1) * width))
            pick = (iota(shape, 0) == iota(shape, 1) * cuts + c).astype(BF16)
            part = dot(pick, piece)
            folded = part if folded is None else folded + part
        out_ref[:, :, features:] = folded.astype(BF16).reshape(sources, main, width)


def pack_sum(parts, sources, pack):
    main, _, _, width = pack
    features = parts[0].shape[1]
    return pl.pallas_call(
        functools.partial(pack_kernel, pack),
        out_shape=jax.ShapeDtypeStruct((sources, main, features + width), BF16),
        compiler_params=params(24),
        cost_estimate=cost(parts[0].size * 16, parts[0].size * 8),
        name="pack_sum",
    )(*parts)


def combine_kernel(pack, back_ref, main_ref, extra_ref, gates_ref, out_ref):
    main, extra, cuts, width = pack
    sources = back_ref.shape[0]
    tokens, features = out_ref.shape
    back = back_ref[:, :, :features].reshape(sources * main, features)
    folded = back_ref[:, :, features:].reshape(sources * main, width) if extra else None
    total = None
    for k in range(2):
        rows = dot(main_ref[k], back)
        if extra:
            chosen = extra_ref[k]
            at = iota(chosen.shape, 1) % cuts
            pieces = [
                dot(jnp.where(at == c, chosen, jnp.zeros_like(chosen)), folded) for c in range(cuts)
            ]
            rows = rows + jnp.concatenate(pieces, axis=1)
        weighed = rows * gates_ref[k][:, :1]
        total = weighed if total is None else total + weighed
    out_ref[...] = total.astype(BF16)


def combine(back, weights, tokens, features, pack):
    return pl.pallas_call(
        functools.partial(combine_kernel, pack),
        out_shape=jax.ShapeDtypeStruct((tokens, features), BF16),
        compiler_params=params(40),
        cost_estimate=cost(4 * tokens * back.size, back.size * 2),
        name="combine",
    )(back, *weights)


def spread_states(values, spread_ref):
    for t in range(spread_ref.shape[0]):
        spread_ref[t] = jnp.broadcast_to(values[:, t : t + 1], spread_ref.shape[1:])


def fill_readers(values, readers_ref):
    states, tokens = values.shape
    shape = (states, 8 * states)
    copy = (iota(shape, 1) % states == iota(shape, 0)).astype(BF16)
    wide = (tokens, 8 * states)
    own = iota(wide, 1) // states == iota(wide, 0) % 8
    high = values.astype(BF16)
    low = (values - high.astype(F32)).astype(BF16)
    for place, part in enumerate((high, low)):
        rows = lax.dot_general(part, copy, (((0,), (0,)), ((), ())), preferred_element_type=F32)
        rows = jnp.where(own, rows, 0.0)
        for g in range(tokens // 8):
            readers_ref[g, place * 8 : place * 8 + 8] = rows[g * 8 : g * 8 + 8]


def read_out(readers, stacked):
    both = dot(readers.astype(BF16), jnp.concatenate(stacked, axis=0))
    return both[:8] + both[8:]


def tiled_lanes(value, lanes):
    return jnp.concatenate([value] * (lanes // value.shape[1]), axis=1)


def scan_kernel(
    x_ref, edge_ref, low_ref, dtw_ref, dtb_ref, alog_ref, cw_ref, cb_ref, skip_ref, bc_ref,
    read_ref, cum_ref, ends_ref, padded, delta_ref, fed_ref, b_ref, readers_ref,
):
    tokens, lanes = x_ref.shape
    taps = cw_ref.shape[0]
    states = alog_ref.shape[0]

    @pl.when(pl.program_id(0) == 0)
    def _():
        spread_states(bc_ref[0], b_ref)
        fill_readers(bc_ref[1], readers_ref)

    padded[8:] = x_ref[...].astype(F32)
    padded[8 - (taps - 1) : 8] = edge_ref[...].astype(F32)
    conv = jnp.broadcast_to(cb_ref[...], (tokens, lanes))
    for k in range(taps):
        at = 8 - (taps - 1) + k
        conv = conv + cw_ref[k : k + 1] * padded[at : at + tokens]
    act = conv * jax.nn.sigmoid(conv)
    raw = dot(low_ref[...], dtw_ref[...]) + dtb_ref[...]
    delta = jnp.maximum(raw, 0.0) + jnp.log1p(jnp.exp(-jnp.abs(raw)))
    delta_ref[...] = delta
    fed_ref[...] = delta * act
    read_ref[...] = skip_ref[...] * act
    rates = -jnp.exp(alog_ref[...]) * LOG2E

    def eight(g, carry):
        state, running = carry
        at = pl.multiple_of(g * 8, 8)
        delta8 = delta_ref[pl.ds(at, 8)]
        fed8 = fed_ref[pl.ds(at, 8)]
        stacked, sums = [], []
        for i in range(8):
            step = delta8[i : i + 1]
            running = running + step
            factor = jnp.exp2(rates * step)
            state = factor * state + tiled_lanes(b_ref[at + i], lanes) * fed8[i : i + 1]
            stacked.append(state.astype(BF16))
            sums.append(running)
        read_ref[pl.ds(at, 8)] += read_out(readers_ref[g], stacked)
        cum_ref[pl.ds(at, 8)] = jnp.concatenate(sums, axis=0)
        return state, running

    state, running = lax.fori_loop(
        0, tokens // 8, eight, (jnp.zeros((states, lanes), F32), jnp.zeros((1, lanes), F32))
    )
    ends_ref[:states] = state.astype(BF16)
    ends_ref[states:] = jnp.exp2(rates * running).astype(BF16)


def scan(x_in, edge, dt_low, dt_weight, dt_bias, a_log, conv_weight, conv_bias, d_skip, b_and_c):
    tokens, channels = x_in.shape
    states = a_log.shape[0]
    lanes = math.gcd(512, channels)

    def cut(rows):
        return pl.BlockSpec((rows, lanes), lambda i: (0, i))

    def whole(a):
        zeros = (0,) * a.ndim
        return pl.BlockSpec(a.shape, lambda i: zeros)

    return pl.pallas_call(
        scan_kernel,
        grid=(channels // lanes,),
        in_specs=[
            cut(tokens), cut(edge.shape[0]), whole(dt_low), cut(dt_weight.shape[0]), cut(1),
            cut(states), cut(conv_weight.shape[0]), cut(1), cut(1), whole(b_and_c),
        ],
        out_specs=(cut(tokens), cut(tokens), cut(2 * states)),
        out_shape=(
            pltpu.HBM((tokens, channels), F32),
            pltpu.HBM((tokens, channels), F32),
            jax.ShapeDtypeStruct((2 * states, channels), BF16),
        ),
        scratch_shapes=[
            pltpu.VMEM((tokens + 8, lanes), F32),
            pltpu.VMEM((tokens, lanes), F32),
            pltpu.VMEM((tokens, lanes), F32),
            pltpu.VMEM((tokens, states, 128), F32),
            pltpu.VMEM((tokens // 8, 16, 8 * states), F32),
        ],
        compiler_params=params(40),
        cost_estimate=cost(
            tokens * channels * states * 8, tokens * channels * 12, tokens * channels * states
        ),
        name="scan",
    )(
        *in_hbm(x_in),
        edge,
        *in_hbm(
            dt_low, dt_weight, dt_bias[None], a_log, conv_weight, conv_bias[None], d_skip[None],
            b_and_c,
        ),
    )


def prefix_kernel(ends_ref, out_ref):
    blocks, states, lanes = out_ref.shape
    entering = jnp.zeros((states, lanes), F32)
    for i in range(blocks):
        out_ref[i] = entering.astype(BF16)
        entering = (
            ends_ref[i, states:].astype(F32) * entering + ends_ref[i, :states].astype(F32)
        )


def prefix(ends):
    blocks, both, lanes = ends.shape
    return pl.pallas_call(
        prefix_kernel,
        out_shape=jax.ShapeDtypeStruct((blocks, both // 2, lanes), BF16),
        compiler_params=params(16),
        cost_estimate=cost(ends.size, ends.size * 3),
        name="prefix",
    )(ends)


def finish_kernel(read_ref, cum_ref, z_ref, enter_ref, alog_ref, bc_ref, out_ref, sum_ref, readers_ref):
    tokens, lanes = z_ref.shape

    @pl.when(pl.program_id(0) == 0)
    def _():
        fill_readers(bc_ref[1], readers_ref)

    rates = -jnp.exp(alog_ref[...]) * LOG2E
    entering = enter_ref[...].astype(F32)

    def eight(g, carry):
        at = pl.multiple_of(g * 8, 8)
        cum8 = cum_ref[pl.ds(at, 8)]
        stacked = []
        for i in range(8):
            stacked.append((jnp.exp2(rates * cum8[i : i + 1]) * entering).astype(BF16))
        sum_ref[pl.ds(at, 8)] = read_out(readers_ref[g], stacked)
        return carry

    lax.fori_loop(0, tokens // 8, eight, 0)
    z = z_ref[...].astype(F32)
    out_ref[...] = ((read_ref[...] + sum_ref[...]) * (z * jax.nn.sigmoid(z))).astype(BF16)


def finish(read, cum, z_gate, entering, a_log, b_and_c):
    tokens, channels = z_gate.shape
    states = a_log.shape[0]
    lanes = math.gcd(512, channels)

    def cut(rows):
        return pl.BlockSpec((rows, lanes), lambda i: (0, i))

    return pl.pallas_call(
        finish_kernel,
        grid=(channels // lanes,),
        in_specs=[
            cut(tokens), cut(tokens), cut(tokens), cut(states), cut(states),
            pl.BlockSpec(b_and_c.shape, lambda i: (0, 0, 0)),
        ],
        out_specs=cut(tokens),
        out_shape=jax.ShapeDtypeStruct((tokens, channels), BF16),
        scratch_shapes=[
            pltpu.VMEM((tokens, lanes), F32),
            pltpu.VMEM((tokens // 8, 16, 8 * states), F32),
        ],
        compiler_params=params(40),
        cost_estimate=cost(
            tokens * channels * states * 5, tokens * channels * 12, tokens * channels * states
        ),
        name="finish",
    )(*in_hbm(read, cum, z_gate), entering, *in_hbm(a_log, b_and_c))


def turned(value, axis, by):
    count = lax.axis_size(axis)
    return lax.ppermute(value, axis, [(i, (i + by) % count) for i in range(count)])


def turned_within(value, copies, by):
    count = lax.axis_size("seq")
    return lax.ppermute(
        value, "seq", [(i, i // copies * copies + (i + by) % copies) for i in range(count)]
    )


def exchanged(value, copies):
    count = lax.axis_size("seq")
    groups = [list(range(m, count, copies)) for m in range(copies)]
    return lax.all_to_all(
        value, "seq", split_axis=0, concat_axis=0, tiled=True, axis_index_groups=groups
    )


def after(value, *others):
    return lax.optimization_barrier((value, *others))[0]


def local(
    x_in,
    z_gate,
    dt_low,
    dt_weight,
    dt_bias,
    a_log,
    conv_weight,
    conv_bias,
    d_skip,
    b_and_c,
    hidden,
    router,
    expert_ids,
    w_gate,
    w_down,
):
    blocks = lax.axis_size("seq")
    feature_parts = lax.axis_size("exp")
    tokens, features = hidden.shape
    experts = router.shape[1]
    copies = blocks // experts
    pack = packing(features)
    ids = expert_ids.T

    edge = x_in[tokens - (conv_weight.shape[0] - 1) :]
    edge = lax.ppermute(edge, "seq", [(i, i + 1) for i in range(blocks - 1)])
    outgoing, logits = route(ids, hidden, router.T, 1, pack)
    outgoing = after(outgoing, edge)
    arrived = exchanged(outgoing.reshape((experts,) + outgoing.shape[2:]), copies)

    read, cum, ends = scan(
        x_in, edge, dt_low, dt_weight, dt_bias, a_log, conv_weight, conv_bias, d_skip, b_and_c
    )
    both, channels = ends.shape
    arrived = after(arrived, ends)
    ends = lax.all_to_all(
        ends.reshape(both, blocks, channels // blocks).transpose(1, 0, 2),
        "seq", split_axis=0, concat_axis=0, tiled=True,
    )

    rows = [unpack(arrived, features, pack)]
    for d in range(1, copies):
        rows.append(turned_within(rows[0], copies, d))
    gated = []
    for part in rows:
        if len(gated) == 1:
            entering = prefix(after(ends, gated[0][0]))
            part = after(part, entering)
        else:
            part = after(part, gated[-1][0] if gated else ends)
        own = gate(part, w_gate)
        gated.append([own] + [turned(own, "exp", d) for d in range(1, feature_parts)])
    entering = after(entering, gated[-1][0])
    entering = lax.all_to_all(entering, "seq", split_axis=0, concat_axis=0, tiled=True)
    gated[-1] = list(lax.optimization_barrier((*gated[-1], entering))[:-1])

    made = []
    for parts in gated[1:] + gated[:1]:
        made.append(down(parts, w_down, BF16 if len(made) < copies - 1 else F32))
    sums = [made[-1]]
    for d in range(1, copies):
        sums.append(turned_within(made[d - 1], copies, -d))
    packed = pack_sum(sums, experts, pack)
    back = exchanged(packed, copies)

    logits = lax.psum(after(logits, packed), "exp")
    weights = blend_weights(ids, logits, 1, pack)
    entering = entering.transpose(1, 0, 2).reshape(both // 2, channels)
    mamba_out = finish(read, cum, z_gate, after(entering, packed), a_log, b_and_c)
    moe_out = combine(back, weights, tokens, features, pack)
    return mamba_out, moe_out


def solution(mesh):
    return jax.shard_map(
        local,
        mesh=mesh,
        in_specs=(
            P("seq", "exp"),
            P("seq", "exp"),
            P("seq", None),
            P(None, "exp"),
            P("exp"),
            P(None, "exp"),
            P(None, "exp"),
            P("exp"),
            P("exp"),
            P(None, None, "seq"),
            P("seq", "exp"),
            P("exp", None),
            P("seq", None),
            P("exp", "seq"),
            P("seq", "exp"),
        ),
        out_specs=(P("seq", "exp"), P("seq", "exp")),
        check_vma=False,
    )
```

```python
import functools
import math

import jax
import jax.numpy as jnp
from jax import lax
from jax.experimental import pallas as pl
from jax.experimental.pallas import tpu as pltpu
from jax.sharding import PartitionSpec as P

CAP = 18
MIB = 1 << 20
LOG2E = math.log2(math.e)
F32 = jnp.float32
BF16 = jnp.bfloat16


def params(limit):
    return pltpu.CompilerParams(vmem_limit_bytes=limit * MIB)


def cost(flops, moved, transcendentals=0):
    return pl.CostEstimate(
        flops=int(flops), bytes_accessed=int(moved), transcendentals=int(transcendentals)
    )


def in_hbm(*arrays):
    return [pltpu.with_memory_space_constraint(a, pltpu.HBM) for a in arrays]


def iota(shape, dim):
    return lax.broadcasted_iota(jnp.int32, shape, dim)


def dot(a, b):
    return jnp.dot(a, b, preferred_element_type=F32)


def dot_nt(a, b):
    return lax.dot_general(a, b, (((1,), (1,)), ((), ())), preferred_element_type=F32)


def packing(features):
    main = CAP // 16 * 16
    extra = CAP - main
    cuts = main // extra if extra and main % extra == 0 else 0
    if cuts and features % (cuts * 128) == 0:
        return main, extra, cuts, features // cuts
    return -(-CAP // 16) * 16, 0, 0, 0


def hits_and_slots(ids, experts):
    tokens = ids.shape[1]
    of = iota((experts, tokens), 0)
    hits = [(of == ids[k : k + 1]).astype(F32) for k in range(2)]
    before = (iota((tokens, tokens), 0) < iota((tokens, tokens), 1)).astype(BF16)
    earlier = dot((hits[0] + hits[1]).astype(BF16), before)
    slots = [jnp.sum(h * earlier, axis=0, keepdims=True).astype(jnp.int32) for h in hits]
    return hits, slots


def route_kernel(pack, ids_ref, hidden_ref, router_ref, out_ref, logits_ref):
    main, extra, cuts, width = pack
    experts, copies = out_ref.shape[:2]
    tokens, features = hidden_ref.shape
    ids = ids_ref[...]
    _, slots = hits_and_slots(ids, experts)
    hidden = hidden_ref[...]
    row = iota((experts * main, tokens), 0)
    picked = None
    for k in range(2):
        key = jnp.where(slots[k] < main, ids[k : k + 1] * main + slots[k], -1)
        hit = row == key
        picked = hit if picked is None else picked | hit
    packed = dot(picked.astype(BF16), hidden).astype(BF16)
    for e in range(experts):
        for m in range(copies):
            out_ref[e, m, :, :features] = packed[e * main : (e + 1) * main]
    if extra:
        picked = None
        for k in range(2):
            key = jnp.where(slots[k] >= main, ids[k : k + 1] * extra + slots[k] - main, -1)
            hit = row // cuts == key
            picked = hit if picked is None else picked | hit
        total = None
        for c in range(cuts):
            chosen = (picked & (row % cuts == c)).astype(BF16)
            part = dot(chosen, hidden[:, c * width : (c + 1) * width])
            total = part if total is None else total + part
        total = total.astype(BF16)
        for e in range(experts):
            for m in range(copies):
                out_ref[e, m, :, features:] = total[e * main : (e + 1) * main]
    logits_ref[...] = dot_nt(hidden, router_ref[...])


def route(ids, hidden, router, copies, pack):
    main, _, _, width = pack
    tokens, features = hidden.shape
    experts = router.shape[0]
    return pl.pallas_call(
        functools.partial(route_kernel, pack),
        out_shape=(
            jax.ShapeDtypeStruct((experts, copies, main, features + width), BF16),
            jax.ShapeDtypeStruct((tokens, experts), F32),
        ),
        compiler_params=params(40),
        cost_estimate=cost(2 * tokens * experts * main * features * 2, hidden.size * 8),
        name="route",
    )(*in_hbm(ids, hidden, router))


def weights_kernel(pack, copies, ids_ref, *refs):
    logits_refs, (main_ref, extra_ref, gates_ref) = refs[:-3], refs[-3:]
    main, extra, cuts, _ = pack
    tokens, experts = logits_refs[0].shape
    ids = ids_ref[...]
    hits, slots = hits_and_slots(ids, experts)
    eye = (iota((tokens, tokens), 0) == iota((tokens, tokens), 1)).astype(BF16)
    logits = logits_refs[0][...]
    for ref in logits_refs[1:]:
        logits = logits + ref[...]
    columns = [dot_nt(eye, h.astype(BF16)) for h in hits]
    picked = [jnp.sum(c * logits, axis=1, keepdims=True) for c in columns]
    expert = iota((tokens, experts), 1).astype(F32)
    total = experts * copies * main
    col = iota((tokens, total), 1)
    for k in range(2):
        gate = jax.nn.sigmoid(picked[k] - picked[1 - k])
        gates_ref[k] = jnp.broadcast_to(gate, gates_ref.shape[1:])
        named = jnp.sum(columns[k] * expert, axis=1, keepdims=True).astype(jnp.int32)
        wide = jnp.broadcast_to(slots[k].astype(F32), (8, tokens)).astype(BF16)
        slot = dot_nt(eye, wide)[:, :1].astype(jnp.int32)
        mine = col // (copies * main) == named
        main_ref[k] = (mine & (col % main == slot)).astype(BF16)
        if extra:
            place = (col % main) // cuts + main
            extra_ref[k] = (mine & (place == slot)).astype(BF16)
        else:
            extra_ref[k] = jnp.zeros(extra_ref.shape[1:], BF16)


def blend_weights(ids, logits, copies, pack):
    tokens, experts = logits[0].shape
    total = experts * copies * pack[0]
    return pl.pallas_call(
        functools.partial(weights_kernel, pack, copies),
        out_shape=(
            jax.ShapeDtypeStruct((2, tokens, total), BF16),
            jax.ShapeDtypeStruct((2, tokens, total), BF16),
            jax.ShapeDtypeStruct((2, tokens, 128), F32),
        ),
        compiler_params=params(40),
        cost_estimate=cost(2 * tokens * total * 16, tokens * total * 8),
        name="blend_weights",
    )(*in_hbm(ids), *logits)


ANYWHERE = pl.BlockSpec(memory_space=pl.ANY)
INSIDE = pl.BlockSpec(memory_space=pltpu.VMEM)
AHEAD = 6


def streamed(from_ref, to_ref, sems, dim, chunk, use, begin=None):
    count = from_ref.shape[dim] // chunk

    def copy(i):
        at = pl.ds(pl.multiple_of(i * chunk, chunk), chunk)
        part = (slice(None), at) if dim else (at, slice(None))
        return pltpu.make_async_copy(from_ref.at[part], to_ref.at[part], sems.at[i])

    for i in range(min(AHEAD, count)):
        copy(i).start()
    if begin is not None:
        begin()

    def step(i, carry):
        copy(i).wait()

        @pl.when(i + AHEAD < count)
        def _():
            copy(i + AHEAD).start()

        use(i)
        return carry

    lax.fori_loop(0, count, step, 0)


def gate_kernel(chunk, x_ref, w_ref, out_ref, held_ref, sems):
    def use(i):
        at = pl.ds(pl.multiple_of(i * chunk, chunk), chunk)
        out_ref[:, at] = dot(x_ref[...], held_ref[:, at]).astype(BF16)

    streamed(w_ref, held_ref, sems, 1, chunk, use)


def gate(x, w_gate):
    rows, features = x.shape
    amount = w_gate.shape[1]
    chunk = math.gcd(512, amount)
    return pl.pallas_call(
        functools.partial(gate_kernel, chunk),
        in_specs=[INSIDE, ANYWHERE],
        out_specs=INSIDE,
        out_shape=jax.ShapeDtypeStruct((rows, amount), BF16),
        scratch_shapes=[
            pltpu.VMEM(w_gate.shape, BF16),
            pltpu.SemaphoreType.DMA((amount // chunk,)),
        ],
        compiler_params=params(44),
        cost_estimate=cost(rows, rows),
        name="gate",
    )(x, *in_hbm(w_gate))


def fill_acted(chunk, part_refs, acted_ref):
    def piece(i):
        at = pl.ds(pl.multiple_of(i * chunk, chunk), chunk)
        total = part_refs[0][:, at].astype(F32)
        for ref in part_refs[1:]:
            total = total + ref[:, at].astype(F32)
        acted_ref[:, at] = (total * jax.nn.sigmoid(total)).astype(BF16)

    pl.loop(0, acted_ref.shape[1] // chunk)(piece)


def down_kernel(chunk, *refs):
    part_refs, w_ref, out_ref, acted_ref, held_ref, sems = refs[:-5], *refs[-5:]

    def use(i):
        at = pl.ds(pl.multiple_of(i * chunk, chunk), chunk)
        out_ref[:, at] = dot(acted_ref[...], held_ref[:, at]).astype(out_ref.dtype)

    def begin():
        fill_acted(math.gcd(512, acted_ref.shape[1]), part_refs, acted_ref)

    streamed(w_ref, held_ref, sems, 1, chunk, use, begin)


def down(parts, w_down, dtype):
    rows, amount = parts[0].shape
    features = w_down.shape[1]
    chunk = math.gcd(256, features)
    return pl.pallas_call(
        functools.partial(down_kernel, chunk),
        in_specs=[INSIDE] * len(parts) + [ANYWHERE],
        out_specs=INSIDE,
        out_shape=jax.ShapeDtypeStruct((rows, features), dtype),
        scratch_shapes=[
            pltpu.VMEM((rows, amount), BF16),
            pltpu.VMEM(w_down.shape, BF16),
            pltpu.SemaphoreType.DMA((features // chunk,)),
        ],
        compiler_params=params(48),
        cost_estimate=cost(rows, rows),
        name="down",
    )(*parts, *in_hbm(w_down))


def unpack_kernel(pack, arrived_ref, out_ref):
    main, extra, cuts, width = pack
    sources = arrived_ref.shape[0]
    features = out_ref.shape[1]
    out_ref[: sources * main] = arrived_ref[:, :, :features].reshape(sources * main, features)
    if extra:
        folded = arrived_ref[:, :, features:].reshape(sources * main, width)
        shape = (sources * extra, sources * main)
        for c in range(cuts):
            pick = (iota(shape, 1) == iota(shape, 0) * cuts + c).astype(BF16)
            out_ref[sources * main :, c * width : (c + 1) * width] = dot(pick, folded).astype(BF16)


def unpack(arrived, features, pack):
    main, extra, _, _ = pack
    rows = arrived.shape[0] * (main + extra)
    return pl.pallas_call(
        functools.partial(unpack_kernel, pack),
        out_shape=jax.ShapeDtypeStruct((rows, features), BF16),
        compiler_params=params(24),
        cost_estimate=cost(arrived.size * 16, arrived.size * 4),
        name="unpack",
    )(arrived)


def pack_kernel(pack, *refs):
    main, extra, cuts, width = pack
    part_refs, out_ref = refs[:-1], refs[-1]
    sources = out_ref.shape[0]
    features = part_refs[0].shape[1]
    first = sources * main

    def total(rows, columns):
        value = part_refs[0][rows, columns].astype(F32)
        for ref in part_refs[1:]:
            value = value + ref[rows, columns].astype(F32)
        return value.astype(BF16)

    made = total(slice(0, first), slice(0, features))
    out_ref[:, :, :features] = made.reshape(sources, main, features)
    if extra:
        shape = (sources * main, sources * extra)
        folded = None
        for c in range(cuts):
            piece = total(slice(first, None), slice(c * width, (c + 1) * width))
            pick = (iota(shape, 0) == iota(shape, 1) * cuts + c).astype(BF16)
            part = dot(pick, piece)
            folded = part if folded is None else folded + part
        out_ref[:, :, features:] = folded.astype(BF16).reshape(sources, main, width)


def pack_sum(parts, sources, pack):
    main, _, _, width = pack
    features = parts[0].shape[1]
    return pl.pallas_call(
        functools.partial(pack_kernel, pack),
        out_shape=jax.ShapeDtypeStruct((sources, main, features + width), BF16),
        compiler_params=params(24),
        cost_estimate=cost(parts[0].size * 16, parts[0].size * 8),
        name="pack_sum",
    )(*parts)


def combine_kernel(pack, back_ref, main_ref, extra_ref, gates_ref, out_ref):
    main, extra, cuts, width = pack
    sources = back_ref.shape[0]
    tokens, features = out_ref.shape
    back = back_ref[:, :, :features].reshape(sources * main, features)
    folded = back_ref[:, :, features:].reshape(sources * main, width) if extra else None
    total = None
    for k in range(2):
        rows = dot(main_ref[k], back)
        if extra:
            chosen = extra_ref[k]
            at = iota(chosen.shape, 1) % cuts
            pieces = [
                dot(jnp.where(at == c, chosen, jnp.zeros_like(chosen)), folded) for c in range(cuts)
            ]
            rows = rows + jnp.concatenate(pieces, axis=1)
        weighed = rows * gates_ref[k][:, :1]
        total = weighed if total is None else total + weighed
    out_ref[...] = total.astype(BF16)


def combine(back, weights, tokens, features, pack):
    return pl.pallas_call(
        functools.partial(combine_kernel, pack),
        out_shape=jax.ShapeDtypeStruct((tokens, features), BF16),
        compiler_params=params(40),
        cost_estimate=cost(4 * tokens * back.size, back.size * 2),
        name="combine",
    )(back, *weights)


def spread_states(values, spread_ref):
    for t in range(spread_ref.shape[0]):
        spread_ref[t] = jnp.broadcast_to(values[:, t : t + 1], spread_ref.shape[1:])


def row_sums(parts):
    place = iota(parts[0].shape, 0)
    for stride in (4, 2, 1):
        low = place & stride == 0
        half = len(parts) // 2
        joined = []
        for a, b in zip(parts[:half], parts[half:]):
            kept = jnp.where(low, a, b)
            moved = jnp.where(low, b, a)
            if stride == 4:
                other = pltpu.roll(moved, 4, 0)
            else:
                other = jnp.where(low, pltpu.roll(moved, 8 - stride, 0), pltpu.roll(moved, stride, 0))
            joined.append(kept + other)
        parts = joined
    return parts[0]


def state_sum(value):
    total = value[:8]
    for at in range(8, value.shape[0], 8):
        total = total + value[at : at + 8]
    return total


def tiled_lanes(value, lanes):
    return jnp.concatenate([value] * (lanes // value.shape[1]), axis=1)


def scan_kernel(
    x_ref, edge_ref, low_ref, dtw_ref, dtb_ref, alog_ref, cw_ref, cb_ref, skip_ref, bc_ref,
    read_ref, cum_ref, ends_ref, padded, delta_ref, fed_ref, totals_ref, b_ref, c_ref,
):
    tokens, lanes = x_ref.shape
    taps = cw_ref.shape[0]
    states = alog_ref.shape[0]

    @pl.when(pl.program_id(0) == 0)
    def _():
        spread_states(bc_ref[0], b_ref)
        spread_states(bc_ref[1], c_ref)
        totals_ref[...] = jnp.zeros_like(totals_ref)

    padded[8:] = x_ref[...].astype(F32)
    padded[8 - (taps - 1) : 8] = edge_ref[...].astype(F32)
    conv = jnp.broadcast_to(cb_ref[...], (tokens, lanes))
    for k in range(taps):
        at = 8 - (taps - 1) + k
        conv = conv + cw_ref[k : k + 1] * padded[at : at + tokens]
    act = conv * jax.nn.sigmoid(conv)
    raw = dot(low_ref[...], dtw_ref[...]) + dtb_ref[...]
    delta = jnp.maximum(raw, 0.0) + jnp.log1p(jnp.exp(-jnp.abs(raw)))
    delta_ref[...] = delta
    fed_ref[...] = delta * act
    read_ref[...] = skip_ref[...] * act
    rates = -jnp.exp(alog_ref[...]) * LOG2E

    def eight(g, carry):
        state, running = carry
        at = pl.multiple_of(g * 8, 8)
        delta8 = delta_ref[pl.ds(at, 8)]
        fed8 = fed_ref[pl.ds(at, 8)]
        reads, sums = [], []
        for i in range(8):
            step = delta8[i : i + 1]
            running = running + step
            factor = jnp.exp2(rates * step)
            state = factor * state + tiled_lanes(b_ref[at + i], lanes) * fed8[i : i + 1]
            reads.append(state_sum(tiled_lanes(c_ref[at + i], lanes) * state))
            sums.append(running)
        read_ref[pl.ds(at, 8)] += row_sums(reads)
        cum_ref[pl.ds(at, 8)] = jnp.concatenate(sums, axis=0)
        return state, running

    state, running = lax.fori_loop(
        0, tokens // 8, eight, (jnp.zeros((states, lanes), F32), jnp.zeros((1, lanes), F32))
    )
    step, steps = pl.program_id(0), pl.num_programs(0)
    ends_ref[:, pl.ds(pl.multiple_of(step * lanes, lanes), lanes)] = state.astype(BF16)
    high = running.astype(BF16).astype(F32)
    totals_ref[pl.ds(step, 1)] = high
    totals_ref[pl.ds(steps + step, 1)] = running - high

    @pl.when(step == steps - 1)
    def _():
        ends_ref[:, ends_ref.shape[1] - lanes :] = totals_ref[...].astype(BF16)


def scan(x_in, edge, dt_low, dt_weight, dt_bias, a_log, conv_weight, conv_bias, d_skip, b_and_c):
    tokens, channels = x_in.shape
    states = a_log.shape[0]
    lanes = math.gcd(512, channels)

    def cut(rows):
        return pl.BlockSpec((rows, lanes), lambda i: (0, i))

    def whole(a):
        zeros = (0,) * a.ndim
        return pl.BlockSpec(a.shape, lambda i: zeros)

    return pl.pallas_call(
        scan_kernel,
        grid=(channels // lanes,),
        in_specs=[
            cut(tokens), cut(edge.shape[0]), whole(dt_low), cut(dt_weight.shape[0]), cut(1),
            cut(states), cut(conv_weight.shape[0]), cut(1), cut(1), whole(b_and_c),
        ],
        out_specs=(
            cut(tokens),
            cut(tokens),
            pl.BlockSpec((states, channels + lanes), lambda i: (0, 0)),
        ),
        out_shape=(
            pltpu.HBM((tokens, channels), F32),
            pltpu.HBM((tokens, channels), F32),
            jax.ShapeDtypeStruct((states, channels + lanes), BF16),
        ),
        scratch_shapes=[
            pltpu.VMEM((tokens + 8, lanes), F32),
            pltpu.VMEM((tokens, lanes), F32),
            pltpu.VMEM((tokens, lanes), F32),
            pltpu.VMEM((states, lanes), F32),
            pltpu.VMEM((tokens, states, 128), F32),
            pltpu.VMEM((tokens, states, 128), F32),
        ],
        compiler_params=params(40),
        cost_estimate=cost(
            tokens * channels * states * 8, tokens * channels * 12, tokens * channels * states
        ),
        name="scan",
    )(
        *in_hbm(x_in),
        edge,
        *in_hbm(
            dt_low, dt_weight, dt_bias[None], a_log, conv_weight, conv_bias[None], d_skip[None],
            b_and_c,
        ),
    )


def finish_kernel(
    read_ref, cum_ref, z_ref, ends_ref, totals_ref, alog_ref, bc_ref, out_ref, sum_ref, wide_ref, c_ref
):
    tokens, lanes = z_ref.shape
    states = alog_ref.shape[0]
    step, steps = pl.program_id(0), pl.num_programs(0)

    @pl.when(step == 0)
    def _():
        spread_states(bc_ref[1], c_ref)
        wide_ref[...] = totals_ref[...].astype(F32)

    rates = -jnp.exp(alog_ref[...]) * LOG2E

    def block(j, entering):
        at = pl.multiple_of(j * states, states)
        total = wide_ref[pl.ds(at + step, 1)] + wide_ref[pl.ds(at + steps + step, 1)]
        return jnp.exp2(rates * total) * entering + ends_ref[pl.ds(at, states)].astype(F32)

    entering = lax.fori_loop(0, lax.axis_index("seq"), block, jnp.zeros((states, lanes), F32))

    def eight(g, carry):
        at = pl.multiple_of(g * 8, 8)
        cum8 = cum_ref[pl.ds(at, 8)]
        reads = []
        for i in range(8):
            kept = jnp.exp2(rates * cum8[i : i + 1]) * entering
            reads.append(state_sum(tiled_lanes(c_ref[at + i], lanes) * kept))
        sum_ref[pl.ds(at, 8)] = row_sums(reads)
        return carry

    lax.fori_loop(0, tokens // 8, eight, 0)
    z = z_ref[...].astype(F32)
    out_ref[...] = ((read_ref[...] + sum_ref[...]) * (z * jax.nn.sigmoid(z))).astype(BF16)


def finish(read, cum, z_gate, ends, a_log, b_and_c):
    tokens, channels = z_gate.shape
    states = a_log.shape[0]
    rows, width = ends.shape
    lanes = width - channels

    def cut(rows):
        return pl.BlockSpec((rows, lanes), lambda i: (0, i))

    return pl.pallas_call(
        finish_kernel,
        grid=(channels // lanes,),
        in_specs=[
            cut(tokens), cut(tokens), cut(tokens), cut(rows),
            pl.BlockSpec((rows, lanes), lambda i: (0, channels // lanes)),
            cut(states),
            pl.BlockSpec(b_and_c.shape, lambda i: (0, 0, 0)),
        ],
        out_specs=cut(tokens),
        out_shape=jax.ShapeDtypeStruct((tokens, channels), BF16),
        scratch_shapes=[
            pltpu.VMEM((tokens, lanes), F32),
            pltpu.VMEM((rows, lanes), F32),
            pltpu.VMEM((tokens, states, 128), F32),
        ],
        compiler_params=params(40),
        cost_estimate=cost(
            tokens * channels * states * 5, tokens * channels * 12, tokens * channels * states
        ),
        name="finish",
    )(*in_hbm(read, cum, z_gate, ends, ends, a_log, b_and_c))


def turned(value, axis, by):
    count = lax.axis_size(axis)
    return lax.ppermute(value, axis, [(i, (i + by) % count) for i in range(count)])


def turned_within(value, copies, by):
    count = lax.axis_size("seq")
    return lax.ppermute(
        value, "seq", [(i, i // copies * copies + (i + by) % copies) for i in range(count)]
    )


def exchanged(value, copies):
    count = lax.axis_size("seq")
    groups = [list(range(m, count, copies)) for m in range(copies)]
    return lax.all_to_all(
        value, "seq", split_axis=0, concat_axis=0, tiled=True, axis_index_groups=groups
    )


def after(value, *others):
    return lax.optimization_barrier((value, *others))[0]


def local(
    x_in,
    z_gate,
    dt_low,
    dt_weight,
    dt_bias,
    a_log,
    conv_weight,
    conv_bias,
    d_skip,
    b_and_c,
    hidden,
    router,
    expert_ids,
    w_gate,
    w_down,
):
    blocks = lax.axis_size("seq")
    feature_parts = lax.axis_size("exp")
    tokens, features = hidden.shape
    experts = router.shape[1]
    copies = blocks // experts
    pack = packing(features)
    ids = expert_ids.T

    edge = x_in[tokens - (conv_weight.shape[0] - 1) :]
    edge = lax.ppermute(edge, "seq", [(i, i + 1) for i in range(blocks - 1)])
    outgoing, logits = route(ids, hidden, router.T, 1, pack)
    outgoing = after(outgoing, edge)
    arrived = exchanged(outgoing.reshape((experts,) + outgoing.shape[2:]), copies)

    read, cum, ends = scan(
        x_in, edge, dt_low, dt_weight, dt_bias, a_log, conv_weight, conv_bias, d_skip, b_and_c
    )
    arrived = after(arrived, ends)
    ends = lax.all_gather(ends, "seq", tiled=True)
    logits = [logits] + [turned(logits, "exp", d) for d in range(1, feature_parts)]
    weights = blend_weights(ids, logits, 1, pack)

    rows = [unpack(arrived, features, pack)]
    for d in range(1, copies):
        rows.append(turned_within(rows[0], copies, d))
    gated = []
    for part in rows:
        if gated:
            part = after(part, gated[-1][0])
        own = gate(part, w_gate)
        gated.append([own] + [turned(own, "exp", d) for d in range(1, feature_parts)])
    made = []
    for parts in gated[1:] + gated[:1]:
        made.append(down(parts, w_down, BF16 if len(made) < copies - 1 else F32))
    sums = [made[-1]]
    for d in range(1, copies):
        sums.append(turned_within(made[d - 1], copies, -d))
    packed = pack_sum(sums, experts, pack)
    back = exchanged(packed, copies)

    mamba_out = finish(read, cum, z_gate, after(ends, packed), a_log, b_and_c)
    back = after(back, mamba_out)
    moe_out = combine(back, weights, tokens, features, pack)
    return mamba_out, moe_out


def solution(mesh):
    return jax.shard_map(
        local,
        mesh=mesh,
        in_specs=(
            P("seq", "exp"),
            P("seq", "exp"),
            P("seq", None),
            P(None, "exp"),
            P("exp"),
            P(None, "exp"),
            P(None, "exp"),
            P("exp"),
            P("exp"),
            P(None, None, "seq"),
            P("seq", "exp"),
            P("exp", None),
            P("seq", None),
            P("exp", "seq"),
            P("seq", "exp"),
        ),
        out_specs=(P("seq", "exp"), P("seq", "exp")),
        check_vma=False,
    )
```

```python
import functools
import math

import jax
import jax.numpy as jnp
from jax import lax
from jax.experimental import pallas as pl
from jax.experimental.pallas import tpu as pltpu
from jax.sharding import PartitionSpec as P

CAP = 18
MIB = 1 << 20
LOG2E = math.log2(math.e)
F32 = jnp.float32
BF16 = jnp.bfloat16


def params(limit):
    return pltpu.CompilerParams(vmem_limit_bytes=limit * MIB)


def cost(flops, moved, transcendentals=0):
    return pl.CostEstimate(
        flops=int(flops), bytes_accessed=int(moved), transcendentals=int(transcendentals)
    )


def in_hbm(*arrays):
    return [pltpu.with_memory_space_constraint(a, pltpu.HBM) for a in arrays]


def iota(shape, dim):
    return lax.broadcasted_iota(jnp.int32, shape, dim)


def dot(a, b):
    return jnp.dot(a, b, preferred_element_type=F32)


def dot_nt(a, b):
    return lax.dot_general(a, b, (((1,), (1,)), ((), ())), preferred_element_type=F32)


def packing(features):
    main = CAP // 16 * 16
    extra = CAP - main
    cuts = main // extra if extra and main % extra == 0 else 0
    if cuts and features % (cuts * 128) == 0:
        return main, extra, cuts, features // cuts
    return -(-CAP // 16) * 16, 0, 0, 0


def hits_and_slots(ids, experts):
    tokens = ids.shape[1]
    of = iota((experts, tokens), 0)
    hits = [(of == ids[k : k + 1]).astype(F32) for k in range(2)]
    before = (iota((tokens, tokens), 0) < iota((tokens, tokens), 1)).astype(BF16)
    earlier = dot((hits[0] + hits[1]).astype(BF16), before)
    slots = [jnp.sum(h * earlier, axis=0, keepdims=True).astype(jnp.int32) for h in hits]
    return hits, slots


def route_kernel(pack, ids_ref, hidden_ref, router_ref, out_ref, logits_ref):
    main, extra, cuts, width = pack
    experts, copies = out_ref.shape[:2]
    tokens, features = hidden_ref.shape
    ids = ids_ref[...]
    _, slots = hits_and_slots(ids, experts)
    hidden = hidden_ref[...]
    row = iota((experts * main, tokens), 0)
    picked = None
    for k in range(2):
        key = jnp.where(slots[k] < main, ids[k : k + 1] * main + slots[k], -1)
        hit = row == key
        picked = hit if picked is None else picked | hit
    packed = dot(picked.astype(BF16), hidden).astype(BF16)
    for e in range(experts):
        for m in range(copies):
            out_ref[e, m, :, :features] = packed[e * main : (e + 1) * main]
    if extra:
        picked = None
        for k in range(2):
            key = jnp.where(slots[k] >= main, ids[k : k + 1] * extra + slots[k] - main, -1)
            hit = row // cuts == key
            picked = hit if picked is None else picked | hit
        total = None
        for c in range(cuts):
            chosen = (picked & (row % cuts == c)).astype(BF16)
            part = dot(chosen, hidden[:, c * width : (c + 1) * width])
            total = part if total is None else total + part
        total = total.astype(BF16)
        for e in range(experts):
            for m in range(copies):
                out_ref[e, m, :, features:] = total[e * main : (e + 1) * main]
    logits_ref[...] = dot_nt(hidden, router_ref[...])


def route(ids, hidden, router, copies, pack):
    main, _, _, width = pack
    tokens, features = hidden.shape
    experts = router.shape[0]
    return pl.pallas_call(
        functools.partial(route_kernel, pack),
        out_shape=(
            jax.ShapeDtypeStruct((experts, copies, main, features + width), BF16),
            jax.ShapeDtypeStruct((tokens, experts), F32),
        ),
        compiler_params=params(40),
        cost_estimate=cost(2 * tokens * experts * main * features * 2, hidden.size * 8),
        name="route",
    )(*in_hbm(ids, hidden, router))


def weights_kernel(pack, copies, ids_ref, *refs):
    logits_refs, (main_ref, extra_ref, gates_ref) = refs[:-3], refs[-3:]
    main, extra, cuts, _ = pack
    tokens, experts = logits_refs[0].shape
    ids = ids_ref[...]
    hits, slots = hits_and_slots(ids, experts)
    eye = (iota((tokens, tokens), 0) == iota((tokens, tokens), 1)).astype(BF16)
    logits = logits_refs[0][...]
    for ref in logits_refs[1:]:
        logits = logits + ref[...]
    columns = [dot_nt(eye, h.astype(BF16)) for h in hits]
    picked = [jnp.sum(c * logits, axis=1, keepdims=True) for c in columns]
    expert = iota((tokens, experts), 1).astype(F32)
    total = experts * copies * main
    col = iota((tokens, total), 1)
    for k in range(2):
        gate = jax.nn.sigmoid(picked[k] - picked[1 - k])
        gates_ref[k] = jnp.broadcast_to(gate, gates_ref.shape[1:])
        named = jnp.sum(columns[k] * expert, axis=1, keepdims=True).astype(jnp.int32)
        wide = jnp.broadcast_to(slots[k].astype(F32), (8, tokens)).astype(BF16)
        slot = dot_nt(eye, wide)[:, :1].astype(jnp.int32)
        mine = col // (copies * main) == named
        main_ref[k] = (mine & (col % main == slot)).astype(BF16)
        if extra:
            place = (col % main) // cuts + main
            extra_ref[k] = (mine & (place == slot)).astype(BF16)
        else:
            extra_ref[k] = jnp.zeros(extra_ref.shape[1:], BF16)


def blend_weights(ids, logits, copies, pack):
    tokens, experts = logits[0].shape
    total = experts * copies * pack[0]
    return pl.pallas_call(
        functools.partial(weights_kernel, pack, copies),
        out_shape=(
            jax.ShapeDtypeStruct((2, tokens, total), BF16),
            jax.ShapeDtypeStruct((2, tokens, total), BF16),
            jax.ShapeDtypeStruct((2, tokens, 128), F32),
        ),
        compiler_params=params(40),
        cost_estimate=cost(2 * tokens * total * 16, tokens * total * 8),
        name="blend_weights",
    )(*in_hbm(ids), *logits)


ANYWHERE = pl.BlockSpec(memory_space=pl.ANY)
INSIDE = pl.BlockSpec(memory_space=pltpu.VMEM)
AHEAD = 6


def streamed(from_ref, to_ref, sems, dim, chunk, use, begin=None):
    count = from_ref.shape[dim] // chunk

    def copy(i):
        at = pl.ds(pl.multiple_of(i * chunk, chunk), chunk)
        part = (slice(None), at) if dim else (at, slice(None))
        return pltpu.make_async_copy(from_ref.at[part], to_ref.at[part], sems.at[i])

    for i in range(min(AHEAD, count)):
        copy(i).start()
    if begin is not None:
        begin()

    def step(i, carry):
        copy(i).wait()

        @pl.when(i + AHEAD < count)
        def _():
            copy(i + AHEAD).start()

        use(i)
        return carry

    lax.fori_loop(0, count, step, 0)


def gate_kernel(chunk, x_ref, w_ref, out_ref, held_ref, sems):
    def use(i):
        at = pl.ds(pl.multiple_of(i * chunk, chunk), chunk)
        out_ref[:, at] = dot(x_ref[...], held_ref[:, at]).astype(BF16)

    streamed(w_ref, held_ref, sems, 1, chunk, use)


def gate(x, w_gate):
    rows, features = x.shape
    amount = w_gate.shape[1]
    chunk = math.gcd(512, amount)
    return pl.pallas_call(
        functools.partial(gate_kernel, chunk),
        in_specs=[INSIDE, ANYWHERE],
        out_specs=INSIDE,
        out_shape=jax.ShapeDtypeStruct((rows, amount), BF16),
        scratch_shapes=[
            pltpu.VMEM(w_gate.shape, BF16),
            pltpu.SemaphoreType.DMA((amount // chunk,)),
        ],
        compiler_params=params(44),
        cost_estimate=cost(2 * rows * features * amount, features * amount * 2),
        name="gate",
    )(x, *in_hbm(w_gate))


def fill_acted(chunk, part_refs, acted_ref):
    def piece(i):
        at = pl.ds(pl.multiple_of(i * chunk, chunk), chunk)
        total = part_refs[0][:, at].astype(F32)
        for ref in part_refs[1:]:
            total = total + ref[:, at].astype(F32)
        acted_ref[:, at] = (total * jax.nn.sigmoid(total)).astype(BF16)

    pl.loop(0, acted_ref.shape[1] // chunk)(piece)


def down_kernel(chunk, *refs):
    part_refs, w_ref, out_ref, acted_ref, held_ref, sems = refs[:-5], *refs[-5:]

    def use(i):
        at = pl.ds(pl.multiple_of(i * chunk, chunk), chunk)
        out_ref[:, at] = dot(acted_ref[...], held_ref[:, at]).astype(out_ref.dtype)

    def begin():
        fill_acted(math.gcd(512, acted_ref.shape[1]), part_refs, acted_ref)

    streamed(w_ref, held_ref, sems, 1, chunk, use, begin)


def down(parts, w_down, dtype):
    rows, amount = parts[0].shape
    features = w_down.shape[1]
    chunk = math.gcd(256, features)
    return pl.pallas_call(
        functools.partial(down_kernel, chunk),
        in_specs=[INSIDE] * len(parts) + [ANYWHERE],
        out_specs=INSIDE,
        out_shape=jax.ShapeDtypeStruct((rows, features), dtype),
        scratch_shapes=[
            pltpu.VMEM((rows, amount), BF16),
            pltpu.VMEM(w_down.shape, BF16),
            pltpu.SemaphoreType.DMA((features // chunk,)),
        ],
        compiler_params=params(48),
        cost_estimate=cost(2 * rows * features * amount, features * amount * 2),
        name="down",
    )(*parts, *in_hbm(w_down))


def unpack_kernel(pack, arrived_ref, out_ref):
    main, extra, cuts, width = pack
    sources = arrived_ref.shape[0]
    features = out_ref.shape[1]
    out_ref[: sources * main] = arrived_ref[:, :, :features].reshape(sources * main, features)
    if extra:
        folded = arrived_ref[:, :, features:].reshape(sources * main, width)
        shape = (sources * extra, sources * main)
        for c in range(cuts):
            pick = (iota(shape, 1) == iota(shape, 0) * cuts + c).astype(BF16)
            out_ref[sources * main :, c * width : (c + 1) * width] = dot(pick, folded).astype(BF16)


def unpack(arrived, features, pack):
    main, extra, _, _ = pack
    rows = arrived.shape[0] * (main + extra)
    return pl.pallas_call(
        functools.partial(unpack_kernel, pack),
        out_shape=jax.ShapeDtypeStruct((rows, features), BF16),
        compiler_params=params(24),
        cost_estimate=cost(arrived.size * 16, arrived.size * 4),
        name="unpack",
    )(arrived)


def pack_kernel(pack, *refs):
    main, extra, cuts, width = pack
    part_refs, out_ref = refs[:-1], refs[-1]
    sources = out_ref.shape[0]
    features = part_refs[0].shape[1]
    first = sources * main

    def total(rows, columns):
        value = part_refs[0][rows, columns].astype(F32)
        for ref in part_refs[1:]:
            value = value + ref[rows, columns].astype(F32)
        return value.astype(BF16)

    made = total(slice(0, first), slice(0, features))
    out_ref[:, :, :features] = made.reshape(sources, main, features)
    if extra:
        shape = (sources * main, sources * extra)
        folded = None
        for c in range(cuts):
            piece = total(slice(first, None), slice(c * width, (c + 1) * width))
            pick = (iota(shape, 0) == iota(shape, 1) * cuts + c).astype(BF16)
            part = dot(pick, piece)
            folded = part if folded is None else folded + part
        out_ref[:, :, features:] = folded.astype(BF16).reshape(sources, main, width)


def pack_sum(parts, sources, pack):
    main, _, _, width = pack
    features = parts[0].shape[1]
    return pl.pallas_call(
        functools.partial(pack_kernel, pack),
        out_shape=jax.ShapeDtypeStruct((sources, main, features + width), BF16),
        compiler_params=params(24),
        cost_estimate=cost(parts[0].size * 16, parts[0].size * 8),
        name="pack_sum",
    )(*parts)


def combine_kernel(pack, back_ref, main_ref, extra_ref, gates_ref, out_ref):
    main, extra, cuts, width = pack
    sources = back_ref.shape[0]
    tokens, features = out_ref.shape
    back = back_ref[:, :, :features].reshape(sources * main, features)
    folded = back_ref[:, :, features:].reshape(sources * main, width) if extra else None
    total = None
    for k in range(2):
        rows = dot(main_ref[k], back)
        if extra:
            chosen = extra_ref[k]
            at = iota(chosen.shape, 1) % cuts
            pieces = [
                dot(jnp.where(at == c, chosen, jnp.zeros_like(chosen)), folded) for c in range(cuts)
            ]
            rows = rows + jnp.concatenate(pieces, axis=1)
        weighed = rows * gates_ref[k][:, :1]
        total = weighed if total is None else total + weighed
    out_ref[...] = total.astype(BF16)


def combine(back, weights, tokens, features, pack):
    return pl.pallas_call(
        functools.partial(combine_kernel, pack),
        out_shape=jax.ShapeDtypeStruct((tokens, features), BF16),
        compiler_params=params(40),
        cost_estimate=cost(4 * tokens * back.size, back.size * 2),
        name="combine",
    )(back, *weights)


def spread_states(values, spread_ref):
    for t in range(spread_ref.shape[0]):
        spread_ref[t] = jnp.broadcast_to(values[:, t : t + 1], spread_ref.shape[1:])


def row_sums(parts):
    place = iota(parts[0].shape, 0)
    for stride in (4, 2, 1):
        low = place & stride == 0
        half = len(parts) // 2
        joined = []
        for a, b in zip(parts[:half], parts[half:]):
            kept = jnp.where(low, a, b)
            moved = jnp.where(low, b, a)
            if stride == 4:
                other = pltpu.roll(moved, 4, 0)
            else:
                other = jnp.where(low, pltpu.roll(moved, 8 - stride, 0), pltpu.roll(moved, stride, 0))
            joined.append(kept + other)
        parts = joined
    return parts[0]


def state_sum(value):
    total = value[:8]
    for at in range(8, value.shape[0], 8):
        total = total + value[at : at + 8]
    return total


def tiled_lanes(value, lanes):
    return jnp.concatenate([value] * (lanes // value.shape[1]), axis=1)


def scan_kernel(
    x_ref, edge_ref, low_ref, dtw_ref, dtb_ref, alog_ref, cw_ref, cb_ref, skip_ref, bc_ref,
    read_ref, cum_ref, ends_ref, padded, delta_ref, fed_ref, b_ref, c_ref,
):
    tokens, lanes = x_ref.shape
    taps = cw_ref.shape[0]
    states = alog_ref.shape[0]

    @pl.when(pl.program_id(0) == 0)
    def _():
        spread_states(bc_ref[0], b_ref)
        spread_states(bc_ref[1], c_ref)

    padded[8:] = x_ref[...].astype(F32)
    padded[8 - (taps - 1) : 8] = edge_ref[...].astype(F32)
    conv = jnp.broadcast_to(cb_ref[...], (tokens, lanes))
    for k in range(taps):
        at = 8 - (taps - 1) + k
        conv = conv + cw_ref[k : k + 1] * padded[at : at + tokens]
    act = conv * jax.nn.sigmoid(conv)
    raw = dot(low_ref[...], dtw_ref[...]) + dtb_ref[...]
    delta = jnp.maximum(raw, 0.0) + jnp.log1p(jnp.exp(-jnp.abs(raw)))
    delta_ref[...] = delta
    fed_ref[...] = delta * act
    read_ref[...] = skip_ref[...] * act
    rates = -jnp.exp(alog_ref[...]) * LOG2E

    def eight(g, carry):
        state, running = carry
        at = pl.multiple_of(g * 8, 8)
        delta8 = delta_ref[pl.ds(at, 8)]
        fed8 = fed_ref[pl.ds(at, 8)]
        reads, sums = [], []
        for i in range(8):
            step = delta8[i : i + 1]
            running = running + step
            factor = jnp.exp2(rates * step)
            state = factor * state + tiled_lanes(b_ref[at + i], lanes) * fed8[i : i + 1]
            reads.append(state_sum(tiled_lanes(c_ref[at + i], lanes) * state))
            sums.append(running)
        read_ref[pl.ds(at, 8)] += row_sums(reads)
        cum_ref[pl.ds(at, 8)] = jnp.concatenate(sums, axis=0)
        return state, running

    state, running = lax.fori_loop(
        0, tokens // 8, eight, (jnp.zeros((states, lanes), F32), jnp.zeros((1, lanes), F32))
    )
    ends_ref[:states] = state.astype(BF16)
    ends_ref[states:] = jnp.exp2(rates * running).astype(BF16)


def scan(x_in, edge, dt_low, dt_weight, dt_bias, a_log, conv_weight, conv_bias, d_skip, b_and_c):
    tokens, channels = x_in.shape
    states = a_log.shape[0]
    lanes = math.gcd(512, channels)

    def cut(rows):
        return pl.BlockSpec((rows, lanes), lambda i: (0, i))

    def whole(a):
        zeros = (0,) * a.ndim
        return pl.BlockSpec(a.shape, lambda i: zeros)

    return pl.pallas_call(
        scan_kernel,
        grid=(channels // lanes,),
        in_specs=[
            cut(tokens), cut(edge.shape[0]), whole(dt_low), cut(dt_weight.shape[0]), cut(1),
            cut(states), cut(conv_weight.shape[0]), cut(1), cut(1), whole(b_and_c),
        ],
        out_specs=(cut(tokens), cut(tokens), cut(2 * states)),
        out_shape=(
            pltpu.HBM((tokens, channels), F32),
            pltpu.HBM((tokens, channels), F32),
            jax.ShapeDtypeStruct((2 * states, channels), BF16),
        ),
        scratch_shapes=[
            pltpu.VMEM((tokens + 8, lanes), F32),
            pltpu.VMEM((tokens, lanes), F32),
            pltpu.VMEM((tokens, lanes), F32),
            pltpu.VMEM((tokens, states, 128), F32),
            pltpu.VMEM((tokens, states, 128), F32),
        ],
        compiler_params=params(40),
        cost_estimate=cost(
            tokens * channels * states * 8, tokens * channels * 12, tokens * channels * states
        ),
        name="scan",
    )(
        *in_hbm(x_in),
        edge,
        *in_hbm(
            dt_low, dt_weight, dt_bias[None], a_log, conv_weight, conv_bias[None], d_skip[None],
            b_and_c,
        ),
    )


def link_kernel(later_ref, earlier_ref, out_ref):
    states = out_ref.shape[0] // 2
    decay = later_ref[states:].astype(F32)
    end = later_ref[:states].astype(F32) + decay * earlier_ref[:states].astype(F32)
    out_ref[:states] = end.astype(BF16)
    out_ref[states:] = (decay * earlier_ref[states:].astype(F32)).astype(BF16)


def link(later, earlier):
    return pl.pallas_call(
        link_kernel,
        out_shape=jax.ShapeDtypeStruct(later.shape, BF16),
        compiler_params=params(16),
        cost_estimate=cost(later.size * 2, later.size * 6),
        name="link",
    )(later, earlier)


def finish_kernel(
    read_ref, cum_ref, z_ref, later_ref, earlier_ref, alog_ref, bc_ref, out_ref, sum_ref, c_ref
):
    tokens, lanes = z_ref.shape
    states = alog_ref.shape[0]

    @pl.when(pl.program_id(0) == 0)
    def _():
        spread_states(bc_ref[1], c_ref)

    rates = -jnp.exp(alog_ref[...]) * LOG2E
    entering = later_ref[:states].astype(F32)
    entering = entering + later_ref[states:].astype(F32) * earlier_ref[...].astype(F32)

    def eight(g, carry):
        at = pl.multiple_of(g * 8, 8)
        cum8 = cum_ref[pl.ds(at, 8)]
        reads = []
        for i in range(8):
            kept = jnp.exp2(rates * cum8[i : i + 1]) * entering
            reads.append(state_sum(tiled_lanes(c_ref[at + i], lanes) * kept))
        sum_ref[pl.ds(at, 8)] = row_sums(reads)
        return carry

    lax.fori_loop(0, tokens // 8, eight, 0)
    z = z_ref[...].astype(F32)
    out_ref[...] = ((read_ref[...] + sum_ref[...]) * (z * jax.nn.sigmoid(z))).astype(BF16)


def finish(read, cum, z_gate, later, earlier, a_log, b_and_c):
    tokens, channels = z_gate.shape
    states = a_log.shape[0]
    lanes = math.gcd(512, channels)

    def cut(rows):
        return pl.BlockSpec((rows, lanes), lambda i: (0, i))

    return pl.pallas_call(
        finish_kernel,
        grid=(channels // lanes,),
        in_specs=[
            cut(tokens), cut(tokens), cut(tokens), cut(2 * states), cut(states), cut(states),
            pl.BlockSpec(b_and_c.shape, lambda i: (0, 0, 0)),
        ],
        out_specs=cut(tokens),
        out_shape=jax.ShapeDtypeStruct((tokens, channels), BF16),
        scratch_shapes=[
            pltpu.VMEM((tokens, lanes), F32),
            pltpu.VMEM((tokens, states, 128), F32),
        ],
        compiler_params=params(40),
        cost_estimate=cost(
            tokens * channels * states * 5, tokens * channels * 12, tokens * channels * states
        ),
        name="finish",
    )(*in_hbm(read, cum, z_gate), later, earlier, *in_hbm(a_log, b_and_c))


def shifted(value, by):
    count = lax.axis_size("seq")
    return lax.ppermute(value, "seq", [(i, i + by) for i in range(count - by)])


def turned(value, axis, by):
    count = lax.axis_size(axis)
    return lax.ppermute(value, axis, [(i, (i + by) % count) for i in range(count)])


def turned_within(value, copies, by):
    count = lax.axis_size("seq")
    return lax.ppermute(
        value, "seq", [(i, i // copies * copies + (i + by) % copies) for i in range(count)]
    )


def exchanged(value, copies):
    count = lax.axis_size("seq")
    groups = [list(range(m, count, copies)) for m in range(copies)]
    return lax.all_to_all(
        value, "seq", split_axis=0, concat_axis=0, tiled=True, axis_index_groups=groups
    )


def after(value, *others):
    return lax.optimization_barrier((value, others))[0]


def local(
    x_in,
    z_gate,
    dt_low,
    dt_weight,
    dt_bias,
    a_log,
    conv_weight,
    conv_bias,
    d_skip,
    b_and_c,
    hidden,
    router,
    expert_ids,
    w_gate,
    w_down,
):
    blocks = lax.axis_size("seq")
    feature_parts = lax.axis_size("exp")
    tokens, features = hidden.shape
    experts = router.shape[1]
    copies = blocks // experts
    pack = packing(features)
    ids = expert_ids.T

    edge = shifted(x_in[tokens - (conv_weight.shape[0] - 1) :], 1)
    outgoing, logits = route(ids, hidden, router.T, 1, pack)
    outgoing = after(outgoing, edge)
    arrived = exchanged(outgoing.reshape((experts,) + outgoing.shape[2:]), copies)

    read, cum, ends = scan(
        x_in, edge, dt_low, dt_weight, dt_bias, a_log, conv_weight, conv_bias, d_skip, b_and_c
    )
    arrived = after(arrived, ends)

    spans = [1, 2]
    while spans[-1] * 2 < blocks:
        spans.append(spans[-1] * 2)
    state = ends
    pending = [shifted(ends, by) for by in spans[:2]]
    spans = spans[1:]

    def linked(state, pending, spans, *marks):
        if pending is None or not spans:
            return state, pending, spans
        state = link(*after(tuple(pending), *marks))
        span, spans = spans[0], spans[1:]
        if not spans:
            return state, [shifted(state[: state.shape[0] // 2], span)], spans
        return state, [state, shifted(state, span)], spans

    rows = [unpack(arrived, features, pack)]
    for d in range(1, copies):
        rows.append(turned_within(rows[0], copies, d))
    gated = []
    for part in rows:
        if gated:
            state, pending, spans = linked(state, pending, spans, gated[-1][0])
            part = after(part, gated[-1][0], state)
        own = gate(part, w_gate)
        gated.append([own] + [turned(own, "exp", d) for d in range(1, feature_parts)])
    made = []
    for parts in gated[1:] + gated[:1]:
        parts = lax.optimization_barrier((*parts, state))[:-1]
        made.append(down(parts, w_down, BF16 if len(made) < copies - 1 else F32))
        state, pending, spans = linked(state, pending, spans, made[-1])
    while spans:
        state, pending, spans = linked(state, pending, spans)

    logits = after(logits, made[0])
    logits = [logits] + [turned(logits, "exp", d) for d in range(1, feature_parts)]
    weights = blend_weights(ids, logits, 1, pack)
    sums = [after(made[-1], weights[2])]
    for d in range(1, copies):
        sums.append(turned_within(made[d - 1], copies, -d))
    packed = pack_sum(sums, experts, pack)
    back = exchanged(packed, copies)

    mamba_out = finish(read, cum, z_gate, state, after(pending[0], packed), a_log, b_and_c)
    back = after(back, mamba_out)
    moe_out = combine(back, weights, tokens, features, pack)
    return mamba_out, moe_out


def solution(mesh):
    return jax.shard_map(
        local,
        mesh=mesh,
        in_specs=(
            P("seq", "exp"),
            P("seq", "exp"),
            P("seq", None),
            P(None, "exp"),
            P("exp"),
            P(None, "exp"),
            P(None, "exp"),
            P("exp"),
            P("exp"),
            P(None, None, "seq"),
            P("seq", "exp"),
            P("exp", None),
            P("seq", None),
            P("exp", "seq"),
            P("seq", "exp"),
        ),
        out_specs=(P("seq", "exp"), P("seq", "exp")),
        check_vma=False,
    )
```

```python
import functools
import math

import jax
import jax.numpy as jnp
from jax import lax
from jax.experimental import pallas as pl
from jax.experimental.pallas import tpu as pltpu
from jax.sharding import PartitionSpec as P

CAP = 18
MIB = 1 << 20
LOG2E = math.log2(math.e)
F32 = jnp.float32
BF16 = jnp.bfloat16


def params(limit):
    return pltpu.CompilerParams(vmem_limit_bytes=limit * MIB)


def cost(flops, moved, transcendentals=0):
    return pl.CostEstimate(
        flops=int(flops), bytes_accessed=int(moved), transcendentals=int(transcendentals)
    )


def in_hbm(*arrays):
    return [pltpu.with_memory_space_constraint(a, pltpu.HBM) for a in arrays]


def iota(shape, dim):
    return lax.broadcasted_iota(jnp.int32, shape, dim)


def dot(a, b):
    return jnp.dot(a, b, preferred_element_type=F32)


def dot_nt(a, b):
    return lax.dot_general(a, b, (((1,), (1,)), ((), ())), preferred_element_type=F32)


def packing(features):
    main = CAP // 16 * 16
    extra = CAP - main
    cuts = main // extra if extra and main % extra == 0 else 0
    if cuts and features % (cuts * 128) == 0:
        return main, extra, cuts, features // cuts
    return -(-CAP // 16) * 16, 0, 0, 0


def hits_and_slots(ids, experts):
    tokens = ids.shape[1]
    of = iota((experts, tokens), 0)
    hits = [(of == ids[k : k + 1]).astype(F32) for k in range(2)]
    before = (iota((tokens, tokens), 0) < iota((tokens, tokens), 1)).astype(BF16)
    earlier = dot((hits[0] + hits[1]).astype(BF16), before)
    slots = [jnp.sum(h * earlier, axis=0, keepdims=True).astype(jnp.int32) for h in hits]
    return hits, slots


def route_kernel(pack, ids_ref, hidden_ref, router_ref, out_ref, logits_ref):
    main, extra, cuts, width = pack
    experts, copies = out_ref.shape[:2]
    tokens, features = hidden_ref.shape
    ids = ids_ref[...]
    _, slots = hits_and_slots(ids, experts)
    hidden = hidden_ref[...]
    row = iota((experts * main, tokens), 0)
    picked = None
    for k in range(2):
        key = jnp.where(slots[k] < main, ids[k : k + 1] * main + slots[k], -1)
        hit = row == key
        picked = hit if picked is None else picked | hit
    packed = dot(picked.astype(BF16), hidden).astype(BF16)
    for e in range(experts):
        for m in range(copies):
            out_ref[e, m, :, :features] = packed[e * main : (e + 1) * main]
    if extra:
        picked = None
        for k in range(2):
            key = jnp.where(slots[k] >= main, ids[k : k + 1] * extra + slots[k] - main, -1)
            hit = row // cuts == key
            picked = hit if picked is None else picked | hit
        total = None
        for c in range(cuts):
            chosen = (picked & (row % cuts == c)).astype(BF16)
            part = dot(chosen, hidden[:, c * width : (c + 1) * width])
            total = part if total is None else total + part
        total = total.astype(BF16)
        for e in range(experts):
            for m in range(copies):
                out_ref[e, m, :, features:] = total[e * main : (e + 1) * main]
    logits_ref[...] = dot_nt(hidden, router_ref[...])


def route(ids, hidden, router, copies, pack):
    main, _, _, width = pack
    tokens, features = hidden.shape
    experts = router.shape[0]
    return pl.pallas_call(
        functools.partial(route_kernel, pack),
        out_shape=(
            jax.ShapeDtypeStruct((experts, copies, main, features + width), BF16),
            jax.ShapeDtypeStruct((tokens, experts), F32),
        ),
        compiler_params=params(40),
        cost_estimate=cost(2 * tokens * experts * main * features * 2, hidden.size * 8),
        name="route",
    )(*in_hbm(ids, hidden, router))


def weights_kernel(pack, copies, ids_ref, *refs):
    logits_refs, (main_ref, extra_ref, gates_ref) = refs[:-3], refs[-3:]
    main, extra, cuts, _ = pack
    tokens, experts = logits_refs[0].shape
    ids = ids_ref[...]
    hits, slots = hits_and_slots(ids, experts)
    eye = (iota((tokens, tokens), 0) == iota((tokens, tokens), 1)).astype(BF16)
    logits = logits_refs[0][...]
    for ref in logits_refs[1:]:
        logits = logits + ref[...]
    columns = [dot_nt(eye, h.astype(BF16)) for h in hits]
    picked = [jnp.sum(c * logits, axis=1, keepdims=True) for c in columns]
    expert = iota((tokens, experts), 1).astype(F32)
    total = experts * copies * main
    col = iota((tokens, total), 1)
    for k in range(2):
        gate = jax.nn.sigmoid(picked[k] - picked[1 - k])
        gates_ref[k] = jnp.broadcast_to(gate, gates_ref.shape[1:])
        named = jnp.sum(columns[k] * expert, axis=1, keepdims=True).astype(jnp.int32)
        wide = jnp.broadcast_to(slots[k].astype(F32), (8, tokens)).astype(BF16)
        slot = dot_nt(eye, wide)[:, :1].astype(jnp.int32)
        mine = col // (copies * main) == named
        main_ref[k] = (mine & (col % main == slot)).astype(BF16)
        if extra:
            place = (col % main) // cuts + main
            extra_ref[k] = (mine & (place == slot)).astype(BF16)
        else:
            extra_ref[k] = jnp.zeros(extra_ref.shape[1:], BF16)


def blend_weights(ids, logits, copies, pack):
    tokens, experts = logits[0].shape
    total = experts * copies * pack[0]
    return pl.pallas_call(
        functools.partial(weights_kernel, pack, copies),
        out_shape=(
            jax.ShapeDtypeStruct((2, tokens, total), BF16),
            jax.ShapeDtypeStruct((2, tokens, total), BF16),
            jax.ShapeDtypeStruct((2, tokens, 128), F32),
        ),
        compiler_params=params(40),
        cost_estimate=cost(2 * tokens * total * 16, tokens * total * 8),
        name="blend_weights",
    )(*in_hbm(ids), *logits)


ANYWHERE = pl.BlockSpec(memory_space=pl.ANY)
INSIDE = pl.BlockSpec(memory_space=pltpu.VMEM)
AHEAD = 6


def streamed(from_ref, to_ref, sems, dim, chunk, use, begin=None):
    count = from_ref.shape[dim] // chunk

    def copy(i):
        at = pl.ds(pl.multiple_of(i * chunk, chunk), chunk)
        part = (slice(None), at) if dim else (at, slice(None))
        return pltpu.make_async_copy(from_ref.at[part], to_ref.at[part], sems.at[i])

    for i in range(min(AHEAD, count)):
        copy(i).start()
    if begin is not None:
        begin()

    def step(i, carry):
        copy(i).wait()

        @pl.when(i + AHEAD < count)
        def _():
            copy(i + AHEAD).start()

        use(i)
        return carry

    lax.fori_loop(0, count, step, 0)


def gate_kernel(chunk, x_ref, w_ref, out_ref, held_ref, sems):
    def use(i):
        at = pl.ds(pl.multiple_of(i * chunk, chunk), chunk)
        out_ref[:, at] = dot(x_ref[...], held_ref[:, at]).astype(BF16)

    streamed(w_ref, held_ref, sems, 1, chunk, use)


def gate(x, w_gate):
    rows, features = x.shape
    amount = w_gate.shape[1]
    chunk = math.gcd(512, amount)
    return pl.pallas_call(
        functools.partial(gate_kernel, chunk),
        in_specs=[INSIDE, ANYWHERE],
        out_specs=INSIDE,
        out_shape=jax.ShapeDtypeStruct((rows, amount), BF16),
        scratch_shapes=[
            pltpu.VMEM(w_gate.shape, BF16),
            pltpu.SemaphoreType.DMA((amount // chunk,)),
        ],
        compiler_params=params(44),
        cost_estimate=cost(2 * rows * features * amount, features * amount * 2),
        name="gate",
    )(x, *in_hbm(w_gate))


def fill_acted(chunk, part_refs, acted_ref):
    def piece(i):
        at = pl.ds(pl.multiple_of(i * chunk, chunk), chunk)
        total = part_refs[0][:, at].astype(F32)
        for ref in part_refs[1:]:
            total = total + ref[:, at].astype(F32)
        acted_ref[:, at] = (total * jax.nn.sigmoid(total)).astype(BF16)

    pl.loop(0, acted_ref.shape[1] // chunk)(piece)


def down_kernel(chunk, *refs):
    part_refs, w_ref, out_ref, acted_ref, held_ref, sems = refs[:-5], *refs[-5:]

    def use(i):
        at = pl.ds(pl.multiple_of(i * chunk, chunk), chunk)
        out_ref[:, at] = dot(acted_ref[...], held_ref[:, at]).astype(out_ref.dtype)

    def begin():
        fill_acted(math.gcd(512, acted_ref.shape[1]), part_refs, acted_ref)

    streamed(w_ref, held_ref, sems, 1, chunk, use, begin)


def down(parts, w_down, dtype):
    rows, amount = parts[0].shape
    features = w_down.shape[1]
    chunk = math.gcd(256, features)
    return pl.pallas_call(
        functools.partial(down_kernel, chunk),
        in_specs=[INSIDE] * len(parts) + [ANYWHERE],
        out_specs=INSIDE,
        out_shape=jax.ShapeDtypeStruct((rows, features), dtype),
        scratch_shapes=[
            pltpu.VMEM((rows, amount), BF16),
            pltpu.VMEM(w_down.shape, BF16),
            pltpu.SemaphoreType.DMA((features // chunk,)),
        ],
        compiler_params=params(48),
        cost_estimate=cost(2 * rows * features * amount, features * amount * 2),
        name="down",
    )(*parts, *in_hbm(w_down))


def unpack_kernel(pack, arrived_ref, out_ref):
    main, extra, cuts, width = pack
    sources = arrived_ref.shape[0]
    features = out_ref.shape[1]
    out_ref[: sources * main] = arrived_ref[:, :, :features].reshape(sources * main, features)
    if extra:
        folded = arrived_ref[:, :, features:].reshape(sources * main, width)
        shape = (sources * extra, sources * main)
        for c in range(cuts):
            pick = (iota(shape, 1) == iota(shape, 0) * cuts + c).astype(BF16)
            out_ref[sources * main :, c * width : (c + 1) * width] = dot(pick, folded).astype(BF16)


def unpack(arrived, features, pack):
    main, extra, _, _ = pack
    rows = arrived.shape[0] * (main + extra)
    return pl.pallas_call(
        functools.partial(unpack_kernel, pack),
        out_shape=jax.ShapeDtypeStruct((rows, features), BF16),
        compiler_params=params(24),
        cost_estimate=cost(arrived.size * 16, arrived.size * 4),
        name="unpack",
    )(arrived)


def pack_kernel(pack, *refs):
    main, extra, cuts, width = pack
    part_refs, out_ref = refs[:-1], refs[-1]
    sources = out_ref.shape[0]
    features = part_refs[0].shape[1]
    first = sources * main

    def total(rows, columns):
        value = part_refs[0][rows, columns].astype(F32)
        for ref in part_refs[1:]:
            value = value + ref[rows, columns].astype(F32)
        return value.astype(BF16)

    made = total(slice(0, first), slice(0, features))
    out_ref[:, :, :features] = made.reshape(sources, main, features)
    if extra:
        shape = (sources * main, sources * extra)
        folded = None
        for c in range(cuts):
            piece = total(slice(first, None), slice(c * width, (c + 1) * width))
            pick = (iota(shape, 0) == iota(shape, 1) * cuts + c).astype(BF16)
            part = dot(pick, piece)
            folded = part if folded is None else folded + part
        out_ref[:, :, features:] = folded.astype(BF16).reshape(sources, main, width)


def pack_sum(parts, sources, pack):
    main, _, _, width = pack
    features = parts[0].shape[1]
    return pl.pallas_call(
        functools.partial(pack_kernel, pack),
        out_shape=jax.ShapeDtypeStruct((sources, main, features + width), BF16),
        compiler_params=params(24),
        cost_estimate=cost(parts[0].size * 16, parts[0].size * 8),
        name="pack_sum",
    )(*parts)


def combine_kernel(pack, back_ref, main_ref, extra_ref, gates_ref, out_ref):
    main, extra, cuts, width = pack
    sources = back_ref.shape[0]
    tokens, features = out_ref.shape
    back = back_ref[:, :, :features].reshape(sources * main, features)
    folded = back_ref[:, :, features:].reshape(sources * main, width) if extra else None
    total = None
    for k in range(2):
        rows = dot(main_ref[k], back)
        if extra:
            chosen = extra_ref[k]
            at = iota(chosen.shape, 1) % cuts
            pieces = [
                dot(jnp.where(at == c, chosen, jnp.zeros_like(chosen)), folded) for c in range(cuts)
            ]
            rows = rows + jnp.concatenate(pieces, axis=1)
        weighed = rows * gates_ref[k][:, :1]
        total = weighed if total is None else total + weighed
    out_ref[...] = total.astype(BF16)


def combine(back, weights, tokens, features, pack):
    return pl.pallas_call(
        functools.partial(combine_kernel, pack),
        out_shape=jax.ShapeDtypeStruct((tokens, features), BF16),
        compiler_params=params(40),
        cost_estimate=cost(4 * tokens * back.size, back.size * 2),
        name="combine",
    )(back, *weights)


def spread_states(values, spread_ref):
    for t in range(spread_ref.shape[0]):
        spread_ref[t] = jnp.broadcast_to(values[:, t : t + 1], spread_ref.shape[1:])


def row_sums(parts):
    place = iota(parts[0].shape, 0)
    for stride in (4, 2, 1):
        low = place & stride == 0
        half = len(parts) // 2
        joined = []
        for a, b in zip(parts[:half], parts[half:]):
            kept = jnp.where(low, a, b)
            moved = jnp.where(low, b, a)
            if stride == 4:
                other = pltpu.roll(moved, 4, 0)
            else:
                other = jnp.where(low, pltpu.roll(moved, 8 - stride, 0), pltpu.roll(moved, stride, 0))
            joined.append(kept + other)
        parts = joined
    return parts[0]


def state_sum(value):
    total = value[:8]
    for at in range(8, value.shape[0], 8):
        total = total + value[at : at + 8]
    return total


def tiled_lanes(value, lanes):
    return jnp.concatenate([value] * (lanes // value.shape[1]), axis=1)


def scan_kernel(
    x_ref, edge_ref, low_ref, dtw_ref, dtb_ref, alog_ref, cw_ref, cb_ref, skip_ref, bc_ref,
    read_ref, cum_ref, ends_ref, padded, delta_ref, fed_ref, b_ref, c_ref,
):
    tokens, lanes = x_ref.shape
    taps = cw_ref.shape[0]
    states = alog_ref.shape[0]

    @pl.when(pl.program_id(0) == 0)
    def _():
        spread_states(bc_ref[0], b_ref)
        spread_states(bc_ref[1], c_ref)

    padded[8:] = x_ref[...].astype(F32)
    padded[8 - (taps - 1) : 8] = edge_ref[...].astype(F32)
    conv = jnp.broadcast_to(cb_ref[...], (tokens, lanes))
    for k in range(taps):
        at = 8 - (taps - 1) + k
        conv = conv + cw_ref[k : k + 1] * padded[at : at + tokens]
    act = conv * jax.nn.sigmoid(conv)
    raw = dot(low_ref[...], dtw_ref[...]) + dtb_ref[...]
    delta = jnp.maximum(raw, 0.0) + jnp.log1p(jnp.exp(-jnp.abs(raw)))
    delta_ref[...] = delta
    fed_ref[...] = delta * act
    read_ref[...] = skip_ref[...] * act
    rates = -jnp.exp(alog_ref[...]) * LOG2E

    def eight(g, carry):
        state, running = carry
        at = pl.multiple_of(g * 8, 8)
        delta8 = delta_ref[pl.ds(at, 8)]
        fed8 = fed_ref[pl.ds(at, 8)]
        reads, sums = [], []
        for i in range(8):
            step = delta8[i : i + 1]
            running = running + step
            factor = jnp.exp2(rates * step)
            state = factor * state + tiled_lanes(b_ref[at + i], lanes) * fed8[i : i + 1]
            reads.append(state_sum(tiled_lanes(c_ref[at + i], lanes) * state))
            sums.append(running)
        read_ref[pl.ds(at, 8)] += row_sums(reads)
        cum_ref[pl.ds(at, 8)] = jnp.concatenate(sums, axis=0)
        return state, running

    state, running = lax.fori_loop(
        0, tokens // 8, eight, (jnp.zeros((states, lanes), F32), jnp.zeros((1, lanes), F32))
    )
    ends_ref[:states] = state.astype(BF16)
    ends_ref[states:] = jnp.exp2(rates * running).astype(BF16)


def scan(x_in, edge, dt_low, dt_weight, dt_bias, a_log, conv_weight, conv_bias, d_skip, b_and_c):
    tokens, channels = x_in.shape
    states = a_log.shape[0]
    lanes = math.gcd(512, channels)

    def cut(rows):
        return pl.BlockSpec((rows, lanes), lambda i: (0, i))

    def whole(a):
        zeros = (0,) * a.ndim
        return pl.BlockSpec(a.shape, lambda i: zeros)

    return pl.pallas_call(
        scan_kernel,
        grid=(channels // lanes,),
        in_specs=[
            cut(tokens), cut(edge.shape[0]), whole(dt_low), cut(dt_weight.shape[0]), cut(1),
            cut(states), cut(conv_weight.shape[0]), cut(1), cut(1), whole(b_and_c),
        ],
        out_specs=(cut(tokens), cut(tokens), cut(2 * states)),
        out_shape=(
            pltpu.HBM((tokens, channels), F32),
            pltpu.HBM((tokens, channels), F32),
            jax.ShapeDtypeStruct((2 * states, channels), BF16),
        ),
        scratch_shapes=[
            pltpu.VMEM((tokens + 8, lanes), F32),
            pltpu.VMEM((tokens, lanes), F32),
            pltpu.VMEM((tokens, lanes), F32),
            pltpu.VMEM((tokens, states, 128), F32),
            pltpu.VMEM((tokens, states, 128), F32),
        ],
        compiler_params=params(40),
        cost_estimate=cost(
            tokens * channels * states * 8, tokens * channels * 12, tokens * channels * states
        ),
        name="scan",
    )(
        *in_hbm(x_in),
        edge,
        *in_hbm(
            dt_low, dt_weight, dt_bias[None], a_log, conv_weight, conv_bias[None], d_skip[None],
            b_and_c,
        ),
    )


def upper_half(step):
    return (lax.axis_index("seq") >> step) % 2 == 1


def linked(later, earlier):
    states = later.shape[0] // 2
    decay = later[states:]
    return jnp.concatenate([later[:states] + decay * earlier[:states], decay * earlier[states:]], 0)


def link_kernel(step, *refs):
    total_ref, received_ref, prefix_ref = refs[:3] if step else (*refs[:2], None)
    total_out, prefix_out = refs[-2:]
    upper = upper_half(step)
    own, received = total_ref[...].astype(F32), received_ref[...].astype(F32)
    later, earlier = jnp.where(upper, own, received), jnp.where(upper, received, own)
    total_out[...] = linked(later, earlier).astype(BF16)
    if step:
        prefix = prefix_ref[...].astype(F32)
    else:
        states = own.shape[0] // 2
        prefix = (iota(own.shape, 0) >= states).astype(F32)
    prefix_out[...] = jnp.where(upper, linked(prefix, received), prefix).astype(BF16)


def link(step, total, received, prefix):
    shape = jax.ShapeDtypeStruct(total.shape, BF16)
    args = [total, received] + ([prefix] if step else [])
    return pl.pallas_call(
        functools.partial(link_kernel, step),
        out_shape=(shape, shape),
        compiler_params=params(16),
        cost_estimate=cost(total.size * 2, total.size * 6),
        name="link",
    )(*args)


def finish_kernel(
    step, read_ref, cum_ref, z_ref, prefix_ref, received_ref, alog_ref, bc_ref, out_ref, sum_ref, c_ref
):
    tokens, lanes = z_ref.shape
    states = alog_ref.shape[0]

    @pl.when(pl.program_id(0) == 0)
    def _():
        spread_states(bc_ref[1], c_ref)

    rates = -jnp.exp(alog_ref[...]) * LOG2E
    entering = prefix_ref[:states].astype(F32)
    further = entering + prefix_ref[states:].astype(F32) * received_ref[:states].astype(F32)
    entering = jnp.where(upper_half(step), further, entering)

    def eight(g, carry):
        at = pl.multiple_of(g * 8, 8)
        cum8 = cum_ref[pl.ds(at, 8)]
        reads = []
        for i in range(8):
            kept = jnp.exp2(rates * cum8[i : i + 1]) * entering
            reads.append(state_sum(tiled_lanes(c_ref[at + i], lanes) * kept))
        sum_ref[pl.ds(at, 8)] = row_sums(reads)
        return carry

    lax.fori_loop(0, tokens // 8, eight, 0)
    z = z_ref[...].astype(F32)
    out_ref[...] = ((read_ref[...] + sum_ref[...]) * (z * jax.nn.sigmoid(z))).astype(BF16)


def finish(step, read, cum, z_gate, prefix, received, a_log, b_and_c):
    tokens, channels = z_gate.shape
    states = a_log.shape[0]
    lanes = math.gcd(512, channels)

    def cut(rows):
        return pl.BlockSpec((rows, lanes), lambda i: (0, i))

    return pl.pallas_call(
        functools.partial(finish_kernel, step),
        grid=(channels // lanes,),
        in_specs=[
            cut(tokens), cut(tokens), cut(tokens), cut(2 * states), cut(2 * states), cut(states),
            pl.BlockSpec(b_and_c.shape, lambda i: (0, 0, 0)),
        ],
        out_specs=cut(tokens),
        out_shape=jax.ShapeDtypeStruct((tokens, channels), BF16),
        scratch_shapes=[
            pltpu.VMEM((tokens, lanes), F32),
            pltpu.VMEM((tokens, states, 128), F32),
        ],
        compiler_params=params(40),
        cost_estimate=cost(
            tokens * channels * states * 5, tokens * channels * 12, tokens * channels * states
        ),
        name="finish",
    )(*in_hbm(read, cum, z_gate), prefix, received, *in_hbm(a_log, b_and_c))


def swapped(value, by):
    count = lax.axis_size("seq")
    return lax.ppermute(value, "seq", [(i, i ^ by) for i in range(count)])


def turned(value, axis, by):
    count = lax.axis_size(axis)
    return lax.ppermute(value, axis, [(i, (i + by) % count) for i in range(count)])


def turned_within(value, copies, by):
    count = lax.axis_size("seq")
    return lax.ppermute(
        value, "seq", [(i, i // copies * copies + (i + by) % copies) for i in range(count)]
    )


def exchanged(value, copies):
    count = lax.axis_size("seq")
    groups = [list(range(m, count, copies)) for m in range(copies)]
    return lax.all_to_all(
        value, "seq", split_axis=0, concat_axis=0, tiled=True, axis_index_groups=groups
    )


def after(value, *others):
    return lax.optimization_barrier((value, others))[0]


def local(
    x_in,
    z_gate,
    dt_low,
    dt_weight,
    dt_bias,
    a_log,
    conv_weight,
    conv_bias,
    d_skip,
    b_and_c,
    hidden,
    router,
    expert_ids,
    w_gate,
    w_down,
):
    blocks = lax.axis_size("seq")
    feature_parts = lax.axis_size("exp")
    tokens, features = hidden.shape
    experts = router.shape[1]
    copies = blocks // experts
    pack = packing(features)
    ids = expert_ids.T

    edge = x_in[tokens - (conv_weight.shape[0] - 1) :]
    edge = lax.ppermute(edge, "seq", [(i, i + 1) for i in range(blocks - 1)])
    outgoing, logits = route(ids, hidden, router.T, 1, pack)
    outgoing = after(outgoing, edge)
    arrived = exchanged(outgoing.reshape((experts,) + outgoing.shape[2:]), copies)

    read, cum, ends = scan(
        x_in, edge, dt_low, dt_weight, dt_bias, a_log, conv_weight, conv_bias, d_skip, b_and_c
    )
    arrived = after(arrived, ends)

    steps = blocks.bit_length() - 1
    total, prefix, received = ends, None, swapped(ends, 1)
    step = 0

    def advance(*marks):
        nonlocal total, prefix, received, step
        if step < steps - 1:
            total, prefix = link(step, total, after(received, *marks), prefix)
            step += 1
            received = swapped(total, 1 << step)
        return prefix

    rows = [unpack(arrived, features, pack)]
    for d in range(1, copies):
        rows.append(turned_within(rows[0], copies, d))
    gated = []
    for part in rows:
        if len(gated) < 2:
            part = after(part, advance(gated[-1][0] if gated else rows[0]))
        else:
            part = after(part, gated[-1][0])
        own = gate(part, w_gate)
        gated.append([own] + [turned(own, "exp", d) for d in range(1, feature_parts)])
    made = []
    for parts in gated[1:] + gated[:1]:
        if made:
            parts = lax.optimization_barrier((*parts, advance(made[-1])))[:-1]
        made.append(down(parts, w_down, BF16 if len(made) < copies - 1 else F32))
    while step < steps - 1:
        advance()
    received = after(received, made[-1])

    logits = after(logits, made[0])
    logits = [logits] + [turned(logits, "exp", d) for d in range(1, feature_parts)]
    weights = blend_weights(ids, logits, 1, pack)
    sums = [after(made[-1], weights[2], received)]
    for d in range(1, copies):
        sums.append(turned_within(made[d - 1], copies, -d))
    packed = pack_sum(sums, experts, pack)
    back = exchanged(packed, copies)

    received = after(received, packed)
    mamba_out = finish(step, read, cum, z_gate, prefix, received, a_log, b_and_c)
    back = after(back, mamba_out)
    moe_out = combine(back, weights, tokens, features, pack)
    return mamba_out, moe_out


def solution(mesh):
    return jax.shard_map(
        local,
        mesh=mesh,
        in_specs=(
            P("seq", "exp"),
            P("seq", "exp"),
            P("seq", None),
            P(None, "exp"),
            P("exp"),
            P(None, "exp"),
            P(None, "exp"),
            P("exp"),
            P("exp"),
            P(None, None, "seq"),
            P("seq", "exp"),
            P("exp", None),
            P("seq", None),
            P("exp", "seq"),
            P("seq", "exp"),
        ),
        out_specs=(P("seq", "exp"), P("seq", "exp")),
        check_vma=False,
    )
```

```python
import functools
import math

import jax
import jax.numpy as jnp
from jax import lax
from jax.experimental import pallas as pl
from jax.experimental.pallas import tpu as pltpu
from jax.sharding import PartitionSpec as P

CAP = 18
MIB = 1 << 20
LOG2E = math.log2(math.e)
F32 = jnp.float32
BF16 = jnp.bfloat16


def params(limit):
    return pltpu.CompilerParams(vmem_limit_bytes=limit * MIB)


def cost(flops, moved, transcendentals=0):
    return pl.CostEstimate(
        flops=int(flops), bytes_accessed=int(moved), transcendentals=int(transcendentals)
    )


def in_hbm(*arrays):
    return [pltpu.with_memory_space_constraint(a, pltpu.HBM) for a in arrays]


def iota(shape, dim):
    return lax.broadcasted_iota(jnp.int32, shape, dim)


def dot(a, b):
    return jnp.dot(a, b, preferred_element_type=F32)


def dot_nt(a, b):
    return lax.dot_general(a, b, (((1,), (1,)), ((), ())), preferred_element_type=F32)


def packing(features):
    main = CAP // 16 * 16
    extra = CAP - main
    cuts = main // extra if extra and main % extra == 0 else 0
    if cuts and features % (cuts * 128) == 0:
        return main, extra, cuts, features // cuts
    return -(-CAP // 16) * 16, 0, 0, 0


def hits_and_slots(ids, experts):
    tokens = ids.shape[1]
    of = iota((experts, tokens), 0)
    hits = [(of == ids[k : k + 1]).astype(F32) for k in range(2)]
    before = (iota((tokens, tokens), 0) < iota((tokens, tokens), 1)).astype(BF16)
    earlier = dot((hits[0] + hits[1]).astype(BF16), before)
    slots = [jnp.sum(h * earlier, axis=0, keepdims=True).astype(jnp.int32) for h in hits]
    return hits, slots


def route_kernel(pack, ids_ref, hidden_ref, router_ref, out_ref, logits_ref):
    main, extra, cuts, width = pack
    experts, copies = out_ref.shape[:2]
    tokens, features = hidden_ref.shape
    ids = ids_ref[...]
    _, slots = hits_and_slots(ids, experts)
    hidden = hidden_ref[...]
    row = iota((experts * main, tokens), 0)
    picked = None
    for k in range(2):
        key = jnp.where(slots[k] < main, ids[k : k + 1] * main + slots[k], -1)
        hit = row == key
        picked = hit if picked is None else picked | hit
    packed = dot(picked.astype(BF16), hidden).astype(BF16)
    for e in range(experts):
        for m in range(copies):
            out_ref[e, m, :, :features] = packed[e * main : (e + 1) * main]
    if extra:
        picked = None
        for k in range(2):
            key = jnp.where(slots[k] >= main, ids[k : k + 1] * extra + slots[k] - main, -1)
            hit = row // cuts == key
            picked = hit if picked is None else picked | hit
        total = None
        for c in range(cuts):
            chosen = (picked & (row % cuts == c)).astype(BF16)
            part = dot(chosen, hidden[:, c * width : (c + 1) * width])
            total = part if total is None else total + part
        total = total.astype(BF16)
        for e in range(experts):
            for m in range(copies):
                out_ref[e, m, :, features:] = total[e * main : (e + 1) * main]
    logits_ref[...] = dot_nt(hidden, router_ref[...])


def route(ids, hidden, router, copies, pack):
    main, _, _, width = pack
    tokens, features = hidden.shape
    experts = router.shape[0]
    return pl.pallas_call(
        functools.partial(route_kernel, pack),
        out_shape=(
            jax.ShapeDtypeStruct((experts, copies, main, features + width), BF16),
            jax.ShapeDtypeStruct((tokens, experts), F32),
        ),
        compiler_params=params(40),
        cost_estimate=cost(2 * tokens * experts * main * features * 2, hidden.size * 8),
        name="route",
    )(*in_hbm(ids, hidden, router))


def weights_kernel(pack, copies, ids_ref, *refs):
    logits_refs, (main_ref, extra_ref, gates_ref) = refs[:-3], refs[-3:]
    main, extra, cuts, _ = pack
    tokens, experts = logits_refs[0].shape
    ids = ids_ref[...]
    hits, slots = hits_and_slots(ids, experts)
    eye = (iota((tokens, tokens), 0) == iota((tokens, tokens), 1)).astype(BF16)
    logits = logits_refs[0][...]
    for ref in logits_refs[1:]:
        logits = logits + ref[...]
    columns = [dot_nt(eye, h.astype(BF16)) for h in hits]
    picked = [jnp.sum(c * logits, axis=1, keepdims=True) for c in columns]
    expert = iota((tokens, experts), 1).astype(F32)
    total = experts * copies * main
    col = iota((tokens, total), 1)
    for k in range(2):
        gate = jax.nn.sigmoid(picked[k] - picked[1 - k])
        gates_ref[k] = jnp.broadcast_to(gate, gates_ref.shape[1:])
        named = jnp.sum(columns[k] * expert, axis=1, keepdims=True).astype(jnp.int32)
        wide = jnp.broadcast_to(slots[k].astype(F32), (8, tokens)).astype(BF16)
        slot = dot_nt(eye, wide)[:, :1].astype(jnp.int32)
        mine = col // (copies * main) == named
        main_ref[k] = (mine & (col % main == slot)).astype(BF16)
        if extra:
            place = (col % main) // cuts + main
            extra_ref[k] = (mine & (place == slot)).astype(BF16)
        else:
            extra_ref[k] = jnp.zeros(extra_ref.shape[1:], BF16)


def blend_weights(ids, logits, copies, pack):
    tokens, experts = logits[0].shape
    total = experts * copies * pack[0]
    return pl.pallas_call(
        functools.partial(weights_kernel, pack, copies),
        out_shape=(
            jax.ShapeDtypeStruct((2, tokens, total), BF16),
            jax.ShapeDtypeStruct((2, tokens, total), BF16),
            jax.ShapeDtypeStruct((2, tokens, 128), F32),
        ),
        compiler_params=params(40),
        cost_estimate=cost(2 * tokens * total * 16, tokens * total * 8),
        name="blend_weights",
    )(*in_hbm(ids), *logits)


ANYWHERE = pl.BlockSpec(memory_space=pl.ANY)
INSIDE = pl.BlockSpec(memory_space=pltpu.VMEM)
AHEAD = 6


def streamed(from_ref, to_ref, sems, dim, chunk, use, begin=None):
    count = from_ref.shape[dim] // chunk

    def copy(i):
        at = pl.ds(pl.multiple_of(i * chunk, chunk), chunk)
        part = (slice(None), at) if dim else (at, slice(None))
        return pltpu.make_async_copy(from_ref.at[part], to_ref.at[part], sems.at[i])

    for i in range(min(AHEAD, count)):
        copy(i).start()
    if begin is not None:
        begin()

    def step(i, carry):
        copy(i).wait()

        @pl.when(i + AHEAD < count)
        def _():
            copy(i + AHEAD).start()

        use(i)
        return carry

    lax.fori_loop(0, count, step, 0)


def gate_kernel(chunk, x_ref, w_ref, out_ref, held_ref, sems):
    def use(i):
        at = pl.ds(pl.multiple_of(i * chunk, chunk), chunk)
        out_ref[:, at] = dot(x_ref[...], held_ref[:, at]).astype(BF16)

    streamed(w_ref, held_ref, sems, 1, chunk, use)


def gate(x, w_gate):
    rows, features = x.shape
    amount = w_gate.shape[1]
    chunk = math.gcd(512, amount)
    return pl.pallas_call(
        functools.partial(gate_kernel, chunk),
        in_specs=[INSIDE, ANYWHERE],
        out_specs=INSIDE,
        out_shape=jax.ShapeDtypeStruct((rows, amount), BF16),
        scratch_shapes=[
            pltpu.VMEM(w_gate.shape, BF16),
            pltpu.SemaphoreType.DMA((amount // chunk,)),
        ],
        compiler_params=params(44),
        cost_estimate=cost(2 * rows * features * amount, features * amount * 2),
        name="gate",
    )(x, *in_hbm(w_gate))


def fill_acted(chunk, part_refs, acted_ref):
    def piece(i):
        at = pl.ds(pl.multiple_of(i * chunk, chunk), chunk)
        total = part_refs[0][:, at].astype(F32)
        for ref in part_refs[1:]:
            total = total + ref[:, at].astype(F32)
        acted_ref[:, at] = (total * jax.nn.sigmoid(total)).astype(BF16)

    pl.loop(0, acted_ref.shape[1] // chunk)(piece)


def down_kernel(chunk, *refs):
    part_refs, w_ref, out_ref, acted_ref, held_ref, sems = refs[:-5], *refs[-5:]

    def use(i):
        at = pl.ds(pl.multiple_of(i * chunk, chunk), chunk)
        out_ref[:, at] = dot(acted_ref[...], held_ref[:, at]).astype(out_ref.dtype)

    def begin():
        fill_acted(math.gcd(512, acted_ref.shape[1]), part_refs, acted_ref)

    streamed(w_ref, held_ref, sems, 1, chunk, use, begin)


def down(parts, w_down, dtype):
    rows, amount = parts[0].shape
    features = w_down.shape[1]
    chunk = math.gcd(256, features)
    return pl.pallas_call(
        functools.partial(down_kernel, chunk),
        in_specs=[INSIDE] * len(parts) + [ANYWHERE],
        out_specs=INSIDE,
        out_shape=jax.ShapeDtypeStruct((rows, features), dtype),
        scratch_shapes=[
            pltpu.VMEM((rows, amount), BF16),
            pltpu.VMEM(w_down.shape, BF16),
            pltpu.SemaphoreType.DMA((features // chunk,)),
        ],
        compiler_params=params(48),
        cost_estimate=cost(2 * rows * features * amount, features * amount * 2),
        name="down",
    )(*parts, *in_hbm(w_down))


def unpack_kernel(pack, arrived_ref, out_ref):
    main, extra, cuts, width = pack
    sources = arrived_ref.shape[0]
    features = out_ref.shape[1]
    out_ref[: sources * main] = arrived_ref[:, :, :features].reshape(sources * main, features)
    if extra:
        folded = arrived_ref[:, :, features:].reshape(sources * main, width)
        shape = (sources * extra, sources * main)
        for c in range(cuts):
            pick = (iota(shape, 1) == iota(shape, 0) * cuts + c).astype(BF16)
            out_ref[sources * main :, c * width : (c + 1) * width] = dot(pick, folded).astype(BF16)


def unpack(arrived, features, pack):
    main, extra, _, _ = pack
    rows = arrived.shape[0] * (main + extra)
    return pl.pallas_call(
        functools.partial(unpack_kernel, pack),
        out_shape=jax.ShapeDtypeStruct((rows, features), BF16),
        compiler_params=params(24),
        cost_estimate=cost(arrived.size * 16, arrived.size * 4),
        name="unpack",
    )(arrived)


def pack_kernel(pack, *refs):
    main, extra, cuts, width = pack
    part_refs, out_ref = refs[:-1], refs[-1]
    sources = out_ref.shape[0]
    features = part_refs[0].shape[1]
    first = sources * main

    def total(rows, columns):
        value = part_refs[0][rows, columns].astype(F32)
        for ref in part_refs[1:]:
            value = value + ref[rows, columns].astype(F32)
        return value.astype(BF16)

    made = total(slice(0, first), slice(0, features))
    out_ref[:, :, :features] = made.reshape(sources, main, features)
    if extra:
        shape = (sources * main, sources * extra)
        folded = None
        for c in range(cuts):
            piece = total(slice(first, None), slice(c * width, (c + 1) * width))
            pick = (iota(shape, 0) == iota(shape, 1) * cuts + c).astype(BF16)
            part = dot(pick, piece)
            folded = part if folded is None else folded + part
        out_ref[:, :, features:] = folded.astype(BF16).reshape(sources, main, width)


def pack_sum(parts, sources, pack):
    main, _, _, width = pack
    features = parts[0].shape[1]
    return pl.pallas_call(
        functools.partial(pack_kernel, pack),
        out_shape=jax.ShapeDtypeStruct((sources, main, features + width), BF16),
        compiler_params=params(24),
        cost_estimate=cost(parts[0].size * 16, parts[0].size * 8),
        name="pack_sum",
    )(*parts)


def combine_kernel(pack, back_ref, main_ref, extra_ref, gates_ref, out_ref):
    main, extra, cuts, width = pack
    sources = back_ref.shape[0]
    tokens, features = out_ref.shape
    back = back_ref[:, :, :features].reshape(sources * main, features)
    folded = back_ref[:, :, features:].reshape(sources * main, width) if extra else None
    total = None
    for k in range(2):
        rows = dot(main_ref[k], back)
        if extra:
            chosen = extra_ref[k]
            at = iota(chosen.shape, 1) % cuts
            pieces = [
                dot(jnp.where(at == c, chosen, jnp.zeros_like(chosen)), folded) for c in range(cuts)
            ]
            rows = rows + jnp.concatenate(pieces, axis=1)
        weighed = rows * gates_ref[k][:, :1]
        total = weighed if total is None else total + weighed
    out_ref[...] = total.astype(BF16)


def combine(back, weights, tokens, features, pack):
    return pl.pallas_call(
        functools.partial(combine_kernel, pack),
        out_shape=jax.ShapeDtypeStruct((tokens, features), BF16),
        compiler_params=params(40),
        cost_estimate=cost(4 * tokens * back.size, back.size * 2),
        name="combine",
    )(back, *weights)


def spread_states(values, spread_ref):
    for t in range(spread_ref.shape[0]):
        spread_ref[t] = jnp.broadcast_to(values[:, t : t + 1], spread_ref.shape[1:])


def row_sums(parts):
    place = iota(parts[0].shape, 0)
    for stride in (4, 2, 1):
        low = place & stride == 0
        half = len(parts) // 2
        joined = []
        for a, b in zip(parts[:half], parts[half:]):
            kept = jnp.where(low, a, b)
            moved = jnp.where(low, b, a)
            if stride == 4:
                other = pltpu.roll(moved, 4, 0)
            else:
                other = jnp.where(low, pltpu.roll(moved, 8 - stride, 0), pltpu.roll(moved, stride, 0))
            joined.append(kept + other)
        parts = joined
    return parts[0]


def state_sum(value):
    total = value[:8]
    for at in range(8, value.shape[0], 8):
        total = total + value[at : at + 8]
    return total


def tiled_lanes(value, lanes):
    return jnp.concatenate([value] * (lanes // value.shape[1]), axis=1)


def scan_kernel(
    x_ref, edge_ref, low_ref, dtw_ref, dtb_ref, alog_ref, cw_ref, cb_ref, skip_ref, bc_ref,
    read_ref, cum_ref, ends_ref, padded, delta_ref, fed_ref, b_ref, c_ref,
):
    tokens, lanes = x_ref.shape
    taps = cw_ref.shape[0]
    states = alog_ref.shape[0]

    @pl.when(pl.program_id(0) == 0)
    def _():
        spread_states(bc_ref[0], b_ref)
        spread_states(bc_ref[1], c_ref)

    padded[8:] = x_ref[...].astype(F32)
    padded[8 - (taps - 1) : 8] = edge_ref[...].astype(F32)
    conv = jnp.broadcast_to(cb_ref[...], (tokens, lanes))
    for k in range(taps):
        at = 8 - (taps - 1) + k
        conv = conv + cw_ref[k : k + 1] * padded[at : at + tokens]
    act = conv * jax.nn.sigmoid(conv)
    raw = dot(low_ref[...], dtw_ref[...]) + dtb_ref[...]
    delta = jnp.maximum(raw, 0.0) + jnp.log1p(jnp.exp(-jnp.abs(raw)))
    delta_ref[...] = delta
    fed_ref[...] = delta * act
    read_ref[...] = skip_ref[...] * act
    rates = -jnp.exp(alog_ref[...]) * LOG2E

    def eight(g, carry):
        state, running = carry
        at = pl.multiple_of(g * 8, 8)
        delta8 = delta_ref[pl.ds(at, 8)]
        fed8 = fed_ref[pl.ds(at, 8)]
        reads, sums = [], []
        for i in range(8):
            step = delta8[i : i + 1]
            running = running + step
            factor = jnp.exp2(rates * step)
            state = factor * state + tiled_lanes(b_ref[at + i], lanes) * fed8[i : i + 1]
            reads.append(state_sum(tiled_lanes(c_ref[at + i], lanes) * state))
            sums.append(running)
        read_ref[pl.ds(at, 8)] += row_sums(reads)
        cum_ref[pl.ds(at, 8)] = jnp.concatenate(sums, axis=0)
        return state, running

    state, running = lax.fori_loop(
        0, tokens // 8, eight, (jnp.zeros((states, lanes), F32), jnp.zeros((1, lanes), F32))
    )
    ends_ref[:states] = state.astype(BF16)
    ends_ref[states:] = jnp.exp2(rates * running).astype(BF16)


def scan(x_in, edge, dt_low, dt_weight, dt_bias, a_log, conv_weight, conv_bias, d_skip, b_and_c):
    tokens, channels = x_in.shape
    states = a_log.shape[0]
    lanes = math.gcd(512, channels)

    def cut(rows):
        return pl.BlockSpec((rows, lanes), lambda i: (0, i))

    def whole(a):
        zeros = (0,) * a.ndim
        return pl.BlockSpec(a.shape, lambda i: zeros)

    return pl.pallas_call(
        scan_kernel,
        grid=(channels // lanes,),
        in_specs=[
            cut(tokens), cut(edge.shape[0]), whole(dt_low), cut(dt_weight.shape[0]), cut(1),
            cut(states), cut(conv_weight.shape[0]), cut(1), cut(1), whole(b_and_c),
        ],
        out_specs=(cut(tokens), cut(tokens), cut(2 * states)),
        out_shape=(
            pltpu.HBM((tokens, channels), F32),
            pltpu.HBM((tokens, channels), F32),
            jax.ShapeDtypeStruct((2 * states, channels), BF16),
        ),
        scratch_shapes=[
            pltpu.VMEM((tokens + 8, lanes), F32),
            pltpu.VMEM((tokens, lanes), F32),
            pltpu.VMEM((tokens, lanes), F32),
            pltpu.VMEM((tokens, states, 128), F32),
            pltpu.VMEM((tokens, states, 128), F32),
        ],
        compiler_params=params(40),
        cost_estimate=cost(
            tokens * channels * states * 8, tokens * channels * 12, tokens * channels * states
        ),
        name="scan",
    )(
        *in_hbm(x_in),
        edge,
        *in_hbm(
            dt_low, dt_weight, dt_bias[None], a_log, conv_weight, conv_bias[None], d_skip[None],
            b_and_c,
        ),
    )


def upper_half(step):
    return (lax.axis_index("seq") >> step) % 2 == 1


def linked(later, earlier):
    states = later.shape[0] // 2
    decay = later[states:]
    return jnp.concatenate([later[:states] + decay * earlier[:states], decay * earlier[states:]], 0)


def link_kernel(step, *refs):
    total_ref, received_ref, prefix_ref = refs[:3] if step else (*refs[:2], None)
    total_out, prefix_out = refs[-2:]
    upper = upper_half(step)
    own, received = total_ref[...].astype(F32), received_ref[...].astype(F32)
    later, earlier = jnp.where(upper, own, received), jnp.where(upper, received, own)
    total_out[...] = linked(later, earlier).astype(BF16)
    if step:
        prefix = prefix_ref[...].astype(F32)
    else:
        states = own.shape[0] // 2
        prefix = (iota(own.shape, 0) >= states).astype(F32)
    prefix_out[...] = jnp.where(upper, linked(prefix, received), prefix).astype(BF16)


def link(step, total, received, prefix):
    shape = jax.ShapeDtypeStruct(total.shape, BF16)
    args = [total, received] + ([prefix] if step else [])
    return pl.pallas_call(
        functools.partial(link_kernel, step),
        out_shape=(shape, shape),
        compiler_params=params(16),
        cost_estimate=cost(total.size * 2, total.size * 6),
        name="link",
    )(*args)


def finish_kernel(
    step, read_ref, cum_ref, z_ref, prefix_ref, received_ref, alog_ref, bc_ref, out_ref, sum_ref, c_ref
):
    tokens, lanes = z_ref.shape
    states = alog_ref.shape[0]

    @pl.when(pl.program_id(0) == 0)
    def _():
        spread_states(bc_ref[1], c_ref)

    rates = -jnp.exp(alog_ref[...]) * LOG2E
    entering = prefix_ref[:states].astype(F32)
    further = entering + prefix_ref[states:].astype(F32) * received_ref[:states].astype(F32)
    entering = jnp.where(upper_half(step), further, entering)

    def eight(g, carry):
        at = pl.multiple_of(g * 8, 8)
        cum8 = cum_ref[pl.ds(at, 8)]
        reads = []
        for i in range(8):
            kept = jnp.exp2(rates * cum8[i : i + 1]) * entering
            reads.append(state_sum(tiled_lanes(c_ref[at + i], lanes) * kept))
        sum_ref[pl.ds(at, 8)] = row_sums(reads)
        return carry

    lax.fori_loop(0, tokens // 8, eight, 0)
    z = z_ref[...].astype(F32)
    out_ref[...] = ((read_ref[...] + sum_ref[...]) * (z * jax.nn.sigmoid(z))).astype(BF16)


def finish(step, read, cum, z_gate, prefix, received, a_log, b_and_c):
    tokens, channels = z_gate.shape
    states = a_log.shape[0]
    lanes = math.gcd(512, channels)

    def cut(rows):
        return pl.BlockSpec((rows, lanes), lambda i: (0, i))

    return pl.pallas_call(
        functools.partial(finish_kernel, step),
        grid=(channels // lanes,),
        in_specs=[
            cut(tokens), cut(tokens), cut(tokens), cut(2 * states), cut(2 * states), cut(states),
            pl.BlockSpec(b_and_c.shape, lambda i: (0, 0, 0)),
        ],
        out_specs=cut(tokens),
        out_shape=jax.ShapeDtypeStruct((tokens, channels), BF16),
        scratch_shapes=[
            pltpu.VMEM((tokens, lanes), F32),
            pltpu.VMEM((tokens, states, 128), F32),
        ],
        compiler_params=params(40),
        cost_estimate=cost(
            tokens * channels * states * 5, tokens * channels * 12, tokens * channels * states
        ),
        name="finish",
    )(*in_hbm(read, cum, z_gate), prefix, received, *in_hbm(a_log, b_and_c))


def swapped(value, by):
    count = lax.axis_size("seq")
    return lax.ppermute(value, "seq", [(i, i ^ by) for i in range(count)])


def turned(value, axis, by):
    count = lax.axis_size(axis)
    return lax.ppermute(value, axis, [(i, (i + by) % count) for i in range(count)])


def turned_within(value, copies, by):
    count = lax.axis_size("seq")
    return lax.ppermute(
        value, "seq", [(i, i // copies * copies + (i + by) % copies) for i in range(count)]
    )


def exchanged(value, copies):
    count = lax.axis_size("seq")
    groups = [list(range(m, count, copies)) for m in range(copies)]
    return lax.all_to_all(
        value, "seq", split_axis=0, concat_axis=0, tiled=True, axis_index_groups=groups
    )


def after(value, *others):
    return lax.optimization_barrier((value, others))[0]


def local(
    x_in,
    z_gate,
    dt_low,
    dt_weight,
    dt_bias,
    a_log,
    conv_weight,
    conv_bias,
    d_skip,
    b_and_c,
    hidden,
    router,
    expert_ids,
    w_gate,
    w_down,
):
    blocks = lax.axis_size("seq")
    feature_parts = lax.axis_size("exp")
    tokens, features = hidden.shape
    experts = router.shape[1]
    copies = blocks // experts
    pack = packing(features)
    ids = expert_ids.T

    edge = x_in[tokens - (conv_weight.shape[0] - 1) :]
    edge = lax.ppermute(edge, "seq", [(i, i + 1) for i in range(blocks - 1)])
    outgoing, logits = route(ids, hidden, router.T, 1, pack)
    outgoing = after(outgoing, edge)
    arrived = exchanged(outgoing.reshape((experts,) + outgoing.shape[2:]), copies)

    read, cum, ends = scan(
        x_in, edge, dt_low, dt_weight, dt_bias, a_log, conv_weight, conv_bias, d_skip, b_and_c
    )
    arrived = after(arrived, ends)

    steps = blocks.bit_length() - 1
    total, prefix, received = ends, None, swapped(ends, 1)
    step = 0

    def advance(*marks):
        nonlocal total, prefix, received, step
        if step < steps - 1:
            total, prefix = link(step, total, after(received, *marks), prefix)
            step += 1
            received = swapped(total, 1 << step)
        return prefix

    rows = [unpack(arrived, features, pack)]
    for d in range(1, copies):
        rows.append(turned_within(rows[0], copies, d))
    gated = []
    for part in rows:
        if len(gated) == 1:
            part = after(part, advance(gated[-1][0]))
        elif gated:
            part = after(part, gated[-1][0])
        own = gate(part, w_gate)
        gated.append([own] + [turned(own, "exp", d) for d in range(1, feature_parts)])
    logits = after(logits, gated[-1][0])
    logits = [logits] + [turned(logits, "exp", d) for d in range(1, feature_parts)]
    made = []
    for parts in gated[1:] + gated[:1]:
        if made:
            parts = lax.optimization_barrier((*parts, advance(made[-1])))[:-1]
        made.append(down(parts, w_down, BF16 if len(made) < copies - 1 else F32))
    advance(made[-1])
    while step < steps - 1:
        advance()
    sums = [after(made[-1], prefix)]
    for d in range(1, copies):
        sums.append(turned_within(made[d - 1], copies, -d))
    packed = pack_sum(sums, experts, pack)
    back = exchanged(packed, copies)

    weights = blend_weights(ids, after(tuple(logits), packed), 1, pack)
    received = after(received, packed)
    mamba_out = finish(step, read, cum, z_gate, prefix, received, a_log, b_and_c)
    back = after(back, mamba_out)
    moe_out = combine(back, weights, tokens, features, pack)
    return mamba_out, moe_out


def solution(mesh):
    return jax.shard_map(
        local,
        mesh=mesh,
        in_specs=(
            P("seq", "exp"),
            P("seq", "exp"),
            P("seq", None),
            P(None, "exp"),
            P("exp"),
            P(None, "exp"),
            P(None, "exp"),
            P("exp"),
            P("exp"),
            P(None, None, "seq"),
            P("seq", "exp"),
            P("exp", None),
            P("seq", None),
            P("exp", "seq"),
            P("seq", "exp"),
        ),
        out_specs=(P("seq", "exp"), P("seq", "exp")),
        check_vma=False,
    )
```

```python
import functools
import math

import jax
import jax.numpy as jnp
from jax import lax
from jax.experimental import pallas as pl
from jax.experimental.pallas import tpu as pltpu
from jax.sharding import PartitionSpec as P

CAP = 18
MIB = 1 << 20
LOG2E = math.log2(math.e)
F32 = jnp.float32
BF16 = jnp.bfloat16


def params(limit):
    return pltpu.CompilerParams(vmem_limit_bytes=limit * MIB)


def cost(flops, moved, transcendentals=0):
    return pl.CostEstimate(
        flops=int(flops), bytes_accessed=int(moved), transcendentals=int(transcendentals)
    )


def in_hbm(*arrays):
    return [pltpu.with_memory_space_constraint(a, pltpu.HBM) for a in arrays]


def iota(shape, dim):
    return lax.broadcasted_iota(jnp.int32, shape, dim)


def dot(a, b):
    return jnp.dot(a, b, preferred_element_type=F32)


def dot_nt(a, b):
    return lax.dot_general(a, b, (((1,), (1,)), ((), ())), preferred_element_type=F32)


def packing(features):
    main = CAP // 16 * 16
    extra = CAP - main
    cuts = main // extra if extra and main % extra == 0 else 0
    if cuts and features % (cuts * 128) == 0:
        return main, extra, cuts, features // cuts
    return -(-CAP // 16) * 16, 0, 0, 0


def hits_and_slots(ids, experts):
    tokens = ids.shape[1]
    of = iota((experts, tokens), 0)
    hits = [(of == ids[k : k + 1]).astype(F32) for k in range(2)]
    before = (iota((tokens, tokens), 0) < iota((tokens, tokens), 1)).astype(BF16)
    earlier = dot((hits[0] + hits[1]).astype(BF16), before)
    slots = [jnp.sum(h * earlier, axis=0, keepdims=True).astype(jnp.int32) for h in hits]
    return hits, slots


def route_kernel(pack, ids_ref, hidden_ref, router_ref, out_ref, logits_ref):
    main, extra, cuts, width = pack
    experts, copies = out_ref.shape[:2]
    tokens, features = hidden_ref.shape
    ids = ids_ref[...]
    _, slots = hits_and_slots(ids, experts)
    hidden = hidden_ref[...]
    row = iota((experts * main, tokens), 0)
    picked = None
    for k in range(2):
        key = jnp.where(slots[k] < main, ids[k : k + 1] * main + slots[k], -1)
        hit = row == key
        picked = hit if picked is None else picked | hit
    packed = dot(picked.astype(BF16), hidden).astype(BF16)
    for e in range(experts):
        for m in range(copies):
            out_ref[e, m, :, :features] = packed[e * main : (e + 1) * main]
    if extra:
        picked = None
        for k in range(2):
            key = jnp.where(slots[k] >= main, ids[k : k + 1] * extra + slots[k] - main, -1)
            hit = row // cuts == key
            picked = hit if picked is None else picked | hit
        total = None
        for c in range(cuts):
            chosen = (picked & (row % cuts == c)).astype(BF16)
            part = dot(chosen, hidden[:, c * width : (c + 1) * width])
            total = part if total is None else total + part
        total = total.astype(BF16)
        for e in range(experts):
            for m in range(copies):
                out_ref[e, m, :, features:] = total[e * main : (e + 1) * main]
    logits_ref[...] = dot_nt(hidden, router_ref[...])


def route(ids, hidden, router, copies, pack):
    main, _, _, width = pack
    tokens, features = hidden.shape
    experts = router.shape[0]
    return pl.pallas_call(
        functools.partial(route_kernel, pack),
        out_shape=(
            jax.ShapeDtypeStruct((experts, copies, main, features + width), BF16),
            jax.ShapeDtypeStruct((tokens, experts), F32),
        ),
        compiler_params=params(40),
        cost_estimate=cost(2 * tokens * experts * main * features * 2, hidden.size * 8),
        name="route",
    )(*in_hbm(ids, hidden, router))


def weights_kernel(pack, copies, ids_ref, *refs):
    logits_refs, (main_ref, extra_ref, gates_ref) = refs[:-3], refs[-3:]
    main, extra, cuts, _ = pack
    tokens, experts = logits_refs[0].shape
    ids = ids_ref[...]
    hits, slots = hits_and_slots(ids, experts)
    eye = (iota((tokens, tokens), 0) == iota((tokens, tokens), 1)).astype(BF16)
    logits = logits_refs[0][...]
    for ref in logits_refs[1:]:
        logits = logits + ref[...]
    columns = [dot_nt(eye, h.astype(BF16)) for h in hits]
    picked = [jnp.sum(c * logits, axis=1, keepdims=True) for c in columns]
    expert = iota((tokens, experts), 1).astype(F32)
    total = experts * copies * main
    col = iota((tokens, total), 1)
    for k in range(2):
        gate = jax.nn.sigmoid(picked[k] - picked[1 - k])
        gates_ref[k] = jnp.broadcast_to(gate, gates_ref.shape[1:])
        named = jnp.sum(columns[k] * expert, axis=1, keepdims=True).astype(jnp.int32)
        wide = jnp.broadcast_to(slots[k].astype(F32), (8, tokens)).astype(BF16)
        slot = dot_nt(eye, wide)[:, :1].astype(jnp.int32)
        mine = col // (copies * main) == named
        main_ref[k] = (mine & (col % main == slot)).astype(BF16)
        if extra:
            place = (col % main) // cuts + main
            extra_ref[k] = (mine & (place == slot)).astype(BF16)
        else:
            extra_ref[k] = jnp.zeros(extra_ref.shape[1:], BF16)


def blend_weights(ids, logits, copies, pack):
    tokens, experts = logits[0].shape
    total = experts * copies * pack[0]
    return pl.pallas_call(
        functools.partial(weights_kernel, pack, copies),
        out_shape=(
            jax.ShapeDtypeStruct((2, tokens, total), BF16),
            jax.ShapeDtypeStruct((2, tokens, total), BF16),
            jax.ShapeDtypeStruct((2, tokens, 128), F32),
        ),
        compiler_params=params(40),
        cost_estimate=cost(2 * tokens * total * 16, tokens * total * 8),
        name="blend_weights",
    )(*in_hbm(ids), *logits)


ANYWHERE = pl.BlockSpec(memory_space=pl.ANY)
INSIDE = pl.BlockSpec(memory_space=pltpu.VMEM)
AHEAD = 6


def streamed(from_ref, to_ref, sems, dim, chunk, use, begin=None):
    count = from_ref.shape[dim] // chunk

    def copy(i):
        at = pl.ds(pl.multiple_of(i * chunk, chunk), chunk)
        part = (slice(None), at) if dim else (at, slice(None))
        return pltpu.make_async_copy(from_ref.at[part], to_ref.at[part], sems.at[i])

    for i in range(min(AHEAD, count)):
        copy(i).start()
    if begin is not None:
        begin()

    def step(i, carry):
        copy(i).wait()

        @pl.when(i + AHEAD < count)
        def _():
            copy(i + AHEAD).start()

        use(i)
        return carry

    lax.fori_loop(0, count, step, 0)


def gate_kernel(chunk, x_ref, w_ref, out_ref, held_ref, sems):
    def use(i):
        at = pl.ds(pl.multiple_of(i * chunk, chunk), chunk)
        out_ref[:, at] = dot(x_ref[...], held_ref[:, at]).astype(BF16)

    streamed(w_ref, held_ref, sems, 1, chunk, use)


def gate(x, w_gate):
    rows, features = x.shape
    amount = w_gate.shape[1]
    chunk = math.gcd(512, amount)
    return pl.pallas_call(
        functools.partial(gate_kernel, chunk),
        in_specs=[INSIDE, ANYWHERE],
        out_specs=INSIDE,
        out_shape=jax.ShapeDtypeStruct((rows, amount), BF16),
        scratch_shapes=[
            pltpu.VMEM(w_gate.shape, BF16),
            pltpu.SemaphoreType.DMA((amount // chunk,)),
        ],
        compiler_params=params(44),
        cost_estimate=cost(2 * rows * features * amount, features * amount * 2),
        name="gate",
    )(x, *in_hbm(w_gate))


def fill_acted(chunk, part_refs, acted_ref):
    def piece(i):
        at = pl.ds(pl.multiple_of(i * chunk, chunk), chunk)
        total = part_refs[0][:, at].astype(F32)
        for ref in part_refs[1:]:
            total = total + ref[:, at].astype(F32)
        acted_ref[:, at] = (total * jax.nn.sigmoid(total)).astype(BF16)

    pl.loop(0, acted_ref.shape[1] // chunk)(piece)


def down_kernel(chunk, *refs):
    part_refs, w_ref, out_ref, acted_ref, held_ref, sems = refs[:-5], *refs[-5:]

    def use(i):
        at = pl.ds(pl.multiple_of(i * chunk, chunk), chunk)
        out_ref[:, at] = dot(acted_ref[...], held_ref[:, at]).astype(out_ref.dtype)

    def begin():
        fill_acted(math.gcd(512, acted_ref.shape[1]), part_refs, acted_ref)

    streamed(w_ref, held_ref, sems, 1, chunk, use, begin)


def down(parts, w_down, dtype):
    rows, amount = parts[0].shape
    features = w_down.shape[1]
    chunk = math.gcd(256, features)
    return pl.pallas_call(
        functools.partial(down_kernel, chunk),
        in_specs=[INSIDE] * len(parts) + [ANYWHERE],
        out_specs=INSIDE,
        out_shape=jax.ShapeDtypeStruct((rows, features), dtype),
        scratch_shapes=[
            pltpu.VMEM((rows, amount), BF16),
            pltpu.VMEM(w_down.shape, BF16),
            pltpu.SemaphoreType.DMA((features // chunk,)),
        ],
        compiler_params=params(48),
        cost_estimate=cost(2 * rows * features * amount, features * amount * 2),
        name="down",
    )(*parts, *in_hbm(w_down))


def unpack_kernel(pack, arrived_ref, out_ref):
    main, extra, cuts, width = pack
    sources = arrived_ref.shape[0]
    features = out_ref.shape[1]
    out_ref[: sources * main] = arrived_ref[:, :, :features].reshape(sources * main, features)
    if extra:
        folded = arrived_ref[:, :, features:].reshape(sources * main, width)
        shape = (sources * extra, sources * main)
        for c in range(cuts):
            pick = (iota(shape, 1) == iota(shape, 0) * cuts + c).astype(BF16)
            out_ref[sources * main :, c * width : (c + 1) * width] = dot(pick, folded).astype(BF16)


def unpack(arrived, features, pack):
    main, extra, _, _ = pack
    rows = arrived.shape[0] * (main + extra)
    return pl.pallas_call(
        functools.partial(unpack_kernel, pack),
        out_shape=jax.ShapeDtypeStruct((rows, features), BF16),
        compiler_params=params(24),
        cost_estimate=cost(arrived.size * 16, arrived.size * 4),
        name="unpack",
    )(arrived)


def pack_kernel(pack, *refs):
    main, extra, cuts, width = pack
    part_refs, out_ref = refs[:-1], refs[-1]
    sources = out_ref.shape[0]
    features = part_refs[0].shape[1]
    first = sources * main

    def total(rows, columns):
        value = part_refs[0][rows, columns].astype(F32)
        for ref in part_refs[1:]:
            value = value + ref[rows, columns].astype(F32)
        return value.astype(BF16)

    made = total(slice(0, first), slice(0, features))
    out_ref[:, :, :features] = made.reshape(sources, main, features)
    if extra:
        shape = (sources * main, sources * extra)
        folded = None
        for c in range(cuts):
            piece = total(slice(first, None), slice(c * width, (c + 1) * width))
            pick = (iota(shape, 0) == iota(shape, 1) * cuts + c).astype(BF16)
            part = dot(pick, piece)
            folded = part if folded is None else folded + part
        out_ref[:, :, features:] = folded.astype(BF16).reshape(sources, main, width)


def pack_sum(parts, sources, pack):
    main, _, _, width = pack
    features = parts[0].shape[1]
    return pl.pallas_call(
        functools.partial(pack_kernel, pack),
        out_shape=jax.ShapeDtypeStruct((sources, main, features + width), BF16),
        compiler_params=params(24),
        cost_estimate=cost(parts[0].size * 16, parts[0].size * 8),
        name="pack_sum",
    )(*parts)


def combine_kernel(pack, back_ref, main_ref, extra_ref, gates_ref, out_ref):
    main, extra, cuts, width = pack
    sources = back_ref.shape[0]
    tokens, features = out_ref.shape
    back = back_ref[:, :, :features].reshape(sources * main, features)
    folded = back_ref[:, :, features:].reshape(sources * main, width) if extra else None
    total = None
    for k in range(2):
        rows = dot(main_ref[k], back)
        if extra:
            chosen = extra_ref[k]
            at = iota(chosen.shape, 1) % cuts
            pieces = [
                dot(jnp.where(at == c, chosen, jnp.zeros_like(chosen)), folded) for c in range(cuts)
            ]
            rows = rows + jnp.concatenate(pieces, axis=1)
        weighed = rows * gates_ref[k][:, :1]
        total = weighed if total is None else total + weighed
    out_ref[...] = total.astype(BF16)


def combine(back, weights, tokens, features, pack):
    return pl.pallas_call(
        functools.partial(combine_kernel, pack),
        out_shape=jax.ShapeDtypeStruct((tokens, features), BF16),
        compiler_params=params(40),
        cost_estimate=cost(4 * tokens * back.size, back.size * 2),
        name="combine",
    )(back, *weights)


def spread_states(values, spread_ref):
    for t in range(spread_ref.shape[0]):
        spread_ref[t] = jnp.broadcast_to(values[:, t : t + 1], spread_ref.shape[1:])


def row_sums(parts):
    place = iota(parts[0].shape, 0)
    for stride in (4, 2, 1):
        low = place & stride == 0
        half = len(parts) // 2
        joined = []
        for a, b in zip(parts[:half], parts[half:]):
            kept = jnp.where(low, a, b)
            moved = jnp.where(low, b, a)
            if stride == 4:
                other = pltpu.roll(moved, 4, 0)
            else:
                other = jnp.where(low, pltpu.roll(moved, 8 - stride, 0), pltpu.roll(moved, stride, 0))
            joined.append(kept + other)
        parts = joined
    return parts[0]


def state_sum(value):
    total = value[:8]
    for at in range(8, value.shape[0], 8):
        total = total + value[at : at + 8]
    return total


def tiled_lanes(value, lanes):
    return jnp.concatenate([value] * (lanes // value.shape[1]), axis=1)


def scan_kernel(
    x_ref, edge_ref, low_ref, dtw_ref, dtb_ref, alog_ref, cw_ref, cb_ref, skip_ref, bc_ref,
    read_ref, cum_ref, ends_ref, padded, delta_ref, fed_ref, totals_ref, b_ref, c_ref,
):
    tokens, lanes = x_ref.shape
    taps = cw_ref.shape[0]
    states = alog_ref.shape[0]

    @pl.when(pl.program_id(0) == 0)
    def _():
        spread_states(bc_ref[0], b_ref)
        spread_states(bc_ref[1], c_ref)
        totals_ref[...] = jnp.zeros_like(totals_ref)

    padded[8:] = x_ref[...].astype(F32)
    padded[8 - (taps - 1) : 8] = edge_ref[...].astype(F32)
    conv = jnp.broadcast_to(cb_ref[...], (tokens, lanes))
    for k in range(taps):
        at = 8 - (taps - 1) + k
        conv = conv + cw_ref[k : k + 1] * padded[at : at + tokens]
    act = conv * jax.nn.sigmoid(conv)
    raw = dot(low_ref[...], dtw_ref[...]) + dtb_ref[...]
    delta = jnp.maximum(raw, 0.0) + jnp.log1p(jnp.exp(-jnp.abs(raw)))
    delta_ref[...] = delta
    fed_ref[...] = delta * act
    read_ref[...] = skip_ref[...] * act
    rates = -jnp.exp(alog_ref[...]) * LOG2E

    def eight(g, carry):
        state, running = carry
        at = pl.multiple_of(g * 8, 8)
        delta8 = delta_ref[pl.ds(at, 8)]
        fed8 = fed_ref[pl.ds(at, 8)]
        reads, sums = [], []
        for i in range(8):
            step = delta8[i : i + 1]
            running = running + step
            factor = jnp.exp2(rates * step)
            state = factor * state + tiled_lanes(b_ref[at + i], lanes) * fed8[i : i + 1]
            reads.append(state_sum(tiled_lanes(c_ref[at + i], lanes) * state))
            sums.append(running)
        read_ref[pl.ds(at, 8)] += row_sums(reads)
        cum_ref[pl.ds(at, 8)] = jnp.concatenate(sums, axis=0)
        return state, running

    state, running = lax.fori_loop(
        0, tokens // 8, eight, (jnp.zeros((states, lanes), F32), jnp.zeros((1, lanes), F32))
    )
    step, steps = pl.program_id(0), pl.num_programs(0)
    ends_ref[:, pl.ds(pl.multiple_of(step * lanes, lanes), lanes)] = state.astype(BF16)
    high = running.astype(BF16).astype(F32)
    totals_ref[pl.ds(step, 1)] = high
    totals_ref[pl.ds(steps + step, 1)] = running - high

    @pl.when(step == steps - 1)
    def _():
        ends_ref[:, ends_ref.shape[1] - lanes :] = totals_ref[...].astype(BF16)


def scan(x_in, edge, dt_low, dt_weight, dt_bias, a_log, conv_weight, conv_bias, d_skip, b_and_c):
    tokens, channels = x_in.shape
    states = a_log.shape[0]
    lanes = math.gcd(512, channels)

    def cut(rows):
        return pl.BlockSpec((rows, lanes), lambda i: (0, i))

    def whole(a):
        zeros = (0,) * a.ndim
        return pl.BlockSpec(a.shape, lambda i: zeros)

    return pl.pallas_call(
        scan_kernel,
        grid=(channels // lanes,),
        in_specs=[
            cut(tokens), cut(edge.shape[0]), whole(dt_low), cut(dt_weight.shape[0]), cut(1),
            cut(states), cut(conv_weight.shape[0]), cut(1), cut(1), whole(b_and_c),
        ],
        out_specs=(
            cut(tokens),
            cut(tokens),
            pl.BlockSpec((states, channels + lanes), lambda i: (0, 0)),
        ),
        out_shape=(
            pltpu.HBM((tokens, channels), F32),
            pltpu.HBM((tokens, channels), F32),
            jax.ShapeDtypeStruct((states, channels + lanes), BF16),
        ),
        scratch_shapes=[
            pltpu.VMEM((tokens + 8, lanes), F32),
            pltpu.VMEM((tokens, lanes), F32),
            pltpu.VMEM((tokens, lanes), F32),
            pltpu.VMEM((states, lanes), F32),
            pltpu.VMEM((tokens, states, 128), F32),
            pltpu.VMEM((tokens, states, 128), F32),
        ],
        compiler_params=params(40),
        cost_estimate=cost(
            tokens * channels * states * 8, tokens * channels * 12, tokens * channels * states
        ),
        name="scan",
    )(
        *in_hbm(x_in),
        edge,
        *in_hbm(
            dt_low, dt_weight, dt_bias[None], a_log, conv_weight, conv_bias[None], d_skip[None],
            b_and_c,
        ),
    )


def upper_half(step):
    return (lax.axis_index("seq") >> step) % 2 == 1


def link_kernel(step, *refs):
    total_ref, received_ref, alog_ref, prefix_ref = refs[:4] if step else (*refs[:3], None)
    total_out, prefix_out = refs[-2:]
    channels = alog_ref.shape[1]
    lanes = total_ref.shape[1] - channels
    steps = channels // lanes
    upper = upper_half(step)

    def sizes(ref):
        value = ref[:, channels:].astype(F32)
        return value[:steps] + value[steps : 2 * steps]

    def put_sizes(ref, value):
        high = value.astype(BF16).astype(F32)
        rest = jnp.zeros((ref.shape[0] - 2 * steps, lanes), F32)
        parts = [high, value - high] + ([rest] if rest.shape[0] else [])
        ref[:, channels:] = jnp.concatenate(parts, axis=0).astype(BF16)

    own, received = sizes(total_ref), sizes(received_ref)
    before = sizes(prefix_ref) if step else jnp.zeros_like(own)
    later = jnp.where(upper, own, received)
    put_sizes(total_out, own + received)
    put_sizes(prefix_out, before + jnp.where(upper, received, 0.0))
    for i in range(steps):
        at = slice(i * lanes, (i + 1) * lanes)
        rates = -jnp.exp(alog_ref[:, at]) * LOG2E
        mine, theirs = total_ref[:, at].astype(F32), received_ref[:, at].astype(F32)
        last, first = jnp.where(upper, mine, theirs), jnp.where(upper, theirs, mine)
        total_out[:, at] = (last + jnp.exp2(rates * later[i : i + 1]) * first).astype(BF16)
        if step:
            prefix = prefix_ref[:, at].astype(F32)
            further = prefix + jnp.exp2(rates * before[i : i + 1]) * theirs
        else:
            prefix, further = jnp.zeros_like(theirs), theirs
        prefix_out[:, at] = jnp.where(upper, further, prefix).astype(BF16)


def link(step, total, received, a_log, prefix):
    shape = jax.ShapeDtypeStruct(total.shape, BF16)
    args = [total, received, a_log] + ([prefix] if step else [])
    return pl.pallas_call(
        functools.partial(link_kernel, step),
        out_shape=(shape, shape),
        compiler_params=params(16),
        cost_estimate=cost(total.size * 2, total.size * 6),
        name="link",
    )(*args)


def finish_kernel(
    step, read_ref, cum_ref, z_ref, prefix_ref, sizes_ref, received_ref, alog_ref, bc_ref,
    out_ref, sum_ref, wide_ref, c_ref,
):
    tokens, lanes = z_ref.shape
    at, steps = pl.program_id(0), pl.num_programs(0)

    @pl.when(at == 0)
    def _():
        spread_states(bc_ref[1], c_ref)
        wide_ref[...] = sizes_ref[...].astype(F32)

    rates = -jnp.exp(alog_ref[...]) * LOG2E
    entering = prefix_ref[...].astype(F32)
    size = wide_ref[pl.ds(at, 1)] + wide_ref[pl.ds(steps + at, 1)]
    further = entering + jnp.exp2(rates * size) * received_ref[...].astype(F32)
    entering = jnp.where(upper_half(step), further, entering)

    def eight(g, carry):
        at = pl.multiple_of(g * 8, 8)
        cum8 = cum_ref[pl.ds(at, 8)]
        reads = []
        for i in range(8):
            kept = jnp.exp2(rates * cum8[i : i + 1]) * entering
            reads.append(state_sum(tiled_lanes(c_ref[at + i], lanes) * kept))
        sum_ref[pl.ds(at, 8)] = row_sums(reads)
        return carry

    lax.fori_loop(0, tokens // 8, eight, 0)
    z = z_ref[...].astype(F32)
    out_ref[...] = ((read_ref[...] + sum_ref[...]) * (z * jax.nn.sigmoid(z))).astype(BF16)


def finish(step, read, cum, z_gate, prefix, received, a_log, b_and_c):
    tokens, channels = z_gate.shape
    states = a_log.shape[0]
    lanes = math.gcd(512, channels)

    def cut(rows):
        return pl.BlockSpec((rows, lanes), lambda i: (0, i))

    return pl.pallas_call(
        functools.partial(finish_kernel, step),
        grid=(channels // lanes,),
        in_specs=[
            cut(tokens), cut(tokens), cut(tokens), cut(states),
            pl.BlockSpec((states, lanes), lambda i: (0, channels // lanes)), cut(states), cut(states),
            pl.BlockSpec(b_and_c.shape, lambda i: (0, 0, 0)),
        ],
        out_specs=cut(tokens),
        out_shape=jax.ShapeDtypeStruct((tokens, channels), BF16),
        scratch_shapes=[
            pltpu.VMEM((tokens, lanes), F32),
            pltpu.VMEM((states, lanes), F32),
            pltpu.VMEM((tokens, states, 128), F32),
        ],
        compiler_params=params(40),
        cost_estimate=cost(
            tokens * channels * states * 5, tokens * channels * 12, tokens * channels * states
        ),
        name="finish",
    )(*in_hbm(read, cum, z_gate), prefix, prefix, received, *in_hbm(a_log, b_and_c))


def swapped(value, by):
    count = lax.axis_size("seq")
    return lax.ppermute(value, "seq", [(i, i ^ by) for i in range(count)])


def turned(value, axis, by):
    count = lax.axis_size(axis)
    return lax.ppermute(value, axis, [(i, (i + by) % count) for i in range(count)])


def turned_within(value, copies, by):
    count = lax.axis_size("seq")
    return lax.ppermute(
        value, "seq", [(i, i // copies * copies + (i + by) % copies) for i in range(count)]
    )


def exchanged(value, copies):
    count = lax.axis_size("seq")
    groups = [list(range(m, count, copies)) for m in range(copies)]
    return lax.all_to_all(
        value, "seq", split_axis=0, concat_axis=0, tiled=True, axis_index_groups=groups
    )


def after(value, *others):
    return lax.optimization_barrier((value, others))[0]


def local(
    x_in,
    z_gate,
    dt_low,
    dt_weight,
    dt_bias,
    a_log,
    conv_weight,
    conv_bias,
    d_skip,
    b_and_c,
    hidden,
    router,
    expert_ids,
    w_gate,
    w_down,
):
    blocks = lax.axis_size("seq")
    feature_parts = lax.axis_size("exp")
    tokens, features = hidden.shape
    experts = router.shape[1]
    copies = blocks // experts
    pack = packing(features)
    ids = expert_ids.T

    edge = x_in[tokens - (conv_weight.shape[0] - 1) :]
    edge = lax.ppermute(edge, "seq", [(i, i + 1) for i in range(blocks - 1)])
    outgoing, logits = route(ids, hidden, router.T, 1, pack)
    outgoing = after(outgoing, edge)
    arrived = exchanged(outgoing.reshape((experts,) + outgoing.shape[2:]), copies)

    read, cum, ends = scan(
        x_in, edge, dt_low, dt_weight, dt_bias, a_log, conv_weight, conv_bias, d_skip, b_and_c
    )
    logits = [logits] + [turned(logits, "exp", d) for d in range(1, feature_parts)]
    arrived = after(arrived, ends, *logits)

    steps = blocks.bit_length() - 1
    total, prefix, received = ends, None, swapped(ends, 1)
    step = 0

    def advance(*marks):
        nonlocal total, prefix, received, step
        if step < steps - 1:
            total, prefix = link(step, total, after(received, *marks), a_log, prefix)
            step += 1
            received = swapped(total, 1 << step)
        return prefix

    rows = [unpack(arrived, features, pack)]
    for d in range(1, copies):
        rows.append(turned_within(rows[0], copies, d))
    gated = []
    for part in rows:
        if len(gated) == 1:
            part = after(part, advance(gated[-1][0]))
        elif gated:
            part = after(part, gated[-1][0])
        own = gate(part, w_gate)
        if len(gated) == copies - 1:
            own = after(own, advance(own), *(p for parts in gated for p in parts[1:]))
        gated.append([own] + [turned(own, "exp", d) for d in range(1, feature_parts)])
    made = []
    for parts in gated[1:] + gated[:1]:
        product = down(parts, w_down, BF16 if len(made) < copies - 1 else F32)
        if not made:
            product = after(product, advance(product))
        made.append(product)
    while step < steps - 1:
        advance()
    sums = [after(made[-1], received)]
    for d in range(1, copies):
        sums.append(turned_within(made[d - 1], copies, -d))
    packed = pack_sum(sums, experts, pack)
    back = exchanged(packed, copies)

    weights = blend_weights(ids, after(tuple(logits), packed), 1, pack)
    received = after(received, packed)
    mamba_out = finish(step, read, cum, z_gate, prefix, received, a_log, b_and_c)
    back = after(back, mamba_out)
    moe_out = combine(back, weights, tokens, features, pack)
    return mamba_out, moe_out


def solution(mesh):
    return jax.shard_map(
        local,
        mesh=mesh,
        in_specs=(
            P("seq", "exp"),
            P("seq", "exp"),
            P("seq", None),
            P(None, "exp"),
            P("exp"),
            P(None, "exp"),
            P(None, "exp"),
            P("exp"),
            P("exp"),
            P(None, None, "seq"),
            P("seq", "exp"),
            P("exp", None),
            P("seq", None),
            P("exp", "seq"),
            P("seq", "exp"),
        ),
        out_specs=(P("seq", "exp"), P("seq", "exp")),
        check_vma=False,
    )
```

```python
import functools
import math

import jax
import jax.numpy as jnp
from jax import lax
from jax.experimental import pallas as pl
from jax.experimental.pallas import tpu as pltpu
from jax.sharding import PartitionSpec as P

CAP = 18
MIB = 1 << 20
LOG2E = math.log2(math.e)
F32 = jnp.float32
BF16 = jnp.bfloat16


def params(limit):
    return pltpu.CompilerParams(vmem_limit_bytes=limit * MIB)


def cost(flops, moved, transcendentals=0):
    return pl.CostEstimate(
        flops=int(flops), bytes_accessed=int(moved), transcendentals=int(transcendentals)
    )


def in_hbm(*arrays):
    return [pltpu.with_memory_space_constraint(a, pltpu.HBM) for a in arrays]


def iota(shape, dim):
    return lax.broadcasted_iota(jnp.int32, shape, dim)


def dot(a, b):
    return jnp.dot(a, b, preferred_element_type=F32)


def dot_nt(a, b):
    return lax.dot_general(a, b, (((1,), (1,)), ((), ())), preferred_element_type=F32)


def packing(features):
    main = CAP // 16 * 16
    extra = CAP - main
    cuts = main // extra if extra and main % extra == 0 else 0
    if cuts and features % (cuts * 128) == 0:
        return main, extra, cuts, features // cuts
    return -(-CAP // 16) * 16, 0, 0, 0


def hits_and_slots(ids, experts):
    tokens = ids.shape[1]
    of = iota((experts, tokens), 0)
    hits = [(of == ids[k : k + 1]).astype(F32) for k in range(2)]
    before = (iota((tokens, tokens), 0) < iota((tokens, tokens), 1)).astype(BF16)
    earlier = dot((hits[0] + hits[1]).astype(BF16), before)
    slots = [jnp.sum(h * earlier, axis=0, keepdims=True).astype(jnp.int32) for h in hits]
    return hits, slots


def route_kernel(pack, ids_ref, hidden_ref, router_ref, out_ref, logits_ref):
    main, extra, cuts, width = pack
    experts, copies = out_ref.shape[:2]
    tokens, features = hidden_ref.shape
    ids = ids_ref[...]
    _, slots = hits_and_slots(ids, experts)
    hidden = hidden_ref[...]
    row = iota((experts * main, tokens), 0)
    picked = None
    for k in range(2):
        key = jnp.where(slots[k] < main, ids[k : k + 1] * main + slots[k], -1)
        hit = row == key
        picked = hit if picked is None else picked | hit
    packed = dot(picked.astype(BF16), hidden).astype(BF16)
    for e in range(experts):
        for m in range(copies):
            out_ref[e, m, :, :features] = packed[e * main : (e + 1) * main]
    if extra:
        picked = None
        for k in range(2):
            key = jnp.where(slots[k] >= main, ids[k : k + 1] * extra + slots[k] - main, -1)
            hit = row // cuts == key
            picked = hit if picked is None else picked | hit
        total = None
        for c in range(cuts):
            chosen = (picked & (row % cuts == c)).astype(BF16)
            part = dot(chosen, hidden[:, c * width : (c + 1) * width])
            total = part if total is None else total + part
        total = total.astype(BF16)
        for e in range(experts):
            for m in range(copies):
                out_ref[e, m, :, features:] = total[e * main : (e + 1) * main]
    logits_ref[...] = dot_nt(hidden, router_ref[...])


def route(ids, hidden, router, copies, pack):
    main, _, _, width = pack
    tokens, features = hidden.shape
    experts = router.shape[0]
    return pl.pallas_call(
        functools.partial(route_kernel, pack),
        out_shape=(
            jax.ShapeDtypeStruct((experts, copies, main, features + width), BF16),
            jax.ShapeDtypeStruct((tokens, experts), F32),
        ),
        compiler_params=params(40),
        cost_estimate=cost(2 * tokens * experts * main * features * 2, hidden.size * 8),
        name="route",
    )(*in_hbm(ids, hidden, router))


def weights_kernel(pack, copies, ids_ref, *refs):
    logits_refs, (main_ref, extra_ref, gates_ref) = refs[:-3], refs[-3:]
    main, extra, cuts, _ = pack
    tokens, experts = logits_refs[0].shape
    ids = ids_ref[...]
    hits, slots = hits_and_slots(ids, experts)
    eye = (iota((tokens, tokens), 0) == iota((tokens, tokens), 1)).astype(BF16)
    logits = logits_refs[0][...]
    for ref in logits_refs[1:]:
        logits = logits + ref[...]
    columns = [dot_nt(eye, h.astype(BF16)) for h in hits]
    picked = [jnp.sum(c * logits, axis=1, keepdims=True) for c in columns]
    expert = iota((tokens, experts), 1).astype(F32)
    total = experts * copies * main
    col = iota((tokens, total), 1)
    for k in range(2):
        gate = jax.nn.sigmoid(picked[k] - picked[1 - k])
        gates_ref[k] = jnp.broadcast_to(gate, gates_ref.shape[1:])
        named = jnp.sum(columns[k] * expert, axis=1, keepdims=True).astype(jnp.int32)
        wide = jnp.broadcast_to(slots[k].astype(F32), (8, tokens)).astype(BF16)
        slot = dot_nt(eye, wide)[:, :1].astype(jnp.int32)
        mine = col // (copies * main) == named
        main_ref[k] = (mine & (col % main == slot)).astype(BF16)
        if extra:
            place = (col % main) // cuts + main
            extra_ref[k] = (mine & (place == slot)).astype(BF16)
        else:
            extra_ref[k] = jnp.zeros(extra_ref.shape[1:], BF16)


def blend_weights(ids, logits, copies, pack):
    tokens, experts = logits[0].shape
    total = experts * copies * pack[0]
    return pl.pallas_call(
        functools.partial(weights_kernel, pack, copies),
        out_shape=(
            jax.ShapeDtypeStruct((2, tokens, total), BF16),
            jax.ShapeDtypeStruct((2, tokens, total), BF16),
            jax.ShapeDtypeStruct((2, tokens, 128), F32),
        ),
        compiler_params=params(40),
        cost_estimate=cost(2 * tokens * total * 16, tokens * total * 8),
        name="blend_weights",
    )(*in_hbm(ids), *logits)


ANYWHERE = pl.BlockSpec(memory_space=pl.ANY)
INSIDE = pl.BlockSpec(memory_space=pltpu.VMEM)
AHEAD = 6


def streamed(from_ref, to_ref, sems, dim, chunk, use, begin=None):
    count = from_ref.shape[dim] // chunk

    def copy(i):
        at = pl.ds(pl.multiple_of(i * chunk, chunk), chunk)
        part = (slice(None), at) if dim else (at, slice(None))
        return pltpu.make_async_copy(from_ref.at[part], to_ref.at[part], sems.at[i])

    for i in range(min(AHEAD, count)):
        copy(i).start()
    if begin is not None:
        begin()

    def step(i, carry):
        copy(i).wait()

        @pl.when(i + AHEAD < count)
        def _():
            copy(i + AHEAD).start()

        use(i)
        return carry

    lax.fori_loop(0, count, step, 0)


def gate_kernel(chunk, x_ref, w_ref, out_ref, held_ref, sems):
    def use(i):
        at = pl.ds(pl.multiple_of(i * chunk, chunk), chunk)
        out_ref[:, at] = dot(x_ref[...], held_ref[:, at]).astype(BF16)

    streamed(w_ref, held_ref, sems, 1, chunk, use)


def gate(x, w_gate):
    rows, features = x.shape
    amount = w_gate.shape[1]
    chunk = math.gcd(512, amount)
    return pl.pallas_call(
        functools.partial(gate_kernel, chunk),
        in_specs=[INSIDE, ANYWHERE],
        out_specs=INSIDE,
        out_shape=jax.ShapeDtypeStruct((rows, amount), BF16),
        scratch_shapes=[
            pltpu.VMEM(w_gate.shape, BF16),
            pltpu.SemaphoreType.DMA((amount // chunk,)),
        ],
        compiler_params=params(44),
        cost_estimate=cost(2 * rows * features * amount, features * amount * 2),
        name="gate",
    )(x, *in_hbm(w_gate))


def fill_acted(chunk, part_refs, acted_ref):
    def piece(i):
        at = pl.ds(pl.multiple_of(i * chunk, chunk), chunk)
        total = part_refs[0][:, at].astype(F32)
        for ref in part_refs[1:]:
            total = total + ref[:, at].astype(F32)
        acted_ref[:, at] = (total * jax.nn.sigmoid(total)).astype(BF16)

    pl.loop(0, acted_ref.shape[1] // chunk)(piece)


def down_kernel(chunk, *refs):
    part_refs, w_ref, out_ref, acted_ref, held_ref, sems = refs[:-5], *refs[-5:]

    def use(i):
        at = pl.ds(pl.multiple_of(i * chunk, chunk), chunk)
        out_ref[:, at] = dot(acted_ref[...], held_ref[:, at]).astype(out_ref.dtype)

    def begin():
        fill_acted(math.gcd(512, acted_ref.shape[1]), part_refs, acted_ref)

    streamed(w_ref, held_ref, sems, 1, chunk, use, begin)


def down(parts, w_down, dtype):
    rows, amount = parts[0].shape
    features = w_down.shape[1]
    chunk = math.gcd(256, features)
    return pl.pallas_call(
        functools.partial(down_kernel, chunk),
        in_specs=[INSIDE] * len(parts) + [ANYWHERE],
        out_specs=INSIDE,
        out_shape=jax.ShapeDtypeStruct((rows, features), dtype),
        scratch_shapes=[
            pltpu.VMEM((rows, amount), BF16),
            pltpu.VMEM(w_down.shape, BF16),
            pltpu.SemaphoreType.DMA((features // chunk,)),
        ],
        compiler_params=params(48),
        cost_estimate=cost(2 * rows * features * amount, features * amount * 2),
        name="down",
    )(*parts, *in_hbm(w_down))


def unpack_kernel(pack, arrived_ref, out_ref):
    main, extra, cuts, width = pack
    sources = arrived_ref.shape[0]
    features = out_ref.shape[1]
    out_ref[: sources * main] = arrived_ref[:, :, :features].reshape(sources * main, features)
    if extra:
        folded = arrived_ref[:, :, features:].reshape(sources * main, width)
        shape = (sources * extra, sources * main)
        for c in range(cuts):
            pick = (iota(shape, 1) == iota(shape, 0) * cuts + c).astype(BF16)
            out_ref[sources * main :, c * width : (c + 1) * width] = dot(pick, folded).astype(BF16)


def unpack(arrived, features, pack):
    main, extra, _, _ = pack
    rows = arrived.shape[0] * (main + extra)
    return pl.pallas_call(
        functools.partial(unpack_kernel, pack),
        out_shape=jax.ShapeDtypeStruct((rows, features), BF16),
        compiler_params=params(24),
        cost_estimate=cost(arrived.size * 16, arrived.size * 4),
        name="unpack",
    )(arrived)


def pack_kernel(pack, *refs):
    main, extra, cuts, width = pack
    part_refs, out_ref = refs[:-1], refs[-1]
    sources = out_ref.shape[0]
    features = part_refs[0].shape[1]
    first = sources * main

    def total(rows, columns):
        value = part_refs[0][rows, columns].astype(F32)
        for ref in part_refs[1:]:
            value = value + ref[rows, columns].astype(F32)
        return value.astype(BF16)

    made = total(slice(0, first), slice(0, features))
    out_ref[:, :, :features] = made.reshape(sources, main, features)
    if extra:
        shape = (sources * main, sources * extra)
        folded = None
        for c in range(cuts):
            piece = total(slice(first, None), slice(c * width, (c + 1) * width))
            pick = (iota(shape, 0) == iota(shape, 1) * cuts + c).astype(BF16)
            part = dot(pick, piece)
            folded = part if folded is None else folded + part
        out_ref[:, :, features:] = folded.astype(BF16).reshape(sources, main, width)


def pack_sum(parts, sources, pack):
    main, _, _, width = pack
    features = parts[0].shape[1]
    return pl.pallas_call(
        functools.partial(pack_kernel, pack),
        out_shape=jax.ShapeDtypeStruct((sources, main, features + width), BF16),
        compiler_params=params(24),
        cost_estimate=cost(parts[0].size * 16, parts[0].size * 8),
        name="pack_sum",
    )(*parts)


def combine_kernel(pack, back_ref, main_ref, extra_ref, gates_ref, out_ref):
    main, extra, cuts, width = pack
    sources = back_ref.shape[0]
    tokens, features = out_ref.shape
    back = back_ref[:, :, :features].reshape(sources * main, features)
    folded = back_ref[:, :, features:].reshape(sources * main, width) if extra else None
    total = None
    for k in range(2):
        rows = dot(main_ref[k], back)
        if extra:
            chosen = extra_ref[k]
            at = iota(chosen.shape, 1) % cuts
            pieces = [
                dot(jnp.where(at == c, chosen, jnp.zeros_like(chosen)), folded) for c in range(cuts)
            ]
            rows = rows + jnp.concatenate(pieces, axis=1)
        weighed = rows * gates_ref[k][:, :1]
        total = weighed if total is None else total + weighed
    out_ref[...] = total.astype(BF16)


def combine(back, weights, tokens, features, pack):
    return pl.pallas_call(
        functools.partial(combine_kernel, pack),
        out_shape=jax.ShapeDtypeStruct((tokens, features), BF16),
        compiler_params=params(40),
        cost_estimate=cost(4 * tokens * back.size, back.size * 2),
        name="combine",
    )(back, *weights)


def spread_states(values, spread_ref):
    for t in range(spread_ref.shape[0]):
        spread_ref[t] = jnp.broadcast_to(values[:, t : t + 1], spread_ref.shape[1:])


def row_sums(parts):
    place = iota(parts[0].shape, 0)
    for stride in (4, 2, 1):
        low = place & stride == 0
        half = len(parts) // 2
        joined = []
        for a, b in zip(parts[:half], parts[half:]):
            kept = jnp.where(low, a, b)
            moved = jnp.where(low, b, a)
            if stride == 4:
                other = pltpu.roll(moved, 4, 0)
            else:
                other = jnp.where(low, pltpu.roll(moved, 8 - stride, 0), pltpu.roll(moved, stride, 0))
            joined.append(kept + other)
        parts = joined
    return parts[0]


def state_sum(value):
    total = value[:8]
    for at in range(8, value.shape[0], 8):
        total = total + value[at : at + 8]
    return total


def tiled_lanes(value, lanes):
    return jnp.concatenate([value] * (lanes // value.shape[1]), axis=1)


def scan_kernel(
    x_ref, edge_ref, low_ref, dtw_ref, dtb_ref, alog_ref, cw_ref, cb_ref, skip_ref, bc_ref,
    read_ref, cum_ref, ends_ref, padded, delta_ref, fed_ref, totals_ref, b_ref, c_ref,
):
    tokens, lanes = x_ref.shape
    taps = cw_ref.shape[0]
    states = alog_ref.shape[0]

    @pl.when(pl.program_id(0) == 0)
    def _():
        spread_states(bc_ref[0], b_ref)
        spread_states(bc_ref[1], c_ref)
        totals_ref[...] = jnp.zeros_like(totals_ref)

    padded[8:] = x_ref[...].astype(F32)
    padded[8 - (taps - 1) : 8] = edge_ref[...].astype(F32)
    conv = jnp.broadcast_to(cb_ref[...], (tokens, lanes))
    for k in range(taps):
        at = 8 - (taps - 1) + k
        conv = conv + cw_ref[k : k + 1] * padded[at : at + tokens]
    act = conv * jax.nn.sigmoid(conv)
    raw = dot(low_ref[...], dtw_ref[...]) + dtb_ref[...]
    delta = jnp.maximum(raw, 0.0) + jnp.log1p(jnp.exp(-jnp.abs(raw)))
    delta_ref[...] = delta
    fed_ref[...] = delta * act
    read_ref[...] = skip_ref[...] * act
    rates = -jnp.exp(alog_ref[...]) * LOG2E

    def eight(g, carry):
        state, running = carry
        at = pl.multiple_of(g * 8, 8)
        delta8 = delta_ref[pl.ds(at, 8)]
        fed8 = fed_ref[pl.ds(at, 8)]
        reads, sums = [], []
        for i in range(8):
            step = delta8[i : i + 1]
            running = running + step
            factor = jnp.exp2(rates * step)
            state = factor * state + tiled_lanes(b_ref[at + i], lanes) * fed8[i : i + 1]
            reads.append(state_sum(tiled_lanes(c_ref[at + i], lanes) * state))
            sums.append(running)
        read_ref[pl.ds(at, 8)] += row_sums(reads)
        cum_ref[pl.ds(at, 8)] = jnp.concatenate(sums, axis=0)
        return state, running

    state, running = lax.fori_loop(
        0, tokens // 8, eight, (jnp.zeros((states, lanes), F32), jnp.zeros((1, lanes), F32))
    )
    step, steps = pl.program_id(0), pl.num_programs(0)
    ends_ref[:, pl.ds(pl.multiple_of(step * lanes, lanes), lanes)] = state.astype(BF16)
    high = running.astype(BF16).astype(F32)
    totals_ref[pl.ds(step, 1)] = high
    totals_ref[pl.ds(steps + step, 1)] = running - high

    @pl.when(step == steps - 1)
    def _():
        ends_ref[:, ends_ref.shape[1] - lanes :] = totals_ref[...].astype(BF16)


def scan(x_in, edge, dt_low, dt_weight, dt_bias, a_log, conv_weight, conv_bias, d_skip, b_and_c):
    tokens, channels = x_in.shape
    states = a_log.shape[0]
    lanes = math.gcd(512, channels)

    def cut(rows):
        return pl.BlockSpec((rows, lanes), lambda i: (0, i))

    def whole(a):
        zeros = (0,) * a.ndim
        return pl.BlockSpec(a.shape, lambda i: zeros)

    return pl.pallas_call(
        scan_kernel,
        grid=(channels // lanes,),
        in_specs=[
            cut(tokens), cut(edge.shape[0]), whole(dt_low), cut(dt_weight.shape[0]), cut(1),
            cut(states), cut(conv_weight.shape[0]), cut(1), cut(1), whole(b_and_c),
        ],
        out_specs=(
            cut(tokens),
            cut(tokens),
            pl.BlockSpec((states, channels + lanes), lambda i: (0, 0)),
        ),
        out_shape=(
            pltpu.HBM((tokens, channels), F32),
            pltpu.HBM((tokens, channels), F32),
            jax.ShapeDtypeStruct((states, channels + lanes), BF16),
        ),
        scratch_shapes=[
            pltpu.VMEM((tokens + 8, lanes), F32),
            pltpu.VMEM((tokens, lanes), F32),
            pltpu.VMEM((tokens, lanes), F32),
            pltpu.VMEM((states, lanes), F32),
            pltpu.VMEM((tokens, states, 128), F32),
            pltpu.VMEM((tokens, states, 128), F32),
        ],
        compiler_params=params(40),
        cost_estimate=cost(
            tokens * channels * states * 8, tokens * channels * 12, tokens * channels * states
        ),
        name="scan",
    )(
        *in_hbm(x_in),
        edge,
        *in_hbm(
            dt_low, dt_weight, dt_bias[None], a_log, conv_weight, conv_bias[None], d_skip[None],
            b_and_c,
        ),
    )


def upper_half(step):
    return (lax.axis_index("seq") >> step) % 2 == 1


def link_kernel(step, *refs):
    total_ref, received_ref, alog_ref, prefix_ref = refs[:4] if step else (*refs[:3], None)
    total_out, prefix_out = refs[-2:]
    channels = alog_ref.shape[1]
    lanes = total_ref.shape[1] - channels
    steps = channels // lanes
    upper = upper_half(step)

    def sizes(ref):
        value = ref[:, channels:].astype(F32)
        return value[:steps] + value[steps : 2 * steps]

    def put_sizes(ref, value):
        high = value.astype(BF16).astype(F32)
        rest = jnp.zeros((ref.shape[0] - 2 * steps, lanes), F32)
        parts = [high, value - high] + ([rest] if rest.shape[0] else [])
        ref[:, channels:] = jnp.concatenate(parts, axis=0).astype(BF16)

    own, received = sizes(total_ref), sizes(received_ref)
    before = sizes(prefix_ref) if step else jnp.zeros_like(own)
    later = jnp.where(upper, own, received)
    put_sizes(total_out, own + received)
    put_sizes(prefix_out, before + jnp.where(upper, received, 0.0))
    for i in range(steps):
        at = slice(i * lanes, (i + 1) * lanes)
        rates = -jnp.exp(alog_ref[:, at]) * LOG2E
        mine, theirs = total_ref[:, at].astype(F32), received_ref[:, at].astype(F32)
        last, first = jnp.where(upper, mine, theirs), jnp.where(upper, theirs, mine)
        total_out[:, at] = (last + jnp.exp2(rates * later[i : i + 1]) * first).astype(BF16)
        if step:
            prefix = prefix_ref[:, at].astype(F32)
            further = prefix + jnp.exp2(rates * before[i : i + 1]) * theirs
        else:
            prefix, further = jnp.zeros_like(theirs), theirs
        prefix_out[:, at] = jnp.where(upper, further, prefix).astype(BF16)


def link(step, total, received, a_log, prefix):
    shape = jax.ShapeDtypeStruct(total.shape, BF16)
    args = [total, received, a_log] + ([prefix] if step else [])
    return pl.pallas_call(
        functools.partial(link_kernel, step),
        out_shape=(shape, shape),
        compiler_params=params(16),
        cost_estimate=cost(total.size * 2, total.size * 6),
        name="link",
    )(*args)


def finish_kernel(
    step, read_ref, cum_ref, z_ref, prefix_ref, sizes_ref, received_ref, alog_ref, bc_ref,
    out_ref, sum_ref, wide_ref, c_ref,
):
    tokens, lanes = z_ref.shape
    at, steps = pl.program_id(0), pl.num_programs(0)

    @pl.when(at == 0)
    def _():
        spread_states(bc_ref[1], c_ref)
        wide_ref[...] = sizes_ref[...].astype(F32)

    rates = -jnp.exp(alog_ref[...]) * LOG2E
    entering = prefix_ref[...].astype(F32)
    size = wide_ref[pl.ds(at, 1)] + wide_ref[pl.ds(steps + at, 1)]
    further = entering + jnp.exp2(rates * size) * received_ref[...].astype(F32)
    entering = jnp.where(upper_half(step), further, entering)

    def eight(g, carry):
        at = pl.multiple_of(g * 8, 8)
        cum8 = cum_ref[pl.ds(at, 8)]
        reads = []
        for i in range(8):
            kept = jnp.exp2(rates * cum8[i : i + 1]) * entering
            reads.append(state_sum(tiled_lanes(c_ref[at + i], lanes) * kept))
        sum_ref[pl.ds(at, 8)] = row_sums(reads)
        return carry

    lax.fori_loop(0, tokens // 8, eight, 0)
    z = z_ref[...].astype(F32)
    out_ref[...] = ((read_ref[...] + sum_ref[...]) * (z * jax.nn.sigmoid(z))).astype(BF16)


def finish(step, read, cum, z_gate, prefix, received, a_log, b_and_c):
    tokens, channels = z_gate.shape
    states = a_log.shape[0]
    lanes = math.gcd(512, channels)

    def cut(rows):
        return pl.BlockSpec((rows, lanes), lambda i: (0, i))

    return pl.pallas_call(
        functools.partial(finish_kernel, step),
        grid=(channels // lanes,),
        in_specs=[
            cut(tokens), cut(tokens), cut(tokens), cut(states),
            pl.BlockSpec((states, lanes), lambda i: (0, channels // lanes)), cut(states), cut(states),
            pl.BlockSpec(b_and_c.shape, lambda i: (0, 0, 0)),
        ],
        out_specs=cut(tokens),
        out_shape=jax.ShapeDtypeStruct((tokens, channels), BF16),
        scratch_shapes=[
            pltpu.VMEM((tokens, lanes), F32),
            pltpu.VMEM((states, lanes), F32),
            pltpu.VMEM((tokens, states, 128), F32),
        ],
        compiler_params=params(40),
        cost_estimate=cost(
            tokens * channels * states * 5, tokens * channels * 12, tokens * channels * states
        ),
        name="finish",
    )(*in_hbm(read, cum, z_gate), prefix, prefix, received, *in_hbm(a_log, b_and_c))


def swapped(value, by):
    count = lax.axis_size("seq")
    return lax.ppermute(value, "seq", [(i, i ^ by) for i in range(count)])


def turned(value, axis, by):
    count = lax.axis_size(axis)
    return lax.ppermute(value, axis, [(i, (i + by) % count) for i in range(count)])


def turned_within(value, copies, by):
    count = lax.axis_size("seq")
    return lax.ppermute(
        value, "seq", [(i, i // copies * copies + (i + by) % copies) for i in range(count)]
    )


def exchanged(value, copies):
    count = lax.axis_size("seq")
    groups = [list(range(m, count, copies)) for m in range(copies)]
    return lax.all_to_all(
        value, "seq", split_axis=0, concat_axis=0, tiled=True, axis_index_groups=groups
    )


def after(value, *others):
    return lax.optimization_barrier((value, others))[0]


def local(
    x_in,
    z_gate,
    dt_low,
    dt_weight,
    dt_bias,
    a_log,
    conv_weight,
    conv_bias,
    d_skip,
    b_and_c,
    hidden,
    router,
    expert_ids,
    w_gate,
    w_down,
):
    blocks = lax.axis_size("seq")
    feature_parts = lax.axis_size("exp")
    tokens, features = hidden.shape
    experts = router.shape[1]
    copies = blocks // experts
    pack = packing(features)
    ids = expert_ids.T

    edge = x_in[tokens - (conv_weight.shape[0] - 1) :]
    edge = lax.ppermute(edge, "seq", [(i, i + 1) for i in range(blocks - 1)])
    outgoing, logits = route(ids, hidden, router.T, 1, pack)
    outgoing = after(outgoing, edge)
    arrived = exchanged(outgoing.reshape((experts,) + outgoing.shape[2:]), copies)

    read, cum, ends = scan(
        x_in, edge, dt_low, dt_weight, dt_bias, a_log, conv_weight, conv_bias, d_skip, b_and_c
    )
    logits = [logits] + [turned(logits, "exp", d) for d in range(1, feature_parts)]
    arrived = after(arrived, ends, *logits)

    steps = blocks.bit_length() - 1
    total, prefix, received = ends, None, swapped(ends, 1)
    step = 0

    def advance(*marks):
        nonlocal total, prefix, received, step
        if step < steps - 1:
            total, prefix = link(step, total, after(received, *marks), a_log, prefix)
            step += 1
            received = swapped(total, 1 << step)
        return prefix

    rows = [unpack(arrived, features, pack)]
    for d in range(1, copies):
        rows.append(turned_within(rows[0], copies, d))
    gated = []
    for part in rows:
        if gated:
            part = after(part, gated[-1][0])
        own = gate(part, w_gate)
        if len(gated) in (0, copies - 1):
            own = after(own, advance(own, *rows[1:]), *(p for parts in gated for p in parts[1:]))
        gated.append([own] + [turned(own, "exp", d) for d in range(1, feature_parts)])
    made = []
    for parts in gated[1:] + gated[:1]:
        product = down(parts, w_down, BF16 if len(made) < copies - 1 else F32)
        if not made:
            product = after(product, advance(product))
        made.append(product)
    while step < steps - 1:
        advance()
    sums = [after(made[-1], received)]
    for d in range(1, copies):
        sums.append(turned_within(made[d - 1], copies, -d))
    packed = pack_sum(sums, experts, pack)
    back = exchanged(packed, copies)

    weights = blend_weights(ids, after(tuple(logits), packed), 1, pack)
    received = after(received, packed)
    mamba_out = finish(step, read, cum, z_gate, prefix, received, a_log, b_and_c)
    back = after(back, mamba_out)
    moe_out = combine(back, weights, tokens, features, pack)
    return mamba_out, moe_out


def solution(mesh):
    return jax.shard_map(
        local,
        mesh=mesh,
        in_specs=(
            P("seq", "exp"),
            P("seq", "exp"),
            P("seq", None),
            P(None, "exp"),
            P("exp"),
            P(None, "exp"),
            P(None, "exp"),
            P("exp"),
            P("exp"),
            P(None, None, "seq"),
            P("seq", "exp"),
            P("exp", None),
            P("seq", None),
            P("exp", "seq"),
            P("seq", "exp"),
        ),
        out_specs=(P("seq", "exp"), P("seq", "exp")),
        check_vma=False,
    )
```

```python
import functools
import math

import jax
import jax.numpy as jnp
from jax import lax
from jax.experimental import pallas as pl
from jax.experimental.pallas import tpu as pltpu
from jax.sharding import PartitionSpec as P

CAP = 18
MIB = 1 << 20
LOG2E = math.log2(math.e)
F32 = jnp.float32
BF16 = jnp.bfloat16


def params(limit):
    return pltpu.CompilerParams(vmem_limit_bytes=limit * MIB)


def cost(flops, moved, transcendentals=0):
    return pl.CostEstimate(
        flops=int(flops), bytes_accessed=int(moved), transcendentals=int(transcendentals)
    )


def in_hbm(*arrays):
    return [pltpu.with_memory_space_constraint(a, pltpu.HBM) for a in arrays]


def iota(shape, dim):
    return lax.broadcasted_iota(jnp.int32, shape, dim)


def dot(a, b):
    return jnp.dot(a, b, preferred_element_type=F32)


def dot_nt(a, b):
    return lax.dot_general(a, b, (((1,), (1,)), ((), ())), preferred_element_type=F32)


def packing(features):
    main = CAP // 16 * 16
    extra = CAP - main
    cuts = main // extra if extra and main % extra == 0 else 0
    if cuts and features % (cuts * 128) == 0:
        return main, extra, cuts, features // cuts
    return -(-CAP // 16) * 16, 0, 0, 0


def hits_and_slots(ids, experts):
    tokens = ids.shape[1]
    of = iota((experts, tokens), 0)
    hits = [(of == ids[k : k + 1]).astype(F32) for k in range(2)]
    before = (iota((tokens, tokens), 0) < iota((tokens, tokens), 1)).astype(BF16)
    earlier = dot((hits[0] + hits[1]).astype(BF16), before)
    slots = [jnp.sum(h * earlier, axis=0, keepdims=True).astype(jnp.int32) for h in hits]
    return hits, slots


def route_kernel(pack, ids_ref, hidden_ref, router_ref, out_ref, logits_ref):
    main, extra, cuts, width = pack
    experts, copies = out_ref.shape[:2]
    tokens, features = hidden_ref.shape
    ids = ids_ref[...]
    _, slots = hits_and_slots(ids, experts)
    hidden = hidden_ref[...]
    row = iota((experts * main, tokens), 0)
    picked = None
    for k in range(2):
        key = jnp.where(slots[k] < main, ids[k : k + 1] * main + slots[k], -1)
        hit = row == key
        picked = hit if picked is None else picked | hit
    packed = dot(picked.astype(BF16), hidden).astype(BF16)
    for e in range(experts):
        for m in range(copies):
            out_ref[e, m, :, :features] = packed[e * main : (e + 1) * main]
    if extra:
        picked = None
        for k in range(2):
            key = jnp.where(slots[k] >= main, ids[k : k + 1] * extra + slots[k] - main, -1)
            hit = row // cuts == key
            picked = hit if picked is None else picked | hit
        total = None
        for c in range(cuts):
            chosen = (picked & (row % cuts == c)).astype(BF16)
            part = dot(chosen, hidden[:, c * width : (c + 1) * width])
            total = part if total is None else total + part
        total = total.astype(BF16)
        for e in range(experts):
            for m in range(copies):
                out_ref[e, m, :, features:] = total[e * main : (e + 1) * main]
    logits_ref[...] = dot_nt(hidden, router_ref[...])


def route(ids, hidden, router, copies, pack):
    main, _, _, width = pack
    tokens, features = hidden.shape
    experts = router.shape[0]
    return pl.pallas_call(
        functools.partial(route_kernel, pack),
        out_shape=(
            jax.ShapeDtypeStruct((experts, copies, main, features + width), BF16),
            jax.ShapeDtypeStruct((tokens, experts), F32),
        ),
        compiler_params=params(40),
        cost_estimate=cost(2 * tokens * experts * main * features * 2, hidden.size * 8),
        name="route",
    )(*in_hbm(ids, hidden, router))


def weights_kernel(pack, copies, ids_ref, *refs):
    logits_refs, (main_ref, extra_ref, gates_ref) = refs[:-3], refs[-3:]
    main, extra, cuts, _ = pack
    tokens, experts = logits_refs[0].shape
    ids = ids_ref[...]
    hits, slots = hits_and_slots(ids, experts)
    eye = (iota((tokens, tokens), 0) == iota((tokens, tokens), 1)).astype(BF16)
    logits = logits_refs[0][...]
    for ref in logits_refs[1:]:
        logits = logits + ref[...]
    columns = [dot_nt(eye, h.astype(BF16)) for h in hits]
    picked = [jnp.sum(c * logits, axis=1, keepdims=True) for c in columns]
    expert = iota((tokens, experts), 1).astype(F32)
    total = experts * copies * main
    col = iota((tokens, total), 1)
    for k in range(2):
        gate = jax.nn.sigmoid(picked[k] - picked[1 - k])
        gates_ref[k] = jnp.broadcast_to(gate, gates_ref.shape[1:])
        named = jnp.sum(columns[k] * expert, axis=1, keepdims=True).astype(jnp.int32)
        wide = jnp.broadcast_to(slots[k].astype(F32), (8, tokens)).astype(BF16)
        slot = dot_nt(eye, wide)[:, :1].astype(jnp.int32)
        mine = col // (copies * main) == named
        main_ref[k] = (mine & (col % main == slot)).astype(BF16)
        if extra:
            place = (col % main) // cuts + main
            extra_ref[k] = (mine & (place == slot)).astype(BF16)
        else:
            extra_ref[k] = jnp.zeros(extra_ref.shape[1:], BF16)


def blend_weights(ids, logits, copies, pack):
    tokens, experts = logits[0].shape
    total = experts * copies * pack[0]
    return pl.pallas_call(
        functools.partial(weights_kernel, pack, copies),
        out_shape=(
            jax.ShapeDtypeStruct((2, tokens, total), BF16),
            jax.ShapeDtypeStruct((2, tokens, total), BF16),
            jax.ShapeDtypeStruct((2, tokens, 128), F32),
        ),
        compiler_params=params(40),
        cost_estimate=cost(2 * tokens * total * 16, tokens * total * 8),
        name="blend_weights",
    )(*in_hbm(ids), *logits)


ANYWHERE = pl.BlockSpec(memory_space=pl.ANY)
INSIDE = pl.BlockSpec(memory_space=pltpu.VMEM)
AHEAD = 6


def streamed(from_ref, to_ref, sems, dim, chunk, use, begin=None):
    count = from_ref.shape[dim] // chunk

    def copy(i):
        at = pl.ds(pl.multiple_of(i * chunk, chunk), chunk)
        part = (slice(None), at) if dim else (at, slice(None))
        return pltpu.make_async_copy(from_ref.at[part], to_ref.at[part], sems.at[i])

    for i in range(min(AHEAD, count)):
        copy(i).start()
    if begin is not None:
        begin()

    def step(i, carry):
        copy(i).wait()

        @pl.when(i + AHEAD < count)
        def _():
            copy(i + AHEAD).start()

        use(i)
        return carry

    lax.fori_loop(0, count, step, 0)


def gate_kernel(chunk, x_ref, w_ref, out_ref, held_ref, sems):
    def use(i):
        at = pl.ds(pl.multiple_of(i * chunk, chunk), chunk)
        out_ref[:, at] = dot(x_ref[...], held_ref[:, at]).astype(BF16)

    streamed(w_ref, held_ref, sems, 1, chunk, use)


def gate(x, w_gate):
    rows, features = x.shape
    amount = w_gate.shape[1]
    chunk = math.gcd(512, amount)
    return pl.pallas_call(
        functools.partial(gate_kernel, chunk),
        in_specs=[INSIDE, ANYWHERE],
        out_specs=INSIDE,
        out_shape=jax.ShapeDtypeStruct((rows, amount), BF16),
        scratch_shapes=[
            pltpu.VMEM(w_gate.shape, BF16),
            pltpu.SemaphoreType.DMA((amount // chunk,)),
        ],
        compiler_params=params(44),
        cost_estimate=cost(2 * rows * features * amount, features * amount * 2),
        name="gate",
    )(x, *in_hbm(w_gate))


def fill_acted(chunk, part_refs, acted_ref):
    def piece(i):
        at = pl.ds(pl.multiple_of(i * chunk, chunk), chunk)
        total = part_refs[0][:, at].astype(F32)
        for ref in part_refs[1:]:
            total = total + ref[:, at].astype(F32)
        acted_ref[:, at] = (total * jax.nn.sigmoid(total)).astype(BF16)

    pl.loop(0, acted_ref.shape[1] // chunk)(piece)


def down_kernel(chunk, *refs):
    part_refs, w_ref, out_ref, acted_ref, held_ref, sems = refs[:-5], *refs[-5:]

    def use(i):
        at = pl.ds(pl.multiple_of(i * chunk, chunk), chunk)
        out_ref[:, at] = dot(acted_ref[...], held_ref[:, at]).astype(out_ref.dtype)

    def begin():
        fill_acted(math.gcd(512, acted_ref.shape[1]), part_refs, acted_ref)

    streamed(w_ref, held_ref, sems, 1, chunk, use, begin)


def down(parts, w_down, dtype):
    rows, amount = parts[0].shape
    features = w_down.shape[1]
    chunk = math.gcd(256, features)
    return pl.pallas_call(
        functools.partial(down_kernel, chunk),
        in_specs=[INSIDE] * len(parts) + [ANYWHERE],
        out_specs=INSIDE,
        out_shape=jax.ShapeDtypeStruct((rows, features), dtype),
        scratch_shapes=[
            pltpu.VMEM((rows, amount), BF16),
            pltpu.VMEM(w_down.shape, BF16),
            pltpu.SemaphoreType.DMA((features // chunk,)),
        ],
        compiler_params=params(48),
        cost_estimate=cost(2 * rows * features * amount, features * amount * 2),
        name="down",
    )(*parts, *in_hbm(w_down))


def unpack_kernel(pack, arrived_ref, out_ref):
    main, extra, cuts, width = pack
    sources = arrived_ref.shape[0]
    features = out_ref.shape[1]
    out_ref[: sources * main] = arrived_ref[:, :, :features].reshape(sources * main, features)
    if extra:
        folded = arrived_ref[:, :, features:].reshape(sources * main, width)
        shape = (sources * extra, sources * main)
        for c in range(cuts):
            pick = (iota(shape, 1) == iota(shape, 0) * cuts + c).astype(BF16)
            out_ref[sources * main :, c * width : (c + 1) * width] = dot(pick, folded).astype(BF16)


def unpack(arrived, features, pack):
    main, extra, _, _ = pack
    rows = arrived.shape[0] * (main + extra)
    return pl.pallas_call(
        functools.partial(unpack_kernel, pack),
        out_shape=jax.ShapeDtypeStruct((rows, features), BF16),
        compiler_params=params(24),
        cost_estimate=cost(arrived.size * 16, arrived.size * 4),
        name="unpack",
    )(arrived)


def pack_kernel(pack, *refs):
    main, extra, cuts, width = pack
    part_refs, out_ref = refs[:-1], refs[-1]
    sources = out_ref.shape[0]
    features = part_refs[0].shape[1]
    first = sources * main

    def total(rows, columns):
        value = part_refs[0][rows, columns].astype(F32)
        for ref in part_refs[1:]:
            value = value + ref[rows, columns].astype(F32)
        return value.astype(BF16)

    made = total(slice(0, first), slice(0, features))
    out_ref[:, :, :features] = made.reshape(sources, main, features)
    if extra:
        shape = (sources * main, sources * extra)
        folded = None
        for c in range(cuts):
            piece = total(slice(first, None), slice(c * width, (c + 1) * width))
            pick = (iota(shape, 0) == iota(shape, 1) * cuts + c).astype(BF16)
            part = dot(pick, piece)
            folded = part if folded is None else folded + part
        out_ref[:, :, features:] = folded.astype(BF16).reshape(sources, main, width)


def pack_sum(parts, sources, pack):
    main, _, _, width = pack
    features = parts[0].shape[1]
    return pl.pallas_call(
        functools.partial(pack_kernel, pack),
        out_shape=jax.ShapeDtypeStruct((sources, main, features + width), BF16),
        compiler_params=params(24),
        cost_estimate=cost(parts[0].size * 16, parts[0].size * 8),
        name="pack_sum",
    )(*parts)


def combine_kernel(pack, back_ref, main_ref, extra_ref, gates_ref, out_ref):
    main, extra, cuts, width = pack
    sources = back_ref.shape[0]
    tokens, features = out_ref.shape
    back = back_ref[:, :, :features].reshape(sources * main, features)
    folded = back_ref[:, :, features:].reshape(sources * main, width) if extra else None
    total = None
    for k in range(2):
        rows = dot(main_ref[k], back)
        if extra:
            chosen = extra_ref[k]
            at = iota(chosen.shape, 1) % cuts
            pieces = [
                dot(jnp.where(at == c, chosen, jnp.zeros_like(chosen)), folded) for c in range(cuts)
            ]
            rows = rows + jnp.concatenate(pieces, axis=1)
        weighed = rows * gates_ref[k][:, :1]
        total = weighed if total is None else total + weighed
    out_ref[...] = total.astype(BF16)


def combine(back, weights, tokens, features, pack):
    return pl.pallas_call(
        functools.partial(combine_kernel, pack),
        out_shape=jax.ShapeDtypeStruct((tokens, features), BF16),
        compiler_params=params(40),
        cost_estimate=cost(4 * tokens * back.size, back.size * 2),
        name="combine",
    )(back, *weights)


def spread_states(values, spread_ref):
    for t in range(spread_ref.shape[0]):
        spread_ref[t] = jnp.broadcast_to(values[:, t : t + 1], spread_ref.shape[1:])


def row_sums(parts):
    place = iota(parts[0].shape, 0)
    for stride in (4, 2, 1):
        low = place & stride == 0
        half = len(parts) // 2
        joined = []
        for a, b in zip(parts[:half], parts[half:]):
            kept = jnp.where(low, a, b)
            moved = jnp.where(low, b, a)
            if stride == 4:
                other = pltpu.roll(moved, 4, 0)
            else:
                other = jnp.where(low, pltpu.roll(moved, 8 - stride, 0), pltpu.roll(moved, stride, 0))
            joined.append(kept + other)
        parts = joined
    return parts[0]


def state_sum(value):
    total = value[:8]
    for at in range(8, value.shape[0], 8):
        total = total + value[at : at + 8]
    return total


def tiled_lanes(value, lanes):
    return jnp.concatenate([value] * (lanes // value.shape[1]), axis=1)


def scan_kernel(
    x_ref, edge_ref, low_ref, dtw_ref, dtb_ref, alog_ref, cw_ref, cb_ref, skip_ref, bc_ref,
    read_ref, cum_ref, ends_ref, padded, delta_ref, fed_ref, totals_ref, b_ref, c_ref,
):
    tokens, lanes = x_ref.shape
    taps = cw_ref.shape[0]
    states = alog_ref.shape[0]

    @pl.when(pl.program_id(0) == 0)
    def _():
        spread_states(bc_ref[0], b_ref)
        spread_states(bc_ref[1], c_ref)
        totals_ref[...] = jnp.zeros_like(totals_ref)

    padded[8:] = x_ref[...].astype(F32)
    padded[8 - (taps - 1) : 8] = edge_ref[...].astype(F32)
    conv = jnp.broadcast_to(cb_ref[...], (tokens, lanes))
    for k in range(taps):
        at = 8 - (taps - 1) + k
        conv = conv + cw_ref[k : k + 1] * padded[at : at + tokens]
    act = conv * jax.nn.sigmoid(conv)
    raw = dot(low_ref[...], dtw_ref[...]) + dtb_ref[...]
    delta = jnp.maximum(raw, 0.0) + jnp.log1p(jnp.exp(-jnp.abs(raw)))
    delta_ref[...] = delta
    fed_ref[...] = delta * act
    read_ref[...] = skip_ref[...] * act
    rates = -jnp.exp(alog_ref[...]) * LOG2E

    def eight(g, carry):
        state, running = carry
        at = pl.multiple_of(g * 8, 8)
        delta8 = delta_ref[pl.ds(at, 8)]
        fed8 = fed_ref[pl.ds(at, 8)]
        reads, sums = [], []
        for i in range(8):
            step = delta8[i : i + 1]
            running = running + step
            factor = jnp.exp2(rates * step)
            state = factor * state + tiled_lanes(b_ref[at + i], lanes) * fed8[i : i + 1]
            reads.append(state_sum(tiled_lanes(c_ref[at + i], lanes) * state))
            sums.append(running)
        read_ref[pl.ds(at, 8)] += row_sums(reads)
        cum_ref[pl.ds(at, 8)] = jnp.concatenate(sums, axis=0)
        return state, running

    state, running = lax.fori_loop(
        0, tokens // 8, eight, (jnp.zeros((states, lanes), F32), jnp.zeros((1, lanes), F32))
    )
    step, steps = pl.program_id(0), pl.num_programs(0)
    ends_ref[:, pl.ds(pl.multiple_of(step * lanes, lanes), lanes)] = state.astype(BF16)
    high = running.astype(BF16).astype(F32)
    totals_ref[pl.ds(step, 1)] = high
    totals_ref[pl.ds(steps + step, 1)] = running - high

    @pl.when(step == steps - 1)
    def _():
        ends_ref[:, ends_ref.shape[1] - lanes :] = totals_ref[...].astype(BF16)


def scan(x_in, edge, dt_low, dt_weight, dt_bias, a_log, conv_weight, conv_bias, d_skip, b_and_c):
    tokens, channels = x_in.shape
    states = a_log.shape[0]
    lanes = math.gcd(512, channels)

    def cut(rows):
        return pl.BlockSpec((rows, lanes), lambda i: (0, i))

    def whole(a):
        zeros = (0,) * a.ndim
        return pl.BlockSpec(a.shape, lambda i: zeros)

    return pl.pallas_call(
        scan_kernel,
        grid=(channels // lanes,),
        in_specs=[
            cut(tokens), cut(edge.shape[0]), whole(dt_low), cut(dt_weight.shape[0]), cut(1),
            cut(states), cut(conv_weight.shape[0]), cut(1), cut(1), whole(b_and_c),
        ],
        out_specs=(
            cut(tokens),
            cut(tokens),
            pl.BlockSpec((states, channels + lanes), lambda i: (0, 0)),
        ),
        out_shape=(
            pltpu.HBM((tokens, channels), F32),
            pltpu.HBM((tokens, channels), F32),
            jax.ShapeDtypeStruct((states, channels + lanes), BF16),
        ),
        scratch_shapes=[
            pltpu.VMEM((tokens + 8, lanes), F32),
            pltpu.VMEM((tokens, lanes), F32),
            pltpu.VMEM((tokens, lanes), F32),
            pltpu.VMEM((states, lanes), F32),
            pltpu.VMEM((tokens, states, 128), F32),
            pltpu.VMEM((tokens, states, 128), F32),
        ],
        compiler_params=params(40),
        cost_estimate=cost(
            tokens * channels * states * 8, tokens * channels * 12, tokens * channels * states
        ),
        name="scan",
    )(
        *in_hbm(x_in),
        edge,
        *in_hbm(
            dt_low, dt_weight, dt_bias[None], a_log, conv_weight, conv_bias[None], d_skip[None],
            b_and_c,
        ),
    )


def upper_half(step):
    return (lax.axis_index("seq") >> step) % 2 == 1


def link_kernel(step, *refs):
    total_ref, received_ref, alog_ref, prefix_ref = refs[:4] if step else (*refs[:3], None)
    total_out, prefix_out = refs[-2:]
    channels = alog_ref.shape[1]
    lanes = total_ref.shape[1] - channels
    steps = channels // lanes
    upper = upper_half(step)

    def sizes(ref):
        value = ref[:, channels:].astype(F32)
        return value[:steps] + value[steps : 2 * steps]

    def put_sizes(ref, value):
        high = value.astype(BF16).astype(F32)
        rest = jnp.zeros((ref.shape[0] - 2 * steps, lanes), F32)
        parts = [high, value - high] + ([rest] if rest.shape[0] else [])
        ref[:, channels:] = jnp.concatenate(parts, axis=0).astype(BF16)

    own, received = sizes(total_ref), sizes(received_ref)
    before = sizes(prefix_ref) if step else jnp.zeros_like(own)
    later = jnp.where(upper, own, received)
    put_sizes(total_out, own + received)
    put_sizes(prefix_out, before + jnp.where(upper, received, 0.0))
    for i in range(steps):
        at = slice(i * lanes, (i + 1) * lanes)
        rates = -jnp.exp(alog_ref[:, at]) * LOG2E
        mine, theirs = total_ref[:, at].astype(F32), received_ref[:, at].astype(F32)
        last, first = jnp.where(upper, mine, theirs), jnp.where(upper, theirs, mine)
        total_out[:, at] = (last + jnp.exp2(rates * later[i : i + 1]) * first).astype(BF16)
        if step:
            prefix = prefix_ref[:, at].astype(F32)
            further = prefix + jnp.exp2(rates * before[i : i + 1]) * theirs
        else:
            prefix, further = jnp.zeros_like(theirs), theirs
        prefix_out[:, at] = jnp.where(upper, further, prefix).astype(BF16)


def link(step, total, received, a_log, prefix):
    shape = jax.ShapeDtypeStruct(total.shape, BF16)
    args = [total, received, a_log] + ([prefix] if step else [])
    return pl.pallas_call(
        functools.partial(link_kernel, step),
        out_shape=(shape, shape),
        compiler_params=params(16),
        cost_estimate=cost(total.size * 2, total.size * 6),
        name="link",
    )(*args)


def finish_kernel(
    step, read_ref, cum_ref, z_ref, prefix_ref, sizes_ref, received_ref, alog_ref, bc_ref,
    out_ref, sum_ref, wide_ref, c_ref,
):
    tokens, lanes = z_ref.shape
    at, steps = pl.program_id(0), pl.num_programs(0)

    @pl.when(at == 0)
    def _():
        spread_states(bc_ref[1], c_ref)
        wide_ref[...] = sizes_ref[...].astype(F32)

    rates = -jnp.exp(alog_ref[...]) * LOG2E
    entering = prefix_ref[...].astype(F32)
    size = wide_ref[pl.ds(at, 1)] + wide_ref[pl.ds(steps + at, 1)]
    further = entering + jnp.exp2(rates * size) * received_ref[...].astype(F32)
    entering = jnp.where(upper_half(step), further, entering)

    def eight(g, carry):
        at = pl.multiple_of(g * 8, 8)
        cum8 = cum_ref[pl.ds(at, 8)]
        reads = []
        for i in range(8):
            kept = jnp.exp2(rates * cum8[i : i + 1]) * entering
            reads.append(state_sum(tiled_lanes(c_ref[at + i], lanes) * kept))
        sum_ref[pl.ds(at, 8)] = row_sums(reads)
        return carry

    lax.fori_loop(0, tokens // 8, eight, 0)
    z = z_ref[...].astype(F32)
    out_ref[...] = ((read_ref[...] + sum_ref[...]) * (z * jax.nn.sigmoid(z))).astype(BF16)


def finish(step, read, cum, z_gate, prefix, received, a_log, b_and_c):
    tokens, channels = z_gate.shape
    states = a_log.shape[0]
    lanes = math.gcd(512, channels)

    def cut(rows):
        return pl.BlockSpec((rows, lanes), lambda i: (0, i))

    return pl.pallas_call(
        functools.partial(finish_kernel, step),
        grid=(channels // lanes,),
        in_specs=[
            cut(tokens), cut(tokens), cut(tokens), cut(states),
            pl.BlockSpec((states, lanes), lambda i: (0, channels // lanes)), cut(states), cut(states),
            pl.BlockSpec(b_and_c.shape, lambda i: (0, 0, 0)),
        ],
        out_specs=cut(tokens),
        out_shape=jax.ShapeDtypeStruct((tokens, channels), BF16),
        scratch_shapes=[
            pltpu.VMEM((tokens, lanes), F32),
            pltpu.VMEM((states, lanes), F32),
            pltpu.VMEM((tokens, states, 128), F32),
        ],
        compiler_params=params(40),
        cost_estimate=cost(
            tokens * channels * states * 5, tokens * channels * 12, tokens * channels * states
        ),
        name="finish",
    )(*in_hbm(read, cum, z_gate), prefix, prefix, received, *in_hbm(a_log, b_and_c))


def swapped(value, by):
    count = lax.axis_size("seq")
    return lax.ppermute(value, "seq", [(i, i ^ by) for i in range(count)])


def turned(value, axis, by):
    count = lax.axis_size(axis)
    return lax.ppermute(value, axis, [(i, (i + by) % count) for i in range(count)])


def turned_within(value, copies, by):
    count = lax.axis_size("seq")
    return lax.ppermute(
        value, "seq", [(i, i // copies * copies + (i + by) % copies) for i in range(count)]
    )


def exchanged(value, copies):
    count = lax.axis_size("seq")
    groups = [list(range(m, count, copies)) for m in range(copies)]
    return lax.all_to_all(
        value, "seq", split_axis=0, concat_axis=0, tiled=True, axis_index_groups=groups
    )


def after(value, *others):
    return lax.optimization_barrier((value, others))[0]


def local(
    x_in,
    z_gate,
    dt_low,
    dt_weight,
    dt_bias,
    a_log,
    conv_weight,
    conv_bias,
    d_skip,
    b_and_c,
    hidden,
    router,
    expert_ids,
    w_gate,
    w_down,
):
    blocks = lax.axis_size("seq")
    feature_parts = lax.axis_size("exp")
    tokens, features = hidden.shape
    experts = router.shape[1]
    copies = blocks // experts
    pack = packing(features)
    ids = expert_ids.T

    edge = x_in[tokens - (conv_weight.shape[0] - 1) :]
    edge = lax.ppermute(edge, "seq", [(i, i + 1) for i in range(blocks - 1)])
    outgoing, logits = route(ids, hidden, router.T, 1, pack)
    outgoing = after(outgoing, edge)
    arrived = exchanged(outgoing.reshape((experts,) + outgoing.shape[2:]), copies)

    read, cum, ends = scan(
        x_in, edge, dt_low, dt_weight, dt_bias, a_log, conv_weight, conv_bias, d_skip, b_and_c
    )
    logits = [logits] + [turned(logits, "exp", d) for d in range(1, feature_parts)]
    arrived = after(arrived, ends, *logits)

    steps = blocks.bit_length() - 1
    total, prefix, received, step = ends, None, None, 0

    def advance(*marks):
        nonlocal total, prefix, received, step
        if step < steps - 1:
            total, prefix = link(step, total, after(received, *marks), a_log, prefix)
            step += 1
            received = swapped(total, 1 << step)
        return prefix

    rows = [unpack(arrived, features, pack)]
    for d in range(1, copies):
        rows.append(turned_within(rows[0], copies, d))
    gated = []
    for part in rows:
        if gated:
            part = after(part, gated[-1][0])
        own = gate(part, w_gate)
        if not gated:
            own, received = after((own, ends), *rows[1:])
            received = swapped(received, 1)
        if len(gated) == copies - 1:
            own = after(own, advance(own), *(p for parts in gated for p in parts[1:]))
        gated.append([own] + [turned(own, "exp", d) for d in range(1, feature_parts)])
    made = []
    for parts in gated[1:] + gated[:1]:
        product = down(parts, w_down, BF16 if len(made) < copies - 1 else F32)
        if not made:
            product = after(product, advance(product))
        made.append(product)
    advance(made[-1])
    while step < steps - 1:
        advance()
    sums = made[-1:]
    for d in range(1, copies):
        sums.append(turned_within(made[d - 1], copies, -d))
    packed = after(pack_sum(sums, experts, pack), received)
    back = exchanged(packed, copies)

    weights = blend_weights(ids, after(tuple(logits), packed), 1, pack)
    received = after(received, packed)
    mamba_out = finish(step, read, cum, z_gate, prefix, received, a_log, b_and_c)
    back = after(back, mamba_out)
    moe_out = combine(back, weights, tokens, features, pack)
    return mamba_out, moe_out


def solution(mesh):
    return jax.shard_map(
        local,
        mesh=mesh,
        in_specs=(
            P("seq", "exp"),
            P("seq", "exp"),
            P("seq", None),
            P(None, "exp"),
            P("exp"),
            P(None, "exp"),
            P(None, "exp"),
            P("exp"),
            P("exp"),
            P(None, None, "seq"),
            P("seq", "exp"),
            P("exp", None),
            P("seq", None),
            P("exp", "seq"),
            P("seq", "exp"),
        ),
        out_specs=(P("seq", "exp"), P("seq", "exp")),
        check_vma=False,
    )
```

```python
import functools
import math

import jax
import jax.numpy as jnp
from jax import lax
from jax.experimental import pallas as pl
from jax.experimental.pallas import tpu as pltpu
from jax.sharding import PartitionSpec as P

CAP = 18
MIB = 1 << 20
LOG2E = math.log2(math.e)
F32 = jnp.float32
BF16 = jnp.bfloat16


def params(limit):
    return pltpu.CompilerParams(vmem_limit_bytes=limit * MIB)


def cost(flops, moved, transcendentals=0):
    return pl.CostEstimate(
        flops=int(flops), bytes_accessed=int(moved), transcendentals=int(transcendentals)
    )


def in_hbm(*arrays):
    return [pltpu.with_memory_space_constraint(a, pltpu.HBM) for a in arrays]


def iota(shape, dim):
    return lax.broadcasted_iota(jnp.int32, shape, dim)


def dot(a, b):
    return jnp.dot(a, b, preferred_element_type=F32)


def dot_nt(a, b):
    return lax.dot_general(a, b, (((1,), (1,)), ((), ())), preferred_element_type=F32)


def packing(features):
    main = CAP // 16 * 16
    extra = CAP - main
    cuts = main // extra if extra and main % extra == 0 else 0
    if cuts and features % (cuts * 128) == 0:
        return main, extra, cuts, features // cuts
    return -(-CAP // 16) * 16, 0, 0, 0


def hits_and_slots(ids, experts):
    tokens = ids.shape[1]
    of = iota((experts, tokens), 0)
    hits = [(of == ids[k : k + 1]).astype(F32) for k in range(2)]
    before = (iota((tokens, tokens), 0) < iota((tokens, tokens), 1)).astype(BF16)
    earlier = dot((hits[0] + hits[1]).astype(BF16), before)
    slots = [jnp.sum(h * earlier, axis=0, keepdims=True).astype(jnp.int32) for h in hits]
    return hits, slots


def route_kernel(pack, ids_ref, hidden_ref, router_ref, out_ref, logits_ref):
    main, extra, cuts, width = pack
    experts, copies = out_ref.shape[:2]
    tokens, features = hidden_ref.shape
    ids = ids_ref[...]
    _, slots = hits_and_slots(ids, experts)
    hidden = hidden_ref[...]
    row = iota((experts * main, tokens), 0)
    picked = None
    for k in range(2):
        key = jnp.where(slots[k] < main, ids[k : k + 1] * main + slots[k], -1)
        hit = row == key
        picked = hit if picked is None else picked | hit
    packed = dot(picked.astype(BF16), hidden).astype(BF16)
    for e in range(experts):
        for m in range(copies):
            out_ref[e, m, :, :features] = packed[e * main : (e + 1) * main]
    if extra:
        picked = None
        for k in range(2):
            key = jnp.where(slots[k] >= main, ids[k : k + 1] * extra + slots[k] - main, -1)
            hit = row // cuts == key
            picked = hit if picked is None else picked | hit
        total = None
        for c in range(cuts):
            chosen = (picked & (row % cuts == c)).astype(BF16)
            part = dot(chosen, hidden[:, c * width : (c + 1) * width])
            total = part if total is None else total + part
        total = total.astype(BF16)
        for e in range(experts):
            for m in range(copies):
                out_ref[e, m, :, features:] = total[e * main : (e + 1) * main]
    logits_ref[...] = dot_nt(hidden, router_ref[...])


def route(ids, hidden, router, copies, pack):
    main, _, _, width = pack
    tokens, features = hidden.shape
    experts = router.shape[0]
    return pl.pallas_call(
        functools.partial(route_kernel, pack),
        out_shape=(
            jax.ShapeDtypeStruct((experts, copies, main, features + width), BF16),
            jax.ShapeDtypeStruct((tokens, experts), F32),
        ),
        compiler_params=params(40),
        cost_estimate=cost(2 * tokens * experts * main * features * 2, hidden.size * 8),
        name="route",
    )(*in_hbm(ids, hidden, router))


def weights_kernel(pack, copies, ids_ref, *refs):
    logits_refs, (main_ref, extra_ref, gates_ref) = refs[:-3], refs[-3:]
    main, extra, cuts, _ = pack
    tokens, experts = logits_refs[0].shape
    ids = ids_ref[...]
    hits, slots = hits_and_slots(ids, experts)
    eye = (iota((tokens, tokens), 0) == iota((tokens, tokens), 1)).astype(BF16)
    logits = logits_refs[0][...]
    for ref in logits_refs[1:]:
        logits = logits + ref[...]
    columns = [dot_nt(eye, h.astype(BF16)) for h in hits]
    picked = [jnp.sum(c * logits, axis=1, keepdims=True) for c in columns]
    expert = iota((tokens, experts), 1).astype(F32)
    total = experts * copies * main
    col = iota((tokens, total), 1)
    for k in range(2):
        gate = jax.nn.sigmoid(picked[k] - picked[1 - k])
        gates_ref[k] = jnp.broadcast_to(gate, gates_ref.shape[1:])
        named = jnp.sum(columns[k] * expert, axis=1, keepdims=True).astype(jnp.int32)
        wide = jnp.broadcast_to(slots[k].astype(F32), (8, tokens)).astype(BF16)
        slot = dot_nt(eye, wide)[:, :1].astype(jnp.int32)
        mine = col // (copies * main) == named
        main_ref[k] = (mine & (col % main == slot)).astype(BF16)
        if extra:
            place = (col % main) // cuts + main
            extra_ref[k] = (mine & (place == slot)).astype(BF16)
        else:
            extra_ref[k] = jnp.zeros(extra_ref.shape[1:], BF16)


def blend_weights(ids, logits, copies, pack):
    tokens, experts = logits[0].shape
    total = experts * copies * pack[0]
    return pl.pallas_call(
        functools.partial(weights_kernel, pack, copies),
        out_shape=(
            jax.ShapeDtypeStruct((2, tokens, total), BF16),
            jax.ShapeDtypeStruct((2, tokens, total), BF16),
            jax.ShapeDtypeStruct((2, tokens, 128), F32),
        ),
        compiler_params=params(40),
        cost_estimate=cost(2 * tokens * total * 16, tokens * total * 8),
        name="blend_weights",
    )(*in_hbm(ids), *logits)


ANYWHERE = pl.BlockSpec(memory_space=pl.ANY)
INSIDE = pl.BlockSpec(memory_space=pltpu.VMEM)
AHEAD = 6


def streamed(from_ref, to_ref, sems, dim, chunk, use, begin=None):
    count = from_ref.shape[dim] // chunk

    def copy(i):
        at = pl.ds(pl.multiple_of(i * chunk, chunk), chunk)
        part = (slice(None), at) if dim else (at, slice(None))
        return pltpu.make_async_copy(from_ref.at[part], to_ref.at[part], sems.at[i])

    for i in range(min(AHEAD, count)):
        copy(i).start()
    if begin is not None:
        begin()

    def step(i, carry):
        copy(i).wait()

        @pl.when(i + AHEAD < count)
        def _():
            copy(i + AHEAD).start()

        use(i)
        return carry

    lax.fori_loop(0, count, step, 0)


def gate_kernel(chunk, x_ref, w_ref, out_ref, held_ref, sems):
    def use(i):
        at = pl.ds(pl.multiple_of(i * chunk, chunk), chunk)
        out_ref[:, at] = dot(x_ref[...], held_ref[:, at]).astype(BF16)

    streamed(w_ref, held_ref, sems, 1, chunk, use)


def gate(x, w_gate):
    rows, features = x.shape
    amount = w_gate.shape[1]
    chunk = math.gcd(512, amount)
    return pl.pallas_call(
        functools.partial(gate_kernel, chunk),
        in_specs=[INSIDE, ANYWHERE],
        out_specs=INSIDE,
        out_shape=jax.ShapeDtypeStruct((rows, amount), BF16),
        scratch_shapes=[
            pltpu.VMEM(w_gate.shape, BF16),
            pltpu.SemaphoreType.DMA((amount // chunk,)),
        ],
        compiler_params=params(44),
        cost_estimate=cost(2 * rows * features * amount, features * amount * 2),
        name="gate",
    )(x, *in_hbm(w_gate))


def fill_acted(chunk, part_refs, acted_ref):
    def piece(i):
        at = pl.ds(pl.multiple_of(i * chunk, chunk), chunk)
        total = part_refs[0][:, at].astype(F32)
        for ref in part_refs[1:]:
            total = total + ref[:, at].astype(F32)
        acted_ref[:, at] = (total * jax.nn.sigmoid(total)).astype(BF16)

    pl.loop(0, acted_ref.shape[1] // chunk)(piece)


def down_kernel(chunk, *refs):
    part_refs, w_ref, out_ref, acted_ref, held_ref, sems = refs[:-5], *refs[-5:]

    def use(i):
        at = pl.ds(pl.multiple_of(i * chunk, chunk), chunk)
        out_ref[:, at] = dot(acted_ref[...], held_ref[:, at]).astype(out_ref.dtype)

    def begin():
        fill_acted(math.gcd(512, acted_ref.shape[1]), part_refs, acted_ref)

    streamed(w_ref, held_ref, sems, 1, chunk, use, begin)


def down(parts, w_down, dtype):
    rows, amount = parts[0].shape
    features = w_down.shape[1]
    chunk = math.gcd(256, features)
    return pl.pallas_call(
        functools.partial(down_kernel, chunk),
        in_specs=[INSIDE] * len(parts) + [ANYWHERE],
        out_specs=INSIDE,
        out_shape=jax.ShapeDtypeStruct((rows, features), dtype),
        scratch_shapes=[
            pltpu.VMEM((rows, amount), BF16),
            pltpu.VMEM(w_down.shape, BF16),
            pltpu.SemaphoreType.DMA((features // chunk,)),
        ],
        compiler_params=params(48),
        cost_estimate=cost(2 * rows * features * amount, features * amount * 2),
        name="down",
    )(*parts, *in_hbm(w_down))


def unpack_kernel(pack, arrived_ref, out_ref):
    main, extra, cuts, width = pack
    sources = arrived_ref.shape[0]
    features = out_ref.shape[1]
    out_ref[: sources * main] = arrived_ref[:, :, :features].reshape(sources * main, features)
    if extra:
        folded = arrived_ref[:, :, features:].reshape(sources * main, width)
        shape = (sources * extra, sources * main)
        for c in range(cuts):
            pick = (iota(shape, 1) == iota(shape, 0) * cuts + c).astype(BF16)
            out_ref[sources * main :, c * width : (c + 1) * width] = dot(pick, folded).astype(BF16)


def unpack(arrived, features, pack):
    main, extra, _, _ = pack
    rows = arrived.shape[0] * (main + extra)
    return pl.pallas_call(
        functools.partial(unpack_kernel, pack),
        out_shape=jax.ShapeDtypeStruct((rows, features), BF16),
        compiler_params=params(24),
        cost_estimate=cost(arrived.size * 16, arrived.size * 4),
        name="unpack",
    )(arrived)


def pack_kernel(pack, *refs):
    main, extra, cuts, width = pack
    part_refs, out_ref = refs[:-1], refs[-1]
    sources = out_ref.shape[0]
    features = part_refs[0].shape[1]
    first = sources * main

    def total(rows, columns):
        value = part_refs[0][rows, columns].astype(F32)
        for ref in part_refs[1:]:
            value = value + ref[rows, columns].astype(F32)
        return value.astype(BF16)

    made = total(slice(0, first), slice(0, features))
    out_ref[:, :, :features] = made.reshape(sources, main, features)
    if extra:
        shape = (sources * main, sources * extra)
        folded = None
        for c in range(cuts):
            piece = total(slice(first, None), slice(c * width, (c + 1) * width))
            pick = (iota(shape, 0) == iota(shape, 1) * cuts + c).astype(BF16)
            part = dot(pick, piece)
            folded = part if folded is None else folded + part
        out_ref[:, :, features:] = folded.astype(BF16).reshape(sources, main, width)


def pack_sum(parts, sources, pack):
    main, _, _, width = pack
    features = parts[0].shape[1]
    return pl.pallas_call(
        functools.partial(pack_kernel, pack),
        out_shape=jax.ShapeDtypeStruct((sources, main, features + width), BF16),
        compiler_params=params(24),
        cost_estimate=cost(parts[0].size * 16, parts[0].size * 8),
        name="pack_sum",
    )(*parts)


def combine_kernel(pack, back_ref, main_ref, extra_ref, gates_ref, out_ref):
    main, extra, cuts, width = pack
    sources = back_ref.shape[0]
    tokens, features = out_ref.shape
    back = back_ref[:, :, :features].reshape(sources * main, features)
    folded = back_ref[:, :, features:].reshape(sources * main, width) if extra else None
    total = None
    for k in range(2):
        rows = dot(main_ref[k], back)
        if extra:
            chosen = extra_ref[k]
            at = iota(chosen.shape, 1) % cuts
            pieces = [
                dot(jnp.where(at == c, chosen, jnp.zeros_like(chosen)), folded) for c in range(cuts)
            ]
            rows = rows + jnp.concatenate(pieces, axis=1)
        weighed = rows * gates_ref[k][:, :1]
        total = weighed if total is None else total + weighed
    out_ref[...] = total.astype(BF16)


def combine(back, weights, tokens, features, pack):
    return pl.pallas_call(
        functools.partial(combine_kernel, pack),
        out_shape=jax.ShapeDtypeStruct((tokens, features), BF16),
        compiler_params=params(40),
        cost_estimate=cost(4 * tokens * back.size, back.size * 2),
        name="combine",
    )(back, *weights)


def spread_states(values, spread_ref):
    for t in range(spread_ref.shape[0]):
        spread_ref[t] = jnp.broadcast_to(values[:, t : t + 1], spread_ref.shape[1:])


def row_sums(parts):
    place = iota(parts[0].shape, 0)
    for stride in (4, 2, 1):
        low = place & stride == 0
        half = len(parts) // 2
        joined = []
        for a, b in zip(parts[:half], parts[half:]):
            kept = jnp.where(low, a, b)
            moved = jnp.where(low, b, a)
            if stride == 4:
                other = pltpu.roll(moved, 4, 0)
            else:
                other = jnp.where(low, pltpu.roll(moved, 8 - stride, 0), pltpu.roll(moved, stride, 0))
            joined.append(kept + other)
        parts = joined
    return parts[0]


def state_sum(value):
    total = value[:8]
    for at in range(8, value.shape[0], 8):
        total = total + value[at : at + 8]
    return total


def tiled_lanes(value, lanes):
    return jnp.concatenate([value] * (lanes // value.shape[1]), axis=1)


def scan_kernel(
    x_ref, edge_ref, low_ref, dtw_ref, dtb_ref, alog_ref, cw_ref, cb_ref, skip_ref, bc_ref,
    read_ref, cum_ref, ends_ref, padded, delta_ref, fed_ref, totals_ref, b_ref, c_ref,
):
    tokens, lanes = x_ref.shape
    taps = cw_ref.shape[0]
    states = alog_ref.shape[0]

    @pl.when(pl.program_id(0) == 0)
    def _():
        spread_states(bc_ref[0], b_ref)
        spread_states(bc_ref[1], c_ref)
        totals_ref[...] = jnp.zeros_like(totals_ref)

    padded[8:] = x_ref[...].astype(F32)
    padded[8 - (taps - 1) : 8] = edge_ref[...].astype(F32)
    conv = jnp.broadcast_to(cb_ref[...], (tokens, lanes))
    for k in range(taps):
        at = 8 - (taps - 1) + k
        conv = conv + cw_ref[k : k + 1] * padded[at : at + tokens]
    act = conv * jax.nn.sigmoid(conv)
    raw = dot(low_ref[...], dtw_ref[...]) + dtb_ref[...]
    delta = jnp.maximum(raw, 0.0) + jnp.log1p(jnp.exp(-jnp.abs(raw)))
    delta_ref[...] = delta
    fed_ref[...] = delta * act
    read_ref[...] = skip_ref[...] * act
    rates = -jnp.exp(alog_ref[...]) * LOG2E

    def eight(g, carry):
        state, running = carry
        at = pl.multiple_of(g * 8, 8)
        delta8 = delta_ref[pl.ds(at, 8)]
        fed8 = fed_ref[pl.ds(at, 8)]
        reads, sums = [], []
        for i in range(8):
            step = delta8[i : i + 1]
            running = running + step
            factor = jnp.exp2(rates * step)
            state = factor * state + tiled_lanes(b_ref[at + i], lanes) * fed8[i : i + 1]
            reads.append(state_sum(tiled_lanes(c_ref[at + i], lanes) * state))
            sums.append(running)
        read_ref[pl.ds(at, 8)] += row_sums(reads)
        cum_ref[pl.ds(at, 8)] = jnp.concatenate(sums, axis=0)
        return state, running

    state, running = lax.fori_loop(
        0, tokens // 8, eight, (jnp.zeros((states, lanes), F32), jnp.zeros((1, lanes), F32))
    )
    step, steps = pl.program_id(0), pl.num_programs(0)
    ends_ref[:, pl.ds(pl.multiple_of(step * lanes, lanes), lanes)] = state.astype(BF16)
    high = running.astype(BF16).astype(F32)
    totals_ref[pl.ds(step, 1)] = high
    totals_ref[pl.ds(steps + step, 1)] = running - high

    @pl.when(step == steps - 1)
    def _():
        ends_ref[:, ends_ref.shape[1] - lanes :] = totals_ref[...].astype(BF16)


def scan(x_in, edge, dt_low, dt_weight, dt_bias, a_log, conv_weight, conv_bias, d_skip, b_and_c):
    tokens, channels = x_in.shape
    states = a_log.shape[0]
    lanes = math.gcd(512, channels)

    def cut(rows):
        return pl.BlockSpec((rows, lanes), lambda i: (0, i))

    def whole(a):
        zeros = (0,) * a.ndim
        return pl.BlockSpec(a.shape, lambda i: zeros)

    return pl.pallas_call(
        scan_kernel,
        grid=(channels // lanes,),
        in_specs=[
            cut(tokens), cut(edge.shape[0]), whole(dt_low), cut(dt_weight.shape[0]), cut(1),
            cut(states), cut(conv_weight.shape[0]), cut(1), cut(1), whole(b_and_c),
        ],
        out_specs=(
            cut(tokens),
            cut(tokens),
            pl.BlockSpec((states, channels + lanes), lambda i: (0, 0)),
        ),
        out_shape=(
            pltpu.HBM((tokens, channels), F32),
            pltpu.HBM((tokens, channels), F32),
            jax.ShapeDtypeStruct((states, channels + lanes), BF16),
        ),
        scratch_shapes=[
            pltpu.VMEM((tokens + 8, lanes), F32),
            pltpu.VMEM((tokens, lanes), F32),
            pltpu.VMEM((tokens, lanes), F32),
            pltpu.VMEM((states, lanes), F32),
            pltpu.VMEM((tokens, states, 128), F32),
            pltpu.VMEM((tokens, states, 128), F32),
        ],
        compiler_params=params(40),
        cost_estimate=cost(
            tokens * channels * states * 8, tokens * channels * 12, tokens * channels * states
        ),
        name="scan",
    )(
        *in_hbm(x_in),
        edge,
        *in_hbm(
            dt_low, dt_weight, dt_bias[None], a_log, conv_weight, conv_bias[None], d_skip[None],
            b_and_c,
        ),
    )


def upper_half(step):
    return (lax.axis_index("seq") >> step) % 2 == 1


def link_kernel(step, *refs):
    total_ref, received_ref, alog_ref, prefix_ref = refs[:4] if step else (*refs[:3], None)
    total_out, prefix_out = refs[-2:]
    channels = alog_ref.shape[1]
    lanes = total_ref.shape[1] - channels
    steps = channels // lanes
    upper = upper_half(step)

    def sizes(ref):
        value = ref[:, channels:].astype(F32)
        return value[:steps] + value[steps : 2 * steps]

    def put_sizes(ref, value):
        high = value.astype(BF16).astype(F32)
        rest = jnp.zeros((ref.shape[0] - 2 * steps, lanes), F32)
        parts = [high, value - high] + ([rest] if rest.shape[0] else [])
        ref[:, channels:] = jnp.concatenate(parts, axis=0).astype(BF16)

    own, received = sizes(total_ref), sizes(received_ref)
    before = sizes(prefix_ref) if step else jnp.zeros_like(own)
    later = jnp.where(upper, own, received)
    put_sizes(total_out, own + received)
    put_sizes(prefix_out, before + jnp.where(upper, received, 0.0))
    for i in range(steps):
        at = slice(i * lanes, (i + 1) * lanes)
        rates = -jnp.exp(alog_ref[:, at]) * LOG2E
        mine, theirs = total_ref[:, at].astype(F32), received_ref[:, at].astype(F32)
        last, first = jnp.where(upper, mine, theirs), jnp.where(upper, theirs, mine)
        total_out[:, at] = (last + jnp.exp2(rates * later[i : i + 1]) * first).astype(BF16)
        if step:
            prefix = prefix_ref[:, at].astype(F32)
            further = prefix + jnp.exp2(rates * before[i : i + 1]) * theirs
        else:
            prefix, further = jnp.zeros_like(theirs), theirs
        prefix_out[:, at] = jnp.where(upper, further, prefix).astype(BF16)


def link(step, total, received, a_log, prefix):
    shape = jax.ShapeDtypeStruct(total.shape, BF16)
    args = [total, received, a_log] + ([prefix] if step else [])
    return pl.pallas_call(
        functools.partial(link_kernel, step),
        out_shape=(shape, shape),
        compiler_params=params(16),
        cost_estimate=cost(total.size * 2, total.size * 6),
        name="link",
    )(*args)


def finish_kernel(
    step, read_ref, cum_ref, z_ref, alog_ref, bc_ref, prefix_ref, *refs
):
    others, sizes, (out_ref, sum_ref, wide_ref, c_ref) = refs[:3], refs[3:7], refs[7:]
    tokens, lanes = z_ref.shape
    states = alog_ref.shape[0]
    at, steps = pl.program_id(0), pl.num_programs(0)

    @pl.when(at == 0)
    def _():
        spread_states(bc_ref[1], c_ref)
        for i, ref in enumerate(sizes):
            wide_ref[i * states : (i + 1) * states] = ref[...].astype(F32)

    rates = -jnp.exp(alog_ref[...]) * LOG2E

    def decay(i):
        row = i * states + at
        return jnp.exp2(rates * (wide_ref[pl.ds(row, 1)] + wide_ref[pl.ds(row + steps, 1)]))

    mine = lax.axis_index("seq") >> step
    ends = [ref[...].astype(F32) for ref in others]
    decays = [decay(i + 1) for i in range(3)]
    entering = jnp.zeros((states, lanes), F32)
    for group in range(3):
        partner = mine ^ group

        def chosen(values):
            return jnp.where(partner == 1, values[0], jnp.where(partner == 2, values[1], values[2]))

        further = chosen(decays) * entering + chosen(ends)
        entering = jnp.where(group < mine, further, entering)
    entering = prefix_ref[...].astype(F32) + decay(0) * entering

    def eight(g, carry):
        at = pl.multiple_of(g * 8, 8)
        cum8 = cum_ref[pl.ds(at, 8)]
        reads = []
        for i in range(8):
            kept = jnp.exp2(rates * cum8[i : i + 1]) * entering
            reads.append(state_sum(tiled_lanes(c_ref[at + i], lanes) * kept))
        sum_ref[pl.ds(at, 8)] = row_sums(reads)
        return carry

    lax.fori_loop(0, tokens // 8, eight, 0)
    z = z_ref[...].astype(F32)
    out_ref[...] = ((read_ref[...] + sum_ref[...]) * (z * jax.nn.sigmoid(z))).astype(BF16)


def finish(step, read, cum, z_gate, prefix, others, a_log, b_and_c):
    tokens, channels = z_gate.shape
    states = a_log.shape[0]
    lanes = prefix.shape[1] - channels

    def cut(rows):
        return pl.BlockSpec((rows, lanes), lambda i: (0, i))

    sizes = pl.BlockSpec((states, lanes), lambda i: (0, channels // lanes))
    return pl.pallas_call(
        functools.partial(finish_kernel, step),
        grid=(channels // lanes,),
        in_specs=[
            cut(tokens), cut(tokens), cut(tokens), cut(states),
            pl.BlockSpec(b_and_c.shape, lambda i: (0, 0, 0)),
            *[cut(states)] * 4,
            *[sizes] * 4,
        ],
        out_specs=cut(tokens),
        out_shape=jax.ShapeDtypeStruct((tokens, channels), BF16),
        scratch_shapes=[
            pltpu.VMEM((tokens, lanes), F32),
            pltpu.VMEM((4 * states, lanes), F32),
            pltpu.VMEM((tokens, states, 128), F32),
        ],
        compiler_params=params(40),
        cost_estimate=cost(
            tokens * channels * states * 5, tokens * channels * 12, tokens * channels * states
        ),
        name="finish",
    )(*in_hbm(read, cum, z_gate, a_log, b_and_c), *[prefix, *others] * 2)


def swapped(value, by):
    count = lax.axis_size("seq")
    return lax.ppermute(value, "seq", [(i, i ^ by) for i in range(count)])


def turned(value, axis, by):
    count = lax.axis_size(axis)
    return lax.ppermute(value, axis, [(i, (i + by) % count) for i in range(count)])


def turned_within(value, copies, by):
    count = lax.axis_size("seq")
    return lax.ppermute(
        value, "seq", [(i, i // copies * copies + (i + by) % copies) for i in range(count)]
    )


def exchanged(value, copies):
    count = lax.axis_size("seq")
    groups = [list(range(m, count, copies)) for m in range(copies)]
    return lax.all_to_all(
        value, "seq", split_axis=0, concat_axis=0, tiled=True, axis_index_groups=groups
    )


def after(value, *others):
    return lax.optimization_barrier((value, others))[0]


def local(
    x_in,
    z_gate,
    dt_low,
    dt_weight,
    dt_bias,
    a_log,
    conv_weight,
    conv_bias,
    d_skip,
    b_and_c,
    hidden,
    router,
    expert_ids,
    w_gate,
    w_down,
):
    blocks = lax.axis_size("seq")
    feature_parts = lax.axis_size("exp")
    tokens, features = hidden.shape
    experts = router.shape[1]
    copies = blocks // experts
    pack = packing(features)
    ids = expert_ids.T

    edge = x_in[tokens - (conv_weight.shape[0] - 1) :]
    edge = lax.ppermute(edge, "seq", [(i, i + 1) for i in range(blocks - 1)])
    outgoing, logits = route(ids, hidden, router.T, 1, pack)
    outgoing = after(outgoing, edge)
    arrived = exchanged(outgoing.reshape((experts,) + outgoing.shape[2:]), copies)

    read, cum, ends = scan(
        x_in, edge, dt_low, dt_weight, dt_bias, a_log, conv_weight, conv_bias, d_skip, b_and_c
    )
    logits = [logits] + [turned(logits, "exp", d) for d in range(1, feature_parts)]
    arrived = after(arrived, ends, *logits)

    steps = blocks.bit_length() - 3
    total, prefix, received, step = ends, None, None, 0

    def advance(*marks):
        nonlocal total, prefix, received, step
        if step < steps:
            total, prefix = link(step, total, after(received, *marks), a_log, prefix)
            step += 1
            if step < steps:
                received = swapped(total, 1 << step)
            else:
                received = [swapped(total, q << step) for q in (1, 2, 3)]
        return prefix

    rows = [unpack(arrived, features, pack)]
    for d in range(1, copies):
        rows.append(turned_within(rows[0], copies, d))
    gated = []
    for part in rows:
        if gated:
            part = after(part, gated[-1][0])
        own = gate(part, w_gate)
        if not gated:
            own, received = after((own, ends), *rows[1:])
            received = swapped(received, 1)
        if len(gated) == copies - 1:
            own = after(own, advance(own), *(p for parts in gated for p in parts[1:]))
        gated.append([own] + [turned(own, "exp", d) for d in range(1, feature_parts)])
    made = []
    for parts in gated[1:] + gated[:1]:
        product = down(parts, w_down, BF16 if len(made) < copies - 1 else F32)
        if not made:
            product = after(product, advance(product))
        made.append(product)
    while step < steps:
        advance()
    sums = made[-1:]
    for d in range(1, copies):
        sums.append(turned_within(made[d - 1], copies, -d))
    packed = after(pack_sum(sums, experts, pack), *received)
    back = exchanged(packed, copies)

    weights = blend_weights(ids, after(tuple(logits), packed), 1, pack)
    received = after(tuple(received), packed)
    mamba_out = finish(step, read, cum, z_gate, prefix, received, a_log, b_and_c)
    back = after(back, mamba_out)
    moe_out = combine(back, weights, tokens, features, pack)
    return mamba_out, moe_out


def solution(mesh):
    return jax.shard_map(
        local,
        mesh=mesh,
        in_specs=(
            P("seq", "exp"),
            P("seq", "exp"),
            P("seq", None),
            P(None, "exp"),
            P("exp"),
            P(None, "exp"),
            P(None, "exp"),
            P("exp"),
            P("exp"),
            P(None, None, "seq"),
            P("seq", "exp"),
            P("exp", None),
            P("seq", None),
            P("exp", "seq"),
            P("seq", "exp"),
        ),
        out_specs=(P("seq", "exp"), P("seq", "exp")),
        check_vma=False,
    )
```

```python
import functools
import math

import jax
import jax.numpy as jnp
from jax import lax
from jax.experimental import pallas as pl
from jax.experimental.pallas import tpu as pltpu
from jax.sharding import PartitionSpec as P

CAP = 18
MIB = 1 << 20
LOG2E = math.log2(math.e)
F32 = jnp.float32
BF16 = jnp.bfloat16


def params(limit):
    return pltpu.CompilerParams(vmem_limit_bytes=limit * MIB)


def cost(flops, moved, transcendentals=0):
    return pl.CostEstimate(
        flops=int(flops), bytes_accessed=int(moved), transcendentals=int(transcendentals)
    )


def in_hbm(*arrays):
    return [pltpu.with_memory_space_constraint(a, pltpu.HBM) for a in arrays]


def iota(shape, dim):
    return lax.broadcasted_iota(jnp.int32, shape, dim)


def dot(a, b):
    return jnp.dot(a, b, preferred_element_type=F32)


def dot_nt(a, b):
    return lax.dot_general(a, b, (((1,), (1,)), ((), ())), preferred_element_type=F32)


def packing(features):
    main = CAP // 16 * 16
    extra = CAP - main
    cuts = main // extra if extra and main % extra == 0 else 0
    if cuts and features % (cuts * 128) == 0:
        return main, extra, cuts, features // cuts
    return -(-CAP // 16) * 16, 0, 0, 0


def hits_and_slots(ids, experts):
    tokens = ids.shape[1]
    of = iota((experts, tokens), 0)
    hits = [(of == ids[k : k + 1]).astype(F32) for k in range(2)]
    before = (iota((tokens, tokens), 0) < iota((tokens, tokens), 1)).astype(BF16)
    earlier = dot((hits[0] + hits[1]).astype(BF16), before)
    slots = [jnp.sum(h * earlier, axis=0, keepdims=True).astype(jnp.int32) for h in hits]
    return hits, slots


def route_kernel(pack, ids_ref, hidden_ref, router_ref, out_ref, logits_ref):
    main, extra, cuts, width = pack
    experts, copies = out_ref.shape[:2]
    tokens, features = hidden_ref.shape
    ids = ids_ref[...]
    _, slots = hits_and_slots(ids, experts)
    hidden = hidden_ref[...]
    row = iota((experts * main, tokens), 0)
    picked = None
    for k in range(2):
        key = jnp.where(slots[k] < main, ids[k : k + 1] * main + slots[k], -1)
        hit = row == key
        picked = hit if picked is None else picked | hit
    packed = dot(picked.astype(BF16), hidden).astype(BF16)
    for e in range(experts):
        for m in range(copies):
            out_ref[e, m, :, :features] = packed[e * main : (e + 1) * main]
    if extra:
        picked = None
        for k in range(2):
            key = jnp.where(slots[k] >= main, ids[k : k + 1] * extra + slots[k] - main, -1)
            hit = row // cuts == key
            picked = hit if picked is None else picked | hit
        total = None
        for c in range(cuts):
            chosen = (picked & (row % cuts == c)).astype(BF16)
            part = dot(chosen, hidden[:, c * width : (c + 1) * width])
            total = part if total is None else total + part
        total = total.astype(BF16)
        for e in range(experts):
            for m in range(copies):
                out_ref[e, m, :, features:] = total[e * main : (e + 1) * main]
    logits_ref[...] = dot_nt(hidden, router_ref[...])


def route(ids, hidden, router, copies, pack):
    main, _, _, width = pack
    tokens, features = hidden.shape
    experts = router.shape[0]
    return pl.pallas_call(
        functools.partial(route_kernel, pack),
        out_shape=(
            jax.ShapeDtypeStruct((experts, copies, main, features + width), BF16),
            jax.ShapeDtypeStruct((tokens, experts), F32),
        ),
        compiler_params=params(40),
        cost_estimate=cost(2 * tokens * experts * main * features * 2, hidden.size * 8),
        name="route",
    )(*in_hbm(ids, hidden, router))


def weights_kernel(pack, copies, ids_ref, *refs):
    logits_refs, (main_ref, extra_ref, gates_ref) = refs[:-3], refs[-3:]
    main, extra, cuts, _ = pack
    tokens, experts = logits_refs[0].shape
    ids = ids_ref[...]
    hits, slots = hits_and_slots(ids, experts)
    eye = (iota((tokens, tokens), 0) == iota((tokens, tokens), 1)).astype(BF16)
    logits = logits_refs[0][...]
    for ref in logits_refs[1:]:
        logits = logits + ref[...]
    columns = [dot_nt(eye, h.astype(BF16)) for h in hits]
    picked = [jnp.sum(c * logits, axis=1, keepdims=True) for c in columns]
    expert = iota((tokens, experts), 1).astype(F32)
    total = experts * copies * main
    col = iota((tokens, total), 1)
    for k in range(2):
        gate = jax.nn.sigmoid(picked[k] - picked[1 - k])
        gates_ref[k] = jnp.broadcast_to(gate, gates_ref.shape[1:])
        named = jnp.sum(columns[k] * expert, axis=1, keepdims=True).astype(jnp.int32)
        wide = jnp.broadcast_to(slots[k].astype(F32), (8, tokens)).astype(BF16)
        slot = dot_nt(eye, wide)[:, :1].astype(jnp.int32)
        mine = col // (copies * main) == named
        main_ref[k] = (mine & (col % main == slot)).astype(BF16)
        if extra:
            place = (col % main) // cuts + main
            extra_ref[k] = (mine & (place == slot)).astype(BF16)
        else:
            extra_ref[k] = jnp.zeros(extra_ref.shape[1:], BF16)


def blend_weights(ids, logits, copies, pack):
    tokens, experts = logits[0].shape
    total = experts * copies * pack[0]
    return pl.pallas_call(
        functools.partial(weights_kernel, pack, copies),
        out_shape=(
            jax.ShapeDtypeStruct((2, tokens, total), BF16),
            jax.ShapeDtypeStruct((2, tokens, total), BF16),
            jax.ShapeDtypeStruct((2, tokens, 128), F32),
        ),
        compiler_params=params(40),
        cost_estimate=cost(2 * tokens * total * 16, tokens * total * 8),
        name="blend_weights",
    )(*in_hbm(ids), *logits)


ANYWHERE = pl.BlockSpec(memory_space=pl.ANY)
INSIDE = pl.BlockSpec(memory_space=pltpu.VMEM)
AHEAD = 6


def chunk_copy(from_ref, to_ref, sems, dim, chunk):
    def copy(i):
        at = pl.ds(pl.multiple_of(i * chunk, chunk), chunk)
        part = (slice(None), at) if dim else (at, slice(None))
        return pltpu.make_async_copy(from_ref.at[part], to_ref.at[part], sems.at[i])

    return copy, from_ref.shape[dim] // chunk


def streamed(stream, use, begin=None, begun=False, follow=None):
    copy, count = stream
    if not begun:
        for i in range(min(AHEAD, count)):
            copy(i).start()
    if begin is not None:
        begin()

    def step(i, carry):
        copy(i).wait()

        @pl.when(i + AHEAD < count)
        def _():
            copy(i + AHEAD).start()

        if follow is not None:
            later = i - max(count - AHEAD, 0)

            @pl.when((later >= 0) & (later < follow[1]))
            def _():
                follow[0](later).start()

        use(i)
        return carry

    lax.fori_loop(0, count, step, 0)


def gate_first_kernel(chunk, x_ref, w_ref, out_ref, kept_ref, held_ref, kept_sems, sems):
    start = kept_ref.shape[1]
    one = chunk_copy(w_ref.at[:, :start], kept_ref, kept_sems, 1, chunk)
    two = chunk_copy(w_ref.at[:, start:], held_ref, sems, 1, chunk)
    streamed(one, gate_product(chunk, x_ref, kept_ref, out_ref, 0), follow=two)
    for i in range(min(AHEAD, one[1]), min(AHEAD, two[1])):
        two[0](i).start()
    streamed(two, gate_product(chunk, x_ref, held_ref, out_ref, start), begun=True)


def gate_product(chunk, x_ref, from_ref, out_ref, offset):
    def use(i):
        at = pl.ds(pl.multiple_of(i * chunk, chunk), chunk)
        to = pl.ds(pl.multiple_of(offset + i * chunk, chunk), chunk)
        out_ref[:, to] = dot(x_ref[...], from_ref[:, at]).astype(BF16)

    return use


def gate_next_kernel(chunk, x_ref, w_ref, kept_ref, out_ref, held_ref, sems):
    start = kept_ref.shape[1]
    kept = gate_product(chunk, x_ref, kept_ref, out_ref, 0)
    streamed(
        chunk_copy(w_ref.at[:, start:], held_ref, sems, 1, chunk),
        gate_product(chunk, x_ref, held_ref, out_ref, start),
        lambda: pl.loop(0, start // chunk)(kept),
    )


def gate(x, w_gate, kept=None):
    rows, features = x.shape
    amount = w_gate.shape[1]
    chunk = math.gcd(512, amount)
    half = amount // chunk // 2 * chunk
    out = jax.ShapeDtypeStruct((rows, amount), BF16)
    rest = [pltpu.VMEM((features, amount - half), BF16)]
    rest_sems = pltpu.SemaphoreType.DMA(((amount - half) // chunk,))
    hints = dict(
        compiler_params=params(32),
        cost_estimate=cost(2 * rows * features * amount, features * amount * 2),
        name="gate",
    )
    if kept is not None:
        return pl.pallas_call(
            functools.partial(gate_next_kernel, chunk),
            in_specs=[INSIDE, ANYWHERE, INSIDE],
            out_specs=INSIDE,
            out_shape=out,
            scratch_shapes=rest + [rest_sems],
            **hints,
        )(x, *in_hbm(w_gate), kept)
    return pl.pallas_call(
        functools.partial(gate_first_kernel, chunk),
        in_specs=[INSIDE, ANYWHERE],
        out_specs=(INSIDE, INSIDE),
        out_shape=(out, jax.ShapeDtypeStruct((features, half), BF16)),
        scratch_shapes=rest + [pltpu.SemaphoreType.DMA((half // chunk,)), rest_sems],
        **hints,
    )(x, *in_hbm(w_gate))


def fill_acted(chunk, part_refs, acted_ref):
    def piece(i):
        at = pl.ds(pl.multiple_of(i * chunk, chunk), chunk)
        total = part_refs[0][:, at].astype(F32)
        for ref in part_refs[1:]:
            total = total + ref[:, at].astype(F32)
        acted_ref[:, at] = (total * jax.nn.sigmoid(total)).astype(BF16)

    pl.loop(0, acted_ref.shape[1] // chunk)(piece)


def down_kernel(chunk, *refs):
    part_refs, w_ref, out_ref, acted_ref, held_ref, sems = refs[:-5], *refs[-5:]

    def use(i):
        at = pl.ds(pl.multiple_of(i * chunk, chunk), chunk)
        out_ref[:, at] = dot(acted_ref[...], held_ref[:, at]).astype(out_ref.dtype)

    def begin():
        fill_acted(math.gcd(512, acted_ref.shape[1]), part_refs, acted_ref)

    streamed(chunk_copy(w_ref, held_ref, sems, 1, chunk), use, begin)


def down(parts, w_down, dtype):
    rows, amount = parts[0].shape
    features = w_down.shape[1]
    chunk = math.gcd(256, features)
    return pl.pallas_call(
        functools.partial(down_kernel, chunk),
        in_specs=[INSIDE] * len(parts) + [ANYWHERE],
        out_specs=INSIDE,
        out_shape=jax.ShapeDtypeStruct((rows, features), dtype),
        scratch_shapes=[
            pltpu.VMEM((rows, amount), BF16),
            pltpu.VMEM(w_down.shape, BF16),
            pltpu.SemaphoreType.DMA((features // chunk,)),
        ],
        compiler_params=params(48),
        cost_estimate=cost(2 * rows * features * amount, features * amount * 2),
        name="down",
    )(*parts, *in_hbm(w_down))


def unpack_kernel(pack, arrived_ref, out_ref):
    main, extra, cuts, width = pack
    sources = arrived_ref.shape[0]
    features = out_ref.shape[1]
    out_ref[: sources * main] = arrived_ref[:, :, :features].reshape(sources * main, features)
    if extra:
        folded = arrived_ref[:, :, features:].reshape(sources * main, width)
        shape = (sources * extra, sources * main)
        for c in range(cuts):
            pick = (iota(shape, 1) == iota(shape, 0) * cuts + c).astype(BF16)
            out_ref[sources * main :, c * width : (c + 1) * width] = dot(pick, folded).astype(BF16)


def unpack(arrived, features, pack):
    main, extra, _, _ = pack
    rows = arrived.shape[0] * (main + extra)
    return pl.pallas_call(
        functools.partial(unpack_kernel, pack),
        out_shape=jax.ShapeDtypeStruct((rows, features), BF16),
        compiler_params=params(24),
        cost_estimate=cost(arrived.size * 16, arrived.size * 4),
        name="unpack",
    )(arrived)


def pack_kernel(pack, *refs):
    main, extra, cuts, width = pack
    part_refs, out_ref = refs[:-1], refs[-1]
    sources = out_ref.shape[0]
    features = part_refs[0].shape[1]
    first = sources * main

    def total(rows, columns):
        value = part_refs[0][rows, columns].astype(F32)
        for ref in part_refs[1:]:
            value = value + ref[rows, columns].astype(F32)
        return value.astype(BF16)

    made = total(slice(0, first), slice(0, features))
    out_ref[:, :, :features] = made.reshape(sources, main, features)
    if extra:
        shape = (sources * main, sources * extra)
        folded = None
        for c in range(cuts):
            piece = total(slice(first, None), slice(c * width, (c + 1) * width))
            pick = (iota(shape, 0) == iota(shape, 1) * cuts + c).astype(BF16)
            part = dot(pick, piece)
            folded = part if folded is None else folded + part
        out_ref[:, :, features:] = folded.astype(BF16).reshape(sources, main, width)


def pack_sum(parts, sources, pack):
    main, _, _, width = pack
    features = parts[0].shape[1]
    return pl.pallas_call(
        functools.partial(pack_kernel, pack),
        out_shape=jax.ShapeDtypeStruct((sources, main, features + width), BF16),
        compiler_params=params(24),
        cost_estimate=cost(parts[0].size * 16, parts[0].size * 8),
        name="pack_sum",
    )(*parts)


def combine_kernel(pack, back_ref, main_ref, extra_ref, gates_ref, out_ref):
    main, extra, cuts, width = pack
    sources = back_ref.shape[0]
    tokens, features = out_ref.shape
    back = back_ref[:, :, :features].reshape(sources * main, features)
    folded = back_ref[:, :, features:].reshape(sources * main, width) if extra else None
    total = None
    for k in range(2):
        rows = dot(main_ref[k], back)
        if extra:
            chosen = extra_ref[k]
            at = iota(chosen.shape, 1) % cuts
            pieces = [
                dot(jnp.where(at == c, chosen, jnp.zeros_like(chosen)), folded) for c in range(cuts)
            ]
            rows = rows + jnp.concatenate(pieces, axis=1)
        weighed = rows * gates_ref[k][:, :1]
        total = weighed if total is None else total + weighed
    out_ref[...] = total.astype(BF16)


def combine(back, weights, tokens, features, pack):
    return pl.pallas_call(
        functools.partial(combine_kernel, pack),
        out_shape=jax.ShapeDtypeStruct((tokens, features), BF16),
        compiler_params=params(40),
        cost_estimate=cost(4 * tokens * back.size, back.size * 2),
        name="combine",
    )(back, *weights)


def spread_states(values, spread_ref):
    for t in range(spread_ref.shape[0]):
        spread_ref[t] = jnp.broadcast_to(values[:, t : t + 1], spread_ref.shape[1:])


def row_sums(parts):
    place = iota(parts[0].shape, 0)
    for stride in (4, 2, 1):
        low = place & stride == 0
        half = len(parts) // 2
        joined = []
        for a, b in zip(parts[:half], parts[half:]):
            kept = jnp.where(low, a, b)
            moved = jnp.where(low, b, a)
            if stride == 4:
                other = pltpu.roll(moved, 4, 0)
            else:
                other = jnp.where(low, pltpu.roll(moved, 8 - stride, 0), pltpu.roll(moved, stride, 0))
            joined.append(kept + other)
        parts = joined
    return parts[0]


def state_sum(value):
    total = value[:8]
    for at in range(8, value.shape[0], 8):
        total = total + value[at : at + 8]
    return total


def tiled_lanes(value, lanes):
    return jnp.concatenate([value] * (lanes // value.shape[1]), axis=1)


def scan_kernel(
    x_ref, edge_ref, low_ref, dtw_ref, dtb_ref, alog_ref, cw_ref, cb_ref, skip_ref, bc_ref,
    read_ref, cum_ref, ends_ref, padded, delta_ref, fed_ref, totals_ref, b_ref, c_ref,
):
    tokens, lanes = x_ref.shape
    taps = cw_ref.shape[0]
    states = alog_ref.shape[0]

    @pl.when(pl.program_id(0) == 0)
    def _():
        spread_states(bc_ref[0], b_ref)
        spread_states(bc_ref[1], c_ref)
        totals_ref[...] = jnp.zeros_like(totals_ref)

    padded[8:] = x_ref[...].astype(F32)
    padded[8 - (taps - 1) : 8] = edge_ref[...].astype(F32)
    conv = jnp.broadcast_to(cb_ref[...], (tokens, lanes))
    for k in range(taps):
        at = 8 - (taps - 1) + k
        conv = conv + cw_ref[k : k + 1] * padded[at : at + tokens]
    act = conv * jax.nn.sigmoid(conv)
    raw = dot(low_ref[...], dtw_ref[...]) + dtb_ref[...]
    delta = jnp.maximum(raw, 0.0) + jnp.log1p(jnp.exp(-jnp.abs(raw)))
    delta_ref[...] = delta
    fed_ref[...] = delta * act
    read_ref[...] = skip_ref[...] * act
    rates = -jnp.exp(alog_ref[...]) * LOG2E

    def eight(g, carry):
        state, running = carry
        at = pl.multiple_of(g * 8, 8)
        delta8 = delta_ref[pl.ds(at, 8)]
        fed8 = fed_ref[pl.ds(at, 8)]
        reads, sums = [], []
        for i in range(8):
            step = delta8[i : i + 1]
            running = running + step
            factor = jnp.exp2(rates * step)
            state = factor * state + tiled_lanes(b_ref[at + i], lanes) * fed8[i : i + 1]
            reads.append(state_sum(tiled_lanes(c_ref[at + i], lanes) * state))
            sums.append(running)
        read_ref[pl.ds(at, 8)] += row_sums(reads)
        cum_ref[pl.ds(at, 8)] = jnp.concatenate(sums, axis=0)
        return state, running

    state, running = lax.fori_loop(
        0, tokens // 8, eight, (jnp.zeros((states, lanes), F32), jnp.zeros((1, lanes), F32))
    )
    step, steps = pl.program_id(0), pl.num_programs(0)
    ends_ref[:, pl.ds(pl.multiple_of(step * lanes, lanes), lanes)] = state.astype(BF16)
    high = running.astype(BF16).astype(F32)
    totals_ref[pl.ds(step, 1)] = high
    totals_ref[pl.ds(steps + step, 1)] = running - high

    @pl.when(step == steps - 1)
    def _():
        ends_ref[:, ends_ref.shape[1] - lanes :] = totals_ref[...].astype(BF16)


def scan(x_in, edge, dt_low, dt_weight, dt_bias, a_log, conv_weight, conv_bias, d_skip, b_and_c):
    tokens, channels = x_in.shape
    states = a_log.shape[0]
    lanes = math.gcd(512, channels)

    def cut(rows):
        return pl.BlockSpec((rows, lanes), lambda i: (0, i))

    def whole(a):
        zeros = (0,) * a.ndim
        return pl.BlockSpec(a.shape, lambda i: zeros)

    return pl.pallas_call(
        scan_kernel,
        grid=(channels // lanes,),
        in_specs=[
            cut(tokens), cut(edge.shape[0]), whole(dt_low), cut(dt_weight.shape[0]), cut(1),
            cut(states), cut(conv_weight.shape[0]), cut(1), cut(1), whole(b_and_c),
        ],
        out_specs=(
            cut(tokens),
            cut(tokens),
            pl.BlockSpec((states, channels + lanes), lambda i: (0, 0)),
        ),
        out_shape=(
            pltpu.HBM((tokens, channels), F32),
            pltpu.HBM((tokens, channels), F32),
            jax.ShapeDtypeStruct((states, channels + lanes), BF16),
        ),
        scratch_shapes=[
            pltpu.VMEM((tokens + 8, lanes), F32),
            pltpu.VMEM((tokens, lanes), F32),
            pltpu.VMEM((tokens, lanes), F32),
            pltpu.VMEM((states, lanes), F32),
            pltpu.VMEM((tokens, states, 128), F32),
            pltpu.VMEM((tokens, states, 128), F32),
        ],
        compiler_params=params(40),
        cost_estimate=cost(
            tokens * channels * states * 8, tokens * channels * 12, tokens * channels * states
        ),
        name="scan",
    )(
        *in_hbm(x_in),
        edge,
        *in_hbm(
            dt_low, dt_weight, dt_bias[None], a_log, conv_weight, conv_bias[None], d_skip[None],
            b_and_c,
        ),
    )


def upper_half(step):
    return (lax.axis_index("seq") >> step) % 2 == 1


def link_kernel(step, *refs):
    total_ref, received_ref, alog_ref, prefix_ref = refs[:4] if step else (*refs[:3], None)
    total_out, prefix_out = refs[-2:]
    channels = alog_ref.shape[1]
    lanes = total_ref.shape[1] - channels
    steps = channels // lanes
    upper = upper_half(step)

    def sizes(ref):
        value = ref[:, channels:].astype(F32)
        return value[:steps] + value[steps : 2 * steps]

    def put_sizes(ref, value):
        high = value.astype(BF16).astype(F32)
        rest = jnp.zeros((ref.shape[0] - 2 * steps, lanes), F32)
        parts = [high, value - high] + ([rest] if rest.shape[0] else [])
        ref[:, channels:] = jnp.concatenate(parts, axis=0).astype(BF16)

    own, received = sizes(total_ref), sizes(received_ref)
    before = sizes(prefix_ref) if step else jnp.zeros_like(own)
    later = jnp.where(upper, own, received)
    put_sizes(total_out, own + received)
    put_sizes(prefix_out, before + jnp.where(upper, received, 0.0))
    for i in range(steps):
        at = slice(i * lanes, (i + 1) * lanes)
        rates = -jnp.exp(alog_ref[:, at]) * LOG2E
        mine, theirs = total_ref[:, at].astype(F32), received_ref[:, at].astype(F32)
        last, first = jnp.where(upper, mine, theirs), jnp.where(upper, theirs, mine)
        total_out[:, at] = (last + jnp.exp2(rates * later[i : i + 1]) * first).astype(BF16)
        if step:
            prefix = prefix_ref[:, at].astype(F32)
            further = prefix + jnp.exp2(rates * before[i : i + 1]) * theirs
        else:
            prefix, further = jnp.zeros_like(theirs), theirs
        prefix_out[:, at] = jnp.where(upper, further, prefix).astype(BF16)


def link(step, total, received, a_log, prefix):
    shape = jax.ShapeDtypeStruct(total.shape, BF16)
    args = [total, received, a_log] + ([prefix] if step else [])
    return pl.pallas_call(
        functools.partial(link_kernel, step),
        out_shape=(shape, shape),
        compiler_params=params(16),
        cost_estimate=cost(total.size * 2, total.size * 6),
        name="link",
    )(*args)


def finish_kernel(
    step, read_ref, cum_ref, z_ref, alog_ref, bc_ref, prefix_ref, *refs
):
    others, sizes, (out_ref, sum_ref, wide_ref, c_ref) = refs[:3], refs[3:7], refs[7:]
    tokens, lanes = z_ref.shape
    states = alog_ref.shape[0]
    at, steps = pl.program_id(0), pl.num_programs(0)

    @pl.when(at == 0)
    def _():
        spread_states(bc_ref[1], c_ref)
        for i, ref in enumerate(sizes):
            wide_ref[i * states : (i + 1) * states] = ref[...].astype(F32)

    rates = -jnp.exp(alog_ref[...]) * LOG2E

    def decay(i):
        row = i * states + at
        return jnp.exp2(rates * (wide_ref[pl.ds(row, 1)] + wide_ref[pl.ds(row + steps, 1)]))

    mine = lax.axis_index("seq") >> step
    ends = [ref[...].astype(F32) for ref in others]
    decays = [decay(i + 1) for i in range(3)]
    entering = jnp.zeros((states, lanes), F32)
    for group in range(3):
        partner = mine ^ group

        def chosen(values):
            return jnp.where(partner == 1, values[0], jnp.where(partner == 2, values[1], values[2]))

        further = chosen(decays) * entering + chosen(ends)
        entering = jnp.where(group < mine, further, entering)
    entering = prefix_ref[...].astype(F32) + decay(0) * entering

    def eight(g, carry):
        at = pl.multiple_of(g * 8, 8)
        cum8 = cum_ref[pl.ds(at, 8)]
        reads = []
        for i in range(8):
            kept = jnp.exp2(rates * cum8[i : i + 1]) * entering
            reads.append(state_sum(tiled_lanes(c_ref[at + i], lanes) * kept))
        sum_ref[pl.ds(at, 8)] = row_sums(reads)
        return carry

    lax.fori_loop(0, tokens // 8, eight, 0)
    z = z_ref[...].astype(F32)
    out_ref[...] = ((read_ref[...] + sum_ref[...]) * (z * jax.nn.sigmoid(z))).astype(BF16)


def finish(step, read, cum, z_gate, prefix, others, a_log, b_and_c):
    tokens, channels = z_gate.shape
    states = a_log.shape[0]
    lanes = prefix.shape[1] - channels

    def cut(rows):
        return pl.BlockSpec((rows, lanes), lambda i: (0, i))

    sizes = pl.BlockSpec((states, lanes), lambda i: (0, channels // lanes))
    return pl.pallas_call(
        functools.partial(finish_kernel, step),
        grid=(channels // lanes,),
        in_specs=[
            cut(tokens), cut(tokens), cut(tokens), cut(states),
            pl.BlockSpec(b_and_c.shape, lambda i: (0, 0, 0)),
            *[cut(states)] * 4,
            *[sizes] * 4,
        ],
        out_specs=cut(tokens),
        out_shape=jax.ShapeDtypeStruct((tokens, channels), BF16),
        scratch_shapes=[
            pltpu.VMEM((tokens, lanes), F32),
            pltpu.VMEM((4 * states, lanes), F32),
            pltpu.VMEM((tokens, states, 128), F32),
        ],
        compiler_params=params(40),
        cost_estimate=cost(
            tokens * channels * states * 5, tokens * channels * 12, tokens * channels * states
        ),
        name="finish",
    )(*in_hbm(read, cum, z_gate, a_log, b_and_c), *[prefix, *others] * 2)


def swapped(value, by):
    count = lax.axis_size("seq")
    return lax.ppermute(value, "seq", [(i, i ^ by) for i in range(count)])


def turned(value, axis, by):
    count = lax.axis_size(axis)
    return lax.ppermute(value, axis, [(i, (i + by) % count) for i in range(count)])


def turned_within(value, copies, by):
    count = lax.axis_size("seq")
    return lax.ppermute(
        value, "seq", [(i, i // copies * copies + (i + by) % copies) for i in range(count)]
    )


def exchanged(value, copies):
    count = lax.axis_size("seq")
    groups = [list(range(m, count, copies)) for m in range(copies)]
    return lax.all_to_all(
        value, "seq", split_axis=0, concat_axis=0, tiled=True, axis_index_groups=groups
    )


def after(value, *others):
    return lax.optimization_barrier((value, others))[0]


def local(
    x_in,
    z_gate,
    dt_low,
    dt_weight,
    dt_bias,
    a_log,
    conv_weight,
    conv_bias,
    d_skip,
    b_and_c,
    hidden,
    router,
    expert_ids,
    w_gate,
    w_down,
):
    blocks = lax.axis_size("seq")
    feature_parts = lax.axis_size("exp")
    tokens, features = hidden.shape
    experts = router.shape[1]
    copies = blocks // experts
    pack = packing(features)
    ids = expert_ids.T

    edge = x_in[tokens - (conv_weight.shape[0] - 1) :]
    edge = lax.ppermute(edge, "seq", [(i, i + 1) for i in range(blocks - 1)])
    outgoing, logits = route(ids, hidden, router.T, 1, pack)
    outgoing = after(outgoing, edge)
    arrived = exchanged(outgoing.reshape((experts,) + outgoing.shape[2:]), copies)

    read, cum, ends = scan(
        x_in, edge, dt_low, dt_weight, dt_bias, a_log, conv_weight, conv_bias, d_skip, b_and_c
    )
    logits = [logits] + [turned(logits, "exp", d) for d in range(1, feature_parts)]
    arrived = after(arrived, ends, *logits)

    steps = blocks.bit_length() - 3
    total, prefix, received, step = ends, None, None, 0

    def advance(*marks):
        nonlocal total, prefix, received, step
        if step < steps:
            total, prefix = link(step, total, after(received, *marks), a_log, prefix)
            step += 1
            if step < steps:
                received = swapped(total, 1 << step)
            else:
                received = [swapped(total, q << step) for q in (1, 2, 3)]
        return prefix

    rows = [unpack(arrived, features, pack)]
    for d in range(1, copies):
        rows.append(turned_within(rows[0], copies, d))
    gated = []
    for part in rows:
        if gated:
            part = after(part, gated[-1][0])
            own = gate(part, w_gate, kept)
        else:
            own, kept = gate(part, w_gate)
            own, received = after((own, ends), *rows[1:])
            received = swapped(received, 1)
        if len(gated) == copies - 1:
            own = after(own, advance(own), *(p for parts in gated for p in parts[1:]))
        gated.append([own] + [turned(own, "exp", d) for d in range(1, feature_parts)])
    made = []
    for parts in gated[1:] + gated[:1]:
        product = down(parts, w_down, BF16 if len(made) < copies - 1 else F32)
        if not made:
            product = after(product, advance(product))
        made.append(product)
    while step < steps:
        advance()
    sums = made[-1:]
    for d in range(1, copies):
        sums.append(turned_within(made[d - 1], copies, -d))
    packed = after(pack_sum(sums, experts, pack), *received)
    back = exchanged(packed, copies)

    weights = blend_weights(ids, after(tuple(logits), packed), 1, pack)
    received = after(tuple(received), packed)
    mamba_out = finish(step, read, cum, z_gate, prefix, received, a_log, b_and_c)
    back = after(back, mamba_out)
    moe_out = combine(back, weights, tokens, features, pack)
    return mamba_out, moe_out


def solution(mesh):
    return jax.shard_map(
        local,
        mesh=mesh,
        in_specs=(
            P("seq", "exp"),
            P("seq", "exp"),
            P("seq", None),
            P(None, "exp"),
            P("exp"),
            P(None, "exp"),
            P(None, "exp"),
            P("exp"),
            P("exp"),
            P(None, None, "seq"),
            P("seq", "exp"),
            P("exp", None),
            P("seq", None),
            P("exp", "seq"),
            P("seq", "exp"),
        ),
        out_specs=(P("seq", "exp"), P("seq", "exp")),
        check_vma=False,
    )
```

```python
import functools
import math

import jax
import jax.numpy as jnp
from jax import lax
from jax.experimental import pallas as pl
from jax.experimental.pallas import tpu as pltpu
from jax.sharding import PartitionSpec as P

CAP = 18
MIB = 1 << 20
LOG2E = math.log2(math.e)
F32 = jnp.float32
BF16 = jnp.bfloat16


def params(limit):
    return pltpu.CompilerParams(vmem_limit_bytes=limit * MIB)


def cost(flops, moved, transcendentals=0):
    return pl.CostEstimate(
        flops=int(flops), bytes_accessed=int(moved), transcendentals=int(transcendentals)
    )


def in_hbm(*arrays):
    return [pltpu.with_memory_space_constraint(a, pltpu.HBM) for a in arrays]


def iota(shape, dim):
    return lax.broadcasted_iota(jnp.int32, shape, dim)


def dot(a, b):
    return jnp.dot(a, b, preferred_element_type=F32)


def dot_nt(a, b):
    return lax.dot_general(a, b, (((1,), (1,)), ((), ())), preferred_element_type=F32)


def packing(features):
    main = CAP // 16 * 16
    extra = CAP - main
    cuts = main // extra if extra and main % extra == 0 else 0
    if cuts and features % (cuts * 128) == 0:
        return main, extra, cuts, features // cuts
    return -(-CAP // 16) * 16, 0, 0, 0


def hits_and_slots(ids, experts):
    tokens = ids.shape[1]
    of = iota((experts, tokens), 0)
    hits = [(of == ids[k : k + 1]).astype(F32) for k in range(2)]
    before = (iota((tokens, tokens), 0) < iota((tokens, tokens), 1)).astype(BF16)
    earlier = dot((hits[0] + hits[1]).astype(BF16), before)
    slots = [jnp.sum(h * earlier, axis=0, keepdims=True).astype(jnp.int32) for h in hits]
    return hits, slots


def route_kernel(pack, ids_ref, hidden_ref, router_ref, out_ref, logits_ref):
    main, extra, cuts, width = pack
    experts, copies = out_ref.shape[:2]
    tokens, features = hidden_ref.shape
    ids = ids_ref[...]
    _, slots = hits_and_slots(ids, experts)
    hidden = hidden_ref[...]
    row = iota((experts * main, tokens), 0)
    picked = None
    for k in range(2):
        key = jnp.where(slots[k] < main, ids[k : k + 1] * main + slots[k], -1)
        hit = row == key
        picked = hit if picked is None else picked | hit
    packed = dot(picked.astype(BF16), hidden).astype(BF16)
    for e in range(experts):
        for m in range(copies):
            out_ref[e, m, :, :features] = packed[e * main : (e + 1) * main]
    if extra:
        picked = None
        for k in range(2):
            key = jnp.where(slots[k] >= main, ids[k : k + 1] * extra + slots[k] - main, -1)
            hit = row // cuts == key
            picked = hit if picked is None else picked | hit
        total = None
        for c in range(cuts):
            chosen = (picked & (row % cuts == c)).astype(BF16)
            part = dot(chosen, hidden[:, c * width : (c + 1) * width])
            total = part if total is None else total + part
        total = total.astype(BF16)
        for e in range(experts):
            for m in range(copies):
                out_ref[e, m, :, features:] = total[e * main : (e + 1) * main]
    logits_ref[...] = dot_nt(hidden, router_ref[...])


def route(ids, hidden, router, copies, pack):
    main, _, _, width = pack
    tokens, features = hidden.shape
    experts = router.shape[0]
    return pl.pallas_call(
        functools.partial(route_kernel, pack),
        out_shape=(
            jax.ShapeDtypeStruct((experts, copies, main, features + width), BF16),
            jax.ShapeDtypeStruct((tokens, experts), F32),
        ),
        compiler_params=params(40),
        cost_estimate=cost(2 * tokens * experts * main * features * 2, hidden.size * 8),
        name="route",
    )(*in_hbm(ids, hidden, router))


def weights_kernel(pack, copies, ids_ref, *refs):
    logits_refs, (main_ref, extra_ref, gates_ref) = refs[:-3], refs[-3:]
    main, extra, cuts, _ = pack
    tokens, experts = logits_refs[0].shape
    ids = ids_ref[...]
    hits, slots = hits_and_slots(ids, experts)
    eye = (iota((tokens, tokens), 0) == iota((tokens, tokens), 1)).astype(BF16)
    logits = logits_refs[0][...]
    for ref in logits_refs[1:]:
        logits = logits + ref[...]
    columns = [dot_nt(eye, h.astype(BF16)) for h in hits]
    picked = [jnp.sum(c * logits, axis=1, keepdims=True) for c in columns]
    expert = iota((tokens, experts), 1).astype(F32)
    total = experts * copies * main
    col = iota((tokens, total), 1)
    for k in range(2):
        gate = jax.nn.sigmoid(picked[k] - picked[1 - k])
        gates_ref[k] = jnp.broadcast_to(gate, gates_ref.shape[1:])
        named = jnp.sum(columns[k] * expert, axis=1, keepdims=True).astype(jnp.int32)
        wide = jnp.broadcast_to(slots[k].astype(F32), (8, tokens)).astype(BF16)
        slot = dot_nt(eye, wide)[:, :1].astype(jnp.int32)
        mine = col // (copies * main) == named
        main_ref[k] = (mine & (col % main == slot)).astype(BF16)
        if extra:
            place = (col % main) // cuts + main
            extra_ref[k] = (mine & (place == slot)).astype(BF16)
        else:
            extra_ref[k] = jnp.zeros(extra_ref.shape[1:], BF16)


def blend_weights(ids, logits, copies, pack):
    tokens, experts = logits[0].shape
    total = experts * copies * pack[0]
    return pl.pallas_call(
        functools.partial(weights_kernel, pack, copies),
        out_shape=(
            jax.ShapeDtypeStruct((2, tokens, total), BF16),
            jax.ShapeDtypeStruct((2, tokens, total), BF16),
            jax.ShapeDtypeStruct((2, tokens, 128), F32),
        ),
        compiler_params=params(40),
        cost_estimate=cost(2 * tokens * total * 16, tokens * total * 8),
        name="blend_weights",
    )(*in_hbm(ids), *logits)


ANYWHERE = pl.BlockSpec(memory_space=pl.ANY)
INSIDE = pl.BlockSpec(memory_space=pltpu.VMEM)
AHEAD = 6


def chunk_copy(from_ref, to_ref, sems, dim, chunk):
    def copy(i):
        at = pl.ds(pl.multiple_of(i * chunk, chunk), chunk)
        part = (slice(None), at) if dim else (at, slice(None))
        return pltpu.make_async_copy(from_ref.at[part], to_ref.at[part], sems.at[i])

    return copy, from_ref.shape[dim] // chunk


def streamed(stream, use, begin=None, begun=False, follow=None):
    copy, count = stream
    if not begun:
        for i in range(min(AHEAD, count)):
            copy(i).start()
    if begin is not None:
        begin()

    def step(i, carry):
        copy(i).wait()

        @pl.when(i + AHEAD < count)
        def _():
            copy(i + AHEAD).start()

        if follow is not None:
            later = i - max(count - AHEAD, 0)

            @pl.when((later >= 0) & (later < follow[1]))
            def _():
                follow[0](later).start()

        use(i)
        return carry

    lax.fori_loop(0, count, step, 0)


def gate_first_kernel(
    chunk, x_ref, w_ref, down_ref, out_ref, kept_ref, kept_down_ref, held_ref, kept_sems, sems, down_sems
):
    start, columns = kept_ref.shape[1], kept_down_ref.shape[1]
    one = chunk_copy(w_ref.at[:, :start], kept_ref, kept_sems, 1, chunk)
    two = chunk_copy(w_ref.at[:, start:], held_ref, sems, 1, chunk)
    copy, count = chunk_copy(
        down_ref.at[:, :columns], kept_down_ref, down_sems, 0, kept_down_ref.shape[0] // down_sems.shape[0]
    )
    streamed(one, gate_product(chunk, x_ref, kept_ref, out_ref, 0), follow=two)
    started = min(AHEAD, one[1])
    for i in range(started, min(AHEAD, two[1])):
        two[0](i).start()
    for i in range(count):
        copy(i).start()
    streamed(two, gate_product(chunk, x_ref, held_ref, out_ref, start), begun=True)
    for i in range(count):
        copy(i).wait()


def gate_product(chunk, x_ref, from_ref, out_ref, offset):
    def use(i):
        at = pl.ds(pl.multiple_of(i * chunk, chunk), chunk)
        to = pl.ds(pl.multiple_of(offset + i * chunk, chunk), chunk)
        out_ref[:, to] = dot(x_ref[...], from_ref[:, at]).astype(BF16)

    return use


def gate_next_kernel(chunk, x_ref, w_ref, kept_ref, out_ref, held_ref, sems):
    start = kept_ref.shape[1]
    kept = gate_product(chunk, x_ref, kept_ref, out_ref, 0)
    streamed(
        chunk_copy(w_ref.at[:, start:], held_ref, sems, 1, chunk),
        gate_product(chunk, x_ref, held_ref, out_ref, start),
        lambda: pl.loop(0, start // chunk)(kept),
    )


def gate(x, w_gate, w_down, kept=None):
    rows, features = x.shape
    amount = w_gate.shape[1]
    chunk = math.gcd(512, amount)
    half = amount // chunk // 2 * chunk
    out = jax.ShapeDtypeStruct((rows, amount), BF16)
    rest = [pltpu.VMEM((features, amount - half), BF16)]
    rest_sems = pltpu.SemaphoreType.DMA(((amount - half) // chunk,))
    hints = dict(
        compiler_params=params(20),
        cost_estimate=cost(2 * rows * features * amount, features * amount * 2),
        name="gate",
    )
    if kept is not None:
        return pl.pallas_call(
            functools.partial(gate_next_kernel, chunk),
            in_specs=[INSIDE, ANYWHERE, INSIDE],
            out_specs=INSIDE,
            out_shape=out,
            scratch_shapes=rest + [rest_sems],
            **hints,
        )(x, *in_hbm(w_gate), kept)
    return pl.pallas_call(
        functools.partial(gate_first_kernel, chunk),
        in_specs=[INSIDE, ANYWHERE, ANYWHERE],
        out_specs=(INSIDE, INSIDE, INSIDE),
        out_shape=(
            out,
            jax.ShapeDtypeStruct((features, half), BF16),
            jax.ShapeDtypeStruct((w_down.shape[0], w_down.shape[1] // 2), BF16),
        ),
        scratch_shapes=rest
        + [
            pltpu.SemaphoreType.DMA((half // chunk,)),
            rest_sems,
            pltpu.SemaphoreType.DMA((4,)),
        ],
        **hints,
    )(x, *in_hbm(w_gate, w_down))


def fill_acted(chunk, part_refs, acted_ref):
    def piece(i):
        at = pl.ds(pl.multiple_of(i * chunk, chunk), chunk)
        total = part_refs[0][:, at].astype(F32)
        for ref in part_refs[1:]:
            total = total + ref[:, at].astype(F32)
        acted_ref[:, at] = (total * jax.nn.sigmoid(total)).astype(BF16)

    pl.loop(0, acted_ref.shape[1] // chunk)(piece)


def down_kernel(chunk, *refs):
    part_refs, w_ref, kept_ref, out_ref, acted_ref, held_ref, sems = refs[:-6], *refs[-6:]
    start = kept_ref.shape[1]
    wide = math.gcd(512, start)

    def product(from_ref, offset, width):
        def use(i):
            at = pl.ds(pl.multiple_of(i * width, width), width)
            to = pl.ds(pl.multiple_of(offset + i * width, math.gcd(offset, width)), width)
            out_ref[:, to] = dot(acted_ref[...], from_ref[:, at]).astype(out_ref.dtype)

        return use

    def begin():
        fill_acted(math.gcd(512, acted_ref.shape[1]), part_refs, acted_ref)
        pl.loop(0, start // wide)(product(kept_ref, 0, wide))

    streamed(
        chunk_copy(w_ref.at[:, start:], held_ref, sems, 1, chunk),
        product(held_ref, start, chunk),
        begin,
    )


def down(parts, w_down, kept, dtype):
    rows, amount = parts[0].shape
    features = w_down.shape[1]
    rest = features - kept.shape[1]
    chunk = math.gcd(256, rest)
    return pl.pallas_call(
        functools.partial(down_kernel, chunk),
        in_specs=[INSIDE] * len(parts) + [ANYWHERE, INSIDE],
        out_specs=INSIDE,
        out_shape=jax.ShapeDtypeStruct((rows, features), dtype),
        scratch_shapes=[
            pltpu.VMEM((rows, amount), BF16),
            pltpu.VMEM((amount, rest), BF16),
            pltpu.SemaphoreType.DMA((rest // chunk,)),
        ],
        compiler_params=params(22),
        cost_estimate=cost(2 * rows * features * amount, features * amount * 2),
        name="down",
    )(*parts, *in_hbm(w_down), kept)


def unpack_kernel(pack, arrived_ref, out_ref):
    main, extra, cuts, width = pack
    sources = arrived_ref.shape[0]
    features = out_ref.shape[1]
    out_ref[: sources * main] = arrived_ref[:, :, :features].reshape(sources * main, features)
    if extra:
        folded = arrived_ref[:, :, features:].reshape(sources * main, width)
        shape = (sources * extra, sources * main)
        for c in range(cuts):
            pick = (iota(shape, 1) == iota(shape, 0) * cuts + c).astype(BF16)
            out_ref[sources * main :, c * width : (c + 1) * width] = dot(pick, folded).astype(BF16)


def unpack(arrived, features, pack):
    main, extra, _, _ = pack
    rows = arrived.shape[0] * (main + extra)
    return pl.pallas_call(
        functools.partial(unpack_kernel, pack),
        out_shape=jax.ShapeDtypeStruct((rows, features), BF16),
        compiler_params=params(24),
        cost_estimate=cost(arrived.size * 16, arrived.size * 4),
        name="unpack",
    )(arrived)


def pack_kernel(pack, *refs):
    main, extra, cuts, width = pack
    part_refs, out_ref = refs[:-1], refs[-1]
    sources = out_ref.shape[0]
    features = part_refs[0].shape[1]
    first = sources * main

    def total(rows, columns):
        value = part_refs[0][rows, columns].astype(F32)
        for ref in part_refs[1:]:
            value = value + ref[rows, columns].astype(F32)
        return value.astype(BF16)

    made = total(slice(0, first), slice(0, features))
    out_ref[:, :, :features] = made.reshape(sources, main, features)
    if extra:
        shape = (sources * main, sources * extra)
        folded = None
        for c in range(cuts):
            piece = total(slice(first, None), slice(c * width, (c + 1) * width))
            pick = (iota(shape, 0) == iota(shape, 1) * cuts + c).astype(BF16)
            part = dot(pick, piece)
            folded = part if folded is None else folded + part
        out_ref[:, :, features:] = folded.astype(BF16).reshape(sources, main, width)


def pack_sum(parts, sources, pack):
    main, _, _, width = pack
    features = parts[0].shape[1]
    return pl.pallas_call(
        functools.partial(pack_kernel, pack),
        out_shape=jax.ShapeDtypeStruct((sources, main, features + width), BF16),
        compiler_params=params(24),
        cost_estimate=cost(parts[0].size * 16, parts[0].size * 8),
        name="pack_sum",
    )(*parts)


def combine_kernel(pack, back_ref, main_ref, extra_ref, gates_ref, out_ref):
    main, extra, cuts, width = pack
    sources = back_ref.shape[0]
    tokens, features = out_ref.shape
    back = back_ref[:, :, :features].reshape(sources * main, features)
    folded = back_ref[:, :, features:].reshape(sources * main, width) if extra else None
    total = None
    for k in range(2):
        rows = dot(main_ref[k], back)
        if extra:
            chosen = extra_ref[k]
            at = iota(chosen.shape, 1) % cuts
            pieces = [
                dot(jnp.where(at == c, chosen, jnp.zeros_like(chosen)), folded) for c in range(cuts)
            ]
            rows = rows + jnp.concatenate(pieces, axis=1)
        weighed = rows * gates_ref[k][:, :1]
        total = weighed if total is None else total + weighed
    out_ref[...] = total.astype(BF16)


def combine(back, weights, tokens, features, pack):
    return pl.pallas_call(
        functools.partial(combine_kernel, pack),
        out_shape=jax.ShapeDtypeStruct((tokens, features), BF16),
        compiler_params=params(40),
        cost_estimate=cost(4 * tokens * back.size, back.size * 2),
        name="combine",
    )(back, *weights)


def spread_states(values, spread_ref):
    for t in range(spread_ref.shape[0]):
        spread_ref[t] = jnp.broadcast_to(values[:, t : t + 1], spread_ref.shape[1:])


def row_sums(parts):
    place = iota(parts[0].shape, 0)
    for stride in (4, 2, 1):
        low = place & stride == 0
        half = len(parts) // 2
        joined = []
        for a, b in zip(parts[:half], parts[half:]):
            kept = jnp.where(low, a, b)
            moved = jnp.where(low, b, a)
            if stride == 4:
                other = pltpu.roll(moved, 4, 0)
            else:
                other = jnp.where(low, pltpu.roll(moved, 8 - stride, 0), pltpu.roll(moved, stride, 0))
            joined.append(kept + other)
        parts = joined
    return parts[0]


def state_sum(value):
    total = value[:8]
    for at in range(8, value.shape[0], 8):
        total = total + value[at : at + 8]
    return total


def tiled_lanes(value, lanes):
    return jnp.concatenate([value] * (lanes // value.shape[1]), axis=1)


def scan_kernel(
    x_ref, edge_ref, low_ref, dtw_ref, dtb_ref, alog_ref, cw_ref, cb_ref, skip_ref, bc_ref,
    read_ref, cum_ref, ends_ref, padded, delta_ref, fed_ref, totals_ref, b_ref, c_ref,
):
    tokens, lanes = x_ref.shape
    taps = cw_ref.shape[0]
    states = alog_ref.shape[0]

    @pl.when(pl.program_id(0) == 0)
    def _():
        spread_states(bc_ref[0], b_ref)
        spread_states(bc_ref[1], c_ref)
        totals_ref[...] = jnp.zeros_like(totals_ref)

    padded[8:] = x_ref[...].astype(F32)
    padded[8 - (taps - 1) : 8] = edge_ref[...].astype(F32)
    conv = jnp.broadcast_to(cb_ref[...], (tokens, lanes))
    for k in range(taps):
        at = 8 - (taps - 1) + k
        conv = conv + cw_ref[k : k + 1] * padded[at : at + tokens]
    act = conv * jax.nn.sigmoid(conv)
    raw = dot(low_ref[...], dtw_ref[...]) + dtb_ref[...]
    delta = jnp.maximum(raw, 0.0) + jnp.log1p(jnp.exp(-jnp.abs(raw)))
    delta_ref[...] = delta
    fed_ref[...] = delta * act
    read_ref[...] = skip_ref[...] * act
    rates = -jnp.exp(alog_ref[...]) * LOG2E

    def eight(g, carry):
        state, running = carry
        at = pl.multiple_of(g * 8, 8)
        delta8 = delta_ref[pl.ds(at, 8)]
        fed8 = fed_ref[pl.ds(at, 8)]
        reads, sums = [], []
        for i in range(8):
            step = delta8[i : i + 1]
            running = running + step
            factor = jnp.exp2(rates * step)
            state = factor * state + tiled_lanes(b_ref[at + i], lanes) * fed8[i : i + 1]
            reads.append(state_sum(tiled_lanes(c_ref[at + i], lanes) * state))
            sums.append(running)
        read_ref[pl.ds(at, 8)] += row_sums(reads)
        cum_ref[pl.ds(at, 8)] = jnp.concatenate(sums, axis=0)
        return state, running

    state, running = lax.fori_loop(
        0, tokens // 8, eight, (jnp.zeros((states, lanes), F32), jnp.zeros((1, lanes), F32))
    )
    step, steps = pl.program_id(0), pl.num_programs(0)
    ends_ref[:, pl.ds(pl.multiple_of(step * lanes, lanes), lanes)] = state.astype(BF16)
    high = running.astype(BF16).astype(F32)
    totals_ref[pl.ds(step, 1)] = high
    totals_ref[pl.ds(steps + step, 1)] = running - high

    @pl.when(step == steps - 1)
    def _():
        ends_ref[:, ends_ref.shape[1] - lanes :] = totals_ref[...].astype(BF16)


def scan(x_in, edge, dt_low, dt_weight, dt_bias, a_log, conv_weight, conv_bias, d_skip, b_and_c):
    tokens, channels = x_in.shape
    states = a_log.shape[0]
    lanes = math.gcd(512, channels)

    def cut(rows):
        return pl.BlockSpec((rows, lanes), lambda i: (0, i))

    def whole(a):
        zeros = (0,) * a.ndim
        return pl.BlockSpec(a.shape, lambda i: zeros)

    return pl.pallas_call(
        scan_kernel,
        grid=(channels // lanes,),
        in_specs=[
            cut(tokens), cut(edge.shape[0]), whole(dt_low), cut(dt_weight.shape[0]), cut(1),
            cut(states), cut(conv_weight.shape[0]), cut(1), cut(1), whole(b_and_c),
        ],
        out_specs=(
            cut(tokens),
            cut(tokens),
            pl.BlockSpec((states, channels + lanes), lambda i: (0, 0)),
        ),
        out_shape=(
            pltpu.HBM((tokens, channels), F32),
            pltpu.HBM((tokens, channels), F32),
            jax.ShapeDtypeStruct((states, channels + lanes), BF16),
        ),
        scratch_shapes=[
            pltpu.VMEM((tokens + 8, lanes), F32),
            pltpu.VMEM((tokens, lanes), F32),
            pltpu.VMEM((tokens, lanes), F32),
            pltpu.VMEM((states, lanes), F32),
            pltpu.VMEM((tokens, states, 128), F32),
            pltpu.VMEM((tokens, states, 128), F32),
        ],
        compiler_params=params(40),
        cost_estimate=cost(
            tokens * channels * states * 8, tokens * channels * 12, tokens * channels * states
        ),
        name="scan",
    )(
        *in_hbm(x_in),
        edge,
        *in_hbm(
            dt_low, dt_weight, dt_bias[None], a_log, conv_weight, conv_bias[None], d_skip[None],
            b_and_c,
        ),
    )


def upper_half(step):
    return (lax.axis_index("seq") >> step) % 2 == 1


def link_kernel(step, *refs):
    total_ref, received_ref, alog_ref, prefix_ref = refs[:4] if step else (*refs[:3], None)
    total_out, prefix_out = refs[-2:]
    channels = alog_ref.shape[1]
    lanes = total_ref.shape[1] - channels
    steps = channels // lanes
    upper = upper_half(step)

    def sizes(ref):
        value = ref[:, channels:].astype(F32)
        return value[:steps] + value[steps : 2 * steps]

    def put_sizes(ref, value):
        high = value.astype(BF16).astype(F32)
        rest = jnp.zeros((ref.shape[0] - 2 * steps, lanes), F32)
        parts = [high, value - high] + ([rest] if rest.shape[0] else [])
        ref[:, channels:] = jnp.concatenate(parts, axis=0).astype(BF16)

    own, received = sizes(total_ref), sizes(received_ref)
    before = sizes(prefix_ref) if step else jnp.zeros_like(own)
    later = jnp.where(upper, own, received)
    put_sizes(total_out, own + received)
    put_sizes(prefix_out, before + jnp.where(upper, received, 0.0))
    for i in range(steps):
        at = slice(i * lanes, (i + 1) * lanes)
        rates = -jnp.exp(alog_ref[:, at]) * LOG2E
        mine, theirs = total_ref[:, at].astype(F32), received_ref[:, at].astype(F32)
        last, first = jnp.where(upper, mine, theirs), jnp.where(upper, theirs, mine)
        total_out[:, at] = (last + jnp.exp2(rates * later[i : i + 1]) * first).astype(BF16)
        if step:
            prefix = prefix_ref[:, at].astype(F32)
            further = prefix + jnp.exp2(rates * before[i : i + 1]) * theirs
        else:
            prefix, further = jnp.zeros_like(theirs), theirs
        prefix_out[:, at] = jnp.where(upper, further, prefix).astype(BF16)


def link(step, total, received, a_log, prefix):
    shape = jax.ShapeDtypeStruct(total.shape, BF16)
    args = [total, received, a_log] + ([prefix] if step else [])
    return pl.pallas_call(
        functools.partial(link_kernel, step),
        out_shape=(shape, shape),
        compiler_params=params(16),
        cost_estimate=cost(total.size * 2, total.size * 6),
        name="link",
    )(*args)


def finish_kernel(
    step, read_ref, cum_ref, z_ref, alog_ref, bc_ref, prefix_ref, *refs
):
    others, sizes, (out_ref, sum_ref, wide_ref, c_ref) = refs[:3], refs[3:7], refs[7:]
    tokens, lanes = z_ref.shape
    states = alog_ref.shape[0]
    at, steps = pl.program_id(0), pl.num_programs(0)

    @pl.when(at == 0)
    def _():
        spread_states(bc_ref[1], c_ref)
        for i, ref in enumerate(sizes):
            wide_ref[i * states : (i + 1) * states] = ref[...].astype(F32)

    rates = -jnp.exp(alog_ref[...]) * LOG2E

    def decay(i):
        row = i * states + at
        return jnp.exp2(rates * (wide_ref[pl.ds(row, 1)] + wide_ref[pl.ds(row + steps, 1)]))

    mine = lax.axis_index("seq") >> step
    ends = [ref[...].astype(F32) for ref in others]
    decays = [decay(i + 1) for i in range(3)]
    entering = jnp.zeros((states, lanes), F32)
    for group in range(3):
        partner = mine ^ group

        def chosen(values):
            return jnp.where(partner == 1, values[0], jnp.where(partner == 2, values[1], values[2]))

        further = chosen(decays) * entering + chosen(ends)
        entering = jnp.where(group < mine, further, entering)
    entering = prefix_ref[...].astype(F32) + decay(0) * entering

    def eight(g, carry):
        at = pl.multiple_of(g * 8, 8)
        cum8 = cum_ref[pl.ds(at, 8)]
        reads = []
        for i in range(8):
            kept = jnp.exp2(rates * cum8[i : i + 1]) * entering
            reads.append(state_sum(tiled_lanes(c_ref[at + i], lanes) * kept))
        sum_ref[pl.ds(at, 8)] = row_sums(reads)
        return carry

    lax.fori_loop(0, tokens // 8, eight, 0)
    z = z_ref[...].astype(F32)
    out_ref[...] = ((read_ref[...] + sum_ref[...]) * (z * jax.nn.sigmoid(z))).astype(BF16)


def finish(step, read, cum, z_gate, prefix, others, a_log, b_and_c):
    tokens, channels = z_gate.shape
    states = a_log.shape[0]
    lanes = prefix.shape[1] - channels

    def cut(rows):
        return pl.BlockSpec((rows, lanes), lambda i: (0, i))

    sizes = pl.BlockSpec((states, lanes), lambda i: (0, channels // lanes))
    return pl.pallas_call(
        functools.partial(finish_kernel, step),
        grid=(channels // lanes,),
        in_specs=[
            cut(tokens), cut(tokens), cut(tokens), cut(states),
            pl.BlockSpec(b_and_c.shape, lambda i: (0, 0, 0)),
            *[cut(states)] * 4,
            *[sizes] * 4,
        ],
        out_specs=cut(tokens),
        out_shape=jax.ShapeDtypeStruct((tokens, channels), BF16),
        scratch_shapes=[
            pltpu.VMEM((tokens, lanes), F32),
            pltpu.VMEM((4 * states, lanes), F32),
            pltpu.VMEM((tokens, states, 128), F32),
        ],
        compiler_params=params(40),
        cost_estimate=cost(
            tokens * channels * states * 5, tokens * channels * 12, tokens * channels * states
        ),
        name="finish",
    )(*in_hbm(read, cum, z_gate, a_log, b_and_c), *[prefix, *others] * 2)


def swapped(value, by):
    count = lax.axis_size("seq")
    return lax.ppermute(value, "seq", [(i, i ^ by) for i in range(count)])


def turned(value, axis, by):
    count = lax.axis_size(axis)
    return lax.ppermute(value, axis, [(i, (i + by) % count) for i in range(count)])


def turned_within(value, copies, by):
    count = lax.axis_size("seq")
    return lax.ppermute(
        value, "seq", [(i, i // copies * copies + (i + by) % copies) for i in range(count)]
    )


def exchanged(value, copies):
    count = lax.axis_size("seq")
    groups = [list(range(m, count, copies)) for m in range(copies)]
    return lax.all_to_all(
        value, "seq", split_axis=0, concat_axis=0, tiled=True, axis_index_groups=groups
    )


def after(value, *others):
    return lax.optimization_barrier((value, others))[0]


def local(
    x_in,
    z_gate,
    dt_low,
    dt_weight,
    dt_bias,
    a_log,
    conv_weight,
    conv_bias,
    d_skip,
    b_and_c,
    hidden,
    router,
    expert_ids,
    w_gate,
    w_down,
):
    blocks = lax.axis_size("seq")
    feature_parts = lax.axis_size("exp")
    tokens, features = hidden.shape
    experts = router.shape[1]
    copies = blocks // experts
    pack = packing(features)
    ids = expert_ids.T

    edge = x_in[tokens - (conv_weight.shape[0] - 1) :]
    edge = lax.ppermute(edge, "seq", [(i, i + 1) for i in range(blocks - 1)])
    outgoing, logits = route(ids, hidden, router.T, 1, pack)
    outgoing = after(outgoing, edge)
    arrived = exchanged(outgoing.reshape((experts,) + outgoing.shape[2:]), copies)

    read, cum, ends = scan(
        x_in, edge, dt_low, dt_weight, dt_bias, a_log, conv_weight, conv_bias, d_skip, b_and_c
    )
    logits = [logits] + [turned(logits, "exp", d) for d in range(1, feature_parts)]
    arrived = after(arrived, ends, *logits)

    steps = blocks.bit_length() - 3
    total, prefix, received, step = ends, None, None, 0

    def advance(*marks):
        nonlocal total, prefix, received, step
        if step < steps:
            total, prefix = link(step, total, after(received, *marks), a_log, prefix)
            step += 1
            if step < steps:
                received = swapped(total, 1 << step)
            else:
                received = [swapped(total, q << step) for q in (1, 2, 3)]
        return prefix

    rows = [unpack(arrived, features, pack)]
    for d in range(1, copies):
        rows.append(turned_within(rows[0], copies, d))
    gated = []
    for part in rows:
        if gated:
            part = after(part, gated[-1][0])
            own = gate(part, w_gate, w_down, kept)
        else:
            own, kept, kept_down = gate(part, w_gate, w_down)
            own, received = after((own, ends), *rows[1:])
            received = swapped(received, 1)
        if len(gated) == copies - 1:
            own = after(own, advance(own), *(p for parts in gated for p in parts[1:]))
        gated.append([own] + [turned(own, "exp", d) for d in range(1, feature_parts)])
    made = []
    for parts in gated[1:] + gated[:1]:
        product = down(parts, w_down, kept_down, BF16 if len(made) < copies - 1 else F32)
        if not made:
            product = after(product, advance(product))
        made.append(product)
    while step < steps:
        advance()
    sums = made[-1:]
    for d in range(1, copies):
        sums.append(turned_within(made[d - 1], copies, -d))
    packed = after(pack_sum(sums, experts, pack), *received)
    back = exchanged(packed, copies)

    weights = blend_weights(ids, after(tuple(logits), packed), 1, pack)
    received = after(tuple(received), packed)
    mamba_out = finish(step, read, cum, z_gate, prefix, received, a_log, b_and_c)
    back = after(back, mamba_out)
    moe_out = combine(back, weights, tokens, features, pack)
    return mamba_out, moe_out


def solution(mesh):
    return jax.shard_map(
        local,
        mesh=mesh,
        in_specs=(
            P("seq", "exp"),
            P("seq", "exp"),
            P("seq", None),
            P(None, "exp"),
            P("exp"),
            P(None, "exp"),
            P(None, "exp"),
            P("exp"),
            P("exp"),
            P(None, None, "seq"),
            P("seq", "exp"),
            P("exp", None),
            P("seq", None),
            P("exp", "seq"),
            P("seq", "exp"),
        ),
        out_specs=(P("seq", "exp"), P("seq", "exp")),
        check_vma=False,
    )
```

```python
import functools
import math

import jax
import jax.numpy as jnp
from jax import lax
from jax.experimental import pallas as pl
from jax.experimental.pallas import tpu as pltpu
from jax.sharding import PartitionSpec as P

CAP = 18
MIB = 1 << 20
LOG2E = math.log2(math.e)
F32 = jnp.float32
BF16 = jnp.bfloat16


def params(limit):
    return pltpu.CompilerParams(vmem_limit_bytes=limit * MIB)


def cost(flops, moved, transcendentals=0):
    return pl.CostEstimate(
        flops=int(flops), bytes_accessed=int(moved), transcendentals=int(transcendentals)
    )


def in_hbm(*arrays):
    return [pltpu.with_memory_space_constraint(a, pltpu.HBM) for a in arrays]


def iota(shape, dim):
    return lax.broadcasted_iota(jnp.int32, shape, dim)


def dot(a, b):
    return jnp.dot(a, b, preferred_element_type=F32)


def dot_nt(a, b):
    return lax.dot_general(a, b, (((1,), (1,)), ((), ())), preferred_element_type=F32)


def packing(features):
    main = CAP // 16 * 16
    extra = CAP - main
    cuts = main // extra if extra and main % extra == 0 else 0
    if cuts and features % (cuts * 128) == 0:
        return main, extra, cuts, features // cuts
    return -(-CAP // 16) * 16, 0, 0, 0


def hits_and_slots(ids, experts):
    tokens = ids.shape[1]
    of = iota((experts, tokens), 0)
    hits = [(of == ids[k : k + 1]).astype(F32) for k in range(2)]
    before = (iota((tokens, tokens), 0) < iota((tokens, tokens), 1)).astype(BF16)
    earlier = dot((hits[0] + hits[1]).astype(BF16), before)
    slots = [jnp.sum(h * earlier, axis=0, keepdims=True).astype(jnp.int32) for h in hits]
    return hits, slots


def route_kernel(pack, ids_ref, hidden_ref, router_ref, out_ref, logits_ref):
    main, extra, cuts, width = pack
    experts, copies = out_ref.shape[:2]
    tokens, features = hidden_ref.shape
    ids = ids_ref[...]
    _, slots = hits_and_slots(ids, experts)
    hidden = hidden_ref[...]
    row = iota((experts * main, tokens), 0)
    picked = None
    for k in range(2):
        key = jnp.where(slots[k] < main, ids[k : k + 1] * main + slots[k], -1)
        hit = row == key
        picked = hit if picked is None else picked | hit
    packed = dot(picked.astype(BF16), hidden).astype(BF16)
    for e in range(experts):
        for m in range(copies):
            out_ref[e, m, :, :features] = packed[e * main : (e + 1) * main]
    if extra:
        picked = None
        for k in range(2):
            key = jnp.where(slots[k] >= main, ids[k : k + 1] * extra + slots[k] - main, -1)
            hit = row // cuts == key
            picked = hit if picked is None else picked | hit
        total = None
        for c in range(cuts):
            chosen = (picked & (row % cuts == c)).astype(BF16)
            part = dot(chosen, hidden[:, c * width : (c + 1) * width])
            total = part if total is None else total + part
        total = total.astype(BF16)
        for e in range(experts):
            for m in range(copies):
                out_ref[e, m, :, features:] = total[e * main : (e + 1) * main]
    logits_ref[...] = dot_nt(hidden, router_ref[...])


def route(ids, hidden, router, copies, pack):
    main, _, _, width = pack
    tokens, features = hidden.shape
    experts = router.shape[0]
    return pl.pallas_call(
        functools.partial(route_kernel, pack),
        out_shape=(
            jax.ShapeDtypeStruct((experts, copies, main, features + width), BF16),
            jax.ShapeDtypeStruct((tokens, experts), F32),
        ),
        compiler_params=params(40),
        cost_estimate=cost(2 * tokens * experts * main * features * 2, hidden.size * 8),
        name="route",
    )(*in_hbm(ids, hidden, router))


def weights_kernel(pack, copies, ids_ref, *refs):
    logits_refs, (main_ref, extra_ref, gates_ref) = refs[:-3], refs[-3:]
    main, extra, cuts, _ = pack
    tokens, experts = logits_refs[0].shape
    ids = ids_ref[...]
    hits, slots = hits_and_slots(ids, experts)
    eye = (iota((tokens, tokens), 0) == iota((tokens, tokens), 1)).astype(BF16)
    logits = logits_refs[0][...]
    for ref in logits_refs[1:]:
        logits = logits + ref[...]
    columns = [dot_nt(eye, h.astype(BF16)) for h in hits]
    picked = [jnp.sum(c * logits, axis=1, keepdims=True) for c in columns]
    expert = iota((tokens, experts), 1).astype(F32)
    total = experts * copies * main
    col = iota((tokens, total), 1)
    for k in range(2):
        gate = jax.nn.sigmoid(picked[k] - picked[1 - k])
        gates_ref[k] = jnp.broadcast_to(gate, gates_ref.shape[1:])
        named = jnp.sum(columns[k] * expert, axis=1, keepdims=True).astype(jnp.int32)
        wide = jnp.broadcast_to(slots[k].astype(F32), (8, tokens)).astype(BF16)
        slot = dot_nt(eye, wide)[:, :1].astype(jnp.int32)
        mine = col // (copies * main) == named
        main_ref[k] = (mine & (col % main == slot)).astype(BF16)
        if extra:
            place = (col % main) // cuts + main
            extra_ref[k] = (mine & (place == slot)).astype(BF16)
        else:
            extra_ref[k] = jnp.zeros(extra_ref.shape[1:], BF16)


def blend_weights(ids, logits, copies, pack):
    tokens, experts = logits[0].shape
    total = experts * copies * pack[0]
    return pl.pallas_call(
        functools.partial(weights_kernel, pack, copies),
        out_shape=(
            jax.ShapeDtypeStruct((2, tokens, total), BF16),
            jax.ShapeDtypeStruct((2, tokens, total), BF16),
            jax.ShapeDtypeStruct((2, tokens, 128), F32),
        ),
        compiler_params=params(40),
        cost_estimate=cost(2 * tokens * total * 16, tokens * total * 8),
        name="blend_weights",
    )(*in_hbm(ids), *logits)


ANYWHERE = pl.BlockSpec(memory_space=pl.ANY)
INSIDE = pl.BlockSpec(memory_space=pltpu.VMEM)
AHEAD = 6


def chunk_copy(from_ref, to_ref, sems, dim, chunk):
    def copy(i):
        at = pl.ds(pl.multiple_of(i * chunk, chunk), chunk)
        part = (slice(None), at) if dim else (at, slice(None))
        return pltpu.make_async_copy(from_ref.at[part], to_ref.at[part], sems.at[i])

    return copy, from_ref.shape[dim] // chunk


def streamed(stream, use, begin=None, begun=False, follow=None):
    copy, count = stream
    if not begun:
        for i in range(min(AHEAD, count)):
            copy(i).start()
    if begin is not None:
        begin()

    def step(i, carry):
        copy(i).wait()

        @pl.when(i + AHEAD < count)
        def _():
            copy(i + AHEAD).start()

        if follow is not None:
            later = i - max(count - AHEAD, 0)

            @pl.when((later >= 0) & (later < follow[1]))
            def _():
                follow[0](later).start()

        use(i)
        return carry

    lax.fori_loop(0, count, step, 0)


def gate_first_kernel(
    chunk, x_ref, w_ref, down_ref, out_ref, kept_ref, kept_down_ref, held_ref, kept_sems, sems, down_sems
):
    start, columns = kept_ref.shape[1], kept_down_ref.shape[1]
    one = chunk_copy(w_ref.at[:, :start], kept_ref, kept_sems, 1, chunk)
    two = chunk_copy(w_ref.at[:, start:], held_ref, sems, 1, chunk)
    copy, count = chunk_copy(
        down_ref.at[:, :columns], kept_down_ref, down_sems, 0, kept_down_ref.shape[0] // down_sems.shape[0]
    )
    streamed(one, gate_product(chunk, x_ref, kept_ref, out_ref, 0), follow=two)
    started = min(AHEAD, one[1])
    for i in range(started, min(AHEAD, two[1])):
        two[0](i).start()
    for i in range(count):
        copy(i).start()
    streamed(two, gate_product(chunk, x_ref, held_ref, out_ref, start), begun=True)
    for i in range(count):
        copy(i).wait()


def gate_product(chunk, x_ref, from_ref, out_ref, offset):
    def use(i):
        at = pl.ds(pl.multiple_of(i * chunk, chunk), chunk)
        to = pl.ds(pl.multiple_of(offset + i * chunk, chunk), chunk)
        out_ref[:, to] = dot(x_ref[...], from_ref[:, at]).astype(BF16)

    return use


def gate_next_kernel(chunk, x_ref, w_ref, kept_ref, out_ref, held_ref, sems):
    start = kept_ref.shape[1]
    kept = gate_product(chunk, x_ref, kept_ref, out_ref, 0)
    streamed(
        chunk_copy(w_ref.at[:, start:], held_ref, sems, 1, chunk),
        gate_product(chunk, x_ref, held_ref, out_ref, start),
        lambda: pl.loop(0, start // chunk)(kept),
    )


def gate(x, w_gate, w_down, kept=None):
    rows, features = x.shape
    amount = w_gate.shape[1]
    chunk = math.gcd(512, amount)
    half = amount // chunk // 2 * chunk
    out = jax.ShapeDtypeStruct((rows, amount), BF16)
    rest = [pltpu.VMEM((features, amount - half), BF16)]
    rest_sems = pltpu.SemaphoreType.DMA(((amount - half) // chunk,))
    hints = dict(
        compiler_params=params(20),
        cost_estimate=cost(2 * rows * features * amount, features * amount * 2),
        name="gate",
    )
    if kept is not None:
        return pl.pallas_call(
            functools.partial(gate_next_kernel, chunk),
            in_specs=[INSIDE, ANYWHERE, INSIDE],
            out_specs=INSIDE,
            out_shape=out,
            scratch_shapes=rest + [rest_sems],
            **hints,
        )(x, *in_hbm(w_gate), kept)
    return pl.pallas_call(
        functools.partial(gate_first_kernel, chunk),
        in_specs=[INSIDE, ANYWHERE, ANYWHERE],
        out_specs=(INSIDE, INSIDE, INSIDE),
        out_shape=(
            out,
            jax.ShapeDtypeStruct((features, half), BF16),
            jax.ShapeDtypeStruct((w_down.shape[0], w_down.shape[1] // 2), BF16),
        ),
        scratch_shapes=rest
        + [
            pltpu.SemaphoreType.DMA((half // chunk,)),
            rest_sems,
            pltpu.SemaphoreType.DMA((4,)),
        ],
        **hints,
    )(x, *in_hbm(w_gate, w_down))


def fill_acted(chunk, part_refs, acted_ref):
    def piece(i):
        at = pl.ds(pl.multiple_of(i * chunk, chunk), chunk)
        total = part_refs[0][:, at].astype(F32)
        for ref in part_refs[1:]:
            total = total + ref[:, at].astype(F32)
        acted_ref[:, at] = (total * jax.nn.sigmoid(total)).astype(BF16)

    pl.loop(0, acted_ref.shape[1] // chunk)(piece)


def down_kernel(chunk, *refs):
    part_refs, w_ref, kept_ref, out_ref, acted_ref, held_ref, sems = refs[:-6], *refs[-6:]
    start = kept_ref.shape[1]
    wide = math.gcd(512, start)

    def product(from_ref, offset, width):
        def use(i):
            at = pl.ds(pl.multiple_of(i * width, width), width)
            to = pl.ds(pl.multiple_of(offset + i * width, math.gcd(offset, width)), width)
            out_ref[:, to] = dot(acted_ref[...], from_ref[:, at]).astype(out_ref.dtype)

        return use

    def begin():
        fill_acted(math.gcd(512, acted_ref.shape[1]), part_refs, acted_ref)
        pl.loop(0, start // wide)(product(kept_ref, 0, wide))

    streamed(
        chunk_copy(w_ref.at[:, start:], held_ref, sems, 1, chunk),
        product(held_ref, start, chunk),
        begin,
    )


def down(parts, w_down, kept, dtype):
    rows, amount = parts[0].shape
    features = w_down.shape[1]
    rest = features - kept.shape[1]
    chunk = math.gcd(256, rest)
    return pl.pallas_call(
        functools.partial(down_kernel, chunk),
        in_specs=[INSIDE] * len(parts) + [ANYWHERE, INSIDE],
        out_specs=INSIDE,
        out_shape=jax.ShapeDtypeStruct((rows, features), dtype),
        scratch_shapes=[
            pltpu.VMEM((rows, amount), BF16),
            pltpu.VMEM((amount, rest), BF16),
            pltpu.SemaphoreType.DMA((rest // chunk,)),
        ],
        compiler_params=params(22),
        cost_estimate=cost(2 * rows * features * amount, features * amount * 2),
        name="down",
    )(*parts, *in_hbm(w_down), kept)


def unpack_kernel(pack, arrived_ref, out_ref):
    main, extra, cuts, width = pack
    sources = arrived_ref.shape[0]
    features = out_ref.shape[1]
    out_ref[: sources * main] = arrived_ref[:, :, :features].reshape(sources * main, features)
    if extra:
        folded = arrived_ref[:, :, features:].reshape(sources * main, width)
        shape = (sources * extra, sources * main)
        for c in range(cuts):
            pick = (iota(shape, 1) == iota(shape, 0) * cuts + c).astype(BF16)
            out_ref[sources * main :, c * width : (c + 1) * width] = dot(pick, folded).astype(BF16)


def unpack(arrived, features, pack):
    main, extra, _, _ = pack
    rows = arrived.shape[0] * (main + extra)
    return pl.pallas_call(
        functools.partial(unpack_kernel, pack),
        out_shape=jax.ShapeDtypeStruct((rows, features), BF16),
        compiler_params=params(24),
        cost_estimate=cost(arrived.size * 16, arrived.size * 4),
        name="unpack",
    )(arrived)


def pack_kernel(pack, *refs):
    main, extra, cuts, width = pack
    part_refs, out_ref = refs[:-1], refs[-1]
    sources = out_ref.shape[0]
    features = part_refs[0].shape[1]
    first = sources * main

    def total(rows, columns):
        value = part_refs[0][rows, columns].astype(F32)
        for ref in part_refs[1:]:
            value = value + ref[rows, columns].astype(F32)
        return value.astype(BF16)

    made = total(slice(0, first), slice(0, features))
    out_ref[:, :, :features] = made.reshape(sources, main, features)
    if extra:
        shape = (sources * main, sources * extra)
        folded = None
        for c in range(cuts):
            piece = total(slice(first, None), slice(c * width, (c + 1) * width))
            pick = (iota(shape, 0) == iota(shape, 1) * cuts + c).astype(BF16)
            part = dot(pick, piece)
            folded = part if folded is None else folded + part
        out_ref[:, :, features:] = folded.astype(BF16).reshape(sources, main, width)


def pack_sum(parts, sources, pack):
    main, _, _, width = pack
    features = parts[0].shape[1]
    return pl.pallas_call(
        functools.partial(pack_kernel, pack),
        out_shape=jax.ShapeDtypeStruct((sources, main, features + width), BF16),
        compiler_params=params(24),
        cost_estimate=cost(parts[0].size * 16, parts[0].size * 8),
        name="pack_sum",
    )(*parts)


def combine_kernel(pack, back_ref, main_ref, extra_ref, gates_ref, out_ref):
    main, extra, cuts, width = pack
    sources = back_ref.shape[0]
    tokens, features = out_ref.shape
    back = back_ref[:, :, :features].reshape(sources * main, features)
    folded = back_ref[:, :, features:].reshape(sources * main, width) if extra else None
    total = None
    for k in range(2):
        rows = dot(main_ref[k], back)
        if extra:
            chosen = extra_ref[k]
            at = iota(chosen.shape, 1) % cuts
            pieces = [
                dot(jnp.where(at == c, chosen, jnp.zeros_like(chosen)), folded) for c in range(cuts)
            ]
            rows = rows + jnp.concatenate(pieces, axis=1)
        weighed = rows * gates_ref[k][:, :1]
        total = weighed if total is None else total + weighed
    out_ref[...] = total.astype(BF16)


def combine(back, weights, tokens, features, pack):
    return pl.pallas_call(
        functools.partial(combine_kernel, pack),
        out_shape=jax.ShapeDtypeStruct((tokens, features), BF16),
        compiler_params=params(40),
        cost_estimate=cost(4 * tokens * back.size, back.size * 2),
        name="combine",
    )(back, *weights)


def spread_states(values, spread_ref):
    for t in range(spread_ref.shape[0]):
        spread_ref[t] = jnp.broadcast_to(values[:, t : t + 1], spread_ref.shape[1:])


def row_sums(parts):
    place = iota(parts[0].shape, 0)
    for stride in (4, 2, 1):
        low = place & stride == 0
        half = len(parts) // 2
        joined = []
        for a, b in zip(parts[:half], parts[half:]):
            kept = jnp.where(low, a, b)
            moved = jnp.where(low, b, a)
            if stride == 4:
                other = pltpu.roll(moved, 4, 0)
            else:
                other = jnp.where(low, pltpu.roll(moved, 8 - stride, 0), pltpu.roll(moved, stride, 0))
            joined.append(kept + other)
        parts = joined
    return parts[0]


def state_sum(value):
    total = value[:8]
    for at in range(8, value.shape[0], 8):
        total = total + value[at : at + 8]
    return total


def tiled_lanes(value, lanes):
    return jnp.concatenate([value] * (lanes // value.shape[1]), axis=1)


def scan_kernel(
    x_ref, edge_ref, low_ref, dtw_ref, dtb_ref, alog_ref, cw_ref, cb_ref, skip_ref, bc_ref,
    read_ref, cum_ref, ends_ref, padded, delta_ref, fed_ref, totals_ref, b_ref, c_ref,
):
    tokens, lanes = x_ref.shape
    taps = cw_ref.shape[0]
    states = alog_ref.shape[0]

    @pl.when(pl.program_id(0) == 0)
    def _():
        spread_states(bc_ref[0], b_ref)
        spread_states(bc_ref[1], c_ref)
        totals_ref[...] = jnp.zeros_like(totals_ref)

    padded[8:] = x_ref[...].astype(F32)
    padded[8 - (taps - 1) : 8] = edge_ref[...].astype(F32)
    conv = jnp.broadcast_to(cb_ref[...], (tokens, lanes))
    for k in range(taps):
        at = 8 - (taps - 1) + k
        conv = conv + cw_ref[k : k + 1] * padded[at : at + tokens]
    act = conv * jax.nn.sigmoid(conv)
    raw = dot(low_ref[...], dtw_ref[...]) + dtb_ref[...]
    delta = jnp.maximum(raw, 0.0) + jnp.log1p(jnp.exp(-jnp.abs(raw)))
    delta_ref[...] = delta
    fed_ref[...] = delta * act
    read_ref[...] = skip_ref[...] * act
    rates = -jnp.exp(alog_ref[...]) * LOG2E

    def eight(g, carry):
        state, running = carry
        at = pl.multiple_of(g * 8, 8)
        delta8 = delta_ref[pl.ds(at, 8)]
        fed8 = fed_ref[pl.ds(at, 8)]
        reads, sums = [], []
        for i in range(8):
            step = delta8[i : i + 1]
            running = running + step
            factor = jnp.exp2(rates * step)
            state = factor * state + tiled_lanes(b_ref[at + i], lanes) * fed8[i : i + 1]
            reads.append(state_sum(tiled_lanes(c_ref[at + i], lanes) * state))
            sums.append(running)
        read_ref[pl.ds(at, 8)] += row_sums(reads)
        cum_ref[pl.ds(at, 8)] = jnp.concatenate(sums, axis=0)
        return state, running

    state, running = lax.fori_loop(
        0, tokens // 8, eight, (jnp.zeros((states, lanes), F32), jnp.zeros((1, lanes), F32))
    )
    step, steps = pl.program_id(0), pl.num_programs(0)
    ends_ref[:, pl.ds(pl.multiple_of(step * lanes, lanes), lanes)] = state.astype(BF16)
    high = running.astype(BF16).astype(F32)
    totals_ref[pl.ds(step, 1)] = high
    totals_ref[pl.ds(steps + step, 1)] = running - high

    @pl.when(step == steps - 1)
    def _():
        ends_ref[:, ends_ref.shape[1] - lanes :] = totals_ref[...].astype(BF16)


def scan(x_in, edge, dt_low, dt_weight, dt_bias, a_log, conv_weight, conv_bias, d_skip, b_and_c):
    tokens, channels = x_in.shape
    states = a_log.shape[0]
    lanes = math.gcd(512, channels)

    def cut(rows):
        return pl.BlockSpec((rows, lanes), lambda i: (0, i))

    def whole(a):
        zeros = (0,) * a.ndim
        return pl.BlockSpec(a.shape, lambda i: zeros)

    return pl.pallas_call(
        scan_kernel,
        grid=(channels // lanes,),
        in_specs=[
            cut(tokens), cut(edge.shape[0]), whole(dt_low), cut(dt_weight.shape[0]), cut(1),
            cut(states), cut(conv_weight.shape[0]), cut(1), cut(1), whole(b_and_c),
        ],
        out_specs=(
            cut(tokens),
            cut(tokens),
            pl.BlockSpec((states, channels + lanes), lambda i: (0, 0)),
        ),
        out_shape=(
            pltpu.HBM((tokens, channels), F32),
            pltpu.HBM((tokens, channels), F32),
            jax.ShapeDtypeStruct((states, channels + lanes), BF16),
        ),
        scratch_shapes=[
            pltpu.VMEM((tokens + 8, lanes), F32),
            pltpu.VMEM((tokens, lanes), F32),
            pltpu.VMEM((tokens, lanes), F32),
            pltpu.VMEM((states, lanes), F32),
            pltpu.VMEM((tokens, states, 128), F32),
            pltpu.VMEM((tokens, states, 128), F32),
        ],
        compiler_params=params(40),
        cost_estimate=cost(
            tokens * channels * states * 8, tokens * channels * 12, tokens * channels * states
        ),
        name="scan",
    )(
        *in_hbm(x_in),
        edge,
        *in_hbm(
            dt_low, dt_weight, dt_bias[None], a_log, conv_weight, conv_bias[None], d_skip[None],
            b_and_c,
        ),
    )


def upper_half(step):
    return (lax.axis_index("seq") >> step) % 2 == 1


def link_kernel(step, *refs):
    total_ref, received_ref, alog_ref, prefix_ref = refs[:4] if step else (*refs[:3], None)
    total_out, prefix_out = refs[-2:]
    channels = alog_ref.shape[1]
    lanes = total_ref.shape[1] - channels
    steps = channels // lanes
    upper = upper_half(step)

    def sizes(ref):
        value = ref[:, channels:].astype(F32)
        return value[:steps] + value[steps : 2 * steps]

    def put_sizes(ref, value):
        high = value.astype(BF16).astype(F32)
        rest = jnp.zeros((ref.shape[0] - 2 * steps, lanes), F32)
        parts = [high, value - high] + ([rest] if rest.shape[0] else [])
        ref[:, channels:] = jnp.concatenate(parts, axis=0).astype(BF16)

    own, received = sizes(total_ref), sizes(received_ref)
    before = sizes(prefix_ref) if step else jnp.zeros_like(own)
    later = jnp.where(upper, own, received)
    put_sizes(total_out, own + received)
    put_sizes(prefix_out, before + jnp.where(upper, received, 0.0))
    for i in range(steps):
        at = slice(i * lanes, (i + 1) * lanes)
        rates = -jnp.exp(alog_ref[:, at]) * LOG2E
        mine, theirs = total_ref[:, at].astype(F32), received_ref[:, at].astype(F32)
        last, first = jnp.where(upper, mine, theirs), jnp.where(upper, theirs, mine)
        total_out[:, at] = (last + jnp.exp2(rates * later[i : i + 1]) * first).astype(BF16)
        if step:
            prefix = prefix_ref[:, at].astype(F32)
            further = prefix + jnp.exp2(rates * before[i : i + 1]) * theirs
        else:
            prefix, further = jnp.zeros_like(theirs), theirs
        prefix_out[:, at] = jnp.where(upper, further, prefix).astype(BF16)


def link(step, total, received, a_log, prefix):
    shape = jax.ShapeDtypeStruct(total.shape, BF16)
    args = [total, received, a_log] + ([prefix] if step else [])
    return pl.pallas_call(
        functools.partial(link_kernel, step),
        out_shape=(shape, shape),
        compiler_params=params(16),
        cost_estimate=cost(total.size * 2, total.size * 6),
        name="link",
    )(*args)


def finish_kernel(
    step, read_ref, cum_ref, z_ref, alog_ref, bc_ref, prefix_ref, *refs
):
    others, sizes, (out_ref, sum_ref, wide_ref, c_ref) = refs[:3], refs[3:7], refs[7:]
    tokens, lanes = z_ref.shape
    states = alog_ref.shape[0]
    at, steps = pl.program_id(0), pl.num_programs(0)

    @pl.when(at == 0)
    def _():
        spread_states(bc_ref[1], c_ref)
        for i, ref in enumerate(sizes):
            wide_ref[i * states : (i + 1) * states] = ref[...].astype(F32)

    rates = -jnp.exp(alog_ref[...]) * LOG2E

    def decay(i):
        row = i * states + at
        return jnp.exp2(rates * (wide_ref[pl.ds(row, 1)] + wide_ref[pl.ds(row + steps, 1)]))

    mine = lax.axis_index("seq") >> step
    ends = [ref[...].astype(F32) for ref in others]
    decays = [decay(i + 1) for i in range(3)]
    entering = jnp.zeros((states, lanes), F32)
    for group in range(3):
        partner = mine ^ group

        def chosen(values):
            return jnp.where(partner == 1, values[0], jnp.where(partner == 2, values[1], values[2]))

        further = chosen(decays) * entering + chosen(ends)
        entering = jnp.where(group < mine, further, entering)
    entering = prefix_ref[...].astype(F32) + decay(0) * entering

    def eight(g, carry):
        at = pl.multiple_of(g * 8, 8)
        cum8 = cum_ref[pl.ds(at, 8)]
        reads = []
        for i in range(8):
            kept = jnp.exp2(rates * cum8[i : i + 1]) * entering
            reads.append(state_sum(tiled_lanes(c_ref[at + i], lanes) * kept))
        sum_ref[pl.ds(at, 8)] = row_sums(reads)
        return carry

    lax.fori_loop(0, tokens // 8, eight, 0)
    z = z_ref[...].astype(F32)
    out_ref[...] = ((read_ref[...] + sum_ref[...]) * (z * jax.nn.sigmoid(z))).astype(BF16)


def finish(step, read, cum, z_gate, prefix, others, a_log, b_and_c):
    tokens, channels = z_gate.shape
    states = a_log.shape[0]
    lanes = prefix.shape[1] - channels

    def cut(rows):
        return pl.BlockSpec((rows, lanes), lambda i: (0, i))

    sizes = pl.BlockSpec((states, lanes), lambda i: (0, channels // lanes))
    return pl.pallas_call(
        functools.partial(finish_kernel, step),
        grid=(channels // lanes,),
        in_specs=[
            cut(tokens), cut(tokens), cut(tokens), cut(states),
            pl.BlockSpec(b_and_c.shape, lambda i: (0, 0, 0)),
            *[cut(states)] * 4,
            *[sizes] * 4,
        ],
        out_specs=cut(tokens),
        out_shape=jax.ShapeDtypeStruct((tokens, channels), BF16),
        scratch_shapes=[
            pltpu.VMEM((tokens, lanes), F32),
            pltpu.VMEM((4 * states, lanes), F32),
            pltpu.VMEM((tokens, states, 128), F32),
        ],
        compiler_params=params(40),
        cost_estimate=cost(
            tokens * channels * states * 5, tokens * channels * 12, tokens * channels * states
        ),
        name="finish",
    )(*in_hbm(read, cum, z_gate, a_log, b_and_c), *[prefix, *others] * 2)


def swapped(value, by):
    count = lax.axis_size("seq")
    return lax.ppermute(value, "seq", [(i, i ^ by) for i in range(count)])


def turned(value, axis, by):
    count = lax.axis_size(axis)
    return lax.ppermute(value, axis, [(i, (i + by) % count) for i in range(count)])


def turned_within(value, copies, by):
    count = lax.axis_size("seq")
    return lax.ppermute(
        value, "seq", [(i, i // copies * copies + (i + by) % copies) for i in range(count)]
    )


def exchanged(value, copies):
    count = lax.axis_size("seq")
    groups = [list(range(m, count, copies)) for m in range(copies)]
    return lax.all_to_all(
        value, "seq", split_axis=0, concat_axis=0, tiled=True, axis_index_groups=groups
    )


def after(value, *others):
    return lax.optimization_barrier((value, others))[0]


def local(
    x_in,
    z_gate,
    dt_low,
    dt_weight,
    dt_bias,
    a_log,
    conv_weight,
    conv_bias,
    d_skip,
    b_and_c,
    hidden,
    router,
    expert_ids,
    w_gate,
    w_down,
):
    blocks = lax.axis_size("seq")
    feature_parts = lax.axis_size("exp")
    tokens, features = hidden.shape
    experts = router.shape[1]
    copies = blocks // experts
    pack = packing(features)
    ids = expert_ids.T

    edge = x_in[tokens - (conv_weight.shape[0] - 1) :]
    edge = lax.ppermute(edge, "seq", [(i, i + 1) for i in range(blocks - 1)])
    outgoing, logits = route(ids, hidden, router.T, 1, pack)
    outgoing = after(outgoing, edge)
    arrived = exchanged(outgoing.reshape((experts,) + outgoing.shape[2:]), copies)

    read, cum, ends = scan(
        x_in, edge, dt_low, dt_weight, dt_bias, a_log, conv_weight, conv_bias, d_skip, b_and_c
    )
    arrived = after(arrived, ends)

    steps = blocks.bit_length() - 3
    total, prefix, received, step = ends, None, None, 0

    def advance(*marks):
        nonlocal total, prefix, received, step
        if step < steps:
            total, prefix = link(step, total, after(received, *marks), a_log, prefix)
            step += 1
            if step < steps:
                received = swapped(total, 1 << step)
            else:
                received = [swapped(total, q << step) for q in (1, 2, 3)]
        return prefix

    rows = [unpack(arrived, features, pack)]
    for d in range(1, copies):
        rows.append(turned_within(rows[0], copies, d))
    gated = []
    for part in rows:
        if gated:
            part = after(part, gated[-1][0])
            own = gate(part, w_gate, w_down, kept)
        else:
            own, kept, kept_down = gate(part, w_gate, w_down)
            own, received, logits = after((own, ends, logits), *rows[1:])
            received = swapped(received, 1)
            logits = [logits] + [turned(logits, "exp", d) for d in range(1, feature_parts)]
        if len(gated) == copies - 1:
            marks = [p for parts in gated for p in parts[1:]] + logits
            own = after(own, advance(own), *marks)
        gated.append([own] + [turned(own, "exp", d) for d in range(1, feature_parts)])
    made = []
    for parts in gated[1:] + gated[:1]:
        product = down(parts, w_down, kept_down, BF16 if len(made) < copies - 1 else F32)
        if not made:
            product = after(product, advance(product))
        made.append(product)
    while step < steps:
        advance()
    sums = made[-1:]
    for d in range(1, copies):
        sums.append(turned_within(made[d - 1], copies, -d))
    packed = after(pack_sum(sums, experts, pack), *received)
    back = exchanged(packed, copies)

    weights = blend_weights(ids, after(tuple(logits), packed), 1, pack)
    received = after(tuple(received), packed)
    mamba_out = finish(step, read, cum, z_gate, prefix, received, a_log, b_and_c)
    back = after(back, mamba_out)
    moe_out = combine(back, weights, tokens, features, pack)
    return mamba_out, moe_out


def solution(mesh):
    return jax.shard_map(
        local,
        mesh=mesh,
        in_specs=(
            P("seq", "exp"),
            P("seq", "exp"),
            P("seq", None),
            P(None, "exp"),
            P("exp"),
            P(None, "exp"),
            P(None, "exp"),
            P("exp"),
            P("exp"),
            P(None, None, "seq"),
            P("seq", "exp"),
            P("exp", None),
            P("seq", None),
            P("exp", "seq"),
            P("seq", "exp"),
        ),
        out_specs=(P("seq", "exp"), P("seq", "exp")),
        check_vma=False,
    )
```

```python
import functools
import math

import jax
import jax.numpy as jnp
from jax import lax
from jax.experimental import pallas as pl
from jax.experimental.pallas import tpu as pltpu
from jax.sharding import PartitionSpec as P

CAP = 18
MIB = 1 << 20
LOG2E = math.log2(math.e)
F32 = jnp.float32
BF16 = jnp.bfloat16


def params(limit):
    return pltpu.CompilerParams(vmem_limit_bytes=limit * MIB)


def cost(flops, moved, transcendentals=0):
    return pl.CostEstimate(
        flops=int(flops), bytes_accessed=int(moved), transcendentals=int(transcendentals)
    )


def in_hbm(*arrays):
    return [pltpu.with_memory_space_constraint(a, pltpu.HBM) for a in arrays]


def iota(shape, dim):
    return lax.broadcasted_iota(jnp.int32, shape, dim)


def dot(a, b):
    return jnp.dot(a, b, preferred_element_type=F32)


def dot_nt(a, b):
    return lax.dot_general(a, b, (((1,), (1,)), ((), ())), preferred_element_type=F32)


def packing(features):
    main = CAP // 16 * 16
    extra = CAP - main
    cuts = main // extra if extra and main % extra == 0 else 0
    if cuts and features % (cuts * 128) == 0:
        return main, extra, cuts, features // cuts
    return -(-CAP // 16) * 16, 0, 0, 0


def hits_and_slots(ids, experts):
    tokens = ids.shape[1]
    of = iota((experts, tokens), 0)
    hits = [(of == ids[k : k + 1]).astype(F32) for k in range(2)]
    before = (iota((tokens, tokens), 0) < iota((tokens, tokens), 1)).astype(BF16)
    earlier = dot((hits[0] + hits[1]).astype(BF16), before)
    slots = [jnp.sum(h * earlier, axis=0, keepdims=True).astype(jnp.int32) for h in hits]
    return hits, slots


def route_kernel(pack, ids_ref, hidden_ref, router_ref, out_ref, logits_ref):
    main, extra, cuts, width = pack
    experts, copies = out_ref.shape[:2]
    tokens, features = hidden_ref.shape
    ids = ids_ref[...]
    _, slots = hits_and_slots(ids, experts)
    hidden = hidden_ref[...]
    row = iota((experts * main, tokens), 0)
    picked = None
    for k in range(2):
        key = jnp.where(slots[k] < main, ids[k : k + 1] * main + slots[k], -1)
        hit = row == key
        picked = hit if picked is None else picked | hit
    packed = dot(picked.astype(BF16), hidden).astype(BF16)
    for e in range(experts):
        for m in range(copies):
            out_ref[e, m, :, :features] = packed[e * main : (e + 1) * main]
    if extra:
        picked = None
        for k in range(2):
            key = jnp.where(slots[k] >= main, ids[k : k + 1] * extra + slots[k] - main, -1)
            hit = row // cuts == key
            picked = hit if picked is None else picked | hit
        total = None
        for c in range(cuts):
            chosen = (picked & (row % cuts == c)).astype(BF16)
            part = dot(chosen, hidden[:, c * width : (c + 1) * width])
            total = part if total is None else total + part
        total = total.astype(BF16)
        for e in range(experts):
            for m in range(copies):
                out_ref[e, m, :, features:] = total[e * main : (e + 1) * main]
    logits_ref[...] = dot_nt(hidden, router_ref[...])


def route(ids, hidden, router, copies, pack):
    main, _, _, width = pack
    tokens, features = hidden.shape
    experts = router.shape[0]
    return pl.pallas_call(
        functools.partial(route_kernel, pack),
        out_shape=(
            jax.ShapeDtypeStruct((experts, copies, main, features + width), BF16),
            jax.ShapeDtypeStruct((tokens, experts), F32),
        ),
        compiler_params=params(40),
        cost_estimate=cost(2 * tokens * experts * main * features * 2, hidden.size * 8),
        name="route",
    )(*in_hbm(ids, hidden, router))


def weights_kernel(pack, copies, ids_ref, *refs):
    logits_refs, (main_ref, extra_ref, gates_ref) = refs[:-3], refs[-3:]
    main, extra, cuts, _ = pack
    tokens, experts = logits_refs[0].shape
    ids = ids_ref[...]
    hits, slots = hits_and_slots(ids, experts)
    eye = (iota((tokens, tokens), 0) == iota((tokens, tokens), 1)).astype(BF16)
    logits = logits_refs[0][...]
    for ref in logits_refs[1:]:
        logits = logits + ref[...]
    columns = [dot_nt(eye, h.astype(BF16)) for h in hits]
    picked = [jnp.sum(c * logits, axis=1, keepdims=True) for c in columns]
    expert = iota((tokens, experts), 1).astype(F32)
    total = experts * main
    col = iota((tokens, total), 1)
    for k in range(2):
        gate = jax.nn.sigmoid(picked[k] - picked[1 - k])
        gates_ref[k] = jnp.broadcast_to(gate, gates_ref.shape[1:])
        named = jnp.sum(columns[k] * expert, axis=1, keepdims=True).astype(jnp.int32)
        wide = jnp.broadcast_to(slots[k].astype(F32), (8, tokens)).astype(BF16)
        slot = dot_nt(eye, wide)[:, :1].astype(jnp.int32)
        mine = (col // main) ^ own_expert(copies) == named
        main_ref[k] = (mine & (col % main == slot)).astype(BF16)
        if extra:
            place = (col % main) // cuts + main
            extra_ref[k] = (mine & (place == slot)).astype(BF16)
        else:
            extra_ref[k] = jnp.zeros(extra_ref.shape[1:], BF16)


def blend_weights(ids, logits, copies, pack):
    tokens, experts = logits[0].shape
    total = experts * pack[0]
    return pl.pallas_call(
        functools.partial(weights_kernel, pack, copies),
        out_shape=(
            jax.ShapeDtypeStruct((2, tokens, total), BF16),
            jax.ShapeDtypeStruct((2, tokens, total), BF16),
            jax.ShapeDtypeStruct((2, tokens, 128), F32),
        ),
        compiler_params=params(40),
        cost_estimate=cost(2 * tokens * total * 16, tokens * total * 8),
        name="blend_weights",
    )(*in_hbm(ids), *logits)


ANYWHERE = pl.BlockSpec(memory_space=pl.ANY)
INSIDE = pl.BlockSpec(memory_space=pltpu.VMEM)
AHEAD = 6


def chunk_copy(from_ref, to_ref, sems, dim, chunk):
    def copy(i):
        at = pl.ds(pl.multiple_of(i * chunk, chunk), chunk)
        part = (slice(None), at) if dim else (at, slice(None))
        return pltpu.make_async_copy(from_ref.at[part], to_ref.at[part], sems.at[i])

    return copy, from_ref.shape[dim] // chunk


def streamed(stream, use, begin=None, begun=False, follow=None):
    copy, count = stream
    if not begun:
        for i in range(min(AHEAD, count)):
            copy(i).start()
    if begin is not None:
        begin()

    def step(i, carry):
        copy(i).wait()

        @pl.when(i + AHEAD < count)
        def _():
            copy(i + AHEAD).start()

        if follow is not None:
            later = i - max(count - AHEAD, 0)

            @pl.when((later >= 0) & (later < follow[1]))
            def _():
                follow[0](later).start()

        use(i)
        return carry

    lax.fori_loop(0, count, step, 0)


def gate_first_kernel(
    chunk, x_ref, w_ref, down_ref, out_ref, kept_ref, kept_down_ref, held_ref, kept_sems, sems, down_sems
):
    start, columns = kept_ref.shape[1], kept_down_ref.shape[1]
    one = chunk_copy(w_ref.at[:, :start], kept_ref, kept_sems, 1, chunk)
    two = chunk_copy(w_ref.at[:, start:], held_ref, sems, 1, chunk)
    copy, count = chunk_copy(
        down_ref.at[:, :columns], kept_down_ref, down_sems, 0, kept_down_ref.shape[0] // down_sems.shape[0]
    )
    streamed(one, gate_product(chunk, x_ref, kept_ref, out_ref, 0), follow=two)
    started = min(AHEAD, one[1])
    for i in range(started, min(AHEAD, two[1])):
        two[0](i).start()
    for i in range(count):
        copy(i).start()
    streamed(two, gate_product(chunk, x_ref, held_ref, out_ref, start), begun=True)
    for i in range(count):
        copy(i).wait()


def gate_product(chunk, x_ref, from_ref, out_ref, offset):
    def use(i):
        at = pl.ds(pl.multiple_of(i * chunk, chunk), chunk)
        to = pl.ds(pl.multiple_of(offset + i * chunk, chunk), chunk)
        out_ref[:, to] = dot(x_ref[...], from_ref[:, at]).astype(BF16)

    return use


def gate_next_kernel(chunk, x_ref, w_ref, kept_ref, out_ref, held_ref, sems):
    start = kept_ref.shape[1]
    kept = gate_product(chunk, x_ref, kept_ref, out_ref, 0)
    streamed(
        chunk_copy(w_ref.at[:, start:], held_ref, sems, 1, chunk),
        gate_product(chunk, x_ref, held_ref, out_ref, start),
        lambda: pl.loop(0, start // chunk)(kept),
    )


def gate(x, w_gate, w_down, kept=None):
    rows, features = x.shape
    amount = w_gate.shape[1]
    chunk = math.gcd(512, amount)
    half = amount // chunk // 2 * chunk
    out = jax.ShapeDtypeStruct((rows, amount), BF16)
    rest = [pltpu.VMEM((features, amount - half), BF16)]
    rest_sems = pltpu.SemaphoreType.DMA(((amount - half) // chunk,))
    hints = dict(
        compiler_params=params(20),
        cost_estimate=cost(2 * rows * features * amount, features * amount * 2),
        name="gate",
    )
    if kept is not None:
        return pl.pallas_call(
            functools.partial(gate_next_kernel, chunk),
            in_specs=[INSIDE, ANYWHERE, INSIDE],
            out_specs=INSIDE,
            out_shape=out,
            scratch_shapes=rest + [rest_sems],
            **hints,
        )(x, *in_hbm(w_gate), kept)
    return pl.pallas_call(
        functools.partial(gate_first_kernel, chunk),
        in_specs=[INSIDE, ANYWHERE, ANYWHERE],
        out_specs=(INSIDE, INSIDE, INSIDE),
        out_shape=(
            out,
            jax.ShapeDtypeStruct((features, half), BF16),
            jax.ShapeDtypeStruct((w_down.shape[0], w_down.shape[1] // 2), BF16),
        ),
        scratch_shapes=rest
        + [
            pltpu.SemaphoreType.DMA((half // chunk,)),
            rest_sems,
            pltpu.SemaphoreType.DMA((4,)),
        ],
        **hints,
    )(x, *in_hbm(w_gate, w_down))


def fill_acted(chunk, part_refs, acted_ref):
    def piece(i):
        at = pl.ds(pl.multiple_of(i * chunk, chunk), chunk)
        total = part_refs[0][:, at].astype(F32)
        for ref in part_refs[1:]:
            total = total + ref[:, at].astype(F32)
        acted_ref[:, at] = (total * jax.nn.sigmoid(total)).astype(BF16)

    pl.loop(0, acted_ref.shape[1] // chunk)(piece)


def down_kernel(chunk, *refs):
    part_refs, w_ref, kept_ref, out_ref, acted_ref, held_ref, sems = refs[:-6], *refs[-6:]
    start = kept_ref.shape[1]
    wide = math.gcd(512, start)

    def product(from_ref, offset, width):
        def use(i):
            at = pl.ds(pl.multiple_of(i * width, width), width)
            to = pl.ds(pl.multiple_of(offset + i * width, math.gcd(offset, width)), width)
            out_ref[:, to] = dot(acted_ref[...], from_ref[:, at]).astype(out_ref.dtype)

        return use

    def begin():
        fill_acted(math.gcd(512, acted_ref.shape[1]), part_refs, acted_ref)
        pl.loop(0, start // wide)(product(kept_ref, 0, wide))

    streamed(
        chunk_copy(w_ref.at[:, start:], held_ref, sems, 1, chunk),
        product(held_ref, start, chunk),
        begin,
    )


def down(parts, w_down, kept, dtype):
    rows, amount = parts[0].shape
    features = w_down.shape[1]
    rest = features - kept.shape[1]
    chunk = math.gcd(256, rest)
    return pl.pallas_call(
        functools.partial(down_kernel, chunk),
        in_specs=[INSIDE] * len(parts) + [ANYWHERE, INSIDE],
        out_specs=INSIDE,
        out_shape=jax.ShapeDtypeStruct((rows, features), dtype),
        scratch_shapes=[
            pltpu.VMEM((rows, amount), BF16),
            pltpu.VMEM((amount, rest), BF16),
            pltpu.SemaphoreType.DMA((rest // chunk,)),
        ],
        compiler_params=params(22),
        cost_estimate=cost(2 * rows * features * amount, features * amount * 2),
        name="down",
    )(*parts, *in_hbm(w_down), kept)


def unpack_kernel(pack, arrived_ref, out_ref):
    main, extra, cuts, width = pack
    sources = arrived_ref.shape[0]
    features = out_ref.shape[1]
    out_ref[: sources * main] = arrived_ref[:, :, :features].reshape(sources * main, features)
    if extra:
        folded = arrived_ref[:, :, features:].reshape(sources * main, width)
        shape = (sources * extra, sources * main)
        for c in range(cuts):
            pick = (iota(shape, 1) == iota(shape, 0) * cuts + c).astype(BF16)
            out_ref[sources * main :, c * width : (c + 1) * width] = dot(pick, folded).astype(BF16)


def unpack(arrived, features, pack):
    main, extra, _, _ = pack
    rows = arrived.shape[0] * (main + extra)
    return pl.pallas_call(
        functools.partial(unpack_kernel, pack),
        out_shape=jax.ShapeDtypeStruct((rows, features), BF16),
        compiler_params=params(24),
        cost_estimate=cost(arrived.size * 16, arrived.size * 4),
        name="unpack",
    )(arrived)


def own_expert(copies):
    return lax.axis_index("seq") // copies


def pack_kernel(pack, copies, count, *refs):
    main, extra, cuts, width = pack
    part_refs, out_refs = refs[:count], refs[count:]
    if extra:
        out_refs, folded_ref = out_refs[:-1], out_refs[-1]
    sources = len(out_refs)
    features = part_refs[0].shape[1]
    first = sources * main

    def total(rows, columns):
        value = part_refs[0][rows, columns].astype(F32)
        for ref in part_refs[1:]:
            value = value + ref[rows, columns].astype(F32)
        return value.astype(BF16)

    if extra:
        shape = (sources * main, sources * extra)
        folded = None
        for c in range(cuts):
            piece = total(slice(first, None), slice(c * width, (c + 1) * width))
            pick = (iota(shape, 0) == iota(shape, 1) * cuts + c).astype(BF16)
            part = dot(pick, piece)
            folded = part if folded is None else folded + part
        folded_ref[...] = folded
    own = own_expert(copies)
    for q, out_ref in enumerate(out_refs):
        rows = pl.ds(pl.multiple_of((own ^ q) * main, main), main)
        out_ref[:, :features] = total(rows, slice(0, features))
        if extra:
            out_ref[:, features:] = folded_ref[rows].astype(BF16)


def pack_sum(parts, sources, copies, pack):
    main, extra, _, width = pack
    features = parts[0].shape[1]
    return pl.pallas_call(
        functools.partial(pack_kernel, pack, copies, len(parts)),
        out_shape=[jax.ShapeDtypeStruct((main, features + width), BF16)] * sources,
        scratch_shapes=[pltpu.VMEM((sources * main, width), F32)] if extra else [],
        compiler_params=params(24),
        cost_estimate=cost(parts[0].size * 16, parts[0].size * 8),
        name="pack_sum",
    )(*parts)


def combine_kernel(pack, *refs):
    back_refs, (main_ref, extra_ref, gates_ref, out_ref) = refs[:-4], refs[-4:]
    main, extra, cuts, width = pack
    features = out_ref.shape[1]
    back = jnp.concatenate([ref[:, :features] for ref in back_refs], axis=0)
    folded = jnp.concatenate([ref[:, features:] for ref in back_refs], axis=0) if extra else None
    total = None
    for k in range(2):
        rows = dot(main_ref[k], back)
        if extra:
            chosen = extra_ref[k]
            at = iota(chosen.shape, 1) % cuts
            pieces = [
                dot(jnp.where(at == c, chosen, jnp.zeros_like(chosen)), folded) for c in range(cuts)
            ]
            rows = rows + jnp.concatenate(pieces, axis=1)
        weighed = rows * gates_ref[k][:, :1]
        total = weighed if total is None else total + weighed
    out_ref[...] = total.astype(BF16)


def combine(back, weights, tokens, features, pack):
    size = sum(b.size for b in back)
    return pl.pallas_call(
        functools.partial(combine_kernel, pack),
        out_shape=jax.ShapeDtypeStruct((tokens, features), BF16),
        compiler_params=params(40),
        cost_estimate=cost(4 * tokens * size, size * 2),
        name="combine",
    )(*back, *weights)


def spread_states(values, spread_ref):
    for t in range(spread_ref.shape[0]):
        spread_ref[t] = jnp.broadcast_to(values[:, t : t + 1], spread_ref.shape[1:])


def row_sums(parts):
    place = iota(parts[0].shape, 0)
    for stride in (4, 2, 1):
        low = place & stride == 0
        half = len(parts) // 2
        joined = []
        for a, b in zip(parts[:half], parts[half:]):
            kept = jnp.where(low, a, b)
            moved = jnp.where(low, b, a)
            if stride == 4:
                other = pltpu.roll(moved, 4, 0)
            else:
                other = jnp.where(low, pltpu.roll(moved, 8 - stride, 0), pltpu.roll(moved, stride, 0))
            joined.append(kept + other)
        parts = joined
    return parts[0]


def state_sum(value):
    total = value[:8]
    for at in range(8, value.shape[0], 8):
        total = total + value[at : at + 8]
    return total


def tiled_lanes(value, lanes):
    return jnp.concatenate([value] * (lanes // value.shape[1]), axis=1)


def scan_kernel(
    x_ref, edge_ref, low_ref, dtw_ref, dtb_ref, alog_ref, cw_ref, cb_ref, skip_ref, bc_ref,
    read_ref, cum_ref, ends_ref, padded, delta_ref, fed_ref, totals_ref, b_ref, c_ref,
):
    tokens, lanes = x_ref.shape
    taps = cw_ref.shape[0]
    states = alog_ref.shape[0]

    @pl.when(pl.program_id(0) == 0)
    def _():
        spread_states(bc_ref[0], b_ref)
        spread_states(bc_ref[1], c_ref)
        totals_ref[...] = jnp.zeros_like(totals_ref)

    padded[8:] = x_ref[...].astype(F32)
    padded[8 - (taps - 1) : 8] = edge_ref[...].astype(F32)
    conv = jnp.broadcast_to(cb_ref[...], (tokens, lanes))
    for k in range(taps):
        at = 8 - (taps - 1) + k
        conv = conv + cw_ref[k : k + 1] * padded[at : at + tokens]
    act = conv * jax.nn.sigmoid(conv)
    raw = dot(low_ref[...], dtw_ref[...]) + dtb_ref[...]
    delta = jnp.maximum(raw, 0.0) + jnp.log1p(jnp.exp(-jnp.abs(raw)))
    delta_ref[...] = delta
    fed_ref[...] = delta * act
    read_ref[...] = skip_ref[...] * act
    rates = -jnp.exp(alog_ref[...]) * LOG2E

    def eight(g, carry):
        state, running = carry
        at = pl.multiple_of(g * 8, 8)
        delta8 = delta_ref[pl.ds(at, 8)]
        fed8 = fed_ref[pl.ds(at, 8)]
        reads, sums = [], []
        for i in range(8):
            step = delta8[i : i + 1]
            running = running + step
            factor = jnp.exp2(rates * step)
            state = factor * state + tiled_lanes(b_ref[at + i], lanes) * fed8[i : i + 1]
            reads.append(state_sum(tiled_lanes(c_ref[at + i], lanes) * state))
            sums.append(running)
        read_ref[pl.ds(at, 8)] += row_sums(reads)
        cum_ref[pl.ds(at, 8)] = jnp.concatenate(sums, axis=0)
        return state, running

    state, running = lax.fori_loop(
        0, tokens // 8, eight, (jnp.zeros((states, lanes), F32), jnp.zeros((1, lanes), F32))
    )
    step, steps = pl.program_id(0), pl.num_programs(0)
    ends_ref[:, pl.ds(pl.multiple_of(step * lanes, lanes), lanes)] = state.astype(BF16)
    high = running.astype(BF16).astype(F32)
    totals_ref[pl.ds(step, 1)] = high
    totals_ref[pl.ds(steps + step, 1)] = running - high

    @pl.when(step == steps - 1)
    def _():
        ends_ref[:, ends_ref.shape[1] - lanes :] = totals_ref[...].astype(BF16)


def scan(x_in, edge, dt_low, dt_weight, dt_bias, a_log, conv_weight, conv_bias, d_skip, b_and_c):
    tokens, channels = x_in.shape
    states = a_log.shape[0]
    lanes = math.gcd(512, channels)

    def cut(rows):
        return pl.BlockSpec((rows, lanes), lambda i: (0, i))

    def whole(a):
        zeros = (0,) * a.ndim
        return pl.BlockSpec(a.shape, lambda i: zeros)

    return pl.pallas_call(
        scan_kernel,
        grid=(channels // lanes,),
        in_specs=[
            cut(tokens), cut(edge.shape[0]), whole(dt_low), cut(dt_weight.shape[0]), cut(1),
            cut(states), cut(conv_weight.shape[0]), cut(1), cut(1), whole(b_and_c),
        ],
        out_specs=(
            cut(tokens),
            cut(tokens),
            pl.BlockSpec((states, channels + lanes), lambda i: (0, 0)),
        ),
        out_shape=(
            pltpu.HBM((tokens, channels), F32),
            pltpu.HBM((tokens, channels), F32),
            jax.ShapeDtypeStruct((states, channels + lanes), BF16),
        ),
        scratch_shapes=[
            pltpu.VMEM((tokens + 8, lanes), F32),
            pltpu.VMEM((tokens, lanes), F32),
            pltpu.VMEM((tokens, lanes), F32),
            pltpu.VMEM((states, lanes), F32),
            pltpu.VMEM((tokens, states, 128), F32),
            pltpu.VMEM((tokens, states, 128), F32),
        ],
        compiler_params=params(40),
        cost_estimate=cost(
            tokens * channels * states * 8, tokens * channels * 12, tokens * channels * states
        ),
        name="scan",
    )(
        *in_hbm(x_in),
        edge,
        *in_hbm(
            dt_low, dt_weight, dt_bias[None], a_log, conv_weight, conv_bias[None], d_skip[None],
            b_and_c,
        ),
    )


def upper_half(step):
    return (lax.axis_index("seq") >> step) % 2 == 1


def link_kernel(step, *refs):
    total_ref, received_ref, alog_ref, prefix_ref = refs[:4] if step else (*refs[:3], None)
    total_out, prefix_out = refs[-2:]
    channels = alog_ref.shape[1]
    lanes = total_ref.shape[1] - channels
    steps = channels // lanes
    upper = upper_half(step)

    def sizes(ref):
        value = ref[:, channels:].astype(F32)
        return value[:steps] + value[steps : 2 * steps]

    def put_sizes(ref, value):
        high = value.astype(BF16).astype(F32)
        rest = jnp.zeros((ref.shape[0] - 2 * steps, lanes), F32)
        parts = [high, value - high] + ([rest] if rest.shape[0] else [])
        ref[:, channels:] = jnp.concatenate(parts, axis=0).astype(BF16)

    own, received = sizes(total_ref), sizes(received_ref)
    before = sizes(prefix_ref) if step else jnp.zeros_like(own)
    later = jnp.where(upper, own, received)
    put_sizes(total_out, own + received)
    put_sizes(prefix_out, before + jnp.where(upper, received, 0.0))
    for i in range(steps):
        at = slice(i * lanes, (i + 1) * lanes)
        rates = -jnp.exp(alog_ref[:, at]) * LOG2E
        mine, theirs = total_ref[:, at].astype(F32), received_ref[:, at].astype(F32)
        last, first = jnp.where(upper, mine, theirs), jnp.where(upper, theirs, mine)
        total_out[:, at] = (last + jnp.exp2(rates * later[i : i + 1]) * first).astype(BF16)
        if step:
            prefix = prefix_ref[:, at].astype(F32)
            further = prefix + jnp.exp2(rates * before[i : i + 1]) * theirs
        else:
            prefix, further = jnp.zeros_like(theirs), theirs
        prefix_out[:, at] = jnp.where(upper, further, prefix).astype(BF16)


def link(step, total, received, a_log, prefix):
    shape = jax.ShapeDtypeStruct(total.shape, BF16)
    args = [total, received, a_log] + ([prefix] if step else [])
    return pl.pallas_call(
        functools.partial(link_kernel, step),
        out_shape=(shape, shape),
        compiler_params=params(16),
        cost_estimate=cost(total.size * 2, total.size * 6),
        name="link",
    )(*args)


def finish_kernel(
    step, read_ref, cum_ref, z_ref, alog_ref, bc_ref, prefix_ref, *refs
):
    others, sizes, (out_ref, sum_ref, wide_ref, c_ref) = refs[:3], refs[3:7], refs[7:]
    tokens, lanes = z_ref.shape
    states = alog_ref.shape[0]
    at, steps = pl.program_id(0), pl.num_programs(0)

    @pl.when(at == 0)
    def _():
        spread_states(bc_ref[1], c_ref)
        for i, ref in enumerate(sizes):
            wide_ref[i * states : (i + 1) * states] = ref[...].astype(F32)

    rates = -jnp.exp(alog_ref[...]) * LOG2E

    def decay(i):
        row = i * states + at
        return jnp.exp2(rates * (wide_ref[pl.ds(row, 1)] + wide_ref[pl.ds(row + steps, 1)]))

    mine = lax.axis_index("seq") >> step
    ends = [ref[...].astype(F32) for ref in others]
    decays = [decay(i + 1) for i in range(3)]
    entering = jnp.zeros((states, lanes), F32)
    for group in range(3):
        partner = mine ^ group

        def chosen(values):
            return jnp.where(partner == 1, values[0], jnp.where(partner == 2, values[1], values[2]))

        further = chosen(decays) * entering + chosen(ends)
        entering = jnp.where(group < mine, further, entering)
    entering = prefix_ref[...].astype(F32) + decay(0) * entering

    def eight(g, carry):
        at = pl.multiple_of(g * 8, 8)
        cum8 = cum_ref[pl.ds(at, 8)]
        reads = []
        for i in range(8):
            kept = jnp.exp2(rates * cum8[i : i + 1]) * entering
            reads.append(state_sum(tiled_lanes(c_ref[at + i], lanes) * kept))
        sum_ref[pl.ds(at, 8)] = row_sums(reads)
        return carry

    lax.fori_loop(0, tokens // 8, eight, 0)
    z = z_ref[...].astype(F32)
    out_ref[...] = ((read_ref[...] + sum_ref[...]) * (z * jax.nn.sigmoid(z))).astype(BF16)


def finish(step, read, cum, z_gate, prefix, others, a_log, b_and_c):
    tokens, channels = z_gate.shape
    states = a_log.shape[0]
    lanes = prefix.shape[1] - channels

    def cut(rows):
        return pl.BlockSpec((rows, lanes), lambda i: (0, i))

    sizes = pl.BlockSpec((states, lanes), lambda i: (0, channels // lanes))
    return pl.pallas_call(
        functools.partial(finish_kernel, step),
        grid=(channels // lanes,),
        in_specs=[
            cut(tokens), cut(tokens), cut(tokens), cut(states),
            pl.BlockSpec(b_and_c.shape, lambda i: (0, 0, 0)),
            *[cut(states)] * 4,
            *[sizes] * 4,
        ],
        out_specs=cut(tokens),
        out_shape=jax.ShapeDtypeStruct((tokens, channels), BF16),
        scratch_shapes=[
            pltpu.VMEM((tokens, lanes), F32),
            pltpu.VMEM((4 * states, lanes), F32),
            pltpu.VMEM((tokens, states, 128), F32),
        ],
        compiler_params=params(40),
        cost_estimate=cost(
            tokens * channels * states * 5, tokens * channels * 12, tokens * channels * states
        ),
        name="finish",
    )(*in_hbm(read, cum, z_gate, a_log, b_and_c), *[prefix, *others] * 2)


def swapped(value, by):
    count = lax.axis_size("seq")
    return lax.ppermute(value, "seq", [(i, i ^ by) for i in range(count)])


def turned(value, axis, by):
    count = lax.axis_size(axis)
    return lax.ppermute(value, axis, [(i, (i + by) % count) for i in range(count)])


def turned_within(value, copies, by):
    count = lax.axis_size("seq")
    return lax.ppermute(
        value, "seq", [(i, i // copies * copies + (i + by) % copies) for i in range(count)]
    )


def exchanged(value, copies):
    count = lax.axis_size("seq")
    groups = [list(range(m, count, copies)) for m in range(copies)]
    return lax.all_to_all(
        value, "seq", split_axis=0, concat_axis=0, tiled=True, axis_index_groups=groups
    )


def after(value, *others):
    return lax.optimization_barrier((value, others))[0]


def local(
    x_in,
    z_gate,
    dt_low,
    dt_weight,
    dt_bias,
    a_log,
    conv_weight,
    conv_bias,
    d_skip,
    b_and_c,
    hidden,
    router,
    expert_ids,
    w_gate,
    w_down,
):
    blocks = lax.axis_size("seq")
    feature_parts = lax.axis_size("exp")
    tokens, features = hidden.shape
    experts = router.shape[1]
    copies = blocks // experts
    pack = packing(features)
    ids = expert_ids.T

    edge = x_in[tokens - (conv_weight.shape[0] - 1) :]
    edge = lax.ppermute(edge, "seq", [(i, i + 1) for i in range(blocks - 1)])
    outgoing, logits = route(ids, hidden, router.T, 1, pack)
    outgoing = after(outgoing, edge)
    arrived = exchanged(outgoing.reshape((experts,) + outgoing.shape[2:]), copies)

    read, cum, ends = scan(
        x_in, edge, dt_low, dt_weight, dt_bias, a_log, conv_weight, conv_bias, d_skip, b_and_c
    )
    arrived = after(arrived, ends)

    steps = blocks.bit_length() - 3
    total, prefix, received, step = ends, None, None, 0

    def advance(*marks):
        nonlocal total, prefix, received, step
        if step < steps:
            total, prefix = link(step, total, after(received, *marks), a_log, prefix)
            step += 1
            if step < steps:
                received = swapped(total, 1 << step)
            else:
                received = [swapped(total, q << step) for q in (1, 2, 3)]
        return prefix

    rows = [unpack(arrived, features, pack)]
    for d in range(1, copies):
        rows.append(turned_within(rows[0], copies, d))
    gated = []
    for part in rows:
        if gated:
            part = after(part, gated[-1][0])
            own = gate(part, w_gate, w_down, kept)
        else:
            own, kept, kept_down = gate(part, w_gate, w_down)
            own, received, logits = after((own, ends, logits), *rows[1:])
            received = swapped(received, 1)
            logits = [logits] + [turned(logits, "exp", d) for d in range(1, feature_parts)]
        if len(gated) == copies - 1:
            marks = [p for parts in gated for p in parts[1:]] + logits
            own = after(own, advance(own), *marks)
        gated.append([own] + [turned(own, "exp", d) for d in range(1, feature_parts)])
    made = []
    for parts in gated[1:] + gated[:1]:
        product = down(parts, w_down, kept_down, BF16 if len(made) < copies - 1 else F32)
        if not made:
            product = after(product, advance(product))
        made.append(product)
    while step < steps:
        advance()
    sums = made[-1:]
    for d in range(1, copies):
        sums.append(turned_within(made[d - 1], copies, -d))
    packed = after(tuple(pack_sum(sums, experts, copies, pack)), *received)
    back = [packed[0]] + [swapped(packed[q], q * copies) for q in range(1, experts)]

    weights = blend_weights(ids, after(tuple(logits), *packed), copies, pack)
    received = after(tuple(received), *packed)
    mamba_out = finish(step, read, cum, z_gate, prefix, received, a_log, b_and_c)
    back = after(tuple(back), mamba_out)
    moe_out = combine(back, weights, tokens, features, pack)
    return mamba_out, moe_out


def solution(mesh):
    return jax.shard_map(
        local,
        mesh=mesh,
        in_specs=(
            P("seq", "exp"),
            P("seq", "exp"),
            P("seq", None),
            P(None, "exp"),
            P("exp"),
            P(None, "exp"),
            P(None, "exp"),
            P("exp"),
            P("exp"),
            P(None, None, "seq"),
            P("seq", "exp"),
            P("exp", None),
            P("seq", None),
            P("exp", "seq"),
            P("seq", "exp"),
        ),
        out_specs=(P("seq", "exp"), P("seq", "exp")),
        check_vma=False,
    )
```

```python
import functools
import math

import jax
import jax.numpy as jnp
from jax import lax
from jax.experimental import pallas as pl
from jax.experimental.pallas import tpu as pltpu
from jax.sharding import PartitionSpec as P

CAP = 18
MIB = 1 << 20
LOG2E = math.log2(math.e)
F32 = jnp.float32
BF16 = jnp.bfloat16


def params(limit):
    return pltpu.CompilerParams(vmem_limit_bytes=limit * MIB)


def cost(flops, moved, transcendentals=0):
    return pl.CostEstimate(
        flops=int(flops), bytes_accessed=int(moved), transcendentals=int(transcendentals)
    )


def in_hbm(*arrays):
    return [pltpu.with_memory_space_constraint(a, pltpu.HBM) for a in arrays]


def iota(shape, dim):
    return lax.broadcasted_iota(jnp.int32, shape, dim)


def dot(a, b):
    return jnp.dot(a, b, preferred_element_type=F32)


def dot_nt(a, b):
    return lax.dot_general(a, b, (((1,), (1,)), ((), ())), preferred_element_type=F32)


def packing(features):
    main = CAP // 16 * 16
    extra = CAP - main
    cuts = main // extra if extra and main % extra == 0 else 0
    if cuts and features % (cuts * 128) == 0:
        return main, extra, cuts, features // cuts
    return -(-CAP // 16) * 16, 0, 0, 0


def hits_and_slots(ids, experts):
    tokens = ids.shape[1]
    of = iota((experts, tokens), 0)
    hits = [(of == ids[k : k + 1]).astype(F32) for k in range(2)]
    before = (iota((tokens, tokens), 0) < iota((tokens, tokens), 1)).astype(BF16)
    earlier = dot((hits[0] + hits[1]).astype(BF16), before)
    slots = [jnp.sum(h * earlier, axis=0, keepdims=True).astype(jnp.int32) for h in hits]
    return hits, slots


def route_kernel(pack, ids_ref, hidden_ref, router_ref, out_ref, logits_ref):
    main, extra, cuts, width = pack
    experts, copies = out_ref.shape[:2]
    tokens, features = hidden_ref.shape
    ids = ids_ref[...]
    _, slots = hits_and_slots(ids, experts)
    hidden = hidden_ref[...]
    row = iota((experts * main, tokens), 0)
    picked = None
    for k in range(2):
        key = jnp.where(slots[k] < main, ids[k : k + 1] * main + slots[k], -1)
        hit = row == key
        picked = hit if picked is None else picked | hit
    packed = dot(picked.astype(BF16), hidden).astype(BF16)
    for e in range(experts):
        for m in range(copies):
            out_ref[e, m, :, :features] = packed[e * main : (e + 1) * main]
    if extra:
        picked = None
        for k in range(2):
            key = jnp.where(slots[k] >= main, ids[k : k + 1] * extra + slots[k] - main, -1)
            hit = row // cuts == key
            picked = hit if picked is None else picked | hit
        total = None
        for c in range(cuts):
            chosen = (picked & (row % cuts == c)).astype(BF16)
            part = dot(chosen, hidden[:, c * width : (c + 1) * width])
            total = part if total is None else total + part
        total = total.astype(BF16)
        for e in range(experts):
            for m in range(copies):
                out_ref[e, m, :, features:] = total[e * main : (e + 1) * main]
    logits_ref[...] = dot_nt(hidden, router_ref[...])


def route(ids, hidden, router, copies, pack):
    main, _, _, width = pack
    tokens, features = hidden.shape
    experts = router.shape[0]
    return pl.pallas_call(
        functools.partial(route_kernel, pack),
        out_shape=(
            jax.ShapeDtypeStruct((experts, copies, main, features + width), BF16),
            jax.ShapeDtypeStruct((tokens, experts), F32),
        ),
        compiler_params=params(40),
        cost_estimate=cost(2 * tokens * experts * main * features * 2, hidden.size * 8),
        name="route",
    )(*in_hbm(ids, hidden, router))


def weights_kernel(pack, copies, ids_ref, *refs):
    logits_refs, (main_ref, extra_ref, gates_ref) = refs[:-3], refs[-3:]
    main, extra, cuts, _ = pack
    tokens, experts = logits_refs[0].shape
    ids = ids_ref[...]
    hits, slots = hits_and_slots(ids, experts)
    eye = (iota((tokens, tokens), 0) == iota((tokens, tokens), 1)).astype(BF16)
    logits = logits_refs[0][...]
    for ref in logits_refs[1:]:
        logits = logits + ref[...]
    columns = [dot_nt(eye, h.astype(BF16)) for h in hits]
    picked = [jnp.sum(c * logits, axis=1, keepdims=True) for c in columns]
    expert = iota((tokens, experts), 1).astype(F32)
    total = experts * main
    col = iota((tokens, total), 1)
    for k in range(2):
        gate = jax.nn.sigmoid(picked[k] - picked[1 - k])
        gates_ref[k] = jnp.broadcast_to(gate, gates_ref.shape[1:])
        named = jnp.sum(columns[k] * expert, axis=1, keepdims=True).astype(jnp.int32)
        wide = jnp.broadcast_to(slots[k].astype(F32), (8, tokens)).astype(BF16)
        slot = dot_nt(eye, wide)[:, :1].astype(jnp.int32)
        mine = (col // main) ^ own_expert(copies) == named
        main_ref[k] = (mine & (col % main == slot)).astype(BF16)
        if extra:
            place = (col % main) // cuts + main
            extra_ref[k] = (mine & (place == slot)).astype(BF16)
        else:
            extra_ref[k] = jnp.zeros(extra_ref.shape[1:], BF16)


def blend_weights(ids, logits, copies, pack):
    tokens, experts = logits[0].shape
    total = experts * pack[0]
    return pl.pallas_call(
        functools.partial(weights_kernel, pack, copies),
        out_shape=(
            jax.ShapeDtypeStruct((2, tokens, total), BF16),
            jax.ShapeDtypeStruct((2, tokens, total), BF16),
            jax.ShapeDtypeStruct((2, tokens, 128), F32),
        ),
        compiler_params=params(40),
        cost_estimate=cost(2 * tokens * total * 16, tokens * total * 8),
        name="blend_weights",
    )(*in_hbm(ids), *logits)


ANYWHERE = pl.BlockSpec(memory_space=pl.ANY)
INSIDE = pl.BlockSpec(memory_space=pltpu.VMEM)
AHEAD = 6


def chunk_copy(from_ref, to_ref, sems, dim, chunk):
    def copy(i):
        at = pl.ds(pl.multiple_of(i * chunk, chunk), chunk)
        part = (slice(None), at) if dim else (at, slice(None))
        return pltpu.make_async_copy(from_ref.at[part], to_ref.at[part], sems.at[i])

    return copy, from_ref.shape[dim] // chunk


def streamed(stream, use, begin=None, begun=False, follow=None):
    copy, count = stream
    if not begun:
        for i in range(min(AHEAD, count)):
            copy(i).start()
    if begin is not None:
        begin()

    def step(i, carry):
        copy(i).wait()

        @pl.when(i + AHEAD < count)
        def _():
            copy(i + AHEAD).start()

        if follow is not None:
            later = i - max(count - AHEAD, 0)

            @pl.when((later >= 0) & (later < follow[1]))
            def _():
                follow[0](later).start()

        use(i)
        return carry

    lax.fori_loop(0, count, step, 0)


def gate_first_kernel(
    chunk, x_ref, w_ref, down_ref, out_ref, kept_ref, kept_down_ref, held_ref, kept_sems, sems, down_sems
):
    start, columns = kept_ref.shape[1], kept_down_ref.shape[1]
    one = chunk_copy(w_ref.at[:, :start], kept_ref, kept_sems, 1, chunk)
    two = chunk_copy(w_ref.at[:, start:], held_ref, sems, 1, chunk)
    copy, count = chunk_copy(
        down_ref.at[:, :columns], kept_down_ref, down_sems, 0, kept_down_ref.shape[0] // down_sems.shape[0]
    )
    streamed(one, gate_product(chunk, x_ref, kept_ref, out_ref, 0), follow=two)
    started = min(AHEAD, one[1])
    for i in range(started, min(AHEAD, two[1])):
        two[0](i).start()
    for i in range(count):
        copy(i).start()
    streamed(two, gate_product(chunk, x_ref, held_ref, out_ref, start), begun=True)
    for i in range(count):
        copy(i).wait()


def gate_product(chunk, x_ref, from_ref, out_ref, offset):
    def use(i):
        at = pl.ds(pl.multiple_of(i * chunk, chunk), chunk)
        to = pl.ds(pl.multiple_of(offset + i * chunk, chunk), chunk)
        out_ref[:, to] = dot(x_ref[...], from_ref[:, at]).astype(BF16)

    return use


def gate_next_kernel(chunk, x_ref, w_ref, kept_ref, out_ref, held_ref, sems):
    start = kept_ref.shape[1]
    kept = gate_product(chunk, x_ref, kept_ref, out_ref, 0)
    streamed(
        chunk_copy(w_ref.at[:, start:], held_ref, sems, 1, chunk),
        gate_product(chunk, x_ref, held_ref, out_ref, start),
        lambda: pl.loop(0, start // chunk)(kept),
    )


def gate(x, w_gate, w_down, kept=None):
    rows, features = x.shape
    amount = w_gate.shape[1]
    chunk = math.gcd(512, amount)
    half = amount // chunk // 2 * chunk
    out = jax.ShapeDtypeStruct((rows, amount), BF16)
    rest = [pltpu.VMEM((features, amount - half), BF16)]
    rest_sems = pltpu.SemaphoreType.DMA(((amount - half) // chunk,))
    hints = dict(
        compiler_params=params(20),
        cost_estimate=cost(2 * rows * features * amount, features * amount * 2),
        name="gate",
    )
    if kept is not None:
        return pl.pallas_call(
            functools.partial(gate_next_kernel, chunk),
            in_specs=[INSIDE, ANYWHERE, INSIDE],
            out_specs=INSIDE,
            out_shape=out,
            scratch_shapes=rest + [rest_sems],
            **hints,
        )(x, *in_hbm(w_gate), kept)
    return pl.pallas_call(
        functools.partial(gate_first_kernel, chunk),
        in_specs=[INSIDE, ANYWHERE, ANYWHERE],
        out_specs=(INSIDE, INSIDE, INSIDE),
        out_shape=(
            out,
            jax.ShapeDtypeStruct((features, half), BF16),
            jax.ShapeDtypeStruct((w_down.shape[0], w_down.shape[1] // 2), BF16),
        ),
        scratch_shapes=rest
        + [
            pltpu.SemaphoreType.DMA((half // chunk,)),
            rest_sems,
            pltpu.SemaphoreType.DMA((4,)),
        ],
        **hints,
    )(x, *in_hbm(w_gate, w_down))


def fill_acted(chunk, part_refs, acted_ref):
    def piece(i):
        at = pl.ds(pl.multiple_of(i * chunk, chunk), chunk)
        total = part_refs[0][:, at].astype(F32)
        for ref in part_refs[1:]:
            total = total + ref[:, at].astype(F32)
        acted_ref[:, at] = (total * jax.nn.sigmoid(total)).astype(BF16)

    pl.loop(0, acted_ref.shape[1] // chunk)(piece)


def down_kernel(chunk, *refs):
    part_refs, w_ref, kept_ref, out_ref, acted_ref, held_ref, sems = refs[:-6], *refs[-6:]
    start = kept_ref.shape[1]
    wide = math.gcd(512, start)

    def product(from_ref, offset, width):
        def use(i):
            at = pl.ds(pl.multiple_of(i * width, width), width)
            to = pl.ds(pl.multiple_of(offset + i * width, math.gcd(offset, width)), width)
            out_ref[:, to] = dot(acted_ref[...], from_ref[:, at]).astype(out_ref.dtype)

        return use

    def begin():
        fill_acted(math.gcd(512, acted_ref.shape[1]), part_refs, acted_ref)
        pl.loop(0, start // wide)(product(kept_ref, 0, wide))

    streamed(
        chunk_copy(w_ref.at[:, start:], held_ref, sems, 1, chunk),
        product(held_ref, start, chunk),
        begin,
    )


def down(parts, w_down, kept, dtype):
    rows, amount = parts[0].shape
    features = w_down.shape[1]
    rest = features - kept.shape[1]
    chunk = math.gcd(256, rest)
    return pl.pallas_call(
        functools.partial(down_kernel, chunk),
        in_specs=[INSIDE] * len(parts) + [ANYWHERE, INSIDE],
        out_specs=INSIDE,
        out_shape=jax.ShapeDtypeStruct((rows, features), dtype),
        scratch_shapes=[
            pltpu.VMEM((rows, amount), BF16),
            pltpu.VMEM((amount, rest), BF16),
            pltpu.SemaphoreType.DMA((rest // chunk,)),
        ],
        compiler_params=params(22),
        cost_estimate=cost(2 * rows * features * amount, features * amount * 2),
        name="down",
    )(*parts, *in_hbm(w_down), kept)


def unpack_kernel(pack, arrived_ref, out_ref):
    main, extra, cuts, width = pack
    sources = arrived_ref.shape[0]
    features = out_ref.shape[1]
    out_ref[: sources * main] = arrived_ref[:, :, :features].reshape(sources * main, features)
    if extra:
        folded = arrived_ref[:, :, features:].reshape(sources * main, width)
        shape = (sources * extra, sources * main)
        for c in range(cuts):
            pick = (iota(shape, 1) == iota(shape, 0) * cuts + c).astype(BF16)
            out_ref[sources * main :, c * width : (c + 1) * width] = dot(pick, folded).astype(BF16)


def unpack(arrived, features, pack):
    main, extra, _, _ = pack
    rows = arrived.shape[0] * (main + extra)
    return pl.pallas_call(
        functools.partial(unpack_kernel, pack),
        out_shape=jax.ShapeDtypeStruct((rows, features), BF16),
        compiler_params=params(24),
        cost_estimate=cost(arrived.size * 16, arrived.size * 4),
        name="unpack",
    )(arrived)


def own_expert(copies):
    return lax.axis_index("seq") // copies


def pack_kernel(pack, copies, count, *refs):
    main, extra, cuts, width = pack
    part_refs, out_refs = refs[:count], refs[count:]
    if extra:
        out_refs, folded_ref = out_refs[:-1], out_refs[-1]
    sources = len(out_refs)
    features = part_refs[0].shape[1]
    first = sources * main

    def total(rows, columns):
        value = part_refs[0][rows, columns].astype(F32)
        for ref in part_refs[1:]:
            value = value + ref[rows, columns].astype(F32)
        return value.astype(BF16)

    if extra:
        shape = (sources * main, sources * extra)
        folded = None
        for c in range(cuts):
            piece = total(slice(first, None), slice(c * width, (c + 1) * width))
            pick = (iota(shape, 0) == iota(shape, 1) * cuts + c).astype(BF16)
            part = dot(pick, piece)
            folded = part if folded is None else folded + part
        folded_ref[...] = folded
    own = own_expert(copies)
    for q, out_ref in enumerate(out_refs):
        rows = pl.ds(pl.multiple_of((own ^ q) * main, main), main)
        out_ref[:, :features] = total(rows, slice(0, features))
        if extra:
            out_ref[:, features:] = folded_ref[rows].astype(BF16)


def pack_sum(parts, sources, copies, pack):
    main, extra, _, width = pack
    features = parts[0].shape[1]
    return pl.pallas_call(
        functools.partial(pack_kernel, pack, copies, len(parts)),
        out_shape=[jax.ShapeDtypeStruct((main, features + width), BF16)] * sources,
        scratch_shapes=[pltpu.VMEM((sources * main, width), F32)] if extra else [],
        compiler_params=params(24),
        cost_estimate=cost(parts[0].size * 16, parts[0].size * 8),
        name="pack_sum",
    )(*parts)


def combine_kernel(pack, *refs):
    back_refs, (main_ref, extra_ref, gates_ref, out_ref) = refs[:-4], refs[-4:]
    main, extra, cuts, width = pack
    features = out_ref.shape[1]
    back = jnp.concatenate([ref[:, :features] for ref in back_refs], axis=0)
    folded = jnp.concatenate([ref[:, features:] for ref in back_refs], axis=0) if extra else None
    total = None
    for k in range(2):
        rows = dot(main_ref[k], back)
        if extra:
            chosen = extra_ref[k]
            at = iota(chosen.shape, 1) % cuts
            pieces = [
                dot(jnp.where(at == c, chosen, jnp.zeros_like(chosen)), folded) for c in range(cuts)
            ]
            rows = rows + jnp.concatenate(pieces, axis=1)
        weighed = rows * gates_ref[k][:, :1]
        total = weighed if total is None else total + weighed
    out_ref[...] = total.astype(BF16)


def combine(back, weights, tokens, features, pack):
    size = sum(b.size for b in back)
    return pl.pallas_call(
        functools.partial(combine_kernel, pack),
        out_shape=jax.ShapeDtypeStruct((tokens, features), BF16),
        compiler_params=params(40),
        cost_estimate=cost(4 * tokens * size, size * 2),
        name="combine",
    )(*back, *weights)


def spread_states(values, spread_ref):
    for t in range(spread_ref.shape[0]):
        spread_ref[t] = jnp.broadcast_to(values[:, t : t + 1], spread_ref.shape[1:])


def row_sums(parts):
    place = iota(parts[0].shape, 0)
    for stride in (4, 2, 1):
        low = place & stride == 0
        half = len(parts) // 2
        joined = []
        for a, b in zip(parts[:half], parts[half:]):
            kept = jnp.where(low, a, b)
            moved = jnp.where(low, b, a)
            if stride == 4:
                other = pltpu.roll(moved, 4, 0)
            else:
                other = jnp.where(low, pltpu.roll(moved, 8 - stride, 0), pltpu.roll(moved, stride, 0))
            joined.append(kept + other)
        parts = joined
    return parts[0]


def state_sum(value):
    total = value[:8]
    for at in range(8, value.shape[0], 8):
        total = total + value[at : at + 8]
    return total


def tiled_lanes(value, lanes):
    return jnp.concatenate([value] * (lanes // value.shape[1]), axis=1)


def scan_kernel(
    x_ref, edge_ref, low_ref, dtw_ref, dtb_ref, alog_ref, cw_ref, cb_ref, skip_ref, bc_ref,
    read_ref, cum_ref, ends_ref, padded, delta_ref, fed_ref, totals_ref, b_ref, c_ref,
):
    tokens, lanes = x_ref.shape
    taps = cw_ref.shape[0]
    states = alog_ref.shape[0]

    @pl.when(pl.program_id(0) == 0)
    def _():
        spread_states(bc_ref[0], b_ref)
        spread_states(bc_ref[1], c_ref)
        totals_ref[...] = jnp.zeros_like(totals_ref)

    padded[8:] = x_ref[...].astype(F32)
    padded[8 - (taps - 1) : 8] = edge_ref[...].astype(F32)
    conv = jnp.broadcast_to(cb_ref[...], (tokens, lanes))
    for k in range(taps):
        at = 8 - (taps - 1) + k
        conv = conv + cw_ref[k : k + 1] * padded[at : at + tokens]
    act = conv * jax.nn.sigmoid(conv)
    raw = dot(low_ref[...], dtw_ref[...]) + dtb_ref[...]
    delta = jnp.maximum(raw, 0.0) + jnp.log1p(jnp.exp(-jnp.abs(raw)))
    delta_ref[...] = delta
    fed_ref[...] = delta * act
    read_ref[...] = skip_ref[...] * act
    rates = -jnp.exp(alog_ref[...]) * LOG2E

    def eight(g, carry):
        state, running = carry
        at = pl.multiple_of(g * 8, 8)
        delta8 = delta_ref[pl.ds(at, 8)]
        fed8 = fed_ref[pl.ds(at, 8)]
        reads, sums = [], []
        for i in range(8):
            step = delta8[i : i + 1]
            running = running + step
            factor = jnp.exp2(rates * step)
            state = factor * state + tiled_lanes(b_ref[at + i], lanes) * fed8[i : i + 1]
            reads.append(state_sum(tiled_lanes(c_ref[at + i], lanes) * state))
            sums.append(running)
        read_ref[pl.ds(at, 8)] += row_sums(reads)
        cum_ref[pl.ds(at, 8)] = jnp.concatenate(sums, axis=0)
        return state, running

    state, running = lax.fori_loop(
        0, tokens // 8, eight, (jnp.zeros((states, lanes), F32), jnp.zeros((1, lanes), F32))
    )
    step, steps = pl.program_id(0), pl.num_programs(0)
    ends_ref[:, pl.ds(pl.multiple_of(step * lanes, lanes), lanes)] = state.astype(BF16)
    high = running.astype(BF16).astype(F32)
    totals_ref[pl.ds(step, 1)] = high
    totals_ref[pl.ds(steps + step, 1)] = running - high

    @pl.when(step == steps - 1)
    def _():
        ends_ref[:, ends_ref.shape[1] - lanes :] = totals_ref[...].astype(BF16)


def scan(x_in, edge, dt_low, dt_weight, dt_bias, a_log, conv_weight, conv_bias, d_skip, b_and_c):
    tokens, channels = x_in.shape
    states = a_log.shape[0]
    lanes = math.gcd(512, channels)

    def cut(rows):
        return pl.BlockSpec((rows, lanes), lambda i: (0, i))

    def whole(a):
        zeros = (0,) * a.ndim
        return pl.BlockSpec(a.shape, lambda i: zeros)

    return pl.pallas_call(
        scan_kernel,
        grid=(channels // lanes,),
        in_specs=[
            cut(tokens), cut(edge.shape[0]), whole(dt_low), cut(dt_weight.shape[0]), cut(1),
            cut(states), cut(conv_weight.shape[0]), cut(1), cut(1), whole(b_and_c),
        ],
        out_specs=(
            cut(tokens),
            cut(tokens),
            pl.BlockSpec((states, channels + lanes), lambda i: (0, 0)),
        ),
        out_shape=(
            pltpu.HBM((tokens, channels), F32),
            pltpu.HBM((tokens, channels), F32),
            jax.ShapeDtypeStruct((states, channels + lanes), BF16),
        ),
        scratch_shapes=[
            pltpu.VMEM((tokens + 8, lanes), F32),
            pltpu.VMEM((tokens, lanes), F32),
            pltpu.VMEM((tokens, lanes), F32),
            pltpu.VMEM((states, lanes), F32),
            pltpu.VMEM((tokens, states, 128), F32),
            pltpu.VMEM((tokens, states, 128), F32),
        ],
        compiler_params=params(40),
        cost_estimate=cost(
            tokens * channels * states * 8, tokens * channels * 12, tokens * channels * states
        ),
        name="scan",
    )(
        *in_hbm(x_in),
        edge,
        *in_hbm(
            dt_low, dt_weight, dt_bias[None], a_log, conv_weight, conv_bias[None], d_skip[None],
            b_and_c,
        ),
    )


def upper_half(step):
    return (lax.axis_index("seq") >> step) % 2 == 1


def link_kernel(step, *refs):
    total_ref, received_ref, alog_ref, prefix_ref = refs[:4] if step else (*refs[:3], None)
    total_out, prefix_out = refs[-2:]
    channels = alog_ref.shape[1]
    lanes = total_ref.shape[1] - channels
    steps = channels // lanes
    upper = upper_half(step)

    def sizes(ref):
        value = ref[:, channels:].astype(F32)
        return value[:steps] + value[steps : 2 * steps]

    def put_sizes(ref, value):
        high = value.astype(BF16).astype(F32)
        rest = jnp.zeros((ref.shape[0] - 2 * steps, lanes), F32)
        parts = [high, value - high] + ([rest] if rest.shape[0] else [])
        ref[:, channels:] = jnp.concatenate(parts, axis=0).astype(BF16)

    own, received = sizes(total_ref), sizes(received_ref)
    before = sizes(prefix_ref) if step else jnp.zeros_like(own)
    later = jnp.where(upper, own, received)
    put_sizes(total_out, own + received)
    put_sizes(prefix_out, before + jnp.where(upper, received, 0.0))
    for i in range(steps):
        at = slice(i * lanes, (i + 1) * lanes)
        rates = -jnp.exp(alog_ref[:, at]) * LOG2E
        mine, theirs = total_ref[:, at].astype(F32), received_ref[:, at].astype(F32)
        last, first = jnp.where(upper, mine, theirs), jnp.where(upper, theirs, mine)
        total_out[:, at] = (last + jnp.exp2(rates * later[i : i + 1]) * first).astype(BF16)
        if step:
            prefix = prefix_ref[:, at].astype(F32)
            further = prefix + jnp.exp2(rates * before[i : i + 1]) * theirs
        else:
            prefix, further = jnp.zeros_like(theirs), theirs
        prefix_out[:, at] = jnp.where(upper, further, prefix).astype(BF16)


def link(step, total, received, a_log, prefix):
    shape = jax.ShapeDtypeStruct(total.shape, BF16)
    args = [total, received, a_log] + ([prefix] if step else [])
    return pl.pallas_call(
        functools.partial(link_kernel, step),
        out_shape=(shape, shape),
        compiler_params=params(16),
        cost_estimate=cost(total.size * 2, total.size * 6),
        name="link",
    )(*args)


def finish_kernel(
    step, read_ref, cum_ref, z_ref, alog_ref, bc_ref, prefix_ref, *refs
):
    others, sizes, (out_ref, sum_ref, wide_ref, c_ref) = refs[:3], refs[3:7], refs[7:]
    tokens, lanes = z_ref.shape
    states = alog_ref.shape[0]
    at, steps = pl.program_id(0), pl.num_programs(0)

    @pl.when(at == 0)
    def _():
        spread_states(bc_ref[1], c_ref)
        for i, ref in enumerate(sizes):
            wide_ref[i * states : (i + 1) * states] = ref[...].astype(F32)

    rates = -jnp.exp(alog_ref[...]) * LOG2E

    def decay(i):
        row = i * states + at
        return jnp.exp2(rates * (wide_ref[pl.ds(row, 1)] + wide_ref[pl.ds(row + steps, 1)]))

    mine = lax.axis_index("seq") >> step
    ends = [ref[...].astype(F32) for ref in others]
    decays = [decay(i + 1) for i in range(3)]
    entering = jnp.zeros((states, lanes), F32)
    for group in range(3):
        partner = mine ^ group

        def chosen(values):
            return jnp.where(partner == 1, values[0], jnp.where(partner == 2, values[1], values[2]))

        further = chosen(decays) * entering + chosen(ends)
        entering = jnp.where(group < mine, further, entering)
    entering = prefix_ref[...].astype(F32) + decay(0) * entering

    def eight(g, carry):
        at = pl.multiple_of(g * 8, 8)
        cum8 = cum_ref[pl.ds(at, 8)]
        reads = []
        for i in range(8):
            kept = jnp.exp2(rates * cum8[i : i + 1]) * entering
            reads.append(state_sum(tiled_lanes(c_ref[at + i], lanes) * kept))
        sum_ref[pl.ds(at, 8)] = row_sums(reads)
        return carry

    lax.fori_loop(0, tokens // 8, eight, 0)
    z = z_ref[...].astype(F32)
    out_ref[...] = ((read_ref[...] + sum_ref[...]) * (z * jax.nn.sigmoid(z))).astype(BF16)


def finish(step, read, cum, z_gate, prefix, others, a_log, b_and_c):
    tokens, channels = z_gate.shape
    states = a_log.shape[0]
    lanes = prefix.shape[1] - channels

    def cut(rows):
        return pl.BlockSpec((rows, lanes), lambda i: (0, i))

    sizes = pl.BlockSpec((states, lanes), lambda i: (0, channels // lanes))
    return pl.pallas_call(
        functools.partial(finish_kernel, step),
        grid=(channels // lanes,),
        in_specs=[
            cut(tokens), cut(tokens), cut(tokens), cut(states),
            pl.BlockSpec(b_and_c.shape, lambda i: (0, 0, 0)),
            *[cut(states)] * 4,
            *[sizes] * 4,
        ],
        out_specs=cut(tokens),
        out_shape=jax.ShapeDtypeStruct((tokens, channels), BF16),
        scratch_shapes=[
            pltpu.VMEM((tokens, lanes), F32),
            pltpu.VMEM((4 * states, lanes), F32),
            pltpu.VMEM((tokens, states, 128), F32),
        ],
        compiler_params=params(40),
        cost_estimate=cost(
            tokens * channels * states * 5, tokens * channels * 12, tokens * channels * states
        ),
        name="finish",
    )(*in_hbm(read, cum, z_gate, a_log, b_and_c), *[prefix, *others] * 2)


def swapped(value, by):
    count = lax.axis_size("seq")
    return lax.ppermute(value, "seq", [(i, i ^ by) for i in range(count)])


def turned(value, axis, by):
    count = lax.axis_size(axis)
    return lax.ppermute(value, axis, [(i, (i + by) % count) for i in range(count)])


def turned_within(value, copies, by):
    count = lax.axis_size("seq")
    return lax.ppermute(
        value, "seq", [(i, i // copies * copies + (i + by) % copies) for i in range(count)]
    )


def exchanged(value, copies):
    count = lax.axis_size("seq")
    groups = [list(range(m, count, copies)) for m in range(copies)]
    return lax.all_to_all(
        value, "seq", split_axis=0, concat_axis=0, tiled=True, axis_index_groups=groups
    )


def after(value, *others):
    return lax.optimization_barrier((value, others))[0]


def local(
    x_in,
    z_gate,
    dt_low,
    dt_weight,
    dt_bias,
    a_log,
    conv_weight,
    conv_bias,
    d_skip,
    b_and_c,
    hidden,
    router,
    expert_ids,
    w_gate,
    w_down,
):
    blocks = lax.axis_size("seq")
    feature_parts = lax.axis_size("exp")
    tokens, features = hidden.shape
    experts = router.shape[1]
    copies = blocks // experts
    pack = packing(features)
    ids = expert_ids.T

    edge = x_in[tokens - (conv_weight.shape[0] - 1) :]
    edge = lax.ppermute(edge, "seq", [(i, i + 1) for i in range(blocks - 1)])
    outgoing, logits = route(ids, hidden, router.T, 1, pack)
    outgoing = after(outgoing, edge)
    arrived = exchanged(outgoing.reshape((experts,) + outgoing.shape[2:]), copies)

    read, cum, ends = scan(
        x_in, edge, dt_low, dt_weight, dt_bias, a_log, conv_weight, conv_bias, d_skip, b_and_c
    )
    arrived = after(arrived, ends)

    steps = blocks.bit_length() - 3
    total, prefix, received, step = ends, None, None, 0

    def advance(*marks):
        nonlocal total, prefix, received, step
        if step < steps:
            total, prefix = link(step, total, after(received, *marks), a_log, prefix)
            step += 1
            if step < steps:
                received = swapped(total, 1 << step)
            else:
                received = [swapped(total, q << step) for q in (1, 2, 3)]
        return prefix

    rows = [unpack(arrived, features, pack)]
    for d in range(1, copies):
        rows.append(turned_within(rows[0], copies, d))
    gated = []
    for part in rows:
        if gated:
            part = after(part, gated[-1][0])
            own = gate(part, w_gate, w_down, kept)
        else:
            own, kept, kept_down = gate(part, w_gate, w_down)
            own, received, logits = after((own, ends, logits), *rows[1:])
            received = swapped(received, 1)
            logits = [logits] + [turned(logits, "exp", d) for d in range(1, feature_parts)]
        if len(gated) == copies - 1:
            marks = [p for parts in gated for p in parts[1:]] + logits
            own = after(own, advance(own), *marks)
        gated.append([own] + [turned(own, "exp", d) for d in range(1, feature_parts)])
    made = []
    for parts in gated[1:] + gated[:1]:
        product = down(parts, w_down, kept_down, BF16 if len(made) < copies - 1 else F32)
        if not made:
            product = after(product, advance(product))
        made.append(product)
    while step < steps:
        advance()
    weights = blend_weights(ids, after(tuple(logits), made[-1]), copies, pack)
    sums = [after(made[-1], *weights)]
    for d in range(1, copies):
        sums.append(turned_within(made[d - 1], copies, -d))
    packed = after(tuple(pack_sum(sums, experts, copies, pack)), *received)
    back = [packed[0]] + [swapped(packed[q], q * copies) for q in range(1, experts)]

    received = after(tuple(received), *packed)
    mamba_out = finish(step, read, cum, z_gate, prefix, received, a_log, b_and_c)
    back = after(tuple(back), mamba_out)
    moe_out = combine(back, weights, tokens, features, pack)
    return mamba_out, moe_out


def solution(mesh):
    return jax.shard_map(
        local,
        mesh=mesh,
        in_specs=(
            P("seq", "exp"),
            P("seq", "exp"),
            P("seq", None),
            P(None, "exp"),
            P("exp"),
            P(None, "exp"),
            P(None, "exp"),
            P("exp"),
            P("exp"),
            P(None, None, "seq"),
            P("seq", "exp"),
            P("exp", None),
            P("seq", None),
            P("exp", "seq"),
            P("seq", "exp"),
        ),
        out_specs=(P("seq", "exp"), P("seq", "exp")),
        check_vma=False,
    )
```
